128 devices in a mesh: mode: 8 (over x, core), mer: 16 (over z, y).
Axes of the slice: x: 4, y: 4, z: 4, core: 2. Of those that a mesh axis runs over, the one named last changes fastest.
Arguments:
- cotangent: float32 [9, 9, 262144], P(None, None, ('mer', 'mode')), may hold values from -6 to 6
- checkpoint: float32 [9, 9, 262144], P(None, None, ('mer', 'mode')), may hold values from -0.25 to 0.25
- mass: float32 [9, 9, 256], P(None, None, 'mer'), may hold values from 0.5 to 2
- inv_radius_sq: float32 [9, 9, 256], P(None, None, 'mer'), may hold values from 0.25 to 4
- derivative: float32 [9, 9], replicated, may hold values from -2 to 2
Outputs:
- sensitivity: float32 [9, 9, 262144], P(None, None, ('mer', 'mode'))
The draws below stay inside these ranges and needn't reach their ends.
All inputs are finite; a program needn't handle non-finite values.
Results may differ from the reference program's by a relative error of at most 0.0001.
Values sent between devices are 32-bit elements; how exact they have to be, the bound alone decides.
A program may use at most 128 MiB of HBM per device.

```python
import math
import jax
import jax.numpy as jnp
from jax import lax

NODE = 9
MODES = 512
RADIAL = 8
AXIAL_DEV = 2
ITERS = 4
ELEMENTS = 256
AXIAL = 32
MODES_DEV = 64
PLANES = 1024
COEFFS = 262144
N_MODE = 8
N_MER = 16


def levels(key, shape, split, least, top_value):
    gain, own = 1.0, jax.random.fold_in(key, 6)
    for axis_at, parts in split:
        draws = jnp.exp(jax.random.uniform(jax.random.fold_in(own, axis_at), (parts,), jnp.float32, least / len(split), top_value / len(split)))
        gain = gain * jnp.repeat(draws, shape[axis_at] // parts).reshape([-1 if axis == axis_at else 1 for axis in range(len(shape))])
    return gain


def bell_draw(stream_key, shape, width, reach, pieces=(), kind=jnp.bfloat16):
    values = jax.random.normal(stream_key, shape, jnp.float32) * width
    if len(pieces) > 0:
        values = levels(stream_key, shape, pieces, -0.22, 0.18) * values
    return jnp.clip(values, min=-reach, max=reach).astype(kind)


def setup_inputs(seed: int = 0) -> dict:
    key_list = jax.random.split(jax.random.key(seed), 6)
    return {
        "cotangent": bell_draw(key_list[0], (NODE, NODE, COEFFS), 1.0, 6.0, ((2, 128),), jnp.float32),
        "checkpoint": bell_draw(key_list[1], (NODE, NODE, COEFFS), MODES ** -0.5, 0.25, ((2, 128),), jnp.float32),
        "mass": jnp.clip(jnp.exp(math.log(2.0) - 1.3862944 * jax.random.uniform(key_list[2], (NODE, NODE, ELEMENTS), jnp.float32) ** levels(key_list[2], (NODE, NODE, ELEMENTS), ((2, 16),), -0.2, 0.2)), 0.5, 2.0),
        "inv_radius_sq": jnp.clip(jnp.exp(math.log(4.0) - 2.7725887 * jax.random.uniform(key_list[3], (NODE, NODE, ELEMENTS), jnp.float32) ** levels(key_list[3], (NODE, NODE, ELEMENTS), ((2, 16),), -0.2, 0.2)), 0.25, 4.0),
        "derivative": bell_draw(key_list[4], (NODE, NODE), NODE ** -0.5, 2.0, (), jnp.float32),
    }


STEP_RATE = 1.0
AZIMUTH_WEIGHT = 4.0
PENALTY = 1.0
HIGHEST = lax.Precision.HIGHEST


def unpack(flat):
    field = flat.reshape(NODE, NODE, N_MER, N_MODE, AXIAL_DEV, RADIAL, 2, MODES_DEV)
    field = jnp.transpose(field, (6, 3, 7, 0, 1, 2, 4, 5))
    return field.reshape(2, MODES, NODE, NODE, AXIAL, RADIAL)


def repack(field):
    field = field.reshape(2, N_MODE, MODES_DEV, NODE, NODE, N_MER, AXIAL_DEV, RADIAL)
    field = jnp.transpose(field, (3, 4, 5, 1, 6, 7, 0, 2))
    return field.reshape(NODE, NODE, COEFFS)


def helmholtz(field, stiffness, diagonal):
    result = diagonal * field
    result = result + jnp.einsum("ab,cmbjzr->cmajzr", stiffness, field, precision=HIGHEST)
    result = result + jnp.einsum("ab,cmibzr->cmiazr", stiffness, field, precision=HIGHEST)
    jump_axial = field[:, :, :, NODE - 1, :-1, :] - field[:, :, :, 0, 1:, :]
    result = result.at[:, :, :, NODE - 1, :-1, :].add(PENALTY * jump_axial)
    result = result.at[:, :, :, 0, 1:, :].add(-PENALTY * jump_axial)
    jump_radial = field[:, :, NODE - 1, :, :, :-1] - field[:, :, 0, :, :, 1:]
    result = result.at[:, :, NODE - 1, :, :, :-1].add(PENALTY * jump_radial)
    result = result.at[:, :, 0, :, :, 1:].add(-PENALTY * jump_radial)
    return result


def per_mode_dot(first, second):
    return jnp.sum(first * second, axis=(0, 2, 3, 4, 5))


def spread_modes(values):
    return values[None, :, None, None, None, None]


def conjugate_solve(rhs, stiffness, diagonal):
    solution = jnp.zeros_like(rhs)
    residual = rhs
    direction = rhs
    norm_now = per_mode_dot(residual, residual)
    for sweep in range(ITERS):
        applied = helmholtz(direction, stiffness, diagonal)
        step_size = spread_modes(norm_now / per_mode_dot(direction, applied))
        solution = solution + step_size * direction
        residual = residual - step_size * applied
        norm_next = per_mode_dot(residual, residual)
        direction = residual + spread_modes(norm_next / norm_now) * direction
        norm_now = norm_next
    return solution


def to_planes(field):
    spectral = field[0] + 1j * field[1]
    padded = jnp.zeros((PLANES,) + spectral.shape[1:], spectral.dtype).at[:MODES].set(spectral)
    return jnp.real(jnp.fft.ifft(padded, axis=0)) * PLANES


def from_planes(physical):
    spectral = jnp.fft.fft(physical, axis=0)[:MODES]
    return jnp.stack([jnp.real(spectral), jnp.imag(spectral)])


def azimuthal_turn(field, mode_fraction):
    return jnp.stack([-mode_fraction * field[1], mode_fraction * field[0]])


def reference(cotangent, checkpoint, mass, inv_radius_sq, derivative):
    stiffness = jnp.dot(derivative.T, derivative, precision=HIGHEST, preferred_element_type=jnp.float32)
    mass_grid = mass.reshape(NODE, NODE, AXIAL, RADIAL)[None, None]
    inverse_grid = inv_radius_sq.reshape(NODE, NODE, AXIAL, RADIAL)[None, None]
    mode_index = jnp.arange(MODES, dtype=jnp.int32)
    mode_fraction = (mode_index.astype(jnp.float32) / MODES)[:, None, None, None, None]
    diagonal = mass_grid * (STEP_RATE + AZIMUTH_WEIGHT * mode_fraction[None] * mode_fraction[None] * inverse_grid)
    spectral_weight = jnp.where(mode_index == 0, 1.0 / PLANES, 2.0 / PLANES).astype(jnp.float32)
    spectral_weight = spectral_weight[None, :, None, None, None, None]
    initial_state = unpack(checkpoint)
    state_planes = to_planes(initial_state)
    turned_planes = to_planes(azimuthal_turn(initial_state, mode_fraction))
    nonlinear = spectral_weight * from_planes(state_planes * turned_planes)
    next_state = conjugate_solve(mass_grid * (STEP_RATE * initial_state - nonlinear), stiffness, diagonal)
    adjoint = unpack(cotangent)
    for state in (next_state, initial_state):
        multiplier = conjugate_solve(adjoint, stiffness, diagonal)
        weighted = mass_grid * multiplier
        adjoint_planes = to_planes(spectral_weight * weighted)
        state_planes = to_planes(state)
        turned_planes = to_planes(azimuthal_turn(state, mode_fraction))
        first_term = from_planes(turned_planes * adjoint_planes)
        second_term = from_planes(state_planes * adjoint_planes)
        adjoint = STEP_RATE * weighted - (first_term - azimuthal_turn(second_term, mode_fraction))
    return repack(adjoint)
```

```python
import functools
import math

import jax
import jax.numpy as jnp
import ml_dtypes
import numpy as np
from jax import lax
from jax.experimental import pallas as pl
from jax.experimental.pallas import tpu as pltpu
from jax.sharding import PartitionSpec as P

NODE = 9
NODES = NODE * NODE
RADIAL = 8
ITERS = 4
MODES = 512
PLANES = 1024
ELEMENTS = 256
N_MODE = 8
N_MER = 16
ELEM_DEV = 16
GROUPS = 11
PADDED = GROUPS * 8
LANES = 128
AZIMUTH_WEIGHT = 4.0
HIGHEST = lax.Precision.HIGHEST
F32 = jnp.float32
BF16 = jnp.bfloat16


def tables():
    index = np.outer(np.arange(MODES), np.arange(MODES)) % PLANES
    angles = index.astype(np.float64) * (2.0 * math.pi / PLANES)
    out = []
    for values in (np.cos(angles), np.sin(angles)):
        values = values.astype(np.float32)
        high = values.astype(ml_dtypes.bfloat16)
        low = (values - high.astype(np.float32)).astype(ml_dtypes.bfloat16)
        out += [high, low]
    return np.stack(out)


def mix(first, second):
    shape = first.shape
    low = lax.broadcasted_iota(jnp.int32, shape, len(shape) - 2) % 8 < 4
    axis = len(shape) - 2
    return (
        jnp.where(low, first, pltpu.roll(second, 4, axis)),
        jnp.where(low, pltpu.roll(first, 4, axis), second),
    )


def exchange(tiles):
    block = lax.broadcasted_iota(jnp.int32, (8, LANES), 1) // 16
    tiles = list(tiles)
    for bit in (1, 2, 4):
        clear = (block & bit) == 0
        for at in range(8):
            if at & bit:
                continue
            one, two = tiles[at], tiles[at | bit]
            tiles[at] = jnp.where(clear, one, pltpu.roll(two, 16 * bit, 1))
            tiles[at | bit] = jnp.where(clear, pltpu.roll(one, LANES - 16 * bit, 1), two)
    return tiles


def native_to_tiles_kernel(x_ref, out_ref, rows):
    rows[pl.ds(NODES * ELEM_DEV, PADDED * ELEM_DEV - NODES * ELEM_DEV), :] = jnp.zeros(
        ((PADDED - NODES) * ELEM_DEV, LANES), F32
    )
    for i in range(NODE):
        for e in range(ELEM_DEV):
            rows[pl.ds(i * NODE * ELEM_DEV + e, NODE, stride=ELEM_DEV), :] = x_ref[
                i, :, e * LANES : (e + 1) * LANES
            ]
    for group in range(GROUPS):
        turned = rows[group * LANES : (group + 1) * LANES, :].T
        both = turned.reshape(2, 8, 8, LANES)
        even, odd = mix(both[0], both[1])
        out_ref[group] = jnp.stack([even, odd], axis=1).reshape(N_MER, 8, LANES)


def native_to_tiles(x):
    return pl.pallas_call(
        native_to_tiles_kernel,
        out_shape=jax.ShapeDtypeStruct((GROUPS, N_MER, 8, LANES), F32),
        scratch_shapes=[pltpu.VMEM((PADDED * ELEM_DEV, LANES), F32)],
        compiler_params=pltpu.CompilerParams(vmem_limit_bytes=32 << 20),
        name="native_to_tiles",
    )(x)


def tiles_to_native_kernel(t_ref, out_ref, rows):
    for group in range(GROUPS):
        tiles = t_ref[group].reshape(8, 2, 8, LANES)
        real, imag = mix(tiles[:, 0], tiles[:, 1])
        both = jnp.concatenate([real.reshape(64, LANES), imag.reshape(64, LANES)], axis=0)
        rows[group * LANES : (group + 1) * LANES, :] = both.T
    for i in range(NODE):
        for e in range(ELEM_DEV):
            out_ref[i, :, e * LANES : (e + 1) * LANES] = rows[
                pl.ds(i * NODE * ELEM_DEV + e, NODE, stride=ELEM_DEV), :
            ]


def tiles_to_native(tiles):
    return pl.pallas_call(
        tiles_to_native_kernel,
        out_shape=jax.ShapeDtypeStruct((NODE, NODE, ELEM_DEV * LANES), F32),
        scratch_shapes=[pltpu.VMEM((PADDED * ELEM_DEV, LANES), F32)],
        compiler_params=pltpu.CompilerParams(vmem_limit_bytes=32 << 20),
        name="tiles_to_native",
    )(tiles)


def solve_kernel(weigh_in, weigh_out, b_ref, mass_ref, inv_ref, k_ref, out_ref, x, r, p, q, diag, kb):
    halves = (slice(0, LANES), slice(LANES, 2 * LANES))
    mode_group = lax.axis_index("mode")
    place = lax.axis_index("mer")
    sub = lax.broadcasted_iota(jnp.int32, (8, LANES), 0) % 4
    fraction = (mode_group * 64 + place * 4 + sub).astype(F32) / MODES
    azimuth = AZIMUTH_WEIGHT * fraction * fraction
    lane = lax.broadcasted_iota(jnp.int32, (8, LANES), 1)
    not_last = lane % RADIAL != RADIAL - 1
    not_row = lane < LANES - RADIAL

    for a in range(NODE):
        for b in range(NODE):
            kb[a * NODE + b] = jnp.full((8, LANES), k_ref[a, b], F32)

    def load(group, norm):
        for h in range(2):
            tiles = exchange([b_ref[group, 8 * h + at] for at in range(8)])
            for at in range(8):
                node = jnp.minimum(group * 8 + at, NODES - 1)
                mass = mass_ref[node, :, halves[h]]
                inv = inv_ref[node, :, halves[h]]
                diag[group * 8 + at, :, halves[h]] = mass * (1.0 + azimuth * inv)
                value = tiles[at]
                if weigh_in:
                    value = mass * value
                value = jnp.where(group * 8 + at < NODES, value, 0.0)
                r[group * 8 + at, :, halves[h]] = value
                norm = norm + value * value
        return norm

    def total(acc):
        summed = jnp.broadcast_to(jnp.sum(acc, axis=1, keepdims=True), (8, LANES))
        return summed + pltpu.roll(summed, 4, 0)

    zero = jnp.zeros((8, LANES), F32)
    norm = total(lax.fori_loop(0, GROUPS, load, zero))

    alpha = None
    beta = None
    for sweep in range(ITERS):

        def columns(j, _, sweep=sweep, alpha=alpha, beta=beta):
            for h in range(2):
                column = []
                for i in range(NODE):
                    at = i * NODE + j
                    value = r[at, :, halves[h]]
                    if sweep > 0:
                        old = p[at, :, halves[h]]
                        if sweep > 1:
                            x[at, :, halves[h]] = x[at, :, halves[h]] + alpha * old
                        else:
                            x[at, :, halves[h]] = alpha * old
                        value = value + beta * old
                    p[at, :, halves[h]] = value
                    column.append(value)
                jump = jnp.where(
                    not_last, column[8] - pltpu.roll(column[0], LANES - 1, 1), 0.0
                )
                back = pltpu.roll(jump, 1, 1)
                for a in range(NODE):
                    at = a * NODE + j
                    acc = diag[at, :, halves[h]] * column[a]
                    for b in range(NODE):
                        acc = acc + kb[a * NODE + b] * column[b]
                    if a == 0:
                        acc = acc - back
                    if a == NODE - 1:
                        acc = acc + jump
                    q[at, :, halves[h]] = acc
            return 0

        def rows(i, curve):
            row = [[p[i * NODE + b, :, halves[h]] for b in range(NODE)] for h in range(2)]
            ahead = [pltpu.roll(row[h][0], LANES - RADIAL, 1) for h in range(2)]
            jumps = [
                row[0][8] - jnp.where(not_row, ahead[0], ahead[1]),
                jnp.where(not_row, row[1][8] - ahead[1], 0.0),
            ]
            behind = [pltpu.roll(jump, RADIAL, 1) for jump in jumps]
            wrap = lane < RADIAL
            backs = [
                jnp.where(wrap, 0.0, behind[0]),
                jnp.where(wrap, behind[0], behind[1]),
            ]
            for h in range(2):
                for a in range(NODE):
                    at = i * NODE + a
                    acc = q[at, :, halves[h]]
                    for b in range(NODE):
                        acc = acc + kb[a * NODE + b] * row[h][b]
                    if a == 0:
                        acc = acc - backs[h]
                    if a == NODE - 1:
                        acc = acc + jumps[h]
                    q[at, :, halves[h]] = acc
                    curve = curve + row[h][a] * acc
            return curve

        lax.fori_loop(0, NODE, columns, 0)
        alpha = norm / total(lax.fori_loop(0, NODE, rows, zero))
        if sweep == ITERS - 1:
            break

        def step(i, acc, alpha=alpha):
            for b in range(NODE):
                at = i * NODE + b
                for h in range(2):
                    value = r[at, :, halves[h]] - alpha * q[at, :, halves[h]]
                    r[at, :, halves[h]] = value
                    acc = acc + value * value
            return acc

        after = total(lax.fori_loop(0, NODE, step, zero))
        beta = after / norm
        norm = after

    def store(group, _):
        for h in range(2):
            tiles = []
            for at in range(8):
                node = jnp.minimum(group * 8 + at, NODES - 1)
                value = x[node, :, halves[h]] + alpha * p[node, :, halves[h]]
                if weigh_out:
                    value = value * mass_ref[node, :, halves[h]]
                tiles.append(value)
            tiles = exchange(tiles)
            for at in range(8):
                out_ref[group, 8 * h + at] = tiles[at]
        return 0

    lax.fori_loop(0, GROUPS, store, 0)


def solve(tiles, mass, inv, stiffness, weigh_in, weigh_out):
    field = pltpu.VMEM((PADDED, 8, 2 * LANES), F32)
    vmem = pl.BlockSpec(memory_space=pltpu.VMEM)
    return pl.pallas_call(
        functools.partial(solve_kernel, weigh_in, weigh_out),
        out_shape=jax.ShapeDtypeStruct((GROUPS, N_MER, 8, LANES), F32),
        in_specs=[vmem, vmem, vmem, pl.BlockSpec(memory_space=pltpu.SMEM)],
        out_specs=vmem,
        scratch_shapes=[field] * 5 + [pltpu.VMEM((NODES, 8, LANES), F32)],
        compiler_params=pltpu.CompilerParams(vmem_limit_bytes=32 << 20),
        name="solve",
    )(tiles, mass, inv, stiffness)


def split(value):
    high = value.astype(BF16)
    return high, (value - high.astype(F32)).astype(BF16)


def apply(t_ref, which, rows, field):
    high, low = field
    table_high = t_ref[2 * which, rows, :]
    table_low = t_ref[2 * which + 1, rows, :]
    return (
        jnp.dot(table_high, high, preferred_element_type=F32)
        + jnp.dot(table_high, low, preferred_element_type=F32)
        + jnp.dot(table_low, high, preferred_element_type=F32)
    )


def parts_of(u_ref):
    real, imag = [], []
    for slot in range(2):
        tiles = u_ref[:, slot].reshape(MODES // 8, 2, 8, LANES)
        one, two = mix(tiles[:, 0], tiles[:, 1])
        real.append(one.reshape(MODES, LANES))
        imag.append(two.reshape(MODES, LANES))
    return jnp.concatenate(real, axis=1), jnp.concatenate(imag, axis=1)


def parts_to(out_ref, real, imag):
    for slot in range(2):
        lanes = slice(slot * LANES, (slot + 1) * LANES)
        one, two = mix(
            real[:, lanes].reshape(MODES // 8, 8, LANES), imag[:, lanes].reshape(MODES // 8, 8, LANES)
        )
        out_ref[:, slot] = jnp.stack([one, two], axis=1).reshape(MODES // 4, 8, LANES)


def mode_rows(width):
    mode = lax.broadcasted_iota(jnp.int32, (MODES, width), 0)
    fraction = mode.astype(F32) / MODES
    weight = jnp.where(mode == 0, 1.0 / PLANES, 2.0 / PLANES).astype(F32)
    sign = jnp.where(mode % 2 == 0, 1.0, -1.0).astype(F32)
    return fraction, weight, sign


WIDTH = 2 * LANES
ROWS = 128


def to_planes(t_ref, cos_field, sin_field, outs):
    for at in range(MODES // ROWS):
        rows = slice(at * ROWS, (at + 1) * ROWS)
        outs(rows, apply(t_ref, 0, rows, cos_field), apply(t_ref, 1, rows, sin_field))


def first_kernel(u_ref, t_ref, out_ref, planes_ref, plus, minus):
    real, imag = parts_of(u_ref)
    fraction, weight, sign = mode_rows(WIDTH)
    cos_field = split(jnp.concatenate([real, fraction * imag], axis=1))
    sin_field = split(jnp.concatenate([imag, fraction * real], axis=1))
    middle = jnp.sum(sign * real, axis=0, keepdims=True)
    middle_turned = -jnp.sum(sign * fraction * imag, axis=0, keepdims=True)

    def store(rows, cos, sin):
        planes_ref[0, rows, :] = cos[:, :WIDTH] - sin[:, :WIDTH]
        planes_ref[1, rows, :] = cos[:, :WIDTH] + sin[:, :WIDTH]
        planes_ref[2, rows, :] = -cos[:, WIDTH:] - sin[:, WIDTH:]
        planes_ref[3, rows, :] = sin[:, WIDTH:] - cos[:, WIDTH:]

    to_planes(t_ref, cos_field, sin_field, store)
    planes_ref[1, 0:1, :] = middle
    planes_ref[3, 0:1, :] = middle_turned
    low = planes_ref[0] * planes_ref[2]
    high = planes_ref[1] * planes_ref[3]
    first = lax.broadcasted_iota(jnp.int32, (MODES, WIDTH), 0) == 0
    plus[...] = jnp.where(first, low, low + high)
    minus[...] = low - high
    cos_side, sin_side = split(plus[...]), split(minus[...])
    every = slice(0, MODES)
    a = apply(t_ref, 0, every, cos_side) + sign * high[0:1]
    b = -apply(t_ref, 1, every, sin_side)
    parts_to(out_ref, real - weight * a, imag - weight * b)


def finish(t_ref, s_real, s_imag, planes, adjoint, fraction, sign, out_ref):
    first = lax.broadcasted_iota(jnp.int32, (MODES, WIDTH), 0) == 0
    pluses, minuses, middles = [], [], []
    for low, high in ((planes[2], planes[3]), (planes[0], planes[1])):
        low = low * adjoint[0]
        high = high * adjoint[1]
        pluses.append(jnp.where(first, low, low + high))
        minuses.append(low - high)
        middles.append(high[0:1])
    every = slice(0, MODES)
    cos = apply(t_ref, 0, every, split(jnp.concatenate(pluses, axis=1)))
    sin = apply(t_ref, 1, every, split(jnp.concatenate(minuses, axis=1)))
    a1 = cos[:, :WIDTH] + sign * middles[0]
    a2 = cos[:, WIDTH:] + sign * middles[1]
    b1 = -sin[:, :WIDTH]
    b2 = -sin[:, WIDTH:]
    parts_to(out_ref, s_real - a1 - fraction * b2, s_imag - b1 + fraction * a2)


def second_kernel(u_ref, s_ref, t_ref, out_ref, planes):
    real, imag = parts_of(u_ref)
    s_real, s_imag = parts_of(s_ref)
    fraction, weight, sign = mode_rows(WIDTH)
    cos_field = split(jnp.concatenate([real, fraction * imag, weight * s_real], axis=1))
    sin_field = split(jnp.concatenate([imag, fraction * real, weight * s_imag], axis=1))

    def store(rows, cos, sin):
        planes[0, rows, :] = cos[:, :WIDTH] - sin[:, :WIDTH]
        planes[1, rows, :] = cos[:, :WIDTH] + sin[:, :WIDTH]
        planes[2, rows, :] = -cos[:, WIDTH : 2 * WIDTH] - sin[:, WIDTH : 2 * WIDTH]
        planes[3, rows, :] = sin[:, WIDTH : 2 * WIDTH] - cos[:, WIDTH : 2 * WIDTH]
        planes[4, rows, :] = cos[:, 2 * WIDTH :] - sin[:, 2 * WIDTH :]
        planes[5, rows, :] = cos[:, 2 * WIDTH :] + sin[:, 2 * WIDTH :]

    to_planes(t_ref, cos_field, sin_field, store)
    planes[1, 0:1, :] = jnp.sum(sign * real, axis=0, keepdims=True)
    planes[3, 0:1, :] = -jnp.sum(sign * fraction * imag, axis=0, keepdims=True)
    planes[5, 0:1, :] = jnp.sum(sign * weight * s_real, axis=0, keepdims=True)
    finish(
        t_ref,
        s_real,
        s_imag,
        [planes[at] for at in range(4)],
        (planes[4], planes[5]),
        fraction,
        sign,
        out_ref,
    )


def third_kernel(s_ref, u_planes, t_ref, out_ref, planes):
    s_real, s_imag = parts_of(s_ref)
    fraction, weight, sign = mode_rows(WIDTH)

    def store(rows, cos, sin):
        planes[0, rows, :] = cos - sin
        planes[1, rows, :] = cos + sin

    to_planes(t_ref, split(weight * s_real), split(weight * s_imag), store)
    planes[1, 0:1, :] = jnp.sum(sign * weight * s_real, axis=0, keepdims=True)
    finish(
        t_ref,
        s_real,
        s_imag,
        [u_planes[at] for at in range(4)],
        (planes[0], planes[1]),
        fraction,
        sign,
        out_ref,
    )


TILES_SHAPE = jax.ShapeDtypeStruct((MODES // 4, 2, 8, LANES), F32)
PLANES_SHAPE = jax.ShapeDtypeStruct((4, MODES, WIDTH), F32)
PARAMS = pltpu.CompilerParams(vmem_limit_bytes=50 << 20)


def first_stage(u, table):
    field = pltpu.VMEM((MODES, WIDTH), F32)
    return pl.pallas_call(
        first_kernel,
        out_shape=(TILES_SHAPE, PLANES_SHAPE),
        scratch_shapes=[field, field],
        compiler_params=PARAMS,
        name="first_stage",
    )(u, table)


def second_stage(u, s, table):
    return pl.pallas_call(
        second_kernel,
        out_shape=TILES_SHAPE,
        scratch_shapes=[pltpu.VMEM((6, MODES, WIDTH), F32)],
        compiler_params=PARAMS,
        name="second_stage",
    )(u, s, table)


def third_stage(s, u_planes, table):
    return pl.pallas_call(
        third_kernel,
        out_shape=TILES_SHAPE,
        scratch_shapes=[pltpu.VMEM((2, MODES, WIDTH), F32)],
        compiler_params=PARAMS,
        name="third_stage",
    )(s, u_planes, table)


def by_slot(tiles, axis):
    pad = [(0, 0)] * tiles.ndim
    pad[axis] = (0, 16 - GROUPS)
    tiles = jnp.pad(tiles, pad)
    return tiles.reshape(tiles.shape[:axis] + (2, 8) + tiles.shape[axis + 1 :])


def native_to_planes(tiles):
    sent = by_slot(tiles, 0).transpose(1, 0, 2, 3, 4)
    got = lax.all_to_all(sent, "mode", 0, 0)
    return got.transpose(0, 2, 1, 3, 4).reshape(MODES // 4, 2, 8, LANES)


def planes_to_native(tiles):
    sent = tiles.reshape(N_MODE, N_MER, 2, 8, LANES).transpose(0, 2, 1, 3, 4)
    got = lax.all_to_all(sent, "mode", 0, 0)
    return got.transpose(1, 0, 2, 3, 4).reshape(16, N_MER, 8, LANES)[:GROUPS]


def native_to_modes(tiles):
    return lax.all_to_all(tiles.transpose(1, 0, 2, 3), "mer", 0, 0).transpose(1, 0, 2, 3)


def modes_to_planes(tiles):
    sent = by_slot(tiles, 0).transpose(1, 2, 0, 3, 4).reshape(N_MODE * N_MER, 2, 8, LANES)
    return lax.all_to_all(sent, ("mode", "mer"), 0, 0)


def planes_to_modes(tiles):
    got = lax.all_to_all(tiles, ("mode", "mer"), 0, 0)
    got = got.reshape(N_MODE, N_MER, 2, 8, LANES).transpose(2, 0, 1, 3, 4)
    return got.reshape(16, N_MER, 8, LANES)[:GROUPS]


def shards(cotangent, checkpoint, mass, inv_radius_sq, derivative):
    table = jnp.asarray(tables())
    stiffness = jnp.dot(derivative.T, derivative, precision=HIGHEST, preferred_element_type=F32)
    mass = lax.all_gather(mass, "mer", axis=2, tiled=True).reshape(NODES, 1, ELEMENTS)
    inv = lax.all_gather(inv_radius_sq, "mer", axis=2, tiled=True).reshape(NODES, 1, ELEMENTS)
    state = native_to_planes(native_to_tiles(checkpoint))
    rhs, planes = first_stage(state, table)
    rhs = planes_to_modes(rhs)
    weighted = solve(native_to_modes(native_to_tiles(cotangent)), mass, inv, stiffness, False, True)
    weighted = modes_to_planes(weighted)
    later = solve(rhs, mass, inv, stiffness, True, False)
    adjoint = second_stage(modes_to_planes(later), weighted, table)
    weighted = solve(planes_to_modes(adjoint), mass, inv, stiffness, False, True)
    return tiles_to_native(planes_to_native(third_stage(modes_to_planes(weighted), planes, table)))


def solution(mesh):
    return jax.shard_map(
        shards,
        mesh=mesh,
        in_specs=(
            P(None, None, ("mer", "mode")),
            P(None, None, ("mer", "mode")),
            P(None, None, "mer"),
            P(None, None, "mer"),
            P(),
        ),
        out_specs=P(None, None, ("mer", "mode")),
        check_vma=False,
    )
```

```python
import functools
import math

import jax
import jax.numpy as jnp
import ml_dtypes
import numpy as np
from jax import lax
from jax.experimental import pallas as pl
from jax.experimental.pallas import tpu as pltpu
from jax.sharding import PartitionSpec as P

NODE = 9
NODES = NODE * NODE
RADIAL = 8
ITERS = 4
MODES = 512
PLANES = 1024
ELEMENTS = 256
N_MODE = 8
N_MER = 16
ELEM_DEV = 16
GROUPS = 11
PADDED = GROUPS * 8
LANES = 128
AZIMUTH_WEIGHT = 4.0
HIGHEST = lax.Precision.HIGHEST
F32 = jnp.float32
BF16 = jnp.bfloat16


def tables():
    index = np.outer(np.arange(MODES), np.arange(MODES)) % PLANES
    angles = index.astype(np.float64) * (2.0 * math.pi / PLANES)
    out = []
    for values in (np.cos(angles), np.sin(angles)):
        values = values.astype(np.float32)
        high = values.astype(ml_dtypes.bfloat16)
        low = (values - high.astype(np.float32)).astype(ml_dtypes.bfloat16)
        out += [high, low]
    return np.stack(out)


def mix(first, second):
    shape = first.shape
    low = lax.broadcasted_iota(jnp.int32, shape, len(shape) - 2) % 8 < 4
    axis = len(shape) - 2
    return (
        jnp.where(low, first, pltpu.roll(second, 4, axis)),
        jnp.where(low, pltpu.roll(first, 4, axis), second),
    )


def exchange(tiles):
    tiles = list(tiles)
    axis = tiles[0].ndim - 1
    block = lax.broadcasted_iota(jnp.int32, tiles[0].shape, axis) // 16
    for bit in (1, 2, 4):
        clear = (block & bit) == 0
        for at in range(8):
            if at & bit:
                continue
            one, two = tiles[at], tiles[at | bit]
            tiles[at] = jnp.where(clear, one, pltpu.roll(two, 16 * bit, axis))
            tiles[at | bit] = jnp.where(clear, pltpu.roll(one, LANES - 16 * bit, axis), two)
    return tiles


def native_to_tiles(x_ref, out_ref, rows):
    rows[pl.ds(NODES * ELEM_DEV, PADDED * ELEM_DEV - NODES * ELEM_DEV), :] = jnp.zeros(
        ((PADDED - NODES) * ELEM_DEV, LANES), F32
    )
    for i in range(NODE):
        for e in range(ELEM_DEV):
            rows[pl.ds(i * NODE * ELEM_DEV + e, NODE, stride=ELEM_DEV), :] = x_ref[
                i, :, e * LANES : (e + 1) * LANES
            ]
    for group in range(GROUPS):
        turned = rows[group * LANES : (group + 1) * LANES, :].T
        both = turned.reshape(2, 8, 8, LANES)
        even, odd = mix(both[0], both[1])
        out_ref[group // 8, group % 8] = jnp.stack([even, odd], axis=1).reshape(N_MER, 8, LANES)


def tiles_to_native_kernel(t_ref, out_ref, rows):
    for group in range(GROUPS):
        tiles = t_ref[group].reshape(8, 2, 8, LANES)
        real, imag = mix(tiles[:, 0], tiles[:, 1])
        both = jnp.concatenate([real.reshape(64, LANES), imag.reshape(64, LANES)], axis=0)
        rows[group * LANES : (group + 1) * LANES, :] = both.T
    for i in range(NODE):
        for e in range(ELEM_DEV):
            out_ref[i, :, e * LANES : (e + 1) * LANES] = rows[
                pl.ds(i * NODE * ELEM_DEV + e, NODE, stride=ELEM_DEV), :
            ]


def tiles_to_native(tiles):
    return pl.pallas_call(
        tiles_to_native_kernel,
        out_shape=jax.ShapeDtypeStruct((NODE, NODE, ELEM_DEV * LANES), F32),
        scratch_shapes=[pltpu.VMEM((PADDED * ELEM_DEV, LANES), F32)],
        compiler_params=pltpu.CompilerParams(vmem_limit_bytes=32 << 20),
        name="tiles_to_native",
    )(tiles)


def stiffness_tables(d_ref, k_ref):
    def dot(a, b):
        return jnp.dot(a, b, precision=HIGHEST, preferred_element_type=F32)

    derivative = d_ref[...]
    stiffness = lax.dot_general(
        derivative, derivative, (((0,), (0,)), ((), ())), precision=HIGHEST, preferred_element_type=F32
    )

    def pick(shape, node_axis, outer):
        node = lax.broadcasted_iota(jnp.int32, shape, node_axis)
        other = lax.broadcasted_iota(jnp.int32, shape, 1 - node_axis)
        place = node // NODE if outer else node % NODE
        return jnp.where((place == other) & (node < NODES), 1.0, 0.0).astype(F32)

    outer, inner = pick((PADDED, NODE), 0, True), pick((PADDED, NODE), 0, False)
    outer_t, inner_t = pick((NODE, PADDED), 1, True), pick((NODE, PADDED), 1, False)
    whole = dot(dot(outer, stiffness), outer_t) * dot(inner, inner_t)
    whole = whole + dot(dot(inner, stiffness), inner_t) * dot(outer, outer_t)
    high = whole.astype(BF16).astype(F32)
    low = whole - high
    top = jnp.concatenate([high, high], axis=1)
    bottom = jnp.concatenate([low, jnp.zeros_like(low)], axis=1)
    k_ref[...] = jnp.concatenate([top, bottom], axis=0).astype(BF16)


def metric_rows(mass_ref, inverse_ref, rows, out_ref):
    lane = lax.broadcasted_iota(jnp.int32, (ELEM_DEV, LANES), 1) % ELEM_DEV
    element = lax.broadcasted_iota(jnp.int32, (ELEM_DEV, LANES), 0)
    repeat = jnp.where(lane == element, 1.0, 0.0).astype(F32)
    shape = (PADDED, LANES)
    node = lax.broadcasted_iota(jnp.int32, shape, 0)
    block = lax.broadcasted_iota(jnp.int32, shape, 1) // ELEM_DEV
    keep = (node % 8 == block) & (node < NODES)
    for kind, ref in ((0, mass_ref), (1, inverse_ref)):
        for i in range(NODE):
            rows[i * NODE : (i + 1) * NODE, :ELEM_DEV] = ref[i]
        values = jnp.dot(
            rows[:PADDED, :ELEM_DEV], repeat, precision=HIGHEST, preferred_element_type=F32
        )
        values = jnp.where(keep, values, 0.0).reshape(GROUPS, 8, LANES)
        out_ref[kind, :GROUPS] = jnp.sum(values, axis=1)
        out_ref[kind, GROUPS:] = jnp.zeros((16 - GROUPS, LANES), F32)


def metric_tables(m_ref, mode_group, place, mass, diag, faces, turn):
    inverse = diag.at[0]
    for kind, out in ((0, mass), (1, inverse)):
        for h in range(2):
            rows = exchange([m_ref[8 * h + at, kind] for at in range(8)])
            for at in range(8):
                for group in range(GROUPS):
                    turn[h, group, at : at + 1] = rows[at][group : group + 1]
            for group in range(GROUPS):
                out[group * 8 : (group + 1) * 8, h * LANES : (h + 1) * LANES] = turn[h, group, 0:8]
    shape = (PADDED, ELEMENTS)
    node = lax.broadcasted_iota(jnp.int32, shape, 0)
    element = lax.broadcasted_iota(jnp.int32, shape, 1)
    inside = node < NODES
    upper = (node % NODE == NODE - 1) & (element < ELEMENTS - RADIAL) & inside
    lower = (node % NODE == 0) & (element >= RADIAL) & inside
    outer = (node // NODE == NODE - 1) & (element % RADIAL != RADIAL - 1) & inside
    inner = (node // NODE == 0) & (element % RADIAL != 0)
    marks = [jnp.where(mark, 1.0, 0.0).astype(F32) for mark in (upper, lower, outer, inner)]
    for at in range(4):
        faces[at] = marks[at]
    count = marks[0] + marks[1] + marks[2] + marks[3]
    values = inverse[...]
    for n in range(4):
        fraction = (mode_group * 64 + place * 4 + n).astype(F32) / MODES
        diag[n] = mass[...] * (1.0 + AZIMUTH_WEIGHT * fraction * fraction * values) + count


CHUNKS = ((0, 0, 3), (0, 3, 6), (0, 6, 8), (1, 0, 3))


def load_tiles(b_ref, turn, weight, out):
    for slot, start, stop in CHUNKS:
        for h in range(2):
            tiles = exchange([b_ref[slot, start:stop, 8 * h + at] for at in range(8)])
            for at in range(8):
                turn[h, 8 * slot + start : 8 * slot + stop, at * 8 : (at + 1) * 8] = tiles[at]
    for s in range(8):
        for h in range(2):
            lanes = slice(h * LANES, (h + 1) * LANES)
            for group in range(GROUPS):
                rows = slice(group * 8, (group + 1) * 8)
                value = turn[h, group, pl.ds(s, 8, stride=8), :]
                if weight is not None:
                    value = value * weight[rows, lanes]
                out[s, rows, lanes] = value


def store_tiles(value_of, turn, out_ref):
    for s in range(8):
        value = value_of(s)
        for h in range(2):
            for group in range(GROUPS):
                turn[h, group, pl.ds(s, 8, stride=8), :] = value[
                    group * 8 : (group + 1) * 8, h * LANES : (h + 1) * LANES
                ]
    for slot, start, stop in CHUNKS:
        for h in range(2):
            groups = slice(8 * slot + start, 8 * slot + stop)
            tiles = exchange([turn[h, groups, at * 8 : (at + 1) * 8] for at in range(8)])
            for at in range(8):
                out_ref[slot, start:stop, 8 * h + at] = tiles[at]


def total(parts):
    half = parts[:, :LANES] + parts[:, LANES:]
    return jnp.broadcast_to(jnp.sum(half, axis=(0, 1), keepdims=True), (1, ELEMENTS))


def fold(value):
    return jnp.sum(value.reshape(GROUPS, 8, ELEMENTS), axis=0)


def solve(b_ref, out_ref, weigh_in, weigh_out, scratch):
    mass, diag, faces, k_ref, x, r, p, q, turn = scratch
    load_tiles(b_ref, turn, mass if weigh_in else None, r)
    norms = []
    for n in range(4):
        norms.append(total(fold(r[n] * r[n]) + fold(r[n + 4] * r[n + 4])))
    x[...] = jnp.zeros_like(x)
    p[...] = jnp.zeros_like(p)
    empty = jnp.zeros((8, ELEMENTS), F32)
    edge = jnp.zeros((16, ELEMENTS), F32)

    def sweep_body(sweep, carry):
        norms, alphas, betas = carry
        curves = []
        for n in range(4):
            curve = None
            for s in (n, n + 4):
                old = p[s]
                x[s] = x[s] + alphas[n] * old
                now = r[s] + betas[n] * old
                p[s] = now
                high = now.astype(BF16).astype(F32)
                halves = jnp.concatenate([high, now - high], axis=0).astype(BF16)
                image = jnp.dot(k_ref[...], halves, preferred_element_type=F32)
                ahead = pltpu.roll(now[: PADDED - 8], ELEMENTS - RADIAL, 1)
                behind = pltpu.roll(now[8:], RADIAL, 1)
                image = (
                    image[:PADDED]
                    + image[PADDED:]
                    + diag[n] * now
                    - faces[0] * jnp.concatenate([empty, ahead], axis=0)
                    - faces[1] * jnp.concatenate([behind, empty], axis=0)
                )
                outward = pltpu.roll(now[:16], ELEMENTS - 1, 1)
                inward = pltpu.roll(now[72:], 1, 1)
                image = jnp.concatenate(
                    [
                        image[:16] - faces[3, :16] * inward,
                        image[16:72],
                        image[72:] - faces[2, 72:] * outward,
                    ],
                    axis=0,
                )
                q[s] = image
                part = fold(now * image)
                curve = part if curve is None else curve + part
            curves.append(total(curve))
        alphas = [norms[n] / curves[n] for n in range(4)]

        def update():
            after = []
            for n in range(4):
                part = None
                for s in (n, n + 4):
                    value = r[s] - alphas[n] * q[s]
                    r[s] = value
                    add = fold(value * value)
                    part = add if part is None else part + add
                after.append(total(part))
            return after

        after = lax.cond(sweep < ITERS - 1, update, lambda: norms)
        betas = [after[n] / norms[n] for n in range(4)]
        return after, alphas, betas

    none = [jnp.zeros((1, ELEMENTS), F32)] * 4
    norms, alphas, betas = lax.fori_loop(0, ITERS, sweep_body, (norms, none, none))

    def value_of(s):
        value = x[s] + alphas[s % 4] * p[s]
        return value * mass[...] if weigh_out else value

    store_tiles(value_of, turn, out_ref)


FIELD = pltpu.VMEM((8, PADDED, ELEMENTS), F32)
SOLVE_SCRATCH = [
    pltpu.VMEM((PADDED, ELEMENTS), F32),
    pltpu.VMEM((4, PADDED, ELEMENTS), F32),
    pltpu.VMEM((4, PADDED, ELEMENTS), F32),
    pltpu.VMEM((2 * PADDED, 2 * PADDED), BF16),
    FIELD,
    FIELD,
    FIELD,
    FIELD,
    pltpu.VMEM((2, GROUPS, 64, LANES), F32),
]


def split(value):
    high = value.astype(BF16)
    return high, (value - high.astype(F32)).astype(BF16)


def apply(t_ref, which, rows, field):
    high, low = field
    table_high = t_ref[2 * which, rows, :]
    table_low = t_ref[2 * which + 1, rows, :]
    return (
        jnp.dot(table_high, high, preferred_element_type=F32)
        + jnp.dot(table_high, low, preferred_element_type=F32)
        + jnp.dot(table_low, high, preferred_element_type=F32)
    )


def parts_of(u_ref):
    real, imag = [], []
    for slot in range(2):
        tiles = u_ref[slot].reshape(MODES // 8, 2, 8, LANES)
        one, two = mix(tiles[:, 0], tiles[:, 1])
        real.append(one.reshape(MODES, LANES))
        imag.append(two.reshape(MODES, LANES))
    return jnp.concatenate(real, axis=1), jnp.concatenate(imag, axis=1)


def parts_to(out_ref, real, imag):
    for slot in range(2):
        lanes = slice(slot * LANES, (slot + 1) * LANES)
        one, two = mix(
            real[:, lanes].reshape(MODES // 8, 8, LANES), imag[:, lanes].reshape(MODES // 8, 8, LANES)
        )
        out_ref[slot] = jnp.stack([one, two], axis=1).reshape(MODES // 4, 8, LANES)


def mode_rows(width):
    mode = lax.broadcasted_iota(jnp.int32, (MODES, width), 0)
    fraction = mode.astype(F32) / MODES
    weight = jnp.where(mode == 0, 1.0 / PLANES, 2.0 / PLANES).astype(F32)
    sign = jnp.where(mode % 2 == 0, 1.0, -1.0).astype(F32)
    return fraction, weight, sign


WIDTH = 2 * LANES
ROWS = 128


def to_planes(t_ref, cos_field, sin_field, outs):
    for at in range(MODES // ROWS):
        rows = slice(at * ROWS, (at + 1) * ROWS)
        outs(rows, apply(t_ref, 0, rows, cos_field), apply(t_ref, 1, rows, sin_field))


def first_stage(u_ref, t_ref, out_ref, planes_ref):
    real, imag = parts_of(u_ref)
    fraction, weight, sign = mode_rows(WIDTH)
    cos_field = split(jnp.concatenate([real, fraction * imag], axis=1))
    sin_field = split(jnp.concatenate([imag, fraction * real], axis=1))
    middle = jnp.sum(sign * real, axis=0, keepdims=True)
    middle_turned = -jnp.sum(sign * fraction * imag, axis=0, keepdims=True)

    def store(rows, cos, sin):
        planes_ref[0, rows, :] = cos[:, :WIDTH] - sin[:, :WIDTH]
        planes_ref[1, rows, :] = cos[:, :WIDTH] + sin[:, :WIDTH]
        planes_ref[2, rows, :] = -cos[:, WIDTH:] - sin[:, WIDTH:]
        planes_ref[3, rows, :] = sin[:, WIDTH:] - cos[:, WIDTH:]

    to_planes(t_ref, cos_field, sin_field, store)
    planes_ref[1, 0:1, :] = middle
    planes_ref[3, 0:1, :] = middle_turned
    low = planes_ref[0] * planes_ref[2]
    high = planes_ref[1] * planes_ref[3]
    first = lax.broadcasted_iota(jnp.int32, (MODES, WIDTH), 0) == 0
    cos_side, sin_side = split(jnp.where(first, low, low + high)), split(low - high)
    every = slice(0, MODES)
    a = apply(t_ref, 0, every, cos_side) + sign * high[0:1]
    b = -apply(t_ref, 1, every, sin_side)
    parts_to(out_ref, real - weight * a, imag - weight * b)


def finish(t_ref, s_ref, planes, adjoint, at, out_ref):
    s_real, s_imag = parts_of(s_ref)
    fraction, _, sign = mode_rows(WIDTH)
    first = lax.broadcasted_iota(jnp.int32, (MODES, WIDTH), 0) == 0
    pluses, minuses, middles = [], [], []
    for which in (2, 0):
        low = planes[which] * adjoint[at]
        high = planes[which + 1] * adjoint[at + 1]
        pluses.append(jnp.where(first, low, low + high))
        minuses.append(low - high)
        middles.append(high[0:1])
    every = slice(0, MODES)
    cos = apply(t_ref, 0, every, split(jnp.concatenate(pluses, axis=1)))
    sin = apply(t_ref, 1, every, split(jnp.concatenate(minuses, axis=1)))
    a1 = cos[:, :WIDTH] + sign * middles[0]
    a2 = cos[:, WIDTH:] + sign * middles[1]
    b1 = -sin[:, :WIDTH]
    b2 = -sin[:, WIDTH:]
    parts_to(out_ref, s_real - a1 - fraction * b2, s_imag - b1 + fraction * a2)


def second_stage(u_ref, s_ref, t_ref, out_ref, planes):
    real, imag = parts_of(u_ref)
    fraction, weight, sign = mode_rows(WIDTH)

    def store(rows, cos, sin):
        planes[0, rows, :] = cos[:, :WIDTH] - sin[:, :WIDTH]
        planes[1, rows, :] = cos[:, :WIDTH] + sin[:, :WIDTH]
        planes[2, rows, :] = -cos[:, WIDTH:] - sin[:, WIDTH:]
        planes[3, rows, :] = sin[:, WIDTH:] - cos[:, WIDTH:]

    cos_field = split(jnp.concatenate([real, fraction * imag], axis=1))
    sin_field = split(jnp.concatenate([imag, fraction * real], axis=1))
    to_planes(t_ref, cos_field, sin_field, store)
    planes[1, 0:1, :] = jnp.sum(sign * real, axis=0, keepdims=True)
    planes[3, 0:1, :] = -jnp.sum(sign * fraction * imag, axis=0, keepdims=True)
    finish(t_ref, s_ref, planes, planes, 4, out_ref)


def adjoint_planes(s_ref, t_ref, planes):
    s_real, s_imag = parts_of(s_ref)
    _, weight, sign = mode_rows(WIDTH)

    def store(rows, cos, sin):
        planes[4, rows, :] = cos - sin
        planes[5, rows, :] = cos + sin

    to_planes(t_ref, split(weight * s_real), split(weight * s_imag), store)
    planes[5, 0:1, :] = jnp.sum(sign * weight * s_real, axis=0, keepdims=True)


COUNT = N_MODE * N_MER
SPARE = GROUPS - 8


def send(source, target, mode, mer, sems, at):
    pltpu.make_async_remote_copy(
        src_ref=source,
        dst_ref=target,
        send_sem=sems[0].at[at],
        recv_sem=sems[1].at[at],
        device_id={"mode": mode, "mer": mer},
        device_id_type=pl.DeviceIdType.MESH,
    ).start()


def wait(blank, tiles, sem):
    whole = blank.at[pl.ds(0, tiles)]
    pltpu.make_async_copy(whole, whole, sem).wait()


def wait_either(double, blank, tiles_double, tiles_single, sem):
    @pl.when(double)
    def _():
        wait(blank, tiles_double, sem)

    @pl.when(jnp.logical_not(double))
    def _():
        wait(blank, tiles_single, sem)


def place_at(mer, k):
    y = lax.rem(lax.rem(mer, 4) + lax.rem(k, 4), 4)
    z = lax.rem(mer // 4 + k // 4, 4)
    return z * 4 + y


def each_group(mode, act):
    for other in range(N_MODE):

        @pl.when(mode != other)
        def _(other=other):
            act(other)


def each_place(mer, act):
    def body(k, _):
        act(place_at(mer, k))
        return 0

    lax.fori_loop(1, N_MER, body, 0)


def each_other(mode, mer, act):
    def body(place):
        for other in range(N_MODE):
            act(other, place)

    each_place(mer, body)
    each_group(mode, lambda other: act(other, mer))


def program_kernel(
    state_ref,
    cotangent_ref,
    mass_ref,
    inverse_ref,
    d_ref,
    t_ref,
    out_ref,
    rows,
    native_out,
    native_in,
    mode_out,
    mode_in,
    plane_out,
    plane_in,
    metric_out,
    metric_in,
    u_planes,
    planes,
    blank,
    send_sems,
    recv_sems,
    *solve_scratch,
):
    mode = lax.axis_index("mode")
    mer = lax.axis_index("mer")
    me = mode * N_MER + mer
    double = mode < SPARE
    sems = (send_sems, recv_sems)
    sent = []

    barrier = pltpu.get_barrier_semaphore()

    def greet(other, place):
        pl.semaphore_signal(
            barrier,
            inc=1,
            device_id={"mode": other, "mer": place},
            device_id_type=pl.DeviceIdType.MESH,
        )

    each_other(mode, mer, greet)
    native_to_tiles(state_ref, native_out.at[0], rows)
    pl.semaphore_wait(barrier, COUNT - 1)

    def send_to_planes(source, target, at):
        target[:, me] = source[:, mode, mer]

        def act(other, place):
            if other < SPARE:
                send(source.at[:, other, place], target.at[:, me], other, place, sems, at)
            else:
                send(source.at[0, other, place], target.at[0, me], other, place, sems, at)

        each_other(mode, mer, act)
        sent.append((at, 16 * GROUPS - 2, 16 * GROUPS - 1))

    def wait_planes(at):
        wait_either(double, blank, 2 * (COUNT - 1), COUNT - 1, recv_sems.at[at])

    def send_to_modes(source, target, at):
        target[:, mode, mer] = source[:, me]

        @pl.when(double)
        def _():
            def act(other, place):
                index = other * N_MER + place
                send(source.at[:, index], target.at[:, mode, mer], other, place, sems, at)

            each_other(mode, mer, act)

        @pl.when(jnp.logical_not(double))
        def _():
            def act(other, place):
                index = other * N_MER + place
                send(source.at[0, index], target.at[0, mode, mer], other, place, sems, at)

            each_other(mode, mer, act)

        sent.append((at, 2 * (COUNT - 1), COUNT - 1))

    def wait_modes(at):
        wait_either(double, blank, 16 * GROUPS - 2, 16 * GROUPS - 1, recv_sems.at[at])

    mine = pl.ds(pl.multiple_of(mode * N_MER, N_MER), N_MER)
    plane_in[0, :, mine] = native_out[0, :, mode]

    def send_state(other):
        if other < SPARE:
            send(native_out.at[0, :, other], plane_in.at[0, :, mine], other, mer, sems, 0)
        else:
            send(native_out.at[0, 0, other], plane_in.at[0, 0, mine], other, mer, sems, 0)

    each_group(mode, send_state)
    sent.append((0, N_MER * (GROUPS - 2), N_MER * (GROUPS - 1)))

    native_to_tiles(cotangent_ref, native_out.at[1], rows)
    mode_in[0, :, :, mer] = native_out[1, :, :, mer]
    metric_rows(mass_ref, inverse_ref, rows, metric_out)
    metric_in[mer] = metric_out[...]

    def send_cotangent(other):
        send(native_out.at[1, 0, :, other], mode_in.at[0, 0, :, mer], mode, other, sems, 1)
        send(native_out.at[1, 1, 0:SPARE, other], mode_in.at[0, 1, 0:SPARE, mer], mode, other, sems, 1)
        send(metric_out, metric_in.at[mer], mode, other, sems, 2)

    each_place(mer, send_cotangent)
    sent.append((1, (N_MER - 1) * GROUPS, (N_MER - 1) * GROUPS))
    sent.append((2, (N_MER - 1) * 4, (N_MER - 1) * 4))

    mass, diag, faces, k_ref = solve_scratch[:4]
    turn = solve_scratch[8]
    stiffness_tables(d_ref, k_ref)

    wait_either(double, blank, 2 * (N_MODE - 1) * N_MER, (N_MODE - 1) * N_MER, recv_sems.at[0])
    first_stage(plane_in.at[0], t_ref, plane_out.at[0], u_planes)
    send_to_modes(plane_out.at[0], mode_in.at[1], 3)

    wait(blank, (N_MER - 1) * 4, recv_sems.at[2])
    metric_tables(metric_in, mode, mer, mass, diag, faces, turn)
    wait(blank, (N_MER - 1) * GROUPS, recv_sems.at[1])
    solve(mode_in.at[0], mode_out.at[0], False, True, solve_scratch)
    send_to_planes(mode_out.at[0], plane_in.at[1], 4)

    wait_modes(3)
    solve(mode_in.at[1], mode_out.at[1], True, False, solve_scratch)
    send_to_planes(mode_out.at[1], plane_in.at[2], 5)

    wait_planes(4)
    adjoint_planes(plane_in.at[1], t_ref, planes)
    wait_planes(5)
    second_stage(plane_in.at[2], plane_in.at[1], t_ref, plane_out.at[1], planes)
    send_to_modes(plane_out.at[1], mode_in.at[2], 6)

    wait_modes(6)
    solve(mode_in.at[2], mode_out.at[2], False, True, solve_scratch)
    send_to_planes(mode_out.at[2], plane_in.at[3], 7)

    wait_planes(7)
    adjoint_planes(plane_in.at[3], t_ref, planes)
    finish(t_ref, plane_in.at[3], u_planes, planes, 4, plane_out.at[2])

    native_in[:, mode] = plane_out[2, :, mine]

    def send_gradient(other):
        theirs = slice(other * N_MER, (other + 1) * N_MER)

        @pl.when(double)
        def _():
            send(plane_out.at[2, :, theirs], native_in.at[:, mode], other, mer, sems, 8)

        @pl.when(jnp.logical_not(double))
        def _():
            send(plane_out.at[2, 0, theirs], native_in.at[0, mode], other, mer, sems, 8)

    each_group(mode, send_gradient)
    sent.append((8, 2 * (N_MODE - 1) * N_MER, (N_MODE - 1) * N_MER))
    wait_either(double, blank, N_MER * (GROUPS - 2), N_MER * (GROUPS - 1), recv_sems.at[8])
    for group in range(GROUPS):
        out_ref[group] = native_in[group // 8, group % 8]
    for at, tiles_double, tiles_single in sent:
        wait_either(double, blank, tiles_double, tiles_single, send_sems.at[at])


def program(state, cotangent, mass, inverse, derivative, table):
    by_mode = (2, N_MODE, N_MER, 8, LANES)
    by_plane = (2, COUNT, 8, LANES)

    def scratch(count, shape):
        return pltpu.VMEM((count,) + shape, F32)

    return pl.pallas_call(
        program_kernel,
        out_shape=jax.ShapeDtypeStruct((GROUPS, N_MER, 8, LANES), F32),
        in_specs=[pl.BlockSpec(memory_space=pltpu.VMEM)] * 6,
        out_specs=pl.BlockSpec(memory_space=pltpu.VMEM),
        scratch_shapes=[
            pltpu.VMEM((PADDED * ELEM_DEV, LANES), F32),
            scratch(2, by_mode),
            pltpu.VMEM(by_mode, F32),
            scratch(3, by_mode),
            scratch(3, by_mode),
            scratch(3, by_plane),
            scratch(4, by_plane),
            pltpu.VMEM((2, 16, LANES), F32),
            scratch(N_MER, (2, 16, LANES)),
            pltpu.VMEM((4, MODES, WIDTH), F32),
            pltpu.VMEM((6, MODES, WIDTH), F32),
            pltpu.VMEM((2 * COUNT, 8, LANES), F32),
            pltpu.SemaphoreType.DMA((9,)),
            pltpu.SemaphoreType.DMA((9,)),
            *SOLVE_SCRATCH,
        ],
        compiler_params=pltpu.CompilerParams(
            collective_id=0, has_side_effects=True, vmem_limit_bytes=60 << 20
        ),
        name="program",
    )(state, cotangent, mass, inverse, derivative, table)


def shards(cotangent, checkpoint, mass, inv_radius_sq, derivative):
    table = jnp.asarray(tables())
    return tiles_to_native(program(checkpoint, cotangent, mass, inv_radius_sq, derivative, table))


def solution(mesh):
    return jax.shard_map(
        shards,
        mesh=mesh,
        in_specs=(
            P(None, None, ("mer", "mode")),
            P(None, None, ("mer", "mode")),
            P(None, None, "mer"),
            P(None, None, "mer"),
            P(),
        ),
        out_specs=P(None, None, ("mer", "mode")),
        check_vma=False,
    )
```

```python
import functools
import math

import jax
import jax.numpy as jnp
import ml_dtypes
import numpy as np
from jax import lax
from jax.experimental import pallas as pl
from jax.experimental.pallas import tpu as pltpu
from jax.sharding import PartitionSpec as P

NODE = 9
NODES = NODE * NODE
RADIAL = 8
ITERS = 4
MODES = 512
PLANES = 1024
ELEMENTS = 256
N_MODE = 8
N_MER = 16
ELEM_DEV = 16
GROUPS = 11
PADDED = GROUPS * 8
LANES = 128
AZIMUTH_WEIGHT = 4.0
HIGHEST = lax.Precision.HIGHEST
F32 = jnp.float32
BF16 = jnp.bfloat16


def tables():
    order = np.arange(MODES).reshape(4, 2, 64).transpose(1, 0, 2).reshape(-1)
    index = np.outer(order, order) % PLANES
    angles = index.astype(np.float64) * (2.0 * math.pi / PLANES)
    out = []
    for values in (np.cos(angles), np.sin(angles)):
        values = values.astype(np.float32)
        high = values.astype(ml_dtypes.bfloat16)
        low = (values - high.astype(np.float32)).astype(ml_dtypes.bfloat16)
        out += [high, low]
    return np.stack(out)


def mix(first, second):
    shape = first.shape
    low = lax.broadcasted_iota(jnp.int32, shape, len(shape) - 2) % 8 < 4
    axis = len(shape) - 2
    return (
        jnp.where(low, first, pltpu.roll(second, 4, axis)),
        jnp.where(low, pltpu.roll(first, 4, axis), second),
    )


def exchange(tiles):
    tiles = list(tiles)
    axis = tiles[0].ndim - 1
    block = lax.broadcasted_iota(jnp.int32, tiles[0].shape, axis) // 16
    for bit in (1, 2, 4):
        clear = (block & bit) == 0
        for at in range(8):
            if at & bit:
                continue
            one, two = tiles[at], tiles[at | bit]
            tiles[at] = jnp.where(clear, one, pltpu.roll(two, 16 * bit, axis))
            tiles[at | bit] = jnp.where(clear, pltpu.roll(one, LANES - 16 * bit, axis), two)
    return tiles


def native_to_tiles(x_ref, out_ref, rows):
    rows[pl.ds(NODES * ELEM_DEV, PADDED * ELEM_DEV - NODES * ELEM_DEV), :] = jnp.zeros(
        ((PADDED - NODES) * ELEM_DEV, LANES), F32
    )
    for i in range(NODE):
        for e in range(ELEM_DEV):
            rows[pl.ds(i * NODE * ELEM_DEV + e, NODE, stride=ELEM_DEV), :] = x_ref[
                i, :, e * LANES : (e + 1) * LANES
            ]
    for group in range(GROUPS):
        turned = rows[group * LANES : (group + 1) * LANES, :].T
        both = turned.reshape(2, 8, 8, LANES)
        even, odd = mix(both[0], both[1])
        out_ref[group // 8, group % 8] = jnp.stack([even, odd], axis=1).reshape(N_MER, 8, LANES)


def tiles_to_native(t_ref, out_ref, rows):
    for group in range(GROUPS):
        tiles = t_ref[group // 8, group % 8].reshape(8, 2, 8, LANES)
        real, imag = mix(tiles[:, 0], tiles[:, 1])
        both = jnp.concatenate([real.reshape(64, LANES), imag.reshape(64, LANES)], axis=0)
        rows[group * LANES : (group + 1) * LANES, :] = both.T
    for i in range(NODE):
        for e in range(ELEM_DEV):
            out_ref[i, :, e * LANES : (e + 1) * LANES] = rows[
                pl.ds(i * NODE * ELEM_DEV + e, NODE, stride=ELEM_DEV), :
            ]


def stiffness_tables(d_ref, k_ref):
    def dot(a, b):
        return jnp.dot(a, b, precision=HIGHEST, preferred_element_type=F32)

    derivative = d_ref[...]
    stiffness = lax.dot_general(
        derivative, derivative, (((0,), (0,)), ((), ())), precision=HIGHEST, preferred_element_type=F32
    )

    def pick(shape, node_axis, outer):
        node = lax.broadcasted_iota(jnp.int32, shape, node_axis)
        other = lax.broadcasted_iota(jnp.int32, shape, 1 - node_axis)
        place = node // NODE if outer else node % NODE
        return jnp.where((place == other) & (node < NODES), 1.0, 0.0).astype(F32)

    outer, inner = pick((PADDED, NODE), 0, True), pick((PADDED, NODE), 0, False)
    outer_t, inner_t = pick((NODE, PADDED), 1, True), pick((NODE, PADDED), 1, False)
    whole = dot(dot(outer, stiffness), outer_t) * dot(inner, inner_t)
    whole = whole + dot(dot(inner, stiffness), inner_t) * dot(outer, outer_t)
    high = whole.astype(BF16).astype(F32)
    low = whole - high
    top = jnp.concatenate([high, high], axis=1)
    bottom = jnp.concatenate([low, jnp.zeros_like(low)], axis=1)
    k_ref[...] = jnp.concatenate([top, bottom], axis=0).astype(BF16)


def metric_rows(mass_ref, inverse_ref, rows, out_ref):
    lane = lax.broadcasted_iota(jnp.int32, (ELEM_DEV, LANES), 1) % ELEM_DEV
    element = lax.broadcasted_iota(jnp.int32, (ELEM_DEV, LANES), 0)
    repeat = jnp.where(lane == element, 1.0, 0.0).astype(F32)
    shape = (PADDED, LANES)
    node = lax.broadcasted_iota(jnp.int32, shape, 0)
    block = lax.broadcasted_iota(jnp.int32, shape, 1) // ELEM_DEV
    keep = (node % 8 == block) & (node < NODES)
    for kind, ref in ((0, mass_ref), (1, inverse_ref)):
        for i in range(NODE):
            rows[i * NODE : (i + 1) * NODE, :ELEM_DEV] = ref[i]
        values = jnp.dot(
            rows[:PADDED, :ELEM_DEV], repeat, precision=HIGHEST, preferred_element_type=F32
        )
        values = jnp.where(keep, values, 0.0).reshape(GROUPS, 8, LANES)
        out_ref[kind, :GROUPS] = jnp.sum(values, axis=1)
        out_ref[kind, GROUPS:] = jnp.zeros((16 - GROUPS, LANES), F32)


def metric_tables(m_ref, mode_group, place, mass, diag, faces, turn):
    inverse = diag.at[0]
    for kind, out in ((0, mass), (1, inverse)):
        for h in range(2):
            rows = exchange([m_ref[8 * h + at, kind] for at in range(8)])
            for at in range(8):
                for group in range(GROUPS):
                    turn[h, group, at : at + 1] = rows[at][group : group + 1]
            for group in range(GROUPS):
                out[group * 8 : (group + 1) * 8, h * LANES : (h + 1) * LANES] = turn[h, group, 0:8]
    shape = (PADDED, ELEMENTS)
    node = lax.broadcasted_iota(jnp.int32, shape, 0)
    element = lax.broadcasted_iota(jnp.int32, shape, 1)
    inside = node < NODES
    upper = (node % NODE == NODE - 1) & (element < ELEMENTS - RADIAL) & inside
    lower = (node % NODE == 0) & (element >= RADIAL) & inside
    outer = (node // NODE == NODE - 1) & (element % RADIAL != RADIAL - 1) & inside
    inner = (node // NODE == 0) & (element % RADIAL != 0)
    marks = [jnp.where(mark, 1.0, 0.0).astype(F32) for mark in (upper, lower, outer, inner)]
    for at in range(4):
        faces[at] = marks[at]
    count = marks[0] + marks[1] + marks[2] + marks[3]
    values = inverse[...]
    for n in range(4):
        fraction = (mode_group * 64 + place * 4 + n).astype(F32) / MODES
        diag[n] = mass[...] * (1.0 + AZIMUTH_WEIGHT * fraction * fraction * values) + count


CHUNKS = ((0, 0, 3), (0, 3, 6), (0, 6, 8), (1, 0, 3))


def load_tiles(b_ref, turn, weight, out):
    for slot, start, stop in CHUNKS:
        for h in range(2):
            tiles = exchange([b_ref[slot, start:stop, 8 * h + at] for at in range(8)])
            for at in range(8):
                turn[h, 8 * slot + start : 8 * slot + stop, at * 8 : (at + 1) * 8] = tiles[at]
    for s in range(8):
        for h in range(2):
            lanes = slice(h * LANES, (h + 1) * LANES)
            for group in range(GROUPS):
                rows = slice(group * 8, (group + 1) * 8)
                value = turn[h, group, pl.ds(s, 8, stride=8), :]
                if weight is not None:
                    value = value * weight[rows, lanes]
                out[s, rows, lanes] = value


OWNED = (((0, 0), (0, 2), (0, 4), (0, 6), (1, 0), (1, 1), (1, 2)), ((0, 1), (0, 3), (0, 5), (0, 7)))


def store_tiles(value_of, turn, out_ref, emit):
    for core in range(2):
        for s in range(8):
            for slot, at_group in OWNED[core]:
                group = 8 * slot + at_group
                for h in range(2):
                    turn[h, group, pl.ds(s, 8, stride=8), :] = value_of(
                        s, slice(group * 8, (group + 1) * 8), slice(h * LANES, (h + 1) * LANES)
                    )
        for slot, at_group in OWNED[core]:
            for h in range(2):
                group = 8 * slot + at_group
                tiles = exchange([turn[h, group, at * 8 : (at + 1) * 8] for at in range(8)])
                for at in range(8):
                    out_ref[slot, at_group, 8 * h + at] = tiles[at]
        emit(core)


def total(parts):
    half = parts[:, :LANES] + parts[:, LANES:]
    return jnp.broadcast_to(jnp.sum(half, axis=(0, 1), keepdims=True), (1, ELEMENTS))


def fold(value):
    return jnp.sum(value.reshape(GROUPS, 8, ELEMENTS), axis=0)


def solve(b_ref, out_ref, weigh_in, weigh_out, scratch, emit):
    mass, diag, faces, k_ref, x, r, p, q, turn = scratch
    load_tiles(b_ref, turn, mass if weigh_in else None, r)
    norms = []
    for n in range(4):
        norms.append(total(fold(r[n] * r[n]) + fold(r[n + 4] * r[n + 4])))
    x[...] = jnp.zeros_like(x)
    p[...] = jnp.zeros_like(p)
    empty = jnp.zeros((8, ELEMENTS), F32)
    edge = jnp.zeros((16, ELEMENTS), F32)

    def sweep_body(sweep, carry):
        norms, alphas, betas = carry
        curves = []
        for n in range(4):
            curve = None
            for s in (n, n + 4):
                old = p[s]
                x[s] = x[s] + alphas[n] * old
                now = r[s] + betas[n] * old
                p[s] = now
                high = now.astype(BF16).astype(F32)
                halves = jnp.concatenate([high, now - high], axis=0).astype(BF16)
                image = jnp.dot(k_ref[...], halves, preferred_element_type=F32)
                ahead = pltpu.roll(now[: PADDED - 8], ELEMENTS - RADIAL, 1)
                behind = pltpu.roll(now[8:], RADIAL, 1)
                image = (
                    image[:PADDED]
                    + image[PADDED:]
                    + diag[n] * now
                    - faces[0] * jnp.concatenate([empty, ahead], axis=0)
                    - faces[1] * jnp.concatenate([behind, empty], axis=0)
                )
                outward = pltpu.roll(now[:16], ELEMENTS - 1, 1)
                inward = pltpu.roll(now[72:], 1, 1)
                image = jnp.concatenate(
                    [
                        image[:16] - faces[3, :16] * inward,
                        image[16:72],
                        image[72:] - faces[2, 72:] * outward,
                    ],
                    axis=0,
                )
                q[s] = image
                part = fold(now * image)
                curve = part if curve is None else curve + part
            curves.append(total(curve))
        alphas = [norms[n] / curves[n] for n in range(4)]

        def update():
            after = []
            for n in range(4):
                part = None
                for s in (n, n + 4):
                    value = r[s] - alphas[n] * q[s]
                    r[s] = value
                    add = fold(value * value)
                    part = add if part is None else part + add
                after.append(total(part))
            return after

        after = lax.cond(sweep < ITERS - 1, update, lambda: norms)
        betas = [after[n] / norms[n] for n in range(4)]
        return after, alphas, betas

    none = [jnp.zeros((1, ELEMENTS), F32)] * 4
    norms, alphas, betas = lax.fori_loop(0, ITERS, sweep_body, (norms, none, none))

    def value_of(s, rows, lanes):
        value = x[s, rows, lanes] + alphas[s % 4][:, lanes] * p[s, rows, lanes]
        return value * mass[rows, lanes] if weigh_out else value

    store_tiles(value_of, turn, out_ref, emit)


FIELD = pltpu.VMEM((8, PADDED, ELEMENTS), F32)
SOLVE_SCRATCH = [
    pltpu.VMEM((PADDED, ELEMENTS), F32),
    pltpu.VMEM((4, PADDED, ELEMENTS), F32),
    pltpu.VMEM((4, PADDED, ELEMENTS), F32),
    pltpu.VMEM((2 * PADDED, 2 * PADDED), BF16),
    FIELD,
    FIELD,
    FIELD,
    FIELD,
    pltpu.VMEM((2, GROUPS, 64, LANES), F32),
]


def split(value):
    high = value.astype(BF16)
    return high, (value - high.astype(F32)).astype(BF16)


def apply(t_ref, which, rows, field):
    high, low = field
    table_high = t_ref[2 * which, rows, :]
    table_low = t_ref[2 * which + 1, rows, :]
    return (
        jnp.dot(table_high, high, preferred_element_type=F32)
        + jnp.dot(table_high, low, preferred_element_type=F32)
        + jnp.dot(table_low, high, preferred_element_type=F32)
    )


def parts_of(u_ref):
    real, imag = [], []
    for slot in range(2):
        tiles = u_ref[slot].reshape(MODES // 8, 2, 8, LANES)
        one, two = mix(tiles[:, 0], tiles[:, 1])
        real.append(one.reshape(MODES, LANES))
        imag.append(two.reshape(MODES, LANES))
    return jnp.concatenate(real, axis=1), jnp.concatenate(imag, axis=1)


def parts_to(out_ref, half, real, imag):
    count = MODES // 2 // 8
    for slot in range(2):
        lanes = slice(slot * LANES, (slot + 1) * LANES)
        one, two = mix(
            real[:, lanes].reshape(count, 8, LANES), imag[:, lanes].reshape(count, 8, LANES)
        )
        out_ref[slot, 2 * count * half : 2 * count * (half + 1)] = jnp.stack(
            [one, two], axis=1
        ).reshape(2 * count, 8, LANES)


def mode_rows(width):
    row = lax.broadcasted_iota(jnp.int32, (MODES, width), 0)
    mode = (row // 64 % 4 * 2 + row // 256) * 64 + row % 64
    fraction = mode.astype(F32) / MODES
    weight = jnp.where(mode == 0, 1.0 / PLANES, 2.0 / PLANES).astype(F32)
    sign = jnp.where(mode % 2 == 0, 1.0, -1.0).astype(F32)
    return fraction, weight, sign


WIDTH = 2 * LANES
ROWS = 128


def to_planes(t_ref, cos_field, sin_field, outs):
    for at in range(MODES // ROWS):
        rows = slice(at * ROWS, (at + 1) * ROWS)
        outs(rows, apply(t_ref, 0, rows, cos_field), apply(t_ref, 1, rows, sin_field))


def first_stage(u_ref, t_ref, out_ref, planes_ref, emit):
    real, imag = parts_of(u_ref)
    fraction, weight, sign = mode_rows(WIDTH)
    cos_field = split(jnp.concatenate([real, fraction * imag], axis=1))
    sin_field = split(jnp.concatenate([imag, fraction * real], axis=1))
    middle = jnp.sum(sign * real, axis=0, keepdims=True)
    middle_turned = -jnp.sum(sign * fraction * imag, axis=0, keepdims=True)

    def store(rows, cos, sin):
        planes_ref[0, rows, :] = cos[:, :WIDTH] - sin[:, :WIDTH]
        planes_ref[1, rows, :] = cos[:, :WIDTH] + sin[:, :WIDTH]
        planes_ref[2, rows, :] = -cos[:, WIDTH:] - sin[:, WIDTH:]
        planes_ref[3, rows, :] = sin[:, WIDTH:] - cos[:, WIDTH:]

    to_planes(t_ref, cos_field, sin_field, store)
    planes_ref[1, 0:1, :] = middle
    planes_ref[3, 0:1, :] = middle_turned
    low = planes_ref[0] * planes_ref[2]
    high = planes_ref[1] * planes_ref[3]
    first = lax.broadcasted_iota(jnp.int32, (MODES, WIDTH), 0) == 0
    cos_side, sin_side = split(jnp.where(first, low, low + high)), split(low - high)
    for half in range(2):
        rows = slice(half * 256, (half + 1) * 256)
        a = apply(t_ref, 0, rows, cos_side) + sign[rows] * high[0:1]
        b = -apply(t_ref, 1, rows, sin_side)
        parts_to(
            out_ref, half, real[rows] - weight[rows] * a, imag[rows] - weight[rows] * b
        )
        emit(half)


def finish(t_ref, s_ref, planes, adjoint, at, out_ref, emit):
    s_real, s_imag = parts_of(s_ref)
    fraction, _, sign = mode_rows(WIDTH)
    first = lax.broadcasted_iota(jnp.int32, (MODES, WIDTH), 0) == 0
    pluses, minuses, middles = [], [], []
    for which in (2, 0):
        low = planes[which] * adjoint[at]
        high = planes[which + 1] * adjoint[at + 1]
        pluses.append(jnp.where(first, low, low + high))
        minuses.append(low - high)
        middles.append(high[0:1])
    cos_side = split(jnp.concatenate(pluses, axis=1))
    sin_side = split(jnp.concatenate(minuses, axis=1))
    for half in range(2):
        rows = slice(half * 256, (half + 1) * 256)
        cos = apply(t_ref, 0, rows, cos_side)
        sin = apply(t_ref, 1, rows, sin_side)
        a1 = cos[:, :WIDTH] + sign[rows] * middles[0]
        a2 = cos[:, WIDTH:] + sign[rows] * middles[1]
        b1 = -sin[:, :WIDTH]
        b2 = -sin[:, WIDTH:]
        parts_to(
            out_ref,
            half,
            s_real[rows] - a1 - fraction[rows] * b2,
            s_imag[rows] - b1 + fraction[rows] * a2,
        )
        emit(half)


def second_stage(u_ref, s_ref, t_ref, out_ref, planes, emit):
    real, imag = parts_of(u_ref)
    fraction, weight, sign = mode_rows(WIDTH)

    def store(rows, cos, sin):
        planes[0, rows, :] = cos[:, :WIDTH] - sin[:, :WIDTH]
        planes[1, rows, :] = cos[:, :WIDTH] + sin[:, :WIDTH]
        planes[2, rows, :] = -cos[:, WIDTH:] - sin[:, WIDTH:]
        planes[3, rows, :] = sin[:, WIDTH:] - cos[:, WIDTH:]

    cos_field = split(jnp.concatenate([real, fraction * imag], axis=1))
    sin_field = split(jnp.concatenate([imag, fraction * real], axis=1))
    to_planes(t_ref, cos_field, sin_field, store)
    planes[1, 0:1, :] = jnp.sum(sign * real, axis=0, keepdims=True)
    planes[3, 0:1, :] = -jnp.sum(sign * fraction * imag, axis=0, keepdims=True)
    finish(t_ref, s_ref, planes, planes, 4, out_ref, emit)


def adjoint_planes(s_ref, t_ref, planes):
    s_real, s_imag = parts_of(s_ref)
    _, weight, sign = mode_rows(WIDTH)

    def store(rows, cos, sin):
        planes[4, rows, :] = cos - sin
        planes[5, rows, :] = cos + sin

    to_planes(t_ref, split(weight * s_real), split(weight * s_imag), store)
    planes[5, 0:1, :] = jnp.sum(sign * weight * s_real, axis=0, keepdims=True)


COUNT = N_MODE * N_MER
SPARE = GROUPS - 8


def send(source, target, mode, mer, sems, at):
    pltpu.make_async_remote_copy(
        src_ref=source,
        dst_ref=target,
        send_sem=sems[0].at[at],
        recv_sem=sems[1].at[at],
        device_id={"mode": mode, "mer": mer},
        device_id_type=pl.DeviceIdType.MESH,
    ).start()


def wait(blank, tiles, sem):
    whole = blank.at[pl.ds(0, tiles)]
    pltpu.make_async_copy(whole, whole, sem).wait()


def wait_either(double, blank, tiles_double, tiles_single, sem):
    @pl.when(double)
    def _():
        wait(blank, tiles_double, sem)

    @pl.when(jnp.logical_not(double))
    def _():
        wait(blank, tiles_single, sem)


def place_at(mer, k):
    y = lax.rem(lax.rem(mer, 4) + lax.rem(k, 4), 4)
    z = lax.rem(mer // 4 + k // 4, 4)
    return z * 4 + y


def extra(x, mer):
    turn = lax.rem(lax.rem(mer, 4) + mer // 4, 4)
    return lax.rem(x + 4 - turn, 4)


def each_group(mode, cores, act):
    for core in cores:
        for x in range(4):
            other = 2 * x + core

            @pl.when(mode != other)
            def _(other=other):
                act(other)


def each_place(mer, act):
    def body(k, _):
        act(place_at(mer, k))
        return 0

    lax.fori_loop(1, N_MER, body, 0)


def each_other(mode, mer, cores, act):
    def body(place):
        for core in cores:
            for x in range(4):
                act(2 * x + core, place)

    each_place(mer, body)
    each_group(mode, cores, lambda other: act(other, mer))


def order_of(mode):
    return lax.rem(mode, 2) * 4 + mode // 2 if not isinstance(mode, int) else mode % 2 * 4 + mode // 2


def program_kernel(
    state_ref,
    cotangent_hbm,
    mass_ref,
    inverse_ref,
    d_ref,
    t_hbm,
    out_ref,
    cotangent_in,
    t_ref,
    copy_sems,
    rows,
    native_out,
    native_in,
    mode_out,
    mode_in,
    plane_out,
    plane_in,
    metric_out,
    metric_in,
    u_planes,
    planes,
    blank,
    send_sems,
    recv_sems,
    *solve_scratch,
):
    mode = lax.axis_index("mode")
    mer = lax.axis_index("mer")
    me = order_of(mode) * N_MER + mer
    mine_extra = extra(mode // 2, mer)
    double = (lax.rem(mode, 2) == 0) & (mine_extra < SPARE)
    sems = (send_sems, recv_sems)
    sent = []

    cotangent_copy = pltpu.make_async_copy(cotangent_hbm, cotangent_in, copy_sems.at[0])
    table_copy = pltpu.make_async_copy(t_hbm, t_ref, copy_sems.at[1])
    cotangent_copy.start()
    table_copy.start()
    barrier = pltpu.get_barrier_semaphore()

    def greet(other, place):
        pl.semaphore_signal(
            barrier,
            inc=1,
            device_id={"mode": other, "mer": place},
            device_id_type=pl.DeviceIdType.MESH,
        )

    each_other(mode, mer, (0, 1), greet)
    native_to_tiles(state_ref, native_out.at[0], rows)
    pl.semaphore_wait(barrier, COUNT - 1)

    def send_to_planes(source, target, at):
        def act(other, place):
            send(source.at[0, other, place], target.at[0, me], other, place, sems, at)
            if other % 2 == 0:
                index = extra(other // 2, place)

                @pl.when(index < SPARE)
                def _():
                    send(source.at[1, index, place], target.at[1, me], other, place, sems, at)

        def emit(core):
            each_other(mode, mer, (core,), act)
            if core == 1:
                target[0, me] = source[0, mode, mer]
                target[1, me] = source[1, mine_extra, mer]

        sent.append((at, 16 * GROUPS - 2, 16 * GROUPS - 1))
        return emit

    def wait_planes(at):
        wait_either(double, blank, 2 * (COUNT - 1), COUNT - 1, recv_sems.at[at])

    def send_to_modes(source, target, at):
        def act(other, place):
            index = order_of(other) * N_MER + place
            send(source.at[0, index], target.at[0, mode, mer], other, place, sems, at)

        def act_double(other, place):
            index = order_of(other) * N_MER + place
            send(source.at[0, index], target.at[0, mode, mer], other, place, sems, at)
            send(source.at[1, index], target.at[1, mine_extra, mer], other, place, sems, at)

        def emit(core):
            @pl.when(double)
            def _():
                each_other(mode, mer, (core,), act_double)

            @pl.when(jnp.logical_not(double))
            def _():
                each_other(mode, mer, (core,), act)

            if core == 1:
                target[0, mode, mer] = source[0, me]

                @pl.when(double)
                def _():
                    target[1, mine_extra, mer] = source[1, me]

        sent.append((at, 2 * (COUNT - 1), COUNT - 1))
        return emit

    def wait_modes(at):
        wait_either(double, blank, 16 * GROUPS - 2, 16 * GROUPS - 1, recv_sems.at[at])

    mine = pl.ds(pl.multiple_of(order_of(mode) * N_MER, N_MER), N_MER)
    plane_in[0, 0, mine] = native_out[0, 0, mode]
    plane_in[0, 1, mine] = native_out[0, 1, mine_extra]

    def send_state(other):
        send(native_out.at[0, 0, other], plane_in.at[0, 0, mine], other, mer, sems, 0)
        if other % 2 == 0:
            index = extra(other // 2, mer)

            @pl.when(index < SPARE)
            def _():
                send(native_out.at[0, 1, index], plane_in.at[0, 1, mine], other, mer, sems, 0)

    each_group(mode, (0, 1), send_state)
    sent.append((0, N_MER * (GROUPS - 2), N_MER * (GROUPS - 1)))

    cotangent_copy.wait()
    native_to_tiles(cotangent_in, native_out.at[1], rows)
    mode_in[0, :, :, mer] = native_out[1, :, :, mer]
    metric_rows(mass_ref, inverse_ref, rows, metric_out)
    metric_in[mer] = metric_out[...]

    def send_cotangent(other):
        send(native_out.at[1, 0, :, other], mode_in.at[0, 0, :, mer], mode, other, sems, 1)
        send(native_out.at[1, 1, 0:SPARE, other], mode_in.at[0, 1, 0:SPARE, mer], mode, other, sems, 1)
        send(metric_out, metric_in.at[mer], mode, other, sems, 2)

    each_place(mer, send_cotangent)
    sent.append((1, (N_MER - 1) * GROUPS, (N_MER - 1) * GROUPS))
    sent.append((2, (N_MER - 1) * 4, (N_MER - 1) * 4))

    mass, diag, faces, k_ref = solve_scratch[:4]
    turn = solve_scratch[8]
    stiffness_tables(d_ref, k_ref)

    wait_either(double, blank, 2 * (N_MODE - 1) * N_MER, (N_MODE - 1) * N_MER, recv_sems.at[0])
    table_copy.wait()
    emit = send_to_modes(plane_out.at[0], mode_in.at[1], 3)
    first_stage(plane_in.at[0], t_ref, plane_out.at[0], u_planes, emit)

    wait(blank, (N_MER - 1) * 4, recv_sems.at[2])
    metric_tables(metric_in, mode, mer, mass, diag, faces, turn)
    wait(blank, (N_MER - 1) * GROUPS, recv_sems.at[1])
    emit = send_to_planes(mode_out.at[0], plane_in.at[1], 4)
    solve(mode_in.at[0], mode_out.at[0], False, True, solve_scratch, emit)

    wait_modes(3)
    emit = send_to_planes(mode_out.at[1], plane_in.at[2], 5)
    solve(mode_in.at[1], mode_out.at[1], True, False, solve_scratch, emit)

    wait_planes(4)
    adjoint_planes(plane_in.at[1], t_ref, planes)
    wait_planes(5)
    emit = send_to_modes(plane_out.at[1], mode_in.at[2], 6)
    second_stage(plane_in.at[2], plane_in.at[1], t_ref, plane_out.at[1], planes, emit)

    wait_modes(6)
    emit = send_to_planes(mode_out.at[2], plane_in.at[3], 7)
    solve(mode_in.at[2], mode_out.at[2], False, True, solve_scratch, emit)

    wait_planes(7)
    adjoint_planes(plane_in.at[3], t_ref, planes)


    def send_gradient(other):
        theirs = slice(order_of(other) * N_MER, (order_of(other) + 1) * N_MER)
        send(plane_out.at[2, 0, theirs], native_in.at[0, mode], other, mer, sems, 8)

        @pl.when(double)
        def _():
            send(plane_out.at[2, 1, theirs], native_in.at[1, mine_extra], other, mer, sems, 8)

    def emit_gradient(core):
        each_group(mode, (core,), send_gradient)

    finish(t_ref, plane_in.at[3], u_planes, planes, 4, plane_out.at[2], emit_gradient)
    native_in[0, mode] = plane_out[2, 0, mine]

    @pl.when(double)
    def _():
        native_in[1, mine_extra] = plane_out[2, 1, mine]

    sent.append((8, 2 * (N_MODE - 1) * N_MER, (N_MODE - 1) * N_MER))
    wait_either(double, blank, N_MER * (GROUPS - 2), N_MER * (GROUPS - 1), recv_sems.at[8])
    tiles_to_native(native_in, out_ref, rows)
    for at, tiles_double, tiles_single in sent:
        wait_either(double, blank, tiles_double, tiles_single, send_sems.at[at])


def program(state, cotangent, mass, inverse, derivative, table):
    by_mode = (2, N_MODE, N_MER, 8, LANES)
    by_plane = (2, COUNT, 8, LANES)
    vmem = pl.BlockSpec(memory_space=pltpu.VMEM)
    hbm = pl.BlockSpec(memory_space=pl.ANY)

    def scratch(count, shape):
        return pltpu.VMEM((count,) + shape, F32)

    return pl.pallas_call(
        program_kernel,
        out_shape=jax.ShapeDtypeStruct((NODE, NODE, ELEM_DEV * LANES), F32),
        in_specs=[vmem, hbm, vmem, vmem, vmem, hbm],
        out_specs=vmem,
        scratch_shapes=[
            pltpu.VMEM((NODE, NODE, ELEM_DEV * LANES), F32),
            pltpu.VMEM((4, MODES, MODES), BF16),
            pltpu.SemaphoreType.DMA((2,)),
            pltpu.VMEM((PADDED * ELEM_DEV, LANES), F32),
            scratch(2, by_mode),
            pltpu.VMEM(by_mode, F32),
            scratch(3, by_mode),
            scratch(3, by_mode),
            scratch(3, by_plane),
            scratch(4, by_plane),
            pltpu.VMEM((2, 16, LANES), F32),
            scratch(N_MER, (2, 16, LANES)),
            pltpu.VMEM((4, MODES, WIDTH), F32),
            pltpu.VMEM((6, MODES, WIDTH), F32),
            pltpu.VMEM((2 * COUNT, 8, LANES), F32),
            pltpu.SemaphoreType.DMA((9,)),
            pltpu.SemaphoreType.DMA((9,)),
            *SOLVE_SCRATCH,
        ],
        compiler_params=pltpu.CompilerParams(
            collective_id=0, has_side_effects=True, vmem_limit_bytes=60 << 20
        ),
        name="program",
    )(state, cotangent, mass, inverse, derivative, table)


def shards(cotangent, checkpoint, mass, inv_radius_sq, derivative):
    table = jnp.asarray(tables())
    return program(checkpoint, cotangent, mass, inv_radius_sq, derivative, table)


def solution(mesh):
    return jax.shard_map(
        shards,
        mesh=mesh,
        in_specs=(
            P(None, None, ("mer", "mode")),
            P(None, None, ("mer", "mode")),
            P(None, None, "mer"),
            P(None, None, "mer"),
            P(),
        ),
        out_specs=P(None, None, ("mer", "mode")),
        check_vma=False,
    )
```

```python
import functools
import math

import jax
import jax.numpy as jnp
import ml_dtypes
import numpy as np
from jax import lax
from jax.experimental import pallas as pl
from jax.experimental.pallas import tpu as pltpu
from jax.sharding import PartitionSpec as P

NODE = 9
NODES = NODE * NODE
RADIAL = 8
ITERS = 4
MODES = 512
HALF = 256
PLANES = 1024
ELEMENTS = 256
N_MODE = 8
N_MER = 16
ELEM_DEV = 16
GROUPS = 11
PADDED = GROUPS * 8
LANES = 128
AZIMUTH_WEIGHT = 4.0
HIGHEST = lax.Precision.HIGHEST
F32 = jnp.float32
BF16 = jnp.bfloat16


def tables():
    order = np.arange(HALF).reshape(4, 2, HALF // N_MODE).transpose(1, 0, 2).reshape(-1)
    out = []
    for wave in (np.cos, np.sin):
        for odd in range(2):
            index = np.outer(np.arange(HALF), 2 * order + odd) % PLANES
            values = wave(index.astype(np.float64) * (2.0 * math.pi / PLANES)).astype(np.float32)
            high = values.astype(ml_dtypes.bfloat16)
            low = (values - high.astype(np.float32)).astype(ml_dtypes.bfloat16)
            out.append((high, low))
    both = [np.concatenate(pair) for pair in out]
    turned = [np.concatenate([high.T, low.T]) for high, low in out]
    return np.stack(both + turned)


def mix(first, second):
    shape = first.shape
    low = lax.broadcasted_iota(jnp.int32, shape, len(shape) - 2) % 8 < 4
    axis = len(shape) - 2
    return (
        jnp.where(low, first, pltpu.roll(second, 4, axis)),
        jnp.where(low, pltpu.roll(first, 4, axis), second),
    )


def exchange(tiles):
    tiles = list(tiles)
    axis = tiles[0].ndim - 1
    block = lax.broadcasted_iota(jnp.int32, tiles[0].shape, axis) // 16
    for bit in (1, 2, 4):
        clear = (block & bit) == 0
        for at in range(8):
            if at & bit:
                continue
            one, two = tiles[at], tiles[at | bit]
            tiles[at] = jnp.where(clear, one, pltpu.roll(two, 16 * bit, axis))
            tiles[at | bit] = jnp.where(clear, pltpu.roll(one, LANES - 16 * bit, axis), two)
    return tiles


def native_to_tiles(x_ref, out_ref, rows, turn):
    rows[pl.ds(NODES * ELEM_DEV, PADDED * ELEM_DEV - NODES * ELEM_DEV), :] = jnp.zeros(
        ((PADDED - NODES) * ELEM_DEV, LANES), F32
    )
    for i in range(NODE):
        for e in range(ELEM_DEV):
            rows[pl.ds(i * NODE * ELEM_DEV + e, NODE, stride=ELEM_DEV), :] = x_ref[
                i, :, e * LANES : (e + 1) * LANES
            ]
    for group in range(GROUPS):
        turned = rows[group * LANES : (group + 1) * LANES, :].T
        turn[0, group] = turned[:64]
        turn[1, group] = turned[64:]
        for odd in range(2):
            real = turn[0, group, pl.ds(odd, 32, stride=2), :].reshape(4, 8, LANES)
            imag = turn[1, group, pl.ds(odd, 32, stride=2), :].reshape(4, 8, LANES)
            one, two = mix(real, imag)
            out_ref[group // 8, group % 8, odd] = jnp.stack([one, two], axis=1).reshape(8, 8, LANES)


def tiles_to_native(t_ref, out_ref, rows, turn):
    for group in range(GROUPS):
        for odd in range(2):
            tiles = t_ref[group // 8, group % 8, odd].reshape(4, 2, 8, LANES)
            real, imag = mix(tiles[:, 0], tiles[:, 1])
            turn[0, group, pl.ds(odd, 32, stride=2), :] = real.reshape(32, LANES)
            turn[1, group, pl.ds(odd, 32, stride=2), :] = imag.reshape(32, LANES)
        both = jnp.concatenate([turn[0, group], turn[1, group]], axis=0)
        rows[group * LANES : (group + 1) * LANES, :] = both.T
    for i in range(NODE):
        for e in range(ELEM_DEV):
            out_ref[i, :, e * LANES : (e + 1) * LANES] = rows[
                pl.ds(i * NODE * ELEM_DEV + e, NODE, stride=ELEM_DEV), :
            ]


def stiffness_tables(d_ref, k_ref):
    def dot(a, b):
        return jnp.dot(a, b, precision=HIGHEST, preferred_element_type=F32)

    derivative = d_ref[...]
    stiffness = lax.dot_general(
        derivative, derivative, (((0,), (0,)), ((), ())), precision=HIGHEST, preferred_element_type=F32
    )

    def pick(shape, node_axis, outer):
        node = lax.broadcasted_iota(jnp.int32, shape, node_axis)
        other = lax.broadcasted_iota(jnp.int32, shape, 1 - node_axis)
        place = node // NODE if outer else node % NODE
        return jnp.where((place == other) & (node < NODES), 1.0, 0.0).astype(F32)

    outer, inner = pick((PADDED, NODE), 0, True), pick((PADDED, NODE), 0, False)
    outer_t, inner_t = pick((NODE, PADDED), 1, True), pick((NODE, PADDED), 1, False)
    whole = dot(dot(outer, stiffness), outer_t) * dot(inner, inner_t)
    whole = whole + dot(dot(inner, stiffness), inner_t) * dot(outer, outer_t)
    high = whole.astype(BF16).astype(F32)
    low = whole - high
    top = jnp.concatenate([high, high], axis=1)
    bottom = jnp.concatenate([low, jnp.zeros_like(low)], axis=1)
    k_ref[...] = jnp.concatenate([top, bottom], axis=0).astype(BF16)


def metric_rows(mass_ref, inverse_ref, rows, out_ref):
    lane = lax.broadcasted_iota(jnp.int32, (ELEM_DEV, LANES), 1) % ELEM_DEV
    element = lax.broadcasted_iota(jnp.int32, (ELEM_DEV, LANES), 0)
    repeat = jnp.where(lane == element, 1.0, 0.0).astype(F32)
    shape = (PADDED, LANES)
    node = lax.broadcasted_iota(jnp.int32, shape, 0)
    block = lax.broadcasted_iota(jnp.int32, shape, 1) // ELEM_DEV
    keep = (node % 8 == block) & (node < NODES)
    for kind, ref in ((0, mass_ref), (1, inverse_ref)):
        for i in range(NODE):
            rows[i * NODE : (i + 1) * NODE, :ELEM_DEV] = ref[i]
        values = jnp.dot(
            rows[:PADDED, :ELEM_DEV], repeat, precision=HIGHEST, preferred_element_type=F32
        )
        values = jnp.where(keep, values, 0.0).reshape(GROUPS, 8, LANES)
        out_ref[kind, :GROUPS] = jnp.sum(values, axis=1)
        out_ref[kind, GROUPS:] = jnp.zeros((16 - GROUPS, LANES), F32)


def metric_tables(m_ref, mode_group, place, mass, diag, faces, turn):
    inverse = diag.at[0]
    for kind, out in ((0, mass), (1, inverse)):
        for h in range(2):
            rows = exchange([m_ref[8 * h + at, kind] for at in range(8)])
            for at in range(8):
                for group in range(GROUPS):
                    turn[h, group, at : at + 1] = rows[at][group : group + 1]
            for group in range(GROUPS):
                out[group * 8 : (group + 1) * 8, h * LANES : (h + 1) * LANES] = turn[h, group, 0:8]
    shape = (PADDED, ELEMENTS)
    node = lax.broadcasted_iota(jnp.int32, shape, 0)
    element = lax.broadcasted_iota(jnp.int32, shape, 1)
    inside = node < NODES
    upper = (node % NODE == NODE - 1) & (element < ELEMENTS - RADIAL) & inside
    lower = (node % NODE == 0) & (element >= RADIAL) & inside
    outer = (node // NODE == NODE - 1) & (element % RADIAL != RADIAL - 1) & inside
    inner = (node // NODE == 0) & (element % RADIAL != 0)
    marks = [jnp.where(mark, 1.0, 0.0).astype(F32) for mark in (upper, lower, outer, inner)]
    for at in range(4):
        faces[at] = marks[at]
    count = marks[0] + marks[1] + marks[2] + marks[3]
    values = inverse[...]
    for n in range(4):
        number = mode_group * 64 + lax.rem(place, 8) * 8 + 2 * n + place // 8
        fraction = number.astype(F32) / MODES
        diag[n] = mass[...] * (1.0 + AZIMUTH_WEIGHT * fraction * fraction * values) + count


CHUNKS = ((0, 0, 3), (0, 3, 6), (0, 6, 8), (1, 0, 3))


def load_tiles(b_ref, turn, weight, out):
    for slot, start, stop in CHUNKS:
        for h in range(2):
            tiles = exchange([b_ref[slot, start:stop, 8 * h + at] for at in range(8)])
            for at in range(8):
                turn[h, 8 * slot + start : 8 * slot + stop, at * 8 : (at + 1) * 8] = tiles[at]
    for s in range(8):
        for h in range(2):
            lanes = slice(h * LANES, (h + 1) * LANES)
            for group in range(GROUPS):
                rows = slice(group * 8, (group + 1) * 8)
                value = turn[h, group, pl.ds(s, 8, stride=8), :]
                if weight is not None:
                    value = value * weight[rows, lanes]
                out[s, rows, lanes] = value


OWNED = (((1, 0), (1, 1), (1, 2)), ((0, 0), (0, 2), (0, 4), (0, 6)), ((0, 1), (0, 3), (0, 5), (0, 7)))


def store_tiles(value_of, turn, out_ref, emit):
    for phase in range(3):
        for s in range(8):
            for slot, at_group in OWNED[phase]:
                group = 8 * slot + at_group
                for h in range(2):
                    turn[h, group, pl.ds(s, 8, stride=8), :] = value_of(
                        s, slice(group * 8, (group + 1) * 8), slice(h * LANES, (h + 1) * LANES)
                    )
        for slot, at_group in OWNED[phase]:
            for h in range(2):
                group = 8 * slot + at_group
                tiles = exchange([turn[h, group, at * 8 : (at + 1) * 8] for at in range(8)])
                for at in range(8):
                    out_ref[slot, at_group, 8 * h + at] = tiles[at]
        emit(phase)


def total(parts):
    half = parts[:, :LANES] + parts[:, LANES:]
    return jnp.broadcast_to(jnp.sum(half, axis=(0, 1), keepdims=True), (1, ELEMENTS))


def fold(value):
    return jnp.sum(value.reshape(GROUPS, 8, ELEMENTS), axis=0)


def solve(b_ref, out_ref, weigh_in, weigh_out, scratch, emit):
    mass, diag, faces, k_ref, x, r, p, q, turn = scratch
    load_tiles(b_ref, turn, mass if weigh_in else None, r)
    norms = []
    for n in range(4):
        norms.append(total(fold(r[n] * r[n]) + fold(r[n + 4] * r[n + 4])))
    x[...] = jnp.zeros_like(x)
    p[...] = jnp.zeros_like(p)
    empty = jnp.zeros((8, ELEMENTS), F32)
    edge = jnp.zeros((16, ELEMENTS), F32)

    def sweep_body(sweep, carry):
        norms, alphas, betas = carry
        curves = []
        for n in range(4):
            curve = None
            for s in (n, n + 4):
                old = p[s]
                x[s] = x[s] + alphas[n] * old
                now = r[s] + betas[n] * old
                p[s] = now
                high = now.astype(BF16).astype(F32)
                halves = jnp.concatenate([high, now - high], axis=0).astype(BF16)
                image = jnp.dot(k_ref[...], halves, preferred_element_type=F32)
                ahead = pltpu.roll(now[: PADDED - 8], ELEMENTS - RADIAL, 1)
                behind = pltpu.roll(now[8:], RADIAL, 1)
                image = (
                    image[:PADDED]
                    + image[PADDED:]
                    + diag[n] * now
                    - faces[0] * jnp.concatenate([empty, ahead], axis=0)
                    - faces[1] * jnp.concatenate([behind, empty], axis=0)
                )
                outward = pltpu.roll(now[:16], ELEMENTS - 1, 1)
                inward = pltpu.roll(now[72:], 1, 1)
                image = jnp.concatenate(
                    [
                        image[:16] - faces[3, :16] * inward,
                        image[16:72],
                        image[72:] - faces[2, 72:] * outward,
                    ],
                    axis=0,
                )
                q[s] = image
                part = fold(now * image)
                curve = part if curve is None else curve + part
            curves.append(total(curve))
        alphas = [norms[n] / curves[n] for n in range(4)]

        def update():
            after = []
            for n in range(4):
                part = None
                for s in (n, n + 4):
                    value = r[s] - alphas[n] * q[s]
                    r[s] = value
                    add = fold(value * value)
                    part = add if part is None else part + add
                after.append(total(part))
            return after

        after = lax.cond(sweep < ITERS - 1, update, lambda: norms)
        betas = [after[n] / norms[n] for n in range(4)]
        return after, alphas, betas

    none = [jnp.zeros((1, ELEMENTS), F32)] * 4
    norms, alphas, betas = lax.fori_loop(0, ITERS, sweep_body, (norms, none, none))

    def value_of(s, rows, lanes):
        value = x[s, rows, lanes] + alphas[s % 4][:, lanes] * p[s, rows, lanes]
        return value * mass[rows, lanes] if weigh_out else value

    store_tiles(value_of, turn, out_ref, emit)


FIELD = pltpu.VMEM((8, PADDED, ELEMENTS), F32)
SOLVE_SCRATCH = [
    pltpu.VMEM((PADDED, ELEMENTS), F32),
    pltpu.VMEM((4, PADDED, ELEMENTS), F32),
    pltpu.VMEM((4, PADDED, ELEMENTS), F32),
    pltpu.VMEM((2 * PADDED, 2 * PADDED), BF16),
    FIELD,
    FIELD,
    FIELD,
    FIELD,
    pltpu.VMEM((2, GROUPS, 64, LANES), F32),
]


def split(value):
    high = value.astype(BF16)
    return high, (value - high.astype(F32)).astype(BF16)


def apply(t_ref, which, field):
    high, low = split(field)
    width = field.shape[1]
    if width == LANES:
        both = jnp.concatenate([high, low], axis=1)
        out = jnp.dot(t_ref[which], both, preferred_element_type=F32)
        return out[:HALF, :LANES] + out[:HALF, LANES:] + out[HALF:, :LANES]
    out = jnp.dot(t_ref[which], high, preferred_element_type=F32)
    out = out[:HALF] + out[HALF:]
    return out + jnp.dot(t_ref[which, :HALF], low, preferred_element_type=F32)


def parts_of(u_ref):
    out = []
    for odd in range(2):
        tiles = u_ref[odd].reshape(32, 2, 8, LANES)
        one, two = mix(tiles[:, 0], tiles[:, 1])
        out.append((one.reshape(HALF, LANES), two.reshape(HALF, LANES)))
    return out


def parts_to(out_ref, parts):
    for odd in range(2):
        real, imag = parts[odd]
        one, two = mix(real.reshape(32, 8, LANES), imag.reshape(32, 8, LANES))
        out_ref[odd] = jnp.stack([one, two], axis=1).reshape(64, 8, LANES)


def mode_rows(odd):
    row = lax.broadcasted_iota(jnp.int32, (HALF, LANES), 0)
    mode = 2 * ((row // 32 % 4 * 2 + row // 128) * 32 + row % 32) + odd
    fraction = mode.astype(F32) / MODES
    weight = jnp.where(mode == 0, 1.0 / PLANES, 2.0 / PLANES).astype(F32)
    sign = jnp.where(row % 2 == 0, 1.0, -1.0).astype(F32)
    return fraction, weight, sign


def first_row(shape):
    return lax.broadcasted_iota(jnp.int32, shape, 0) == 0


def to_planes(t_ref, cos_fields, sin_fields, out_ref):
    sign = mode_rows(0)[2][:, :1]
    cos_even, cos_odd = apply(t_ref, 0, cos_fields[0]), apply(t_ref, 1, cos_fields[1])
    sin_even, sin_odd = apply(t_ref, 2, sin_fields[0]), apply(t_ref, 3, sin_fields[1])
    quarter_cos = jnp.sum(sign * cos_fields[0], axis=0, keepdims=True)
    quarter_sin = jnp.sum(sign * sin_fields[1], axis=0, keepdims=True)
    cos, sin = cos_even + cos_odd, sin_even + sin_odd
    out_ref[0] = cos - sin
    out_ref[1] = cos + sin
    cos, sin = cos_even - cos_odd, sin_even - sin_odd
    out_ref[2] = cos + sin
    out_ref[3] = cos - sin
    out_ref[1, 0:1] = quarter_cos - quarter_sin
    out_ref[3, 0:1] = quarter_cos + quarter_sin


def from_planes(t_ref, values):
    shape = values[0].shape
    sign = mode_rows(0)[2][:, :1]
    first = first_row(shape)
    quarter, three = values[1][0:1], values[3][0:1]
    one = values[0]
    two = jnp.where(first, 0.0, values[1])
    four = jnp.where(first, 0.0, values[3])
    plus, minus = one + two, one - two
    plus_far, minus_far = values[2] + four, values[2] - four
    a_even = apply(t_ref, 4, plus + plus_far) + sign * (quarter + three)
    a_odd = apply(t_ref, 5, plus - plus_far)
    b_even = -apply(t_ref, 6, minus - minus_far)
    b_odd = -apply(t_ref, 7, minus + minus_far) - sign * (quarter - three)
    return (a_even, b_even), (a_odd, b_odd)


def state_planes(parts, t_ref, out_ref):
    cos_fields, sin_fields = [], []
    for odd in range(2):
        real, imag = parts[odd]
        fraction = mode_rows(odd)[0]
        cos_fields.append(jnp.concatenate([real, -fraction * imag], axis=1))
        sin_fields.append(jnp.concatenate([imag, fraction * real], axis=1))
    to_planes(t_ref, cos_fields, sin_fields, out_ref)


def first_stage(u_ref, t_ref, planes, out_ref):
    parts = parts_of(u_ref)
    state_planes(parts, t_ref, planes)
    values = [planes[at, :, :LANES] * planes[at, :, LANES:] for at in range(4)]
    found = from_planes(t_ref, values)
    out = []
    for odd in range(2):
        weight = mode_rows(odd)[1]
        out.append(tuple(parts[odd][c] - weight * found[odd][c] for c in range(2)))
    parts_to(out_ref, out)


def adjoint_planes(s_ref, t_ref, out_ref):
    parts = parts_of(s_ref)
    weights = [mode_rows(odd)[1] for odd in range(2)]
    to_planes(
        t_ref,
        [weights[odd] * parts[odd][0] for odd in range(2)],
        [weights[odd] * parts[odd][1] for odd in range(2)],
        out_ref,
    )


def finish(t_ref, s_ref, planes, adjoint, out_ref):
    values = []
    for at in range(4):
        factor = adjoint[at]
        values.append(planes[at] * jnp.concatenate([factor, factor], axis=1))
    found = from_planes(t_ref, values)
    parts = parts_of(s_ref)
    out = []
    for odd in range(2):
        fraction = mode_rows(odd)[0]
        a, b = found[odd]
        out.append(
            (
                parts[odd][0] - a[:, LANES:] - fraction * b[:, :LANES],
                parts[odd][1] - b[:, LANES:] + fraction * a[:, :LANES],
            )
        )
    parts_to(out_ref, out)


COUNT = N_MODE * N_MER
SPARE = GROUPS - 8


def send(source, target, mode, mer, sems, at):
    pltpu.make_async_remote_copy(
        src_ref=source,
        dst_ref=target,
        send_sem=sems[0].at[at],
        recv_sem=sems[1].at[at],
        device_id={"mode": mode, "mer": mer},
        device_id_type=pl.DeviceIdType.MESH,
    ).start()


def wait(blank, tiles, sem):
    whole = blank.at[pl.ds(0, tiles)]
    pltpu.make_async_copy(whole, whole, sem).wait()


def wait_either(double, blank, tiles_double, tiles_single, sem):
    @pl.when(double)
    def _():
        wait(blank, tiles_double, sem)

    @pl.when(jnp.logical_not(double))
    def _():
        wait(blank, tiles_single, sem)


def place_at(mer, k):
    y = lax.rem(lax.rem(mer, 4) + lax.rem(k, 4), 4)
    z = lax.rem(mer // 4 + k // 4, 4)
    return z * 4 + y


def extra(x, mer):
    turn = lax.rem(lax.rem(mer, 4) + mer // 4, 4)
    return lax.rem(x + 4 - turn, 4)


def each_group(mode, cores, act):
    for core in cores:
        for x in range(4):
            other = 2 * x + core

            @pl.when(mode != other)
            def _(other=other):
                act(other)


def each_place(mer, act):
    def body(k, _):
        act(place_at(mer, k))
        return 0

    lax.fori_loop(1, N_MER, body, 0)


def each_other(mode, mer, cores, act):
    def body(place):
        for core in cores:
            for x in range(4):
                act(2 * x + core, place)

    each_place(mer, body)
    each_group(mode, cores, lambda other: act(other, mer))


def order_of(mode):
    return lax.rem(mode, 2) * 4 + mode // 2 if not isinstance(mode, int) else mode % 2 * 4 + mode // 2


def program_kernel(
    state_ref,
    cotangent_hbm,
    mass_ref,
    inverse_ref,
    d_ref,
    t_hbm,
    out_ref,
    cotangent_in,
    t_ref,
    copy_sems,
    rows,
    native_out,
    native_in,
    mode_out,
    mode_in,
    plane_out,
    plane_in,
    metric_out,
    metric_in,
    u_planes,
    planes,
    s_planes,
    blank,
    send_sems,
    recv_sems,
    *solve_scratch,
):
    mode = lax.axis_index("mode")
    mer = lax.axis_index("mer")
    odd, eighth = mer // 8, lax.rem(mer, 8)
    row = order_of(mode) * 8 + eighth
    mine_extra = extra(mode // 2, mer)
    double = (lax.rem(mode, 2) == 0) & (mine_extra < SPARE)
    slots = jnp.where(double, 2, 1)
    sems = (send_sems, recv_sems)
    mass, diag, faces, k_ref = solve_scratch[:4]
    turn = solve_scratch[8]
    sent = []

    cotangent_copy = pltpu.make_async_copy(cotangent_hbm, cotangent_in, copy_sems.at[0])
    table_copy = pltpu.make_async_copy(t_hbm, t_ref, copy_sems.at[1])
    cotangent_copy.start()
    table_copy.start()
    barrier = pltpu.get_barrier_semaphore()

    def greet(other, place):
        pl.semaphore_signal(
            barrier,
            inc=1,
            device_id={"mode": other, "mer": place},
            device_id_type=pl.DeviceIdType.MESH,
        )

    each_other(mode, mer, (0, 1), greet)
    native_to_tiles(state_ref, native_out.at[0], rows, turn)
    pl.semaphore_wait(barrier, COUNT - 1)

    def each_slot(act):
        def body(k, _):
            act(slots - 1 - k)
            return 0

        lax.fori_loop(0, slots, body, 0)

    def send_to_planes(source, target, at):
        def act(other, place):
            send(source.at[0, other, place], target.at[0, odd, row], other, place, sems, at)

        def act_extra(other, place):
            index = extra(other // 2, place)

            @pl.when(index < SPARE)
            def _():
                send(source.at[1, index, place], target.at[1, odd, row], other, place, sems, at + 1)

        def emit(phase):
            if phase == 0:
                target[1, odd, row] = source[1, mine_extra, mer]
                each_other(mode, mer, (0,), act_extra)
            else:
                each_other(mode, mer, (phase - 1,), act)
            if phase == 2:
                target[0, odd, row] = source[0, mode, mer]

        sent.append((at, COUNT - 1, COUNT - 1))
        sent.append((at + 1, 16 * SPARE - 1, 16 * SPARE))
        return emit

    def wait_planes(at, slot):
        wait(blank, COUNT - 1, recv_sems.at[at + slot])

    def send_to_modes(source, target, at):
        def emit(slot):
            group = jnp.where(slot == 1, mine_extra, mode)
            target[slot, group, mer] = source[slot, odd, row]

            def act(other, place):
                piece = source.at[slot, place // 8, order_of(other) * 8 + lax.rem(place, 8)]
                send(piece, target.at[slot, group, mer], other, place, sems, at)

            each_other(mode, mer, (0, 1), act)

        sent.append((at, 2 * (COUNT - 1), COUNT - 1))
        return emit

    def wait_modes(at):
        wait_either(double, blank, 16 * GROUPS - 2, 16 * GROUPS - 1, recv_sems.at[at])

    mine = pl.ds(pl.multiple_of(order_of(mode) * 8, 8), 8)
    plane_in[0, 0, :, mine] = native_out[0, 0, mode]
    plane_in[0, 1, :, mine] = native_out[0, 1, mine_extra]

    def send_extra_state(other):
        index = extra(other // 2, mer)

        @pl.when(index < SPARE)
        def _():
            send(native_out.at[0, 1, index], plane_in.at[0, 1, :, mine], other, mer, sems, 1)

    def send_state(other):
        send(native_out.at[0, 0, other], plane_in.at[0, 0, :, mine], other, mer, sems, 0)

    each_group(mode, (0,), send_extra_state)
    each_group(mode, (0, 1), send_state)
    sent.append((0, N_MER * (N_MODE - 1), N_MER * (N_MODE - 1)))
    sent.append((1, N_MER * (SPARE - 1), N_MER * SPARE))

    cotangent_copy.wait()
    native_to_tiles(cotangent_in, native_out.at[1], rows, turn)
    mode_in[0, 0, :, mer] = native_out[1, 0, :, odd, eighth]
    mode_in[0, 1, 0:SPARE, mer] = native_out[1, 1, 0:SPARE, odd, eighth]
    metric_rows(mass_ref, inverse_ref, rows, metric_out)
    metric_in[mer] = metric_out[...]

    def send_cotangent(place):
        which, at = place // 8, lax.rem(place, 8)
        send(native_out.at[1, 0, :, which, at], mode_in.at[0, 0, :, mer], mode, place, sems, 2)
        send(
            native_out.at[1, 1, 0:SPARE, which, at],
            mode_in.at[0, 1, 0:SPARE, mer],
            mode,
            place,
            sems,
            2,
        )
        send(metric_out, metric_in.at[mer], mode, place, sems, 3)

    each_place(mer, send_cotangent)
    sent.append((2, (N_MER - 1) * GROUPS, (N_MER - 1) * GROUPS))
    sent.append((3, (N_MER - 1) * 4, (N_MER - 1) * 4))

    stiffness_tables(d_ref, k_ref)
    table_copy.wait()

    emit_rhs = send_to_modes(plane_out.at[0], mode_in.at[1], 4)

    def first(slot):
        wait(blank, (N_MODE - 1) * N_MER, recv_sems.at[slot])
        first_stage(plane_in.at[0, slot], t_ref, u_planes.at[slot], plane_out.at[0, slot])
        emit_rhs(slot)

    each_slot(first)

    wait(blank, (N_MER - 1) * 4, recv_sems.at[3])
    metric_tables(metric_in, mode, mer, mass, diag, faces, turn)
    wait(blank, (N_MER - 1) * GROUPS, recv_sems.at[2])
    emit = send_to_planes(mode_out.at[0], plane_in.at[1], 5)
    solve(mode_in.at[0], mode_out.at[0], False, True, solve_scratch, emit)

    wait_modes(4)
    emit = send_to_planes(mode_out.at[1], plane_in.at[2], 7)
    solve(mode_in.at[1], mode_out.at[1], True, False, solve_scratch, emit)

    def multiplier(slot):
        wait_planes(5, slot)
        adjoint_planes(plane_in.at[1, slot], t_ref, s_planes.at[slot])

    each_slot(multiplier)
    emit_adjoint = send_to_modes(plane_out.at[1], mode_in.at[2], 9)

    def second(slot):
        wait_planes(7, slot)
        state_planes(parts_of(plane_in.at[2, slot]), t_ref, planes)
        finish(t_ref, plane_in.at[1, slot], planes, s_planes.at[slot], plane_out.at[1, slot])
        emit_adjoint(slot)

    each_slot(second)

    wait_modes(9)
    emit = send_to_planes(mode_out.at[2], plane_in.at[3], 10)
    solve(mode_in.at[2], mode_out.at[2], False, True, solve_scratch, emit)

    def third(slot):
        wait_planes(10, slot)
        adjoint_planes(plane_in.at[3, slot], t_ref, s_planes.at[slot])
        finish(
            t_ref, plane_in.at[3, slot], u_planes.at[slot], s_planes.at[slot], plane_out.at[2, slot]
        )
        group = jnp.where(slot == 1, mine_extra, mode)
        native_in[slot, group] = plane_out[2, slot, :, mine]

        def send_gradient(other):
            theirs = slice(order_of(other) * 8, (order_of(other) + 1) * 8)
            send(plane_out.at[2, slot, :, theirs], native_in.at[slot, group], other, mer, sems, 12)

        each_group(mode, (0, 1), send_gradient)

    each_slot(third)
    sent.append((12, 2 * (N_MODE - 1) * N_MER, (N_MODE - 1) * N_MER))
    wait_either(double, blank, N_MER * (GROUPS - 2), N_MER * (GROUPS - 1), recv_sems.at[12])
    tiles_to_native(native_in, out_ref, rows, turn)
    for at, tiles_double, tiles_single in sent:
        wait_either(double, blank, tiles_double, tiles_single, send_sems.at[at])


def program(state, cotangent, mass, inverse, derivative, table):
    by_mode = (2, N_MODE, N_MER, 8, LANES)
    by_native = (2, N_MODE, 2, 8, 8, LANES)
    by_plane = (2, 2, COUNT // 2, 8, LANES)
    vmem = pl.BlockSpec(memory_space=pltpu.VMEM)
    hbm = pl.BlockSpec(memory_space=pl.ANY)

    def scratch(count, shape):
        return pltpu.VMEM((count,) + shape, F32)

    return pl.pallas_call(
        program_kernel,
        out_shape=jax.ShapeDtypeStruct((NODE, NODE, ELEM_DEV * LANES), F32),
        in_specs=[vmem, hbm, vmem, vmem, vmem, hbm],
        out_specs=vmem,
        scratch_shapes=[
            pltpu.VMEM((NODE, NODE, ELEM_DEV * LANES), F32),
            pltpu.VMEM((8, 2 * HALF, HALF), BF16),
            pltpu.SemaphoreType.DMA((2,)),
            pltpu.VMEM((PADDED * ELEM_DEV, LANES), F32),
            scratch(2, by_native),
            pltpu.VMEM(by_native, F32),
            scratch(3, by_mode),
            scratch(3, by_mode),
            scratch(3, by_plane),
            scratch(4, by_plane),
            pltpu.VMEM((2, 16, LANES), F32),
            scratch(N_MER, (2, 16, LANES)),
            scratch(2, (4, HALF, 2 * LANES)),
            scratch(4, (HALF, 2 * LANES)),
            scratch(2, (4, HALF, LANES)),
            pltpu.VMEM((2 * COUNT, 8, LANES), F32),
            pltpu.SemaphoreType.DMA((13,)),
            pltpu.SemaphoreType.DMA((13,)),
            *SOLVE_SCRATCH,
        ],
        compiler_params=pltpu.CompilerParams(
            collective_id=0, has_side_effects=True, vmem_limit_bytes=60 << 20
        ),
        name="program",
    )(state, cotangent, mass, inverse, derivative, table)


def shards(cotangent, checkpoint, mass, inv_radius_sq, derivative):
    table = jnp.asarray(tables())
    return program(checkpoint, cotangent, mass, inv_radius_sq, derivative, table)


def solution(mesh):
    return jax.shard_map(
        shards,
        mesh=mesh,
        in_specs=(
            P(None, None, ("mer", "mode")),
            P(None, None, ("mer", "mode")),
            P(None, None, "mer"),
            P(None, None, "mer"),
            P(),
        ),
        out_specs=P(None, None, ("mer", "mode")),
        check_vma=False,
    )
```

```python
import functools
import math

import jax
import jax.numpy as jnp
import ml_dtypes
import numpy as np
from jax import lax
from jax.experimental import pallas as pl
from jax.experimental.pallas import tpu as pltpu
from jax.sharding import PartitionSpec as P

NODE = 9
NODES = NODE * NODE
RADIAL = 8
ITERS = 4
MODES = 512
HALF = 256
PLANES = 1024
ELEMENTS = 256
N_MODE = 8
N_MER = 16
ELEM_DEV = 16
GROUPS = 11
PADDED = GROUPS * 8
LANES = 128
AZIMUTH_WEIGHT = 4.0
HIGHEST = lax.Precision.HIGHEST
F32 = jnp.float32
BF16 = jnp.bfloat16


def tables():
    order = np.arange(HALF).reshape(4, 2, HALF // N_MODE).transpose(1, 0, 2).reshape(-1)
    out = []
    for wave in (np.cos, np.sin):
        for odd in range(2):
            index = np.outer(np.arange(HALF), 2 * order + odd) % PLANES
            values = wave(index.astype(np.float64) * (2.0 * math.pi / PLANES)).astype(np.float32)
            high = values.astype(ml_dtypes.bfloat16)
            low = (values - high.astype(np.float32)).astype(ml_dtypes.bfloat16)
            out.append((high, low))
    both = [np.concatenate(pair) for pair in out]
    turned = [np.concatenate([high.T, low.T]) for high, low in out]
    return np.stack(both + turned)


def mix(first, second):
    shape = first.shape
    low = lax.broadcasted_iota(jnp.int32, shape, len(shape) - 2) % 8 < 4
    axis = len(shape) - 2
    return (
        jnp.where(low, first, pltpu.roll(second, 4, axis)),
        jnp.where(low, pltpu.roll(first, 4, axis), second),
    )


def exchange(tiles):
    tiles = list(tiles)
    axis = tiles[0].ndim - 1
    block = lax.broadcasted_iota(jnp.int32, tiles[0].shape, axis) // 16
    for bit in (1, 2, 4):
        clear = (block & bit) == 0
        for at in range(8):
            if at & bit:
                continue
            one, two = tiles[at], tiles[at | bit]
            tiles[at] = jnp.where(clear, one, pltpu.roll(two, 16 * bit, axis))
            tiles[at | bit] = jnp.where(clear, pltpu.roll(one, LANES - 16 * bit, axis), two)
    return tiles


def native_to_tiles(x_ref, out_ref, rows, turn):
    rows[pl.ds(NODES * ELEM_DEV, PADDED * ELEM_DEV - NODES * ELEM_DEV), :] = jnp.zeros(
        ((PADDED - NODES) * ELEM_DEV, LANES), F32
    )
    for i in range(NODE):
        for e in range(ELEM_DEV):
            rows[pl.ds(i * NODE * ELEM_DEV + e, NODE, stride=ELEM_DEV), :] = x_ref[
                i, :, e * LANES : (e + 1) * LANES
            ]
    for group in range(GROUPS):
        turned = rows[group * LANES : (group + 1) * LANES, :].T
        turn[0, group] = turned[:64]
        turn[1, group] = turned[64:]
        for odd in range(2):
            real = turn[0, group, pl.ds(odd, 32, stride=2), :].reshape(4, 8, LANES)
            imag = turn[1, group, pl.ds(odd, 32, stride=2), :].reshape(4, 8, LANES)
            one, two = mix(real, imag)
            out_ref[group // 8, group % 8, odd] = jnp.stack([one, two], axis=1).reshape(8, 8, LANES)


def tiles_to_native(t_ref, out_ref, rows, turn):
    for group in range(GROUPS):
        for odd in range(2):
            tiles = t_ref[group // 8, group % 8, odd].reshape(4, 2, 8, LANES)
            real, imag = mix(tiles[:, 0], tiles[:, 1])
            turn[0, group, pl.ds(odd, 32, stride=2), :] = real.reshape(32, LANES)
            turn[1, group, pl.ds(odd, 32, stride=2), :] = imag.reshape(32, LANES)
        both = jnp.concatenate([turn[0, group], turn[1, group]], axis=0)
        rows[group * LANES : (group + 1) * LANES, :] = both.T
    for i in range(NODE):
        for e in range(ELEM_DEV):
            out_ref[i, :, e * LANES : (e + 1) * LANES] = rows[
                pl.ds(i * NODE * ELEM_DEV + e, NODE, stride=ELEM_DEV), :
            ]


def stiffness_tables(d_ref, k_ref):
    def dot(a, b):
        return jnp.dot(a, b, precision=HIGHEST, preferred_element_type=F32)

    derivative = d_ref[...]
    stiffness = lax.dot_general(
        derivative, derivative, (((0,), (0,)), ((), ())), precision=HIGHEST, preferred_element_type=F32
    )

    def pick(shape, node_axis, outer):
        node = lax.broadcasted_iota(jnp.int32, shape, node_axis)
        other = lax.broadcasted_iota(jnp.int32, shape, 1 - node_axis)
        place = node // NODE if outer else node % NODE
        return jnp.where((place == other) & (node < NODES), 1.0, 0.0).astype(F32)

    outer, inner = pick((PADDED, NODE), 0, True), pick((PADDED, NODE), 0, False)
    outer_t, inner_t = pick((NODE, PADDED), 1, True), pick((NODE, PADDED), 1, False)
    whole = dot(dot(outer, stiffness), outer_t) * dot(inner, inner_t)
    whole = whole + dot(dot(inner, stiffness), inner_t) * dot(outer, outer_t)
    high = whole.astype(BF16).astype(F32)
    low = whole - high
    top = jnp.concatenate([high, high], axis=1)
    bottom = jnp.concatenate([low, jnp.zeros_like(low)], axis=1)
    k_ref[...] = jnp.concatenate([top, bottom], axis=0).astype(BF16)


def metric_rows(mass_ref, inverse_ref, rows, out_ref):
    lane = lax.broadcasted_iota(jnp.int32, (ELEM_DEV, LANES), 1) % ELEM_DEV
    element = lax.broadcasted_iota(jnp.int32, (ELEM_DEV, LANES), 0)
    repeat = jnp.where(lane == element, 1.0, 0.0).astype(F32)
    shape = (PADDED, LANES)
    node = lax.broadcasted_iota(jnp.int32, shape, 0)
    block = lax.broadcasted_iota(jnp.int32, shape, 1) // ELEM_DEV
    keep = (node % 8 == block) & (node < NODES)
    for kind, ref in ((0, mass_ref), (1, inverse_ref)):
        for i in range(NODE):
            rows[i * NODE : (i + 1) * NODE, :ELEM_DEV] = ref[i]
        values = jnp.dot(
            rows[:PADDED, :ELEM_DEV], repeat, precision=HIGHEST, preferred_element_type=F32
        )
        values = jnp.where(keep, values, 0.0).reshape(GROUPS, 8, LANES)
        out_ref[kind, :GROUPS] = jnp.sum(values, axis=1)
        out_ref[kind, GROUPS:] = jnp.zeros((16 - GROUPS, LANES), F32)


def metric_tables(m_ref, mode_group, place, mass, diag, faces, turn):
    inverse = diag.at[0]
    for kind, out in ((0, mass), (1, inverse)):
        for h in range(2):
            rows = exchange([m_ref[8 * h + at, kind] for at in range(8)])
            for at in range(8):
                for group in range(GROUPS):
                    turn[h, group, at : at + 1] = rows[at][group : group + 1]
            for group in range(GROUPS):
                out[group * 8 : (group + 1) * 8, h * LANES : (h + 1) * LANES] = turn[h, group, 0:8]
    shape = (PADDED, ELEMENTS)
    node = lax.broadcasted_iota(jnp.int32, shape, 0)
    element = lax.broadcasted_iota(jnp.int32, shape, 1)
    inside = node < NODES
    upper = (node % NODE == NODE - 1) & (element < ELEMENTS - RADIAL) & inside
    lower = (node % NODE == 0) & (element >= RADIAL) & inside
    outer = (node // NODE == NODE - 1) & (element % RADIAL != RADIAL - 1) & inside
    inner = (node // NODE == 0) & (element % RADIAL != 0)
    marks = [jnp.where(mark, 1.0, 0.0).astype(F32) for mark in (upper, lower, outer, inner)]
    for at in range(4):
        faces[at] = marks[at]
    count = marks[0] + marks[1] + marks[2] + marks[3]
    values = inverse[...]
    for n in range(4):
        number = mode_group * 64 + lax.rem(place, 8) * 8 + 2 * n + place // 8
        fraction = number.astype(F32) / MODES
        diag[n] = mass[...] * (1.0 + AZIMUTH_WEIGHT * fraction * fraction * values) + count


CHUNKS = ((0, 0, 3), (0, 3, 6), (0, 6, 8), (1, 0, 3))


def load_tiles(b_ref, turn, weight, out):
    for slot, start, stop in CHUNKS:
        for h in range(2):
            tiles = exchange([b_ref[slot, start:stop, 8 * h + at] for at in range(8)])
            for at in range(8):
                turn[h, 8 * slot + start : 8 * slot + stop, at * 8 : (at + 1) * 8] = tiles[at]
    for s in range(8):
        for h in range(2):
            lanes = slice(h * LANES, (h + 1) * LANES)
            for group in range(GROUPS):
                rows = slice(group * 8, (group + 1) * 8)
                value = turn[h, group, pl.ds(s, 8, stride=8), :]
                if weight is not None:
                    value = value * weight[rows, lanes]
                out[s, rows, lanes] = value


OWNED = (((1, 0), (1, 1), (1, 2)), ((0, 0), (0, 2), (0, 4), (0, 6)), ((0, 1), (0, 3), (0, 5), (0, 7)))


def store_tiles(value_of, turn, out_ref, emit):
    for phase in range(3):
        for s in range(8):
            for slot, at_group in OWNED[phase]:
                group = 8 * slot + at_group
                for h in range(2):
                    turn[h, group, pl.ds(s, 8, stride=8), :] = value_of(
                        s, slice(group * 8, (group + 1) * 8), slice(h * LANES, (h + 1) * LANES)
                    )
        for slot, at_group in OWNED[phase]:
            for h in range(2):
                group = 8 * slot + at_group
                tiles = exchange([turn[h, group, at * 8 : (at + 1) * 8] for at in range(8)])
                for at in range(8):
                    out_ref[slot, at_group, 8 * h + at] = tiles[at]
        emit(phase)


def total(parts):
    half = parts[:, :LANES] + parts[:, LANES:]
    return jnp.broadcast_to(jnp.sum(half, axis=(0, 1), keepdims=True), (1, ELEMENTS))


def fold(value):
    return jnp.sum(value.reshape(GROUPS, 8, ELEMENTS), axis=0)


def solve(b_ref, out_ref, weigh_in, weigh_out, scratch, emit):
    mass, diag, faces, k_ref, r, p, q, alphas, turn = scratch
    load_tiles(b_ref, turn, mass if weigh_in else None, r)
    norms = tuple(total(fold(r[n] * r[n]) + fold(r[n + 4] * r[n + 4])) for n in range(4))
    p[ITERS - 1] = jnp.zeros_like(p[ITERS - 1])
    empty = jnp.zeros((8, ELEMENTS), F32)

    def operate(sweep, before, n, beta, norm):
        curve = None
        for s in (n, n + 4):
            now = r[s] + beta * p[before, s]
            p[sweep, s] = now
            high = now.astype(BF16).astype(F32)
            halves = jnp.concatenate([high, now - high], axis=0).astype(BF16)
            image = jnp.dot(k_ref[...], halves, preferred_element_type=F32)
            ahead = pltpu.roll(now[: PADDED - 8], ELEMENTS - RADIAL, 1)
            behind = pltpu.roll(now[8:], RADIAL, 1)
            image = (
                image[:PADDED]
                + image[PADDED:]
                + diag[n] * now
                - faces[0] * jnp.concatenate([empty, ahead], axis=0)
                - faces[1] * jnp.concatenate([behind, empty], axis=0)
            )
            outward = pltpu.roll(now[:16], ELEMENTS - 1, 1)
            inward = pltpu.roll(now[72:], 1, 1)
            image = jnp.concatenate(
                [
                    image[:16] - faces[3, :16] * inward,
                    image[16:72],
                    image[72:] - faces[2, 72:] * outward,
                ],
                axis=0,
            )
            q[s] = image
            part = fold(now * image)
            curve = part if curve is None else curve + part
        alpha = norm / total(curve)
        alphas[sweep * 4 + n] = alpha
        return alpha

    def reduce(n, alpha):
        part = None
        for s in (n, n + 4):
            value = r[s] - alpha * q[s]
            r[s] = value
            add = fold(value * value)
            part = add if part is None else part + add
        return total(part)

    def sweep_body(sweep, carry):
        norms, betas = carry
        before = lax.rem(sweep + ITERS - 1, ITERS)
        step, after = [None] * 4, [None] * 4
        for n in range(5):
            if n < 4:
                step[n] = operate(sweep, before, n, betas[n], norms[n])
            if n > 0:
                after[n - 1] = reduce(n - 1, step[n - 1])
        return tuple(after), tuple(after[n] / norms[n] for n in range(4))

    none = (jnp.zeros((1, ELEMENTS), F32),) * 4
    norms, betas = lax.fori_loop(0, ITERS - 1, sweep_body, (norms, none))
    for n in range(4):
        operate(ITERS - 1, ITERS - 2, n, betas[n], norms[n])

    def value_of(s, rows, lanes):
        value = alphas[s % 4, :, lanes] * p[0, s, rows, lanes]
        for sweep in range(1, ITERS):
            value = value + alphas[sweep * 4 + s % 4, :, lanes] * p[sweep, s, rows, lanes]
        return value * mass[rows, lanes] if weigh_out else value

    store_tiles(value_of, turn, out_ref, emit)


FIELD = pltpu.VMEM((8, PADDED, ELEMENTS), F32)
SOLVE_SCRATCH = [
    pltpu.VMEM((PADDED, ELEMENTS), F32),
    pltpu.VMEM((4, PADDED, ELEMENTS), F32),
    pltpu.VMEM((4, PADDED, ELEMENTS), F32),
    pltpu.VMEM((2 * PADDED, 2 * PADDED), BF16),
    FIELD,
    pltpu.VMEM((ITERS, 8, PADDED, ELEMENTS), F32),
    FIELD,
    pltpu.VMEM((ITERS * 4, 1, ELEMENTS), F32),
    pltpu.VMEM((2, GROUPS, 64, LANES), F32),
]


def split(value):
    high = value.astype(BF16)
    return high, (value - high.astype(F32)).astype(BF16)


def apply(t_ref, which, field):
    high, low = split(field)
    width = field.shape[1]
    if width == LANES:
        both = jnp.concatenate([high, low], axis=1)
        out = jnp.dot(t_ref[which], both, preferred_element_type=F32)
        return out[:HALF, :LANES] + out[:HALF, LANES:] + out[HALF:, :LANES]
    out = jnp.dot(t_ref[which], high, preferred_element_type=F32)
    out = out[:HALF] + out[HALF:]
    return out + jnp.dot(t_ref[which, :HALF], low, preferred_element_type=F32)


def parts_of(u_ref):
    out = []
    for odd in range(2):
        tiles = u_ref[odd].reshape(32, 2, 8, LANES)
        one, two = mix(tiles[:, 0], tiles[:, 1])
        out.append((one.reshape(HALF, LANES), two.reshape(HALF, LANES)))
    return out


def parts_to(out_ref, parts):
    for odd in range(2):
        real, imag = parts[odd]
        one, two = mix(real.reshape(32, 8, LANES), imag.reshape(32, 8, LANES))
        out_ref[odd] = jnp.stack([one, two], axis=1).reshape(64, 8, LANES)


def mode_rows(odd):
    row = lax.broadcasted_iota(jnp.int32, (HALF, LANES), 0)
    mode = 2 * ((row // 32 % 4 * 2 + row // 128) * 32 + row % 32) + odd
    fraction = mode.astype(F32) / MODES
    weight = jnp.where(mode == 0, 1.0 / PLANES, 2.0 / PLANES).astype(F32)
    sign = jnp.where(row % 2 == 0, 1.0, -1.0).astype(F32)
    return fraction, weight, sign


def first_row(shape):
    return lax.broadcasted_iota(jnp.int32, shape, 0) == 0


def to_planes(t_ref, cos_fields, sin_fields, out_ref):
    sign = mode_rows(0)[2][:, :1]
    cos_even, cos_odd = apply(t_ref, 0, cos_fields[0]), apply(t_ref, 1, cos_fields[1])
    sin_even, sin_odd = apply(t_ref, 2, sin_fields[0]), apply(t_ref, 3, sin_fields[1])
    quarter_cos = jnp.sum(sign * cos_fields[0], axis=0, keepdims=True)
    quarter_sin = jnp.sum(sign * sin_fields[1], axis=0, keepdims=True)
    cos, sin = cos_even + cos_odd, sin_even + sin_odd
    out_ref[0] = cos - sin
    out_ref[1] = cos + sin
    cos, sin = cos_even - cos_odd, sin_even - sin_odd
    out_ref[2] = cos + sin
    out_ref[3] = cos - sin
    out_ref[1, 0:1] = quarter_cos - quarter_sin
    out_ref[3, 0:1] = quarter_cos + quarter_sin


def from_planes(t_ref, values):
    shape = values[0].shape
    sign = mode_rows(0)[2][:, :1]
    first = first_row(shape)
    quarter, three = values[1][0:1], values[3][0:1]
    one = values[0]
    two = jnp.where(first, 0.0, values[1])
    four = jnp.where(first, 0.0, values[3])
    plus, minus = one + two, one - two
    plus_far, minus_far = values[2] + four, values[2] - four
    a_even = apply(t_ref, 4, plus + plus_far) + sign * (quarter + three)
    a_odd = apply(t_ref, 5, plus - plus_far)
    b_even = -apply(t_ref, 6, minus - minus_far)
    b_odd = -apply(t_ref, 7, minus + minus_far) - sign * (quarter - three)
    return (a_even, b_even), (a_odd, b_odd)


def state_planes(parts, t_ref, out_ref):
    cos_fields, sin_fields = [], []
    for odd in range(2):
        real, imag = parts[odd]
        fraction = mode_rows(odd)[0]
        cos_fields.append(jnp.concatenate([real, -fraction * imag], axis=1))
        sin_fields.append(jnp.concatenate([imag, fraction * real], axis=1))
    to_planes(t_ref, cos_fields, sin_fields, out_ref)


def first_stage(u_ref, t_ref, planes, out_ref):
    parts = parts_of(u_ref)
    state_planes(parts, t_ref, planes)
    values = [planes[at, :, :LANES] * planes[at, :, LANES:] for at in range(4)]
    found = from_planes(t_ref, values)
    out = []
    for odd in range(2):
        weight = mode_rows(odd)[1]
        out.append(tuple(parts[odd][c] - weight * found[odd][c] for c in range(2)))
    parts_to(out_ref, out)


def adjoint_planes(s_ref, t_ref, out_ref):
    parts = parts_of(s_ref)
    weights = [mode_rows(odd)[1] for odd in range(2)]
    to_planes(
        t_ref,
        [weights[odd] * parts[odd][0] for odd in range(2)],
        [weights[odd] * parts[odd][1] for odd in range(2)],
        out_ref,
    )


def finish(t_ref, s_ref, planes, adjoint, out_ref):
    values = []
    for at in range(4):
        factor = adjoint[at]
        values.append(planes[at] * jnp.concatenate([factor, factor], axis=1))
    found = from_planes(t_ref, values)
    parts = parts_of(s_ref)
    out = []
    for odd in range(2):
        fraction = mode_rows(odd)[0]
        a, b = found[odd]
        out.append(
            (
                parts[odd][0] - a[:, LANES:] - fraction * b[:, :LANES],
                parts[odd][1] - b[:, LANES:] + fraction * a[:, :LANES],
            )
        )
    parts_to(out_ref, out)


COUNT = N_MODE * N_MER
SPARE = GROUPS - 8


def send(source, target, mode, mer, sems, at):
    pltpu.make_async_remote_copy(
        src_ref=source,
        dst_ref=target,
        send_sem=sems[0].at[at],
        recv_sem=sems[1].at[at],
        device_id={"mode": mode, "mer": mer},
        device_id_type=pl.DeviceIdType.MESH,
    ).start()


def wait(blank, tiles, sem):
    whole = blank.at[pl.ds(0, tiles)]
    pltpu.make_async_copy(whole, whole, sem).wait()


def wait_either(double, blank, tiles_double, tiles_single, sem):
    @pl.when(double)
    def _():
        wait(blank, tiles_double, sem)

    @pl.when(jnp.logical_not(double))
    def _():
        wait(blank, tiles_single, sem)


def place_at(mer, k):
    step = lax.rem(7 * k, N_MER)
    y = lax.rem(lax.rem(mer, 4) + lax.rem(step, 4), 4)
    z = lax.rem(mer // 4 + step // 4, 4)
    return z * 4 + y


def extra(x, mer):
    turn = lax.rem(lax.rem(mer, 4) + mer // 4, 4)
    return lax.rem(x + 4 - turn, 4)


def groups_on(mode, core):
    x = mode // 2
    return [2 * lax.rem(x + step, 4) + core for step in (1, 3, 2, 0)]


def each_group(mode, cores, act):
    for core in cores:
        one, two, three, own = groups_on(mode, core)
        act(one, core)
        act(two, core)
        act(three, core)

        @pl.when(lax.rem(mode, 2) != core)
        def _(own=own, core=core):
            act(own, core)


def each_place(mer, act):
    def body(k, _):
        act(place_at(mer, k))
        return 0

    lax.fori_loop(1, N_MER, body, 0)


def each_other(mode, mer, cores, act):
    groups = [(other, core) for core in cores for other in groups_on(mode, core)]

    def body(place):
        for other, core in groups:
            act(other, core, place)

    each_place(mer, body)
    each_group(mode, cores, lambda other, core: act(other, core, mer))


def order_of(mode):
    return lax.rem(mode, 2) * 4 + mode // 2


def program_kernel(
    state_ref,
    cotangent_hbm,
    mass_ref,
    inverse_ref,
    d_ref,
    t_hbm,
    out_ref,
    cotangent_in,
    t_ref,
    copy_sems,
    rows,
    native_out,
    native_in,
    mode_out,
    mode_in,
    plane_out,
    plane_in,
    metric_out,
    metric_in,
    u_planes,
    planes,
    s_planes,
    blank,
    send_sems,
    recv_sems,
    *solve_scratch,
):
    mode = lax.axis_index("mode")
    mer = lax.axis_index("mer")
    odd, eighth = mer // 8, lax.rem(mer, 8)
    row = order_of(mode) * 8 + eighth
    mine_extra = extra(mode // 2, mer)
    double = (lax.rem(mode, 2) == 0) & (mine_extra < SPARE)
    slots = jnp.where(double, 2, 1)
    sems = (send_sems, recv_sems)
    mass, diag, faces, k_ref = solve_scratch[:4]
    turn = solve_scratch[8]
    sent = []

    cotangent_copy = pltpu.make_async_copy(cotangent_hbm, cotangent_in, copy_sems.at[0])
    table_copy = pltpu.make_async_copy(t_hbm, t_ref, copy_sems.at[1])
    cotangent_copy.start()
    table_copy.start()
    barrier = pltpu.get_barrier_semaphore()

    def greet(other, core, place):
        pl.semaphore_signal(
            barrier,
            inc=1,
            device_id={"mode": other, "mer": place},
            device_id_type=pl.DeviceIdType.MESH,
        )

    each_other(mode, mer, (0, 1), greet)
    native_to_tiles(state_ref, native_out.at[0], rows, turn)
    pl.semaphore_wait(barrier, COUNT - 1)

    def each_slot(act):
        def body(k, _):
            act(slots - 1 - k)
            return 0

        lax.fori_loop(0, slots, body, 0)

    def send_to_planes(source, target, at):
        def act(other, core, place):
            send(source.at[0, other, place], target.at[0, odd, row], other, place, sems, at)

        def act_extra(other, core, place):
            index = extra(other // 2, place)

            @pl.when(index < SPARE)
            def _():
                send(source.at[1, index, place], target.at[1, odd, row], other, place, sems, at + 1)

        def emit(phase):
            if phase == 0:
                target[1, odd, row] = source[1, mine_extra, mer]
                each_other(mode, mer, (0,), act_extra)
            else:
                each_other(mode, mer, (phase - 1,), act)
            if phase == 2:
                target[0, odd, row] = source[0, mode, mer]

        sent.append((at, COUNT - 1, COUNT - 1))
        sent.append((at + 1, 16 * SPARE - 1, 16 * SPARE))
        return emit

    def wait_planes(at, slot):
        wait(blank, COUNT - 1, recv_sems.at[at + slot])

    def send_to_modes(source, target, at):
        def emit(slot):
            group = jnp.where(slot == 1, mine_extra, mode)
            target[slot, group, mer] = source[slot, odd, row]

            def act(other, core, place):
                piece = source.at[slot, place // 8, order_of(other) * 8 + lax.rem(place, 8)]
                send(piece, target.at[slot, group, mer], other, place, sems, at)

            each_other(mode, mer, (0, 1), act)

        sent.append((at, 2 * (COUNT - 1), COUNT - 1))
        return emit

    def wait_modes(at):
        wait_either(double, blank, 16 * GROUPS - 2, 16 * GROUPS - 1, recv_sems.at[at])

    mine = pl.ds(pl.multiple_of(order_of(mode) * 8, 8), 8)
    plane_in[0, 0, :, mine] = native_out[0, 0, mode]
    plane_in[0, 1, :, mine] = native_out[0, 1, mine_extra]

    def send_extra_state(other, core):
        index = extra(other // 2, mer)

        @pl.when(index < SPARE)
        def _():
            send(native_out.at[0, 1, index], plane_in.at[0, 1, :, mine], other, mer, sems, 1)

    def send_state(other, core):
        send(native_out.at[0, 0, other], plane_in.at[0, 0, :, mine], other, mer, sems, 0)

    each_group(mode, (0,), send_extra_state)
    each_group(mode, (0, 1), send_state)
    sent.append((0, N_MER * (N_MODE - 1), N_MER * (N_MODE - 1)))
    sent.append((1, N_MER * (SPARE - 1), N_MER * SPARE))

    cotangent_copy.wait()
    native_to_tiles(cotangent_in, native_out.at[1], rows, turn)
    mode_in[0, 0, :, mer] = native_out[1, 0, :, odd, eighth]
    mode_in[0, 1, 0:SPARE, mer] = native_out[1, 1, 0:SPARE, odd, eighth]
    metric_rows(mass_ref, inverse_ref, rows, metric_out)
    metric_in[mer] = metric_out[...]

    def send_cotangent(place):
        which, at = place // 8, lax.rem(place, 8)
        send(native_out.at[1, 0, :, which, at], mode_in.at[0, 0, :, mer], mode, place, sems, 2)
        send(
            native_out.at[1, 1, 0:SPARE, which, at],
            mode_in.at[0, 1, 0:SPARE, mer],
            mode,
            place,
            sems,
            2,
        )
        send(metric_out, metric_in.at[mer], mode, place, sems, 3)

    each_place(mer, send_cotangent)
    sent.append((2, (N_MER - 1) * GROUPS, (N_MER - 1) * GROUPS))
    sent.append((3, (N_MER - 1) * 4, (N_MER - 1) * 4))

    stiffness_tables(d_ref, k_ref)
    table_copy.wait()

    emit_rhs = send_to_modes(plane_out.at[0], mode_in.at[1], 4)

    def first(slot):
        wait(blank, (N_MODE - 1) * N_MER, recv_sems.at[slot])
        first_stage(plane_in.at[0, slot], t_ref, u_planes.at[slot], plane_out.at[0, slot])
        emit_rhs(slot)

    each_slot(first)

    wait(blank, (N_MER - 1) * 4, recv_sems.at[3])
    metric_tables(metric_in, mode, mer, mass, diag, faces, turn)
    wait(blank, (N_MER - 1) * GROUPS, recv_sems.at[2])
    emit = send_to_planes(mode_out.at[0], plane_in.at[1], 5)
    solve(mode_in.at[0], mode_out.at[0], False, True, solve_scratch, emit)

    wait_modes(4)
    emit = send_to_planes(mode_out.at[1], plane_in.at[2], 7)
    solve(mode_in.at[1], mode_out.at[1], True, False, solve_scratch, emit)

    def multiplier(slot):
        wait_planes(5, slot)
        adjoint_planes(plane_in.at[1, slot], t_ref, s_planes.at[slot])

    each_slot(multiplier)
    emit_adjoint = send_to_modes(plane_out.at[1], mode_in.at[2], 9)

    def second(slot):
        wait_planes(7, slot)
        state_planes(parts_of(plane_in.at[2, slot]), t_ref, planes)
        finish(t_ref, plane_in.at[1, slot], planes, s_planes.at[slot], plane_out.at[1, slot])
        emit_adjoint(slot)

    each_slot(second)

    wait_modes(9)
    emit = send_to_planes(mode_out.at[2], plane_in.at[3], 10)
    solve(mode_in.at[2], mode_out.at[2], False, True, solve_scratch, emit)

    def third(slot):
        wait_planes(10, slot)
        adjoint_planes(plane_in.at[3, slot], t_ref, s_planes.at[slot])
        finish(
            t_ref, plane_in.at[3, slot], u_planes.at[slot], s_planes.at[slot], plane_out.at[2, slot]
        )
        group = jnp.where(slot == 1, mine_extra, mode)
        native_in[slot, group] = plane_out[2, slot, :, mine]

        def send_gradient(other, core):
            theirs = pl.ds(pl.multiple_of(order_of(other) * 8, 8), 8)
            send(plane_out.at[2, slot, :, theirs], native_in.at[slot, group], other, mer, sems, 12)

        each_group(mode, (0, 1), send_gradient)

    each_slot(third)
    sent.append((12, 2 * (N_MODE - 1) * N_MER, (N_MODE - 1) * N_MER))
    wait_either(double, blank, N_MER * (GROUPS - 2), N_MER * (GROUPS - 1), recv_sems.at[12])
    tiles_to_native(native_in, out_ref, rows, turn)
    for at, tiles_double, tiles_single in sent:
        wait_either(double, blank, tiles_double, tiles_single, send_sems.at[at])


def program(state, cotangent, mass, inverse, derivative, table):
    by_mode = (2, N_MODE, N_MER, 8, LANES)
    by_native = (2, N_MODE, 2, 8, 8, LANES)
    by_plane = (2, 2, COUNT // 2, 8, LANES)
    vmem = pl.BlockSpec(memory_space=pltpu.VMEM)
    hbm = pl.BlockSpec(memory_space=pl.ANY)

    def scratch(count, shape):
        return pltpu.VMEM((count,) + shape, F32)

    return pl.pallas_call(
        program_kernel,
        out_shape=jax.ShapeDtypeStruct((NODE, NODE, ELEM_DEV * LANES), F32),
        in_specs=[vmem, hbm, vmem, vmem, vmem, hbm],
        out_specs=vmem,
        scratch_shapes=[
            pltpu.VMEM((NODE, NODE, ELEM_DEV * LANES), F32),
            pltpu.VMEM((8, 2 * HALF, HALF), BF16),
            pltpu.SemaphoreType.DMA((2,)),
            pltpu.VMEM((PADDED * ELEM_DEV, LANES), F32),
            scratch(2, by_native),
            pltpu.VMEM(by_native, F32),
            scratch(3, by_mode),
            scratch(3, by_mode),
            scratch(3, by_plane),
            scratch(4, by_plane),
            pltpu.VMEM((2, 16, LANES), F32),
            scratch(N_MER, (2, 16, LANES)),
            scratch(2, (4, HALF, 2 * LANES)),
            scratch(4, (HALF, 2 * LANES)),
            scratch(2, (4, HALF, LANES)),
            pltpu.VMEM((2 * COUNT, 8, LANES), F32),
            pltpu.SemaphoreType.DMA((13,)),
            pltpu.SemaphoreType.DMA((13,)),
            *SOLVE_SCRATCH,
        ],
        compiler_params=pltpu.CompilerParams(
            collective_id=0, has_side_effects=True, vmem_limit_bytes=60 << 20
        ),
        name="program",
    )(state, cotangent, mass, inverse, derivative, table)


def shards(cotangent, checkpoint, mass, inv_radius_sq, derivative):
    table = jnp.asarray(tables())
    return program(checkpoint, cotangent, mass, inv_radius_sq, derivative, table)


def solution(mesh):
    return jax.shard_map(
        shards,
        mesh=mesh,
        in_specs=(
            P(None, None, ("mer", "mode")),
            P(None, None, ("mer", "mode")),
            P(None, None, "mer"),
            P(None, None, "mer"),
            P(),
        ),
        out_specs=P(None, None, ("mer", "mode")),
        check_vma=False,
    )
```

```python
import functools
import math

import jax
import jax.numpy as jnp
import ml_dtypes
import numpy as np
from jax import lax
from jax.experimental import pallas as pl
from jax.experimental.pallas import tpu as pltpu
from jax.sharding import PartitionSpec as P

NODE = 9
NODES = NODE * NODE
RADIAL = 8
ITERS = 4
MODES = 512
HALF = 256
PLANES = 1024
ELEMENTS = 256
N_MODE = 8
N_MER = 16
ELEM_DEV = 16
GROUPS = 11
PADDED = GROUPS * 8
LANES = 128
AZIMUTH_WEIGHT = 4.0
HIGHEST = lax.Precision.HIGHEST
F32 = jnp.float32
BF16 = jnp.bfloat16


def tables():
    order = np.arange(HALF).reshape(4, 2, HALF // N_MODE).transpose(1, 0, 2).reshape(-1)
    out = []
    for wave in (np.cos, np.sin):
        for odd in range(2):
            index = np.outer(np.arange(HALF), 2 * order + odd) % PLANES
            values = wave(index.astype(np.float64) * (2.0 * math.pi / PLANES)).astype(np.float32)
            high = values.astype(ml_dtypes.bfloat16)
            low = (values - high.astype(np.float32)).astype(ml_dtypes.bfloat16)
            out.append((high, low))
    both = [np.concatenate(pair) for pair in out]
    turned = [np.concatenate([high.T, low.T]) for high, low in out]
    return np.stack(both + turned)


def mix(first, second):
    shape = first.shape
    low = lax.broadcasted_iota(jnp.int32, shape, len(shape) - 2) % 8 < 4
    axis = len(shape) - 2
    return (
        jnp.where(low, first, pltpu.roll(second, 4, axis)),
        jnp.where(low, pltpu.roll(first, 4, axis), second),
    )


def exchange(tiles):
    tiles = list(tiles)
    axis = tiles[0].ndim - 1
    block = lax.broadcasted_iota(jnp.int32, tiles[0].shape, axis) // 16
    for bit in (1, 2, 4):
        clear = (block & bit) == 0
        for at in range(8):
            if at & bit:
                continue
            one, two = tiles[at], tiles[at | bit]
            tiles[at] = jnp.where(clear, one, pltpu.roll(two, 16 * bit, axis))
            tiles[at | bit] = jnp.where(clear, pltpu.roll(one, LANES - 16 * bit, axis), two)
    return tiles


def native_to_tiles(x_ref, out_ref, rows, turn):
    rows[pl.ds(NODES * ELEM_DEV, PADDED * ELEM_DEV - NODES * ELEM_DEV), :] = jnp.zeros(
        ((PADDED - NODES) * ELEM_DEV, LANES), F32
    )
    for i in range(NODE):
        for e in range(ELEM_DEV):
            rows[pl.ds(i * NODE * ELEM_DEV + e, NODE, stride=ELEM_DEV), :] = x_ref[
                i, :, e * LANES : (e + 1) * LANES
            ]
    for group in range(GROUPS):
        turned = rows[group * LANES : (group + 1) * LANES, :].T
        turn[0, group] = turned[:64]
        turn[1, group] = turned[64:]
        for odd in range(2):
            real = turn[0, group, pl.ds(odd, 32, stride=2), :].reshape(4, 8, LANES)
            imag = turn[1, group, pl.ds(odd, 32, stride=2), :].reshape(4, 8, LANES)
            one, two = mix(real, imag)
            out_ref[group // 8, group % 8, odd] = jnp.stack([one, two], axis=1).reshape(8, 8, LANES)


def tiles_to_native_kernel(t_hbm, out_hbm, tiles_in, rows, turn, native, in_sems, out_sems):
    loads = [
        pltpu.make_async_copy(t_hbm.at[group], tiles_in.at[group], in_sems.at[group])
        for group in range(GROUPS)
    ]
    stores = [
        pltpu.make_async_copy(native.at[i], out_hbm.at[i], out_sems.at[i]) for i in range(NODE)
    ]
    for load in loads:
        load.start()
    done = 0
    for group in range(GROUPS):
        loads[group].wait()
        for odd in range(2):
            tiles = tiles_in[group, odd].reshape(4, 2, 8, LANES)
            real, imag = mix(tiles[:, 0], tiles[:, 1])
            turn[0, group, pl.ds(odd, 32, stride=2), :] = real.reshape(32, LANES)
            turn[1, group, pl.ds(odd, 32, stride=2), :] = imag.reshape(32, LANES)
        both = jnp.concatenate([turn[0, group], turn[1, group]], axis=0)
        rows[group * LANES : (group + 1) * LANES, :] = both.T
        while done < NODE and (done + 1) * NODE <= (group + 1) * 8:
            for e in range(ELEM_DEV):
                native[done, :, e * LANES : (e + 1) * LANES] = rows[
                    pl.ds(done * NODE * ELEM_DEV + e, NODE, stride=ELEM_DEV), :
                ]
            stores[done].start()
            done += 1
    for store in stores:
        store.wait()


def tiles_to_native(tiles):
    hbm = pl.BlockSpec(memory_space=pltpu.HBM)
    shape = (NODE, NODE, ELEM_DEV * LANES)
    return pl.pallas_call(
        tiles_to_native_kernel,
        out_shape=jax.ShapeDtypeStruct(shape, F32),
        in_specs=[hbm],
        out_specs=hbm,
        scratch_shapes=[
            pltpu.VMEM((GROUPS, 2, 8, 8, LANES), F32),
            pltpu.VMEM((PADDED * ELEM_DEV, LANES), F32),
            pltpu.VMEM((2, GROUPS, 64, LANES), F32),
            pltpu.VMEM(shape, F32),
            pltpu.SemaphoreType.DMA((GROUPS,)),
            pltpu.SemaphoreType.DMA((NODE,)),
        ],
        compiler_params=pltpu.CompilerParams(vmem_limit_bytes=62 << 20),
        name="tiles_to_native",
    )(tiles)


def stiffness_tables(d_ref, k_ref):
    def dot(a, b):
        return jnp.dot(a, b, precision=HIGHEST, preferred_element_type=F32)

    derivative = d_ref[...]
    stiffness = lax.dot_general(
        derivative, derivative, (((0,), (0,)), ((), ())), precision=HIGHEST, preferred_element_type=F32
    )

    def pick(shape, node_axis, outer):
        node = lax.broadcasted_iota(jnp.int32, shape, node_axis)
        other = lax.broadcasted_iota(jnp.int32, shape, 1 - node_axis)
        place = node // NODE if outer else node % NODE
        return jnp.where((place == other) & (node < NODES), 1.0, 0.0).astype(F32)

    outer, inner = pick((PADDED, NODE), 0, True), pick((PADDED, NODE), 0, False)
    outer_t, inner_t = pick((NODE, PADDED), 1, True), pick((NODE, PADDED), 1, False)
    whole = dot(dot(outer, stiffness), outer_t) * dot(inner, inner_t)
    whole = whole + dot(dot(inner, stiffness), inner_t) * dot(outer, outer_t)
    high = whole.astype(BF16).astype(F32)
    low = whole - high
    top = jnp.concatenate([high, high], axis=1)
    bottom = jnp.concatenate([low, jnp.zeros_like(low)], axis=1)
    k_ref[...] = jnp.concatenate([top, bottom], axis=0).astype(BF16)


def metric_rows(mass_ref, inverse_ref, rows, out_ref):
    lane = lax.broadcasted_iota(jnp.int32, (ELEM_DEV, LANES), 1) % ELEM_DEV
    element = lax.broadcasted_iota(jnp.int32, (ELEM_DEV, LANES), 0)
    repeat = jnp.where(lane == element, 1.0, 0.0).astype(F32)
    shape = (PADDED, LANES)
    node = lax.broadcasted_iota(jnp.int32, shape, 0)
    block = lax.broadcasted_iota(jnp.int32, shape, 1) // ELEM_DEV
    keep = (node % 8 == block) & (node < NODES)
    for kind, ref in ((0, mass_ref), (1, inverse_ref)):
        for i in range(NODE):
            rows[i * NODE : (i + 1) * NODE, :ELEM_DEV] = ref[i]
        values = jnp.dot(
            rows[:PADDED, :ELEM_DEV], repeat, precision=HIGHEST, preferred_element_type=F32
        )
        values = jnp.where(keep, values, 0.0).reshape(GROUPS, 8, LANES)
        out_ref[kind, :GROUPS] = jnp.sum(values, axis=1)
        out_ref[kind, GROUPS:] = jnp.zeros((16 - GROUPS, LANES), F32)


def metric_tables(m_ref, mode_group, place, mass, diag, faces, turn):
    inverse = diag.at[0]
    for kind, out in ((0, mass), (1, inverse)):
        for h in range(2):
            rows = exchange([m_ref[8 * h + at, kind] for at in range(8)])
            for at in range(8):
                for group in range(GROUPS):
                    turn[h, group, at : at + 1] = rows[at][group : group + 1]
            for group in range(GROUPS):
                out[group * 8 : (group + 1) * 8, h * LANES : (h + 1) * LANES] = turn[h, group, 0:8]
    shape = (PADDED, ELEMENTS)
    node = lax.broadcasted_iota(jnp.int32, shape, 0)
    element = lax.broadcasted_iota(jnp.int32, shape, 1)
    inside = node < NODES
    upper = (node % NODE == NODE - 1) & (element < ELEMENTS - RADIAL) & inside
    lower = (node % NODE == 0) & (element >= RADIAL) & inside
    outer = (node // NODE == NODE - 1) & (element % RADIAL != RADIAL - 1) & inside
    inner = (node // NODE == 0) & (element % RADIAL != 0)
    marks = [jnp.where(mark, 1.0, 0.0).astype(F32) for mark in (upper, lower, outer, inner)]
    for at in range(4):
        faces[at] = marks[at]
    count = marks[0] + marks[1] + marks[2] + marks[3]
    values = inverse[...]
    for n in range(4):
        number = mode_group * 64 + lax.rem(place, 8) * 8 + 2 * n + place // 8
        fraction = number.astype(F32) / MODES
        diag[n] = mass[...] * (1.0 + AZIMUTH_WEIGHT * fraction * fraction * values) + count


def owner_of(extra_group, place):
    return 2 * ((extra_group + place % 4 + place // 4) % 4)


CHUNKS = ((0, 0, 3), (0, 3, 6), (0, 6, 8), (1, 0, 3))


def load_tiles(b_ref, turn, weight, out, by_owner):
    for slot, start, stop in CHUNKS:
        for h in range(2):
            tiles = []
            for place in range(8 * h, 8 * h + 8):
                if slot and by_owner:
                    tiles.append(
                        jnp.stack([b_ref[1, owner_of(at, place), place] for at in range(start, stop)])
                    )
                else:
                    tiles.append(b_ref[slot, start:stop, place])
            tiles = exchange(tiles)
            for at in range(8):
                turn[h, 8 * slot + start : 8 * slot + stop, at * 8 : (at + 1) * 8] = tiles[at]
    for s in range(8):
        for h in range(2):
            lanes = slice(h * LANES, (h + 1) * LANES)
            for group in range(GROUPS):
                rows = slice(group * 8, (group + 1) * 8)
                value = turn[h, group, pl.ds(s, 8, stride=8), :]
                if weight is not None:
                    value = value * weight[rows, lanes]
                out[s, rows, lanes] = value


OWNED = (
    ((1, 0), (1, 1), (1, 2), (0, 0), (0, 2), (0, 4), (0, 6)),
    ((0, 1), (0, 3), (0, 5), (0, 7)),
)


def store_tiles(value_of, turn, out_ref, emit):
    for core in range(2):
        for s in range(8):
            for slot, at_group in OWNED[core]:
                group = 8 * slot + at_group
                for h in range(2):
                    turn[h, group, pl.ds(s, 8, stride=8), :] = value_of(
                        s, slice(group * 8, (group + 1) * 8), slice(h * LANES, (h + 1) * LANES)
                    )
        for slot, at_group in OWNED[core]:
            for h in range(2):
                group = 8 * slot + at_group
                tiles = exchange([turn[h, group, at * 8 : (at + 1) * 8] for at in range(8)])
                for at in range(8):
                    place = 8 * h + at
                    owner = owner_of(at_group, place) if slot else at_group
                    out_ref[slot, owner, place] = tiles[at]
        emit(core)


def total(parts):
    half = parts[:, :LANES] + parts[:, LANES:]
    return jnp.broadcast_to(jnp.sum(half, axis=(0, 1), keepdims=True), (1, ELEMENTS))


def fold(value):
    return jnp.sum(value.reshape(GROUPS, 8, ELEMENTS), axis=0)


def solve(b_ref, out_ref, weigh_in, weigh_out, by_owner, scratch, emit):
    mass, diag, faces, k_ref, r, p, q, alphas, turn = scratch
    load_tiles(b_ref, turn, mass if weigh_in else None, r, by_owner)
    norms = tuple(total(fold(r[n] * r[n]) + fold(r[n + 4] * r[n + 4])) for n in range(4))
    p[ITERS - 1] = jnp.zeros_like(p[ITERS - 1])
    empty = jnp.zeros((8, ELEMENTS), F32)

    def operate(sweep, before, n, beta, norm):
        curve = None
        for s in (n, n + 4):
            now = r[s] + beta * p[before, s]
            p[sweep, s] = now
            high = now.astype(BF16).astype(F32)
            halves = jnp.concatenate([high, now - high], axis=0).astype(BF16)
            image = jnp.dot(k_ref[...], halves, preferred_element_type=F32)
            ahead = pltpu.roll(now[: PADDED - 8], ELEMENTS - RADIAL, 1)
            behind = pltpu.roll(now[8:], RADIAL, 1)
            image = (
                image[:PADDED]
                + image[PADDED:]
                + diag[n] * now
                - faces[0] * jnp.concatenate([empty, ahead], axis=0)
                - faces[1] * jnp.concatenate([behind, empty], axis=0)
            )
            outward = pltpu.roll(now[:16], ELEMENTS - 1, 1)
            inward = pltpu.roll(now[72:], 1, 1)
            image = jnp.concatenate(
                [
                    image[:16] - faces[3, :16] * inward,
                    image[16:72],
                    image[72:] - faces[2, 72:] * outward,
                ],
                axis=0,
            )
            q[s] = image
            part = fold(now * image)
            curve = part if curve is None else curve + part
        alpha = norm / total(curve)
        alphas[sweep * 4 + n] = alpha
        return alpha

    def reduce(n, alpha):
        part = None
        for s in (n, n + 4):
            value = r[s] - alpha * q[s]
            r[s] = value
            add = fold(value * value)
            part = add if part is None else part + add
        return total(part)

    def sweep_body(sweep, carry):
        norms, betas = carry
        before = lax.rem(sweep + ITERS - 1, ITERS)
        step, after = [None] * 4, [None] * 4
        for n in range(5):
            if n < 4:
                step[n] = operate(sweep, before, n, betas[n], norms[n])
            if n > 0:
                after[n - 1] = reduce(n - 1, step[n - 1])
        return tuple(after), tuple(after[n] / norms[n] for n in range(4))

    none = (jnp.zeros((1, ELEMENTS), F32),) * 4
    norms, betas = lax.fori_loop(0, ITERS - 1, sweep_body, (norms, none))
    for n in range(4):
        operate(ITERS - 1, ITERS - 2, n, betas[n], norms[n])

    def value_of(s, rows, lanes):
        value = alphas[s % 4, :, lanes] * p[0, s, rows, lanes]
        for sweep in range(1, ITERS):
            value = value + alphas[sweep * 4 + s % 4, :, lanes] * p[sweep, s, rows, lanes]
        return value * mass[rows, lanes] if weigh_out else value

    store_tiles(value_of, turn, out_ref, emit)


FIELD = pltpu.VMEM((8, PADDED, ELEMENTS), F32)
SOLVE_SCRATCH = [
    pltpu.VMEM((PADDED, ELEMENTS), F32),
    pltpu.VMEM((4, PADDED, ELEMENTS), F32),
    pltpu.VMEM((4, PADDED, ELEMENTS), F32),
    pltpu.VMEM((2 * PADDED, 2 * PADDED), BF16),
    FIELD,
    pltpu.VMEM((ITERS, 8, PADDED, ELEMENTS), F32),
    FIELD,
    pltpu.VMEM((ITERS * 4, 1, ELEMENTS), F32),
    pltpu.VMEM((2, GROUPS, 64, LANES), F32),
]


def split(value):
    high = value.astype(BF16)
    return high, (value - high.astype(F32)).astype(BF16)


def apply(t_ref, which, field):
    high, low = split(field)
    width = field.shape[1]
    if width == LANES:
        both = jnp.concatenate([high, low], axis=1)
        out = jnp.dot(t_ref[which], both, preferred_element_type=F32)
        return out[:HALF, :LANES] + out[:HALF, LANES:] + out[HALF:, :LANES]
    out = jnp.dot(t_ref[which], high, preferred_element_type=F32)
    out = out[:HALF] + out[HALF:]
    return out + jnp.dot(t_ref[which, :HALF], low, preferred_element_type=F32)


def parts_of(u_ref):
    out = []
    for odd in range(2):
        tiles = u_ref[odd].reshape(32, 2, 8, LANES)
        one, two = mix(tiles[:, 0], tiles[:, 1])
        out.append((one.reshape(HALF, LANES), two.reshape(HALF, LANES)))
    return out


def parts_to(out_ref, parts):
    for odd in range(2):
        real, imag = parts[odd]
        one, two = mix(real.reshape(32, 8, LANES), imag.reshape(32, 8, LANES))
        out_ref[odd] = jnp.stack([one, two], axis=1).reshape(64, 8, LANES)


def mode_rows(odd):
    row = lax.broadcasted_iota(jnp.int32, (HALF, LANES), 0)
    mode = 2 * ((row // 32 % 4 * 2 + row // 128) * 32 + row % 32) + odd
    fraction = mode.astype(F32) / MODES
    weight = jnp.where(mode == 0, 1.0 / PLANES, 2.0 / PLANES).astype(F32)
    sign = jnp.where(row % 2 == 0, 1.0, -1.0).astype(F32)
    return fraction, weight, sign


def first_row(shape):
    return lax.broadcasted_iota(jnp.int32, shape, 0) == 0


def to_planes(t_ref, cos_fields, sin_fields, out_ref):
    sign = mode_rows(0)[2][:, :1]
    cos_even, cos_odd = apply(t_ref, 0, cos_fields[0]), apply(t_ref, 1, cos_fields[1])
    sin_even, sin_odd = apply(t_ref, 2, sin_fields[0]), apply(t_ref, 3, sin_fields[1])
    quarter_cos = jnp.sum(sign * cos_fields[0], axis=0, keepdims=True)
    quarter_sin = jnp.sum(sign * sin_fields[1], axis=0, keepdims=True)
    cos, sin = cos_even + cos_odd, sin_even + sin_odd
    out_ref[0] = cos - sin
    out_ref[1] = cos + sin
    cos, sin = cos_even - cos_odd, sin_even - sin_odd
    out_ref[2] = cos + sin
    out_ref[3] = cos - sin
    out_ref[1, 0:1] = quarter_cos - quarter_sin
    out_ref[3, 0:1] = quarter_cos + quarter_sin


def from_planes(t_ref, values):
    shape = values[0].shape
    sign = mode_rows(0)[2][:, :1]
    first = first_row(shape)
    quarter, three = values[1][0:1], values[3][0:1]
    one = values[0]
    two = jnp.where(first, 0.0, values[1])
    four = jnp.where(first, 0.0, values[3])
    plus, minus = one + two, one - two
    plus_far, minus_far = values[2] + four, values[2] - four
    a_even = apply(t_ref, 4, plus + plus_far) + sign * (quarter + three)
    a_odd = apply(t_ref, 5, plus - plus_far)
    b_even = -apply(t_ref, 6, minus - minus_far)
    b_odd = -apply(t_ref, 7, minus + minus_far) - sign * (quarter - three)
    return (a_even, b_even), (a_odd, b_odd)


def state_planes(parts, t_ref, out_ref):
    cos_fields, sin_fields = [], []
    for odd in range(2):
        real, imag = parts[odd]
        fraction = mode_rows(odd)[0]
        cos_fields.append(jnp.concatenate([real, -fraction * imag], axis=1))
        sin_fields.append(jnp.concatenate([imag, fraction * real], axis=1))
    to_planes(t_ref, cos_fields, sin_fields, out_ref)


def first_stage(u_ref, t_ref, planes, out_ref):
    parts = parts_of(u_ref)
    state_planes(parts, t_ref, planes)
    values = [planes[at, :, :LANES] * planes[at, :, LANES:] for at in range(4)]
    found = from_planes(t_ref, values)
    out = []
    for odd in range(2):
        weight = mode_rows(odd)[1]
        out.append(tuple(parts[odd][c] - weight * found[odd][c] for c in range(2)))
    parts_to(out_ref, out)


def adjoint_planes(s_ref, t_ref, out_ref):
    parts = parts_of(s_ref)
    weights = [mode_rows(odd)[1] for odd in range(2)]
    to_planes(
        t_ref,
        [weights[odd] * parts[odd][0] for odd in range(2)],
        [weights[odd] * parts[odd][1] for odd in range(2)],
        out_ref,
    )


def finish(t_ref, s_ref, planes, adjoint, out_ref):
    values = []
    for at in range(4):
        factor = adjoint[at]
        values.append(planes[at] * jnp.concatenate([factor, factor], axis=1))
    found = from_planes(t_ref, values)
    parts = parts_of(s_ref)
    out = []
    for odd in range(2):
        fraction = mode_rows(odd)[0]
        a, b = found[odd]
        out.append(
            (
                parts[odd][0] - a[:, LANES:] - fraction * b[:, :LANES],
                parts[odd][1] - b[:, LANES:] + fraction * a[:, :LANES],
            )
        )
    parts_to(out_ref, out)


COUNT = N_MODE * N_MER
SPARE = GROUPS - 8


def send(source, target, mode, mer, sems, at):
    pltpu.make_async_remote_copy(
        src_ref=source,
        dst_ref=target,
        send_sem=sems[0].at[at],
        recv_sem=sems[1].at[at],
        device_id={"mode": mode, "mer": mer},
        device_id_type=pl.DeviceIdType.MESH,
    ).start()


def wait(blank, tiles, sem):
    whole = blank.at[pl.ds(0, tiles)]
    pltpu.make_async_copy(whole, whole, sem).wait()


def wait_either(double, blank, tiles_double, tiles_single, sem):
    @pl.when(double)
    def _():
        wait(blank, tiles_double, sem)

    @pl.when(jnp.logical_not(double))
    def _():
        wait(blank, tiles_single, sem)


def place_at(mer, k):
    step = lax.rem(7 * k, N_MER)
    y = lax.rem(lax.rem(mer, 4) + lax.rem(step, 4), 4)
    z = lax.rem(mer // 4 + step // 4, 4)
    return z * 4 + y


def extra(x, mer):
    turn = lax.rem(lax.rem(mer, 4) + mer // 4, 4)
    return lax.rem(x + 4 - turn, 4)


def groups_on(mode, core):
    x = mode // 2
    return [2 * lax.rem(x + step, 4) + core for step in (1, 3, 2, 0)]


def each_group(mode, cores, act):
    for core in cores:
        one, two, three, own = groups_on(mode, core)
        act(one, core)
        act(two, core)
        act(three, core)

        @pl.when(lax.rem(mode, 2) != core)
        def _(own=own, core=core):
            act(own, core)


def each_place(mer, act):
    def body(k, _):
        act(place_at(mer, k))
        return 0

    lax.fori_loop(1, N_MER, body, 0)


def each_other(mode, mer, cores, act):
    groups = [(other, core) for core in cores for other in groups_on(mode, core)]

    def body(place):
        for other, core in groups:
            act(other, core, place)

    each_place(mer, body)
    each_group(mode, cores, lambda other, core: act(other, core, mer))


def order_of(mode):
    return lax.rem(mode, 2) * 4 + mode // 2


def program_kernel(
    state_ref,
    cotangent_hbm,
    mass_ref,
    inverse_ref,
    d_ref,
    t_hbm,
    out_hbm,
    cotangent_in,
    t_ref,
    copy_sems,
    rows,
    native_out,
    native_in,
    mode_out,
    mode_in,
    plane_out,
    plane_in,
    metric_out,
    metric_in,
    u_planes,
    planes,
    s_planes,
    ready,
    blank,
    send_sems,
    recv_sems,
    *solve_scratch,
):
    mode = lax.axis_index("mode")
    mer = lax.axis_index("mer")
    odd, eighth = mer // 8, lax.rem(mer, 8)
    row = order_of(mode) * 8 + eighth
    mine_extra = extra(mode // 2, mer)
    double = (lax.rem(mode, 2) == 0) & (mine_extra < SPARE)
    slots = jnp.where(double, 2, 1)
    sems = (send_sems, recv_sems)
    mass, diag, faces, k_ref = solve_scratch[:4]
    turn = solve_scratch[8]
    sent = []

    cotangent_copy = pltpu.make_async_copy(cotangent_hbm, cotangent_in, copy_sems.at[0])
    table_copy = pltpu.make_async_copy(t_hbm, t_ref, copy_sems.at[1])
    cotangent_copy.start()
    table_copy.start()
    barrier = pltpu.get_barrier_semaphore()

    def greet(semaphore, other, place):
        pl.semaphore_signal(
            semaphore,
            inc=1,
            device_id={"mode": other, "mer": place},
            device_id_type=pl.DeviceIdType.MESH,
        )

    each_group(mode, (0, 1), lambda other, core: greet(barrier, other, mer))
    each_place(mer, lambda place: greet(barrier, mode, place))
    native_to_tiles(state_ref, native_out.at[0], rows, turn)
    pl.semaphore_wait(barrier, N_MODE - 1 + N_MER - 1)
    each_group(mode, (0, 1), lambda other, core: greet(ready, other, mer))

    def each_slot(act):
        def body(k, _):
            act(slots - 1 - k)
            return 0

        lax.fori_loop(0, slots, body, 0)

    def send_to_planes(source, target, at):
        def act(other, core, place):
            def single():
                send(source.at[0, other, place], target.at[0, odd, row], other, place, sems, at)

            if core == 1:
                single()
                return
            owns_two = extra(other // 2, place) < SPARE
            pl.when(jnp.logical_not(owns_two))(single)

            @pl.when(owns_two)
            def _():
                send(source.at[:, other, place], target.at[:, odd, row], other, place, sems, at)

        def emit(core):
            each_other(mode, mer, (core,), act)
            if core == 1:
                target[:, odd, row] = source[:, mode, mer]

        sent.append((at, 16 * GROUPS - 2, 16 * GROUPS - 1))
        return emit

    def wait_planes(at):
        wait_either(double, blank, 2 * (COUNT - 1), COUNT - 1, recv_sems.at[at])

    def send_to_modes(source, target, at):
        target[0, mode, mer] = source[0, odd, row]

        def act(other, core, place):
            index = order_of(other) * 8 + lax.rem(place, 8)
            piece = source.at[0, place // 8, index]
            send(piece, target.at[0, mode, mer], other, place, sems, at)

        def act_double(other, core, place):
            index = order_of(other) * 8 + lax.rem(place, 8)
            piece = source.at[:, place // 8, index]
            send(piece, target.at[:, mode, mer], other, place, sems, at)

        @pl.when(double)
        def _():
            target[1, mode, mer] = source[1, odd, row]
            each_other(mode, mer, (0, 1), act_double)

        @pl.when(jnp.logical_not(double))
        def _():
            each_other(mode, mer, (0, 1), act)

        sent.append((at, 2 * (COUNT - 1), COUNT - 1))

    def wait_modes(at):
        wait_either(double, blank, 16 * GROUPS - 2, 16 * GROUPS - 1, recv_sems.at[at])

    mine = pl.ds(pl.multiple_of(order_of(mode) * 8, 8), 8)
    plane_in[0, 0, :, mine] = native_out[0, 0, mode]
    plane_in[0, 1, :, mine] = native_out[0, 1, mine_extra]

    def send_extra_state(other, core):
        index = extra(other // 2, mer)

        @pl.when(index < SPARE)
        def _():
            send(native_out.at[0, 1, index], plane_in.at[0, 1, :, mine], other, mer, sems, 0)

    def send_state(other, core):
        send(native_out.at[0, 0, other], plane_in.at[0, 0, :, mine], other, mer, sems, 0)

    each_group(mode, (0,), send_extra_state)
    each_group(mode, (0, 1), send_state)
    sent.append((0, N_MER * (GROUPS - 2), N_MER * (GROUPS - 1)))

    cotangent_copy.wait()
    native_to_tiles(cotangent_in, native_out.at[1], rows, turn)
    mode_in[0, 0, :, mer] = native_out[1, 0, :, odd, eighth]
    mode_in[0, 1, 0:SPARE, mer] = native_out[1, 1, 0:SPARE, odd, eighth]
    metric_rows(mass_ref, inverse_ref, rows, metric_out)
    metric_in[mer] = metric_out[...]

    def send_cotangent(place):
        which, at = place // 8, lax.rem(place, 8)
        send(native_out.at[1, 0, :, which, at], mode_in.at[0, 0, :, mer], mode, place, sems, 2)
        send(
            native_out.at[1, 1, 0:SPARE, which, at],
            mode_in.at[0, 1, 0:SPARE, mer],
            mode,
            place,
            sems,
            2,
        )
        send(metric_out, metric_in.at[mer], mode, place, sems, 3)

    each_place(mer, send_cotangent)
    sent.append((2, (N_MER - 1) * GROUPS, (N_MER - 1) * GROUPS))
    sent.append((3, (N_MER - 1) * 4, (N_MER - 1) * 4))

    stiffness_tables(d_ref, k_ref)
    table_copy.wait()

    wait_either(double, blank, 2 * (N_MODE - 1) * N_MER, (N_MODE - 1) * N_MER, recv_sems.at[0])

    def first(slot):
        first_stage(plane_in.at[0, slot], t_ref, u_planes.at[slot], plane_out.at[0, slot])

    each_slot(first)
    pl.semaphore_wait(ready, N_MODE - 1)
    send_to_modes(plane_out.at[0], mode_in.at[1], 4)

    wait(blank, (N_MER - 1) * 4, recv_sems.at[3])
    metric_tables(metric_in, mode, mer, mass, diag, faces, turn)
    wait(blank, (N_MER - 1) * GROUPS, recv_sems.at[2])
    emit = send_to_planes(mode_out.at[0], plane_in.at[1], 5)
    solve(mode_in.at[0], mode_out.at[0], False, True, False, solve_scratch, emit)

    wait_modes(4)
    emit = send_to_planes(mode_out.at[1], plane_in.at[2], 6)
    solve(mode_in.at[1], mode_out.at[1], True, False, True, solve_scratch, emit)

    def multiplier(slot):
        adjoint_planes(plane_in.at[1, slot], t_ref, s_planes.at[slot])

    wait_planes(5)
    each_slot(multiplier)

    def second(slot):
        state_planes(parts_of(plane_in.at[2, slot]), t_ref, planes)
        finish(t_ref, plane_in.at[1, slot], planes, s_planes.at[slot], plane_out.at[1, slot])

    wait_planes(6)
    each_slot(second)
    send_to_modes(plane_out.at[1], mode_in.at[2], 7)

    wait_modes(7)
    emit = send_to_planes(mode_out.at[2], plane_in.at[3], 8)
    solve(mode_in.at[2], mode_out.at[2], False, True, True, solve_scratch, emit)

    def third(slot):
        adjoint_planes(plane_in.at[3, slot], t_ref, s_planes.at[slot])
        finish(
            t_ref, plane_in.at[3, slot], u_planes.at[slot], s_planes.at[slot], plane_out.at[2, slot]
        )
        native_in[slot, mode] = plane_out[2, slot, :, mine]

        def send_gradient(other, core):
            theirs = pl.ds(pl.multiple_of(order_of(other) * 8, 8), 8)
            send(plane_out.at[2, slot, :, theirs], native_in.at[slot, mode], other, mer, sems, 9)

        each_group(mode, (0, 1), send_gradient)

    wait_planes(8)
    each_slot(third)
    sent.append((9, 2 * (N_MODE - 1) * N_MER, (N_MODE - 1) * N_MER))
    wait_either(double, blank, N_MER * (GROUPS - 2), N_MER * (GROUPS - 1), recv_sems.at[9])
    turned = lax.rem(lax.rem(mer, 4) + mer // 4, 4)
    copies = [pltpu.make_async_copy(native_in.at[0], out_hbm.at[0:N_MODE], copy_sems.at[2])]
    for index in range(SPARE):
        owner = 2 * lax.rem(index + turned, 4)
        copies.append(
            pltpu.make_async_copy(
                native_in.at[1, owner], out_hbm.at[N_MODE + index], copy_sems.at[3 + index]
            )
        )
    for copy in copies:
        copy.start()
    for at, tiles_double, tiles_single in sent:
        wait_either(double, blank, tiles_double, tiles_single, send_sems.at[at])
    for copy in copies:
        copy.wait()


def program(state, cotangent, mass, inverse, derivative, table):
    by_mode = (2, N_MODE, N_MER, 8, LANES)
    by_native = (2, N_MODE, 2, 8, 8, LANES)
    by_plane = (2, 2, COUNT // 2, 8, LANES)
    vmem = pl.BlockSpec(memory_space=pltpu.VMEM)
    hbm = pl.BlockSpec(memory_space=pl.ANY)

    def scratch(count, shape):
        return pltpu.VMEM((count,) + shape, F32)

    return pl.pallas_call(
        program_kernel,
        out_shape=jax.ShapeDtypeStruct((GROUPS, 2, 8, 8, LANES), F32),
        in_specs=[vmem, hbm, vmem, vmem, vmem, hbm],
        out_specs=hbm,
        scratch_shapes=[
            pltpu.VMEM((NODE, NODE, ELEM_DEV * LANES), F32),
            pltpu.VMEM((8, 2 * HALF, HALF), BF16),
            pltpu.SemaphoreType.DMA((6,)),
            pltpu.VMEM((PADDED * ELEM_DEV, LANES), F32),
            scratch(2, by_native),
            pltpu.VMEM(by_native, F32),
            scratch(3, by_mode),
            scratch(3, by_mode),
            scratch(3, by_plane),
            scratch(4, by_plane),
            pltpu.VMEM((2, 16, LANES), F32),
            scratch(N_MER, (2, 16, LANES)),
            scratch(2, (4, HALF, 2 * LANES)),
            scratch(4, (HALF, 2 * LANES)),
            scratch(2, (4, HALF, LANES)),
            pltpu.SemaphoreType.REGULAR,
            pltpu.VMEM((2 * COUNT, 8, LANES), F32),
            pltpu.SemaphoreType.DMA((10,)),
            pltpu.SemaphoreType.DMA((10,)),
            *SOLVE_SCRATCH,
        ],
        compiler_params=pltpu.CompilerParams(
            collective_id=0, has_side_effects=True, vmem_limit_bytes=60 << 20
        ),
        name="program",
    )(state, cotangent, mass, inverse, derivative, table)


def shards(cotangent, checkpoint, mass, inv_radius_sq, derivative):
    table = jnp.asarray(tables())
    return tiles_to_native(program(checkpoint, cotangent, mass, inv_radius_sq, derivative, table))


def solution(mesh):
    return jax.shard_map(
        shards,
        mesh=mesh,
        in_specs=(
            P(None, None, ("mer", "mode")),
            P(None, None, ("mer", "mode")),
            P(None, None, "mer"),
            P(None, None, "mer"),
            P(),
        ),
        out_specs=P(None, None, ("mer", "mode")),
        check_vma=False,
    )
```

```python
import functools
import math

import jax
import jax.numpy as jnp
import ml_dtypes
import numpy as np
from jax import lax
from jax.experimental import pallas as pl
from jax.experimental.pallas import tpu as pltpu
from jax.sharding import PartitionSpec as P

NODE = 9
NODES = NODE * NODE
RADIAL = 8
ITERS = 4
MODES = 512
HALF = 256
PLANES = 1024
ELEMENTS = 256
N_MODE = 8
N_MER = 16
ELEM_DEV = 16
GROUPS = 11
PADDED = GROUPS * 8
LANES = 128
AZIMUTH_WEIGHT = 4.0
HIGHEST = lax.Precision.HIGHEST
F32 = jnp.float32
BF16 = jnp.bfloat16


def tables():
    order = np.arange(HALF).reshape(4, 2, HALF // N_MODE).transpose(1, 0, 2).reshape(-1)
    out = []
    for wave in (np.cos, np.sin):
        for odd in range(2):
            index = np.outer(np.arange(HALF), 2 * order + odd) % PLANES
            values = wave(index.astype(np.float64) * (2.0 * math.pi / PLANES)).astype(np.float32)
            high = values.astype(ml_dtypes.bfloat16)
            low = (values - high.astype(np.float32)).astype(ml_dtypes.bfloat16)
            out.append((high, low))
    both = [np.concatenate(pair) for pair in out]
    turned = [np.concatenate([high.T, low.T]) for high, low in out]
    return np.stack(both + turned)


def mix(first, second):
    shape = first.shape
    axis = len(shape) - 2
    low = lax.broadcasted_iota(jnp.int32, shape, axis) % 4 < 2
    return (
        jnp.where(low, first, pltpu.roll(second, 2, axis)),
        jnp.where(low, pltpu.roll(first, 6, axis), second),
    )


def exchange(tiles):
    tiles = list(tiles)
    axis = tiles[0].ndim - 1
    block = lax.broadcasted_iota(jnp.int32, tiles[0].shape, axis) // 16
    for bit in (1, 2, 4):
        clear = (block & bit) == 0
        for at in range(8):
            if at & bit:
                continue
            one, two = tiles[at], tiles[at | bit]
            tiles[at] = jnp.where(clear, one, pltpu.roll(two, 16 * bit, axis))
            tiles[at | bit] = jnp.where(clear, pltpu.roll(one, LANES - 16 * bit, axis), two)
    return tiles


def native_to_tiles(x_ref, out_ref, rows, turn):
    rows[pl.ds(NODES * ELEM_DEV, PADDED * ELEM_DEV - NODES * ELEM_DEV), :] = jnp.zeros(
        ((PADDED - NODES) * ELEM_DEV, LANES), F32
    )
    for i in range(NODE):
        for e in range(ELEM_DEV):
            rows[pl.ds(i * NODE * ELEM_DEV + e, NODE, stride=ELEM_DEV), :] = x_ref[
                i, :, e * LANES : (e + 1) * LANES
            ]
    for group in range(GROUPS):
        turned = rows[group * LANES : (group + 1) * LANES, :].T
        turn[0, group] = turned[:64]
        turn[1, group] = turned[64:]
        for odd in range(2):
            real = turn[0, group, pl.ds(odd, 32, stride=2), :].reshape(4, 8, LANES)
            imag = turn[1, group, pl.ds(odd, 32, stride=2), :].reshape(4, 8, LANES)
            one, two = mix(real, imag)
            out_ref[group // 8, group % 8, odd] = jnp.stack([one, two], axis=1).reshape(8, 8, LANES)


def tiles_to_native_kernel(t_hbm, out_hbm, tiles_in, rows, turn, native, in_sems, out_sems):
    load = pltpu.make_async_copy(t_hbm, tiles_in, in_sems.at[0])
    load.start()
    load.wait()
    for group in range(GROUPS):
        for odd in range(2):
            tiles = tiles_in[group, odd].reshape(4, 2, 8, LANES)
            real, imag = mix(tiles[:, 0], tiles[:, 1])
            turn[0, group, pl.ds(odd, 32, stride=2), :] = real.reshape(32, LANES)
            turn[1, group, pl.ds(odd, 32, stride=2), :] = imag.reshape(32, LANES)
        both = jnp.concatenate([turn[0, group], turn[1, group]], axis=0)
        rows[group * LANES : (group + 1) * LANES, :] = both.T
    for i in range(NODE):
        for e in range(ELEM_DEV):
            native[i, :, e * LANES : (e + 1) * LANES] = rows[
                pl.ds(i * NODE * ELEM_DEV + e, NODE, stride=ELEM_DEV), :
            ]
    store = pltpu.make_async_copy(native, out_hbm, out_sems.at[0])
    store.start()
    store.wait()


def tiles_to_native(tiles):
    hbm = pl.BlockSpec(memory_space=pltpu.HBM)
    shape = (NODE, NODE, ELEM_DEV * LANES)
    return pl.pallas_call(
        tiles_to_native_kernel,
        out_shape=jax.ShapeDtypeStruct(shape, F32),
        in_specs=[hbm],
        out_specs=hbm,
        scratch_shapes=[
            pltpu.VMEM((GROUPS, 2, 8, 8, LANES), F32),
            pltpu.VMEM((PADDED * ELEM_DEV, LANES), F32),
            pltpu.VMEM((2, GROUPS, 64, LANES), F32),
            pltpu.VMEM(shape, F32),
            pltpu.SemaphoreType.DMA((1,)),
            pltpu.SemaphoreType.DMA((1,)),
        ],
        compiler_params=pltpu.CompilerParams(vmem_limit_bytes=62 << 20),
        name="tiles_to_native",
    )(tiles)


def stiffness_tables(d_ref, k_ref):
    def dot(a, b):
        return jnp.dot(a, b, precision=HIGHEST, preferred_element_type=F32)

    derivative = d_ref[...]
    stiffness = lax.dot_general(
        derivative, derivative, (((0,), (0,)), ((), ())), precision=HIGHEST, preferred_element_type=F32
    )

    def pick(shape, node_axis, outer):
        node = lax.broadcasted_iota(jnp.int32, shape, node_axis)
        other = lax.broadcasted_iota(jnp.int32, shape, 1 - node_axis)
        place = node // NODE if outer else node % NODE
        return jnp.where((place == other) & (node < NODES), 1.0, 0.0).astype(F32)

    outer, inner = pick((PADDED, NODE), 0, True), pick((PADDED, NODE), 0, False)
    outer_t, inner_t = pick((NODE, PADDED), 1, True), pick((NODE, PADDED), 1, False)
    whole = dot(dot(outer, stiffness), outer_t) * dot(inner, inner_t)
    whole = whole + dot(dot(inner, stiffness), inner_t) * dot(outer, outer_t)
    high = whole.astype(BF16).astype(F32)
    low = whole - high
    top = jnp.concatenate([high, high], axis=1)
    bottom = jnp.concatenate([low, jnp.zeros_like(low)], axis=1)
    k_ref[...] = jnp.concatenate([top, bottom], axis=0).astype(BF16)


def metric_rows(mass_ref, inverse_ref, rows, out_ref):
    lane = lax.broadcasted_iota(jnp.int32, (ELEM_DEV, LANES), 1) % ELEM_DEV
    element = lax.broadcasted_iota(jnp.int32, (ELEM_DEV, LANES), 0)
    repeat = jnp.where(lane == element, 1.0, 0.0).astype(F32)
    shape = (PADDED, LANES)
    node = lax.broadcasted_iota(jnp.int32, shape, 0)
    block = lax.broadcasted_iota(jnp.int32, shape, 1) // ELEM_DEV
    keep = (node % 8 == block) & (node < NODES)
    for kind, ref in ((0, mass_ref), (1, inverse_ref)):
        for i in range(NODE):
            rows[i * NODE : (i + 1) * NODE, :ELEM_DEV] = ref[i]
        values = jnp.dot(
            rows[:PADDED, :ELEM_DEV], repeat, precision=HIGHEST, preferred_element_type=F32
        )
        values = jnp.where(keep, values, 0.0).reshape(GROUPS, 8, LANES)
        out_ref[kind, :GROUPS] = jnp.sum(values, axis=1)
        out_ref[kind, GROUPS:] = jnp.zeros((16 - GROUPS, LANES), F32)


def metric_tables(m_ref, mode_group, place, mass, diag, faces, turn):
    inverse = diag.at[0]
    for kind, out in ((0, mass), (1, inverse)):
        for h in range(2):
            rows = exchange([m_ref[8 * h + at, kind] for at in range(8)])
            for at in range(8):
                for group in range(GROUPS):
                    turn[h, group, at : at + 1] = rows[at][group : group + 1]
            for group in range(GROUPS):
                out[group * 8 : (group + 1) * 8, h * LANES : (h + 1) * LANES] = turn[h, group, 0:8]
    shape = (PADDED, ELEMENTS)
    node = lax.broadcasted_iota(jnp.int32, shape, 0)
    element = lax.broadcasted_iota(jnp.int32, shape, 1)
    inside = node < NODES
    upper = (node % NODE == NODE - 1) & (element < ELEMENTS - RADIAL) & inside
    lower = (node % NODE == 0) & (element >= RADIAL) & inside
    outer = (node // NODE == NODE - 1) & (element % RADIAL != RADIAL - 1) & inside
    inner = (node // NODE == 0) & (element % RADIAL != 0)
    marks = [jnp.where(mark, 1.0, 0.0).astype(F32) for mark in (upper, lower, outer, inner)]
    for at in range(4):
        faces[at] = marks[at]
    count = marks[0] + marks[1] + marks[2] + marks[3]
    values = inverse[...]
    for n in range(4):
        offset = lax.rem(place, 8) // 2 * 8 + lax.rem(place, 2) * 2 + n // 2 * 4 + n % 2
        number = mode_group * 64 + 2 * offset + place // 8
        fraction = number.astype(F32) / MODES
        diag[n] = mass[...] * (1.0 + AZIMUTH_WEIGHT * fraction * fraction * values) + count


def owner_of(extra_group, place):
    return 2 * ((extra_group + place % 4 + place // 4) % 4)


PAIRS = (((0, 2), (4, 6), (8, 9), (10,)), ((1, 3), (5, 7)))


def load_tiles(b_ref, half, turn, weight, out, by_owner):
    rows = slice(4 * half, 4 * half + 4)

    def piece(group, place):
        if group < 8:
            return b_ref[0, group, place, rows]
        return b_ref[1, owner_of(group - 8, place) if by_owner else group - 8, place, rows]

    for at_pair, pair in enumerate(PAIRS[0] + PAIRS[1]):
        for h in range(2):
            tiles = []
            for place in range(8 * h, 8 * h + 8):
                tiles.append(
                    jnp.concatenate([piece(pair[0], place), piece(pair[-1], place)], axis=0)
                )
            tiles = exchange(tiles)
            for at in range(8):
                turn[h, at_pair, at * 8 : (at + 1) * 8] = tiles[at]
            lanes = slice(h * LANES, (h + 1) * LANES)
            for which, group in enumerate(pair):
                nodes = slice(group * 8, (group + 1) * 8)
                for s in range(4):
                    value = turn[h, at_pair, pl.ds(4 * which + s, 8, stride=8), :]
                    if weight is not None:
                        value = value * weight[nodes, lanes]
                    out[4 * half + s, nodes, lanes] = value


def store_tiles(value_of, half, turn, out_ref, emit):
    rows = slice(4 * half, 4 * half + 4)
    for core in range(2):
        for at_pair, pair in enumerate(PAIRS[core]):
            for h in range(2):
                lanes = slice(h * LANES, (h + 1) * LANES)
                for which, group in enumerate(pair):
                    for s in range(4):
                        turn[h, 4 * core + at_pair, pl.ds(4 * which + s, 8, stride=8), :] = value_of(
                            4 * half + s, slice(group * 8, (group + 1) * 8), lanes
                        )
                tiles = [turn[h, 4 * core + at_pair, at * 8 : (at + 1) * 8] for at in range(8)]
                tiles = exchange(tiles)
                for which, group in enumerate(pair):
                    for at in range(8):
                        place = 8 * h + at
                        owner = owner_of(group - 8, place) if group >= 8 else group
                        out_ref[group // 8, owner, place, rows] = tiles[at][
                            4 * which : 4 * which + 4
                        ]
        emit(core, half)


def total(parts):
    half = parts[:, :LANES] + parts[:, LANES:]
    return jnp.broadcast_to(jnp.sum(half, axis=(0, 1), keepdims=True), (1, ELEMENTS))


def fold(value):
    return jnp.sum(value.reshape(GROUPS, 8, ELEMENTS), axis=0)


def solve(b_ref, out_ref, half, weigh_in, weigh_out, by_owner, scratch, emit):
    mass, diag, faces, k_ref, r, p, q, alphas, turn = scratch
    load_tiles(b_ref, half, turn, mass if weigh_in else None, r, by_owner)
    modes = (2 * half, 2 * half + 1)

    def rows_of(n):
        return (4 * half + n % 2, 4 * half + 2 + n % 2)

    def square(n):
        one, two = rows_of(n)
        return total(fold(r[one] * r[one]) + fold(r[two] * r[two]))

    norms = tuple(square(n) for n in modes)
    for n in modes:
        for s in rows_of(n):
            p[ITERS - 1, s] = jnp.zeros((PADDED, ELEMENTS), F32)
    empty = jnp.zeros((8, ELEMENTS), F32)

    def operate(sweep, before, n, beta, norm):
        curve = None
        for s in rows_of(n):
            now = r[s] + beta * p[before, s]
            p[sweep, s] = now
            high = now.astype(BF16).astype(F32)
            halves = jnp.concatenate([high, now - high], axis=0).astype(BF16)
            image = jnp.dot(k_ref[...], halves, preferred_element_type=F32)
            ahead = pltpu.roll(now[: PADDED - 8], ELEMENTS - RADIAL, 1)
            behind = pltpu.roll(now[8:], RADIAL, 1)
            image = (
                image[:PADDED]
                + image[PADDED:]
                + diag[n] * now
                - faces[0] * jnp.concatenate([empty, ahead], axis=0)
                - faces[1] * jnp.concatenate([behind, empty], axis=0)
            )
            outward = pltpu.roll(now[:16], ELEMENTS - 1, 1)
            inward = pltpu.roll(now[72:], 1, 1)
            image = jnp.concatenate(
                [
                    image[:16] - faces[3, :16] * inward,
                    image[16:72],
                    image[72:] - faces[2, 72:] * outward,
                ],
                axis=0,
            )
            q[s] = image
            part = fold(now * image)
            curve = part if curve is None else curve + part
        alpha = norm / total(curve)
        alphas[sweep * 4 + n] = alpha
        return alpha

    def reduce(n, alpha):
        part = None
        for s in rows_of(n):
            value = r[s] - alpha * q[s]
            r[s] = value
            add = fold(value * value)
            part = add if part is None else part + add
        return total(part)

    def sweep_body(sweep, carry):
        norms, betas = carry
        before = lax.rem(sweep + ITERS - 1, ITERS)
        step = [operate(sweep, before, n, betas[n % 2], norms[n % 2]) for n in modes]
        after = tuple(reduce(n, step[n % 2]) for n in modes)
        return after, tuple(after[n] / norms[n] for n in range(2))

    none = (jnp.zeros((1, ELEMENTS), F32),) * 2
    norms, betas = lax.fori_loop(0, ITERS - 1, sweep_body, (norms, none))
    for n in modes:
        operate(ITERS - 1, ITERS - 2, n, betas[n % 2], norms[n % 2])

    def value_of(s, rows, lanes):
        n = s // 4 * 2 + s % 2
        value = alphas[n, :, lanes] * p[0, s, rows, lanes]
        for sweep in range(1, ITERS):
            value = value + alphas[sweep * 4 + n, :, lanes] * p[sweep, s, rows, lanes]
        return value * mass[rows, lanes] if weigh_out else value

    store_tiles(value_of, half, turn, out_ref, emit)


FIELD = pltpu.VMEM((8, PADDED, ELEMENTS), F32)
SOLVE_SCRATCH = [
    pltpu.VMEM((PADDED, ELEMENTS), F32),
    pltpu.VMEM((4, PADDED, ELEMENTS), F32),
    pltpu.VMEM((4, PADDED, ELEMENTS), F32),
    pltpu.VMEM((2 * PADDED, 2 * PADDED), BF16),
    FIELD,
    pltpu.VMEM((ITERS, 8, PADDED, ELEMENTS), F32),
    FIELD,
    pltpu.VMEM((ITERS * 4, 1, ELEMENTS), F32),
    pltpu.VMEM((2, GROUPS, 64, LANES), F32),
]


def split(value):
    high = value.astype(BF16)
    return high, (value - high.astype(F32)).astype(BF16)


def apply(t_ref, which, field):
    high, low = split(field)
    width = field.shape[1]
    if width == LANES:
        both = jnp.concatenate([high, low], axis=1)
        out = jnp.dot(t_ref[which], both, preferred_element_type=F32)
        return out[:HALF, :LANES] + out[:HALF, LANES:] + out[HALF:, :LANES]
    out = jnp.dot(t_ref[which], high, preferred_element_type=F32)
    out = out[:HALF] + out[HALF:]
    return out + jnp.dot(t_ref[which, :HALF], low, preferred_element_type=F32)


def parts_of(u_ref):
    out = []
    for odd in range(2):
        tiles = u_ref[odd].reshape(32, 2, 8, LANES)
        one, two = mix(tiles[:, 0], tiles[:, 1])
        out.append((one.reshape(HALF, LANES), two.reshape(HALF, LANES)))
    return out


def parts_to(out_ref, parts):
    for odd in range(2):
        real, imag = parts[odd]
        one, two = mix(real.reshape(32, 8, LANES), imag.reshape(32, 8, LANES))
        out_ref[odd] = jnp.stack([one, two], axis=1).reshape(64, 8, LANES)


def mode_rows(odd):
    row = lax.broadcasted_iota(jnp.int32, (HALF, LANES), 0)
    mode = 2 * ((row // 32 % 4 * 2 + row // 128) * 32 + row % 32) + odd
    fraction = mode.astype(F32) / MODES
    weight = jnp.where(mode == 0, 1.0 / PLANES, 2.0 / PLANES).astype(F32)
    sign = jnp.where(row % 2 == 0, 1.0, -1.0).astype(F32)
    return fraction, weight, sign


def first_row(shape):
    return lax.broadcasted_iota(jnp.int32, shape, 0) == 0


def to_planes(t_ref, cos_fields, sin_fields, out_ref):
    sign = mode_rows(0)[2][:, :1]
    cos_even, cos_odd = apply(t_ref, 0, cos_fields[0]), apply(t_ref, 1, cos_fields[1])
    sin_even, sin_odd = apply(t_ref, 2, sin_fields[0]), apply(t_ref, 3, sin_fields[1])
    quarter_cos = jnp.sum(sign * cos_fields[0], axis=0, keepdims=True)
    quarter_sin = jnp.sum(sign * sin_fields[1], axis=0, keepdims=True)
    cos, sin = cos_even + cos_odd, sin_even + sin_odd
    out_ref[0] = cos - sin
    out_ref[1] = cos + sin
    cos, sin = cos_even - cos_odd, sin_even - sin_odd
    out_ref[2] = cos + sin
    out_ref[3] = cos - sin
    out_ref[1, 0:1] = quarter_cos - quarter_sin
    out_ref[3, 0:1] = quarter_cos + quarter_sin


def from_planes(t_ref, values):
    shape = values[0].shape
    sign = mode_rows(0)[2][:, :1]
    first = first_row(shape)
    quarter, three = values[1][0:1], values[3][0:1]
    one = values[0]
    two = jnp.where(first, 0.0, values[1])
    four = jnp.where(first, 0.0, values[3])
    plus, minus = one + two, one - two
    plus_far, minus_far = values[2] + four, values[2] - four
    a_even = apply(t_ref, 4, plus + plus_far) + sign * (quarter + three)
    a_odd = apply(t_ref, 5, plus - plus_far)
    b_even = -apply(t_ref, 6, minus - minus_far)
    b_odd = -apply(t_ref, 7, minus + minus_far) - sign * (quarter - three)
    return (a_even, b_even), (a_odd, b_odd)


def state_planes(parts, t_ref, out_ref):
    cos_fields, sin_fields = [], []
    for odd in range(2):
        real, imag = parts[odd]
        fraction = mode_rows(odd)[0]
        cos_fields.append(jnp.concatenate([real, -fraction * imag], axis=1))
        sin_fields.append(jnp.concatenate([imag, fraction * real], axis=1))
    to_planes(t_ref, cos_fields, sin_fields, out_ref)


def first_stage(u_ref, t_ref, planes, out_ref):
    parts = parts_of(u_ref)
    state_planes(parts, t_ref, planes)
    values = [planes[at, :, :LANES] * planes[at, :, LANES:] for at in range(4)]
    found = from_planes(t_ref, values)
    out = []
    for odd in range(2):
        weight = mode_rows(odd)[1]
        out.append(tuple(parts[odd][c] - weight * found[odd][c] for c in range(2)))
    parts_to(out_ref, out)


def adjoint_planes(s_ref, t_ref, out_ref):
    parts = parts_of(s_ref)
    weights = [mode_rows(odd)[1] for odd in range(2)]
    to_planes(
        t_ref,
        [weights[odd] * parts[odd][0] for odd in range(2)],
        [weights[odd] * parts[odd][1] for odd in range(2)],
        out_ref,
    )


def finish(t_ref, s_ref, planes, adjoint, out_ref):
    values = []
    for at in range(4):
        factor = adjoint[at]
        values.append(planes[at] * jnp.concatenate([factor, factor], axis=1))
    found = from_planes(t_ref, values)
    parts = parts_of(s_ref)
    out = []
    for odd in range(2):
        fraction = mode_rows(odd)[0]
        a, b = found[odd]
        out.append(
            (
                parts[odd][0] - a[:, LANES:] - fraction * b[:, :LANES],
                parts[odd][1] - b[:, LANES:] + fraction * a[:, :LANES],
            )
        )
    parts_to(out_ref, out)


COUNT = N_MODE * N_MER
SPARE = GROUPS - 8


def send(source, target, mode, mer, sems, at):
    pltpu.make_async_remote_copy(
        src_ref=source,
        dst_ref=target,
        send_sem=sems[0].at[at],
        recv_sem=sems[1].at[at],
        device_id={"mode": mode, "mer": mer},
        device_id_type=pl.DeviceIdType.MESH,
    ).start()


def wait(blank, tiles, sem, rows=8):
    whole = blank.at[pl.ds(0, tiles), pl.ds(0, rows)]
    pltpu.make_async_copy(whole, whole, sem).wait()


def wait_either(double, blank, tiles_double, tiles_single, sem, rows=8):
    @pl.when(double)
    def _():
        wait(blank, tiles_double, sem, rows)

    @pl.when(jnp.logical_not(double))
    def _():
        wait(blank, tiles_single, sem, rows)


def place_at(mer, k):
    step = lax.rem(7 * k, N_MER)
    y = lax.rem(lax.rem(mer, 4) + lax.rem(step, 4), 4)
    z = lax.rem(mer // 4 + step // 4, 4)
    return z * 4 + y


def extra(x, mer):
    turn = lax.rem(lax.rem(mer, 4) + mer // 4, 4)
    return lax.rem(x + 4 - turn, 4)


def groups_on(mode, core):
    x = mode // 2
    return [2 * lax.rem(x + step, 4) + core for step in (1, 3, 2, 0)]


def each_group(mode, cores, act):
    for core in cores:
        one, two, three, own = groups_on(mode, core)
        act(one, core)
        act(two, core)
        act(three, core)

        @pl.when(lax.rem(mode, 2) != core)
        def _(own=own, core=core):
            act(own, core)


def each_place(mer, act):
    def body(k, _):
        act(place_at(mer, k))
        return 0

    lax.fori_loop(1, N_MER, body, 0)


def each_other(mode, mer, cores, act):
    groups = [(other, core) for core in cores for other in groups_on(mode, core)]

    def body(place):
        for other, core in groups:
            act(other, core, place)

    each_place(mer, body)
    each_group(mode, cores, lambda other, core: act(other, core, mer))


def order_of(mode):
    return lax.rem(mode, 2) * 4 + mode // 2


def program_kernel(
    state_ref,
    cotangent_hbm,
    mass_ref,
    inverse_ref,
    d_ref,
    t_hbm,
    out_hbm,
    cotangent_in,
    t_ref,
    copy_sems,
    rows,
    native_out,
    native_in,
    mode_out,
    mode_in,
    plane_out,
    plane_in,
    metric_out,
    metric_in,
    u_planes,
    planes,
    s_planes,
    ready,
    blank,
    send_sems,
    recv_sems,
    *solve_scratch,
):
    mode = lax.axis_index("mode")
    mer = lax.axis_index("mer")
    odd, eighth = mer // 8, lax.rem(mer, 8)
    row = order_of(mode) * 8 + eighth
    mine_extra = extra(mode // 2, mer)
    double = (lax.rem(mode, 2) == 0) & (mine_extra < SPARE)
    slots = jnp.where(double, 2, 1)
    sems = (send_sems, recv_sems)
    mass, diag, faces, k_ref = solve_scratch[:4]
    turn = solve_scratch[8]
    sent = []

    cotangent_copy = pltpu.make_async_copy(cotangent_hbm, cotangent_in, copy_sems.at[0])
    table_copy = pltpu.make_async_copy(t_hbm, t_ref, copy_sems.at[1])
    cotangent_copy.start()
    table_copy.start()
    barrier = pltpu.get_barrier_semaphore()

    def greet(semaphore, other, place):
        pl.semaphore_signal(
            semaphore,
            inc=1,
            device_id={"mode": other, "mer": place},
            device_id_type=pl.DeviceIdType.MESH,
        )

    each_group(mode, (0, 1), lambda other, core: greet(barrier, other, mer))
    each_place(mer, lambda place: greet(barrier, mode, place))
    native_to_tiles(state_ref, native_out.at[0], rows, turn)
    pl.semaphore_wait(barrier, N_MODE - 1 + N_MER - 1)
    each_group(mode, (0, 1), lambda other, core: greet(ready, other, mer))

    def each_slot(act):
        def body(k, _):
            act(slots - 1 - k)
            return 0

        lax.fori_loop(0, slots, body, 0)

    def send_to_planes(source, target, at):
        def emit(core, half):
            rows = pl.ds(4 * half, 4)

            def act(other, core, place):
                def single():
                    send(
                        source.at[0, other, place, rows],
                        target.at[0, odd, row, rows],
                        other,
                        place,
                        sems,
                        at + half,
                    )

                if core == 1:
                    single()
                    return
                owns_two = extra(other // 2, place) < SPARE
                pl.when(jnp.logical_not(owns_two))(single)

                @pl.when(owns_two)
                def _():
                    send(
                        source.at[:, other, place, rows],
                        target.at[:, odd, row, rows],
                        other,
                        place,
                        sems,
                        at + half,
                    )

            each_other(mode, mer, (core,), act)
            if core == 1:
                target[:, odd, row, 4 * half : 4 * half + 4] = source[
                    :, mode, mer, 4 * half : 4 * half + 4
                ]

        for half in range(2):
            sent.append((at + half, 16 * GROUPS - 2, 16 * GROUPS - 1, 4))
        return emit

    def wait_planes(at):
        for half in range(2):
            wait_either(double, blank, 2 * (COUNT - 1), COUNT - 1, recv_sems.at[at + half], 4)

    def send_to_modes(source, target, at):
        target[0, mode, mer] = source[0, odd, row]

        @pl.when(double)
        def _():
            target[1, mode, mer] = source[1, odd, row]

        for half in range(2):
            rows = pl.ds(4 * half, 4)

            def act(other, core, place, rows=rows, half=half):
                index = order_of(other) * 8 + lax.rem(place, 8)
                piece = source.at[0, place // 8, index, rows]
                send(piece, target.at[0, mode, mer, rows], other, place, sems, at + half)

            def act_double(other, core, place, rows=rows, half=half):
                index = order_of(other) * 8 + lax.rem(place, 8)
                piece = source.at[:, place // 8, index, rows]
                send(piece, target.at[:, mode, mer, rows], other, place, sems, at + half)

            @pl.when(double)
            def _(act_double=act_double):
                each_other(mode, mer, (0, 1), act_double)

            @pl.when(jnp.logical_not(double))
            def _(act=act):
                each_other(mode, mer, (0, 1), act)

            sent.append((at + half, 2 * (COUNT - 1), COUNT - 1, 4))

    def wait_modes(at, half):
        wait_either(
            double, blank, 16 * GROUPS - 2, 16 * GROUPS - 1, recv_sems.at[at + half], 4
        )

    mine = pl.ds(pl.multiple_of(order_of(mode) * 8, 8), 8)
    plane_in[0, 0, :, mine] = native_out[0, 0, mode]
    plane_in[0, 1, :, mine] = native_out[0, 1, mine_extra]

    def send_extra_state(other, core):
        index = extra(other // 2, mer)

        @pl.when(index < SPARE)
        def _():
            send(native_out.at[0, 1, index], plane_in.at[0, 1, :, mine], other, mer, sems, 0)

    def send_state(other, core):
        send(native_out.at[0, 0, other], plane_in.at[0, 0, :, mine], other, mer, sems, 0)

    each_group(mode, (0,), send_extra_state)
    each_group(mode, (0, 1), send_state)
    sent.append((0, N_MER * (GROUPS - 2), N_MER * (GROUPS - 1), 8))

    cotangent_copy.wait()
    native_to_tiles(cotangent_in, native_out.at[1], rows, turn)
    mode_in[0, 0, :, mer] = native_out[1, 0, :, odd, eighth]
    mode_in[0, 1, 0:SPARE, mer] = native_out[1, 1, 0:SPARE, odd, eighth]
    metric_rows(mass_ref, inverse_ref, rows, metric_out)
    metric_in[mer] = metric_out[...]

    def send_cotangent(place):
        which, at = place // 8, lax.rem(place, 8)
        send(native_out.at[1, 0, :, which, at], mode_in.at[0, 0, :, mer], mode, place, sems, 2)
        send(
            native_out.at[1, 1, 0:SPARE, which, at],
            mode_in.at[0, 1, 0:SPARE, mer],
            mode,
            place,
            sems,
            2,
        )
        send(metric_out, metric_in.at[mer], mode, place, sems, 3)

    each_place(mer, send_cotangent)
    sent.append((2, (N_MER - 1) * GROUPS, (N_MER - 1) * GROUPS, 8))
    sent.append((3, (N_MER - 1) * 4, (N_MER - 1) * 4, 8))

    stiffness_tables(d_ref, k_ref)
    table_copy.wait()

    wait_either(double, blank, 2 * (N_MODE - 1) * N_MER, (N_MODE - 1) * N_MER, recv_sems.at[0])

    def first(slot):
        first_stage(plane_in.at[0, slot], t_ref, u_planes.at[slot], plane_out.at[0, slot])

    each_slot(first)
    pl.semaphore_wait(ready, N_MODE - 1)
    send_to_modes(plane_out.at[0], mode_in.at[1], 4)

    wait(blank, (N_MER - 1) * 4, recv_sems.at[3])
    metric_tables(metric_in, mode, mer, mass, diag, faces, turn)
    wait(blank, (N_MER - 1) * GROUPS, recv_sems.at[2])
    emit = send_to_planes(mode_out.at[0], plane_in.at[1], 6)
    for half in range(2):
        solve(mode_in.at[0], mode_out.at[0], half, False, True, False, solve_scratch, emit)

    emit = send_to_planes(mode_out.at[1], plane_in.at[2], 8)
    for half in range(2):
        wait_modes(4, half)
        solve(mode_in.at[1], mode_out.at[1], half, True, False, True, solve_scratch, emit)

    def multiplier(slot):
        adjoint_planes(plane_in.at[1, slot], t_ref, s_planes.at[slot])

    wait_planes(6)
    each_slot(multiplier)

    def second(slot):
        state_planes(parts_of(plane_in.at[2, slot]), t_ref, planes)
        finish(t_ref, plane_in.at[1, slot], planes, s_planes.at[slot], plane_out.at[1, slot])

    wait_planes(8)
    each_slot(second)
    send_to_modes(plane_out.at[1], mode_in.at[2], 10)

    emit = send_to_planes(mode_out.at[2], plane_in.at[3], 12)
    for half in range(2):
        wait_modes(10, half)
        solve(mode_in.at[2], mode_out.at[2], half, False, True, True, solve_scratch, emit)

    def third(slot):
        adjoint_planes(plane_in.at[3, slot], t_ref, s_planes.at[slot])
        finish(
            t_ref, plane_in.at[3, slot], u_planes.at[slot], s_planes.at[slot], plane_out.at[2, slot]
        )
        native_in[slot, mode] = plane_out[2, slot, :, mine]

        def send_gradient(other, core):
            theirs = pl.ds(pl.multiple_of(order_of(other) * 8, 8), 8)
            send(plane_out.at[2, slot, :, theirs], native_in.at[slot, mode], other, mer, sems, 14)

        each_group(mode, (0, 1), send_gradient)

    wait_planes(12)
    each_slot(third)
    sent.append((14, 2 * (N_MODE - 1) * N_MER, (N_MODE - 1) * N_MER, 8))
    wait_either(double, blank, N_MER * (GROUPS - 2), N_MER * (GROUPS - 1), recv_sems.at[14])
    turned = lax.rem(lax.rem(mer, 4) + mer // 4, 4)
    copies = [pltpu.make_async_copy(native_in.at[0], out_hbm.at[0:N_MODE], copy_sems.at[2])]
    for index in range(SPARE):
        owner = 2 * lax.rem(index + turned, 4)
        copies.append(
            pltpu.make_async_copy(
                native_in.at[1, owner], out_hbm.at[N_MODE + index], copy_sems.at[3 + index]
            )
        )
    for copy in copies:
        copy.start()
    for at, tiles_double, tiles_single, rows_each in sent:
        wait_either(double, blank, tiles_double, tiles_single, send_sems.at[at], rows_each)
    for copy in copies:
        copy.wait()


def program(state, cotangent, mass, inverse, derivative, table):
    by_mode = (2, N_MODE, N_MER, 8, LANES)
    by_native = (2, N_MODE, 2, 8, 8, LANES)
    by_plane = (2, 2, COUNT // 2, 8, LANES)
    vmem = pl.BlockSpec(memory_space=pltpu.VMEM)
    hbm = pl.BlockSpec(memory_space=pl.ANY)

    def scratch(count, shape):
        return pltpu.VMEM((count,) + shape, F32)

    return pl.pallas_call(
        program_kernel,
        out_shape=jax.ShapeDtypeStruct((GROUPS, 2, 8, 8, LANES), F32),
        in_specs=[vmem, hbm, vmem, vmem, vmem, hbm],
        out_specs=hbm,
        scratch_shapes=[
            pltpu.VMEM((NODE, NODE, ELEM_DEV * LANES), F32),
            pltpu.VMEM((8, 2 * HALF, HALF), BF16),
            pltpu.SemaphoreType.DMA((6,)),
            pltpu.VMEM((PADDED * ELEM_DEV, LANES), F32),
            scratch(2, by_native),
            pltpu.VMEM(by_native, F32),
            scratch(3, by_mode),
            scratch(3, by_mode),
            scratch(3, by_plane),
            scratch(4, by_plane),
            pltpu.VMEM((2, 16, LANES), F32),
            scratch(N_MER, (2, 16, LANES)),
            scratch(2, (4, HALF, 2 * LANES)),
            scratch(4, (HALF, 2 * LANES)),
            scratch(2, (4, HALF, LANES)),
            pltpu.SemaphoreType.REGULAR,
            pltpu.VMEM((2 * COUNT, 8, LANES), F32),
            pltpu.SemaphoreType.DMA((15,)),
            pltpu.SemaphoreType.DMA((15,)),
            *SOLVE_SCRATCH,
        ],
        compiler_params=pltpu.CompilerParams(
            collective_id=0, has_side_effects=True, vmem_limit_bytes=60 << 20
        ),
        name="program",
    )(state, cotangent, mass, inverse, derivative, table)


def shards(cotangent, checkpoint, mass, inv_radius_sq, derivative):
    table = jnp.asarray(tables())
    return tiles_to_native(program(checkpoint, cotangent, mass, inv_radius_sq, derivative, table))


def solution(mesh):
    return jax.shard_map(
        shards,
        mesh=mesh,
        in_specs=(
            P(None, None, ("mer", "mode")),
            P(None, None, ("mer", "mode")),
            P(None, None, "mer"),
            P(None, None, "mer"),
            P(),
        ),
        out_specs=P(None, None, ("mer", "mode")),
        check_vma=False,
    )
```

```python
import functools
import math

import jax
import jax.numpy as jnp
import ml_dtypes
import numpy as np
from jax import lax
from jax.experimental import pallas as pl
from jax.experimental.pallas import tpu as pltpu
from jax.sharding import PartitionSpec as P

NODE = 9
NODES = NODE * NODE
RADIAL = 8
ITERS = 4
MODES = 512
HALF = 256
PLANES = 1024
ELEMENTS = 256
N_MODE = 8
N_MER = 16
ELEM_DEV = 16
GROUPS = 11
PADDED = GROUPS * 8
LANES = 128
AZIMUTH_WEIGHT = 4.0
HIGHEST = lax.Precision.HIGHEST
F32 = jnp.float32
BF16 = jnp.bfloat16


def tables():
    order = np.arange(HALF).reshape(4, 2, HALF // N_MODE).transpose(1, 0, 2).reshape(-1)
    out = []
    for wave in (np.cos, np.sin):
        for odd in range(2):
            index = np.outer(np.arange(HALF), 2 * order + odd) % PLANES
            values = wave(index.astype(np.float64) * (2.0 * math.pi / PLANES)).astype(np.float32)
            high = values.astype(ml_dtypes.bfloat16)
            low = (values - high.astype(np.float32)).astype(ml_dtypes.bfloat16)
            out.append((high, low))
    both = [np.concatenate(pair) for pair in out]
    turned = [np.concatenate([high.T, low.T]) for high, low in out]
    return np.stack(both + turned)


def mix(first, second):
    shape = first.shape
    axis = len(shape) - 2
    low = lax.broadcasted_iota(jnp.int32, shape, axis) % 4 < 2
    return (
        jnp.where(low, first, pltpu.roll(second, 2, axis)),
        jnp.where(low, pltpu.roll(first, 6, axis), second),
    )


def exchange(tiles):
    tiles = list(tiles)
    axis = tiles[0].ndim - 1
    block = lax.broadcasted_iota(jnp.int32, tiles[0].shape, axis) // 16
    for bit in (1, 2, 4):
        clear = (block & bit) == 0
        for at in range(8):
            if at & bit:
                continue
            one, two = tiles[at], tiles[at | bit]
            tiles[at] = jnp.where(clear, one, pltpu.roll(two, 16 * bit, axis))
            tiles[at | bit] = jnp.where(clear, pltpu.roll(one, LANES - 16 * bit, axis), two)
    return tiles


def native_to_tiles(x_ref, out_ref, rows, turn):
    rows[pl.ds(NODES * ELEM_DEV, PADDED * ELEM_DEV - NODES * ELEM_DEV), :] = jnp.zeros(
        ((PADDED - NODES) * ELEM_DEV, LANES), F32
    )
    for i in range(NODE):
        for e in range(ELEM_DEV):
            rows[pl.ds(i * NODE * ELEM_DEV + e, NODE, stride=ELEM_DEV), :] = x_ref[
                i, :, e * LANES : (e + 1) * LANES
            ]
    for group in range(GROUPS):
        turned = rows[group * LANES : (group + 1) * LANES, :].T
        turn[0, group] = turned[:64]
        turn[1, group] = turned[64:]
        for odd in range(2):
            real = turn[0, group, pl.ds(odd, 32, stride=2), :].reshape(4, 8, LANES)
            imag = turn[1, group, pl.ds(odd, 32, stride=2), :].reshape(4, 8, LANES)
            one, two = mix(real, imag)
            out_ref[group // 8, group % 8, odd] = jnp.stack([one, two], axis=1).reshape(8, 8, LANES)


def tiles_to_native_kernel(t_hbm, out_hbm, tiles_in, rows, turn, native, in_sems, out_sems):
    load = pltpu.make_async_copy(t_hbm, tiles_in, in_sems.at[0])
    load.start()
    load.wait()
    for group in range(GROUPS):
        for odd in range(2):
            tiles = tiles_in[group, odd].reshape(4, 2, 8, LANES)
            real, imag = mix(tiles[:, 0], tiles[:, 1])
            turn[0, group, pl.ds(odd, 32, stride=2), :] = real.reshape(32, LANES)
            turn[1, group, pl.ds(odd, 32, stride=2), :] = imag.reshape(32, LANES)
        both = jnp.concatenate([turn[0, group], turn[1, group]], axis=0)
        rows[group * LANES : (group + 1) * LANES, :] = both.T
    for i in range(NODE):
        for e in range(ELEM_DEV):
            native[i, :, e * LANES : (e + 1) * LANES] = rows[
                pl.ds(i * NODE * ELEM_DEV + e, NODE, stride=ELEM_DEV), :
            ]
    store = pltpu.make_async_copy(native, out_hbm, out_sems.at[0])
    store.start()
    store.wait()


def tiles_to_native(tiles):
    hbm = pl.BlockSpec(memory_space=pltpu.HBM)
    shape = (NODE, NODE, ELEM_DEV * LANES)
    return pl.pallas_call(
        tiles_to_native_kernel,
        out_shape=jax.ShapeDtypeStruct(shape, F32),
        in_specs=[hbm],
        out_specs=hbm,
        scratch_shapes=[
            pltpu.VMEM((GROUPS, 2, 8, 8, LANES), F32),
            pltpu.VMEM((PADDED * ELEM_DEV, LANES), F32),
            pltpu.VMEM((2, GROUPS, 64, LANES), F32),
            pltpu.VMEM(shape, F32),
            pltpu.SemaphoreType.DMA((1,)),
            pltpu.SemaphoreType.DMA((1,)),
        ],
        compiler_params=pltpu.CompilerParams(vmem_limit_bytes=62 << 20),
        name="tiles_to_native",
    )(tiles)


def stiffness_tables(d_ref, k_ref):
    def dot(a, b):
        return jnp.dot(a, b, precision=HIGHEST, preferred_element_type=F32)

    derivative = d_ref[...]
    stiffness = lax.dot_general(
        derivative, derivative, (((0,), (0,)), ((), ())), precision=HIGHEST, preferred_element_type=F32
    )

    def pick(shape, node_axis, outer):
        node = lax.broadcasted_iota(jnp.int32, shape, node_axis)
        other = lax.broadcasted_iota(jnp.int32, shape, 1 - node_axis)
        place = node // NODE if outer else node % NODE
        return jnp.where((place == other) & (node < NODES), 1.0, 0.0).astype(F32)

    outer, inner = pick((PADDED, NODE), 0, True), pick((PADDED, NODE), 0, False)
    outer_t, inner_t = pick((NODE, PADDED), 1, True), pick((NODE, PADDED), 1, False)
    whole = dot(dot(outer, stiffness), outer_t) * dot(inner, inner_t)
    whole = whole + dot(dot(inner, stiffness), inner_t) * dot(outer, outer_t)
    high = whole.astype(BF16).astype(F32)
    low = whole - high
    top = jnp.concatenate([high, high], axis=1)
    bottom = jnp.concatenate([low, jnp.zeros_like(low)], axis=1)
    k_ref[...] = jnp.concatenate([top, bottom], axis=0).astype(BF16)


def metric_rows(mass_ref, inverse_ref, rows, out_ref):
    lane = lax.broadcasted_iota(jnp.int32, (ELEM_DEV, LANES), 1) % ELEM_DEV
    element = lax.broadcasted_iota(jnp.int32, (ELEM_DEV, LANES), 0)
    repeat = jnp.where(lane == element, 1.0, 0.0).astype(F32)
    shape = (PADDED, LANES)
    node = lax.broadcasted_iota(jnp.int32, shape, 0)
    block = lax.broadcasted_iota(jnp.int32, shape, 1) // ELEM_DEV
    keep = (node % 8 == block) & (node < NODES)
    for kind, ref in ((0, mass_ref), (1, inverse_ref)):
        for i in range(NODE):
            rows[i * NODE : (i + 1) * NODE, :ELEM_DEV] = ref[i]
        values = jnp.dot(
            rows[:PADDED, :ELEM_DEV], repeat, precision=HIGHEST, preferred_element_type=F32
        )
        values = jnp.where(keep, values, 0.0).reshape(GROUPS, 8, LANES)
        out_ref[kind, :GROUPS] = jnp.sum(values, axis=1)
        out_ref[kind, GROUPS:] = jnp.zeros((16 - GROUPS, LANES), F32)


def face_tables(faces, count):
    shape = (PADDED, ELEMENTS)
    node = lax.broadcasted_iota(jnp.int32, shape, 0)
    element = lax.broadcasted_iota(jnp.int32, shape, 1)
    inside = node < NODES
    upper = (node % NODE == NODE - 1) & (element < ELEMENTS - RADIAL) & inside
    lower = (node % NODE == 0) & (element >= RADIAL) & inside
    outer = (node // NODE == NODE - 1) & (element % RADIAL != RADIAL - 1) & inside
    inner = (node // NODE == 0) & (element % RADIAL != 0)
    marks = [jnp.where(mark, 1.0, 0.0).astype(F32) for mark in (upper, lower, outer, inner)]
    for at in range(4):
        faces[at] = marks[at]
    count[...] = marks[0] + marks[1] + marks[2] + marks[3]


def metric_tables(m_ref, mode_group, place, mass, diag, count, turn):
    inverse = diag.at[0]
    for kind, out in ((0, mass), (1, inverse)):
        for h in range(2):
            rows = exchange([m_ref[8 * h + at, kind] for at in range(8)])
            for at in range(8):
                for group in range(GROUPS):
                    turn[h, group, at : at + 1] = rows[at][group : group + 1]
            for group in range(GROUPS):
                out[group * 8 : (group + 1) * 8, h * LANES : (h + 1) * LANES] = turn[h, group, 0:8]
    values = inverse[...]
    for n in range(4):
        offset = lax.rem(place, 8) // 2 * 8 + lax.rem(place, 2) * 2 + n // 2 * 4 + n % 2
        number = mode_group * 64 + 2 * offset + place // 8
        fraction = number.astype(F32) / MODES
        diag[n] = mass[...] * (1.0 + AZIMUTH_WEIGHT * fraction * fraction * values) + count[...]


def owner_of(extra_group, place):
    return 2 * ((extra_group + place % 4 + place // 4) % 4)


PAIRS = (((0, 2), (4, 6), (8, 9), (10,)), ((1, 3), (5, 7)))


def load_tiles(b_ref, half, turn, weight, out, by_owner):
    rows = slice(4 * half, 4 * half + 4)

    def piece(group, place):
        if group < 8:
            return b_ref[0, group, place, rows]
        return b_ref[1, owner_of(group - 8, place) if by_owner else group - 8, place, rows]

    for at_pair, pair in enumerate(PAIRS[0] + PAIRS[1]):
        for h in range(2):
            tiles = []
            for place in range(8 * h, 8 * h + 8):
                tiles.append(
                    jnp.concatenate([piece(pair[0], place), piece(pair[-1], place)], axis=0)
                )
            tiles = exchange(tiles)
            for at in range(8):
                turn[h, at_pair, at * 8 : (at + 1) * 8] = tiles[at]
            lanes = slice(h * LANES, (h + 1) * LANES)
            for which, group in enumerate(pair):
                nodes = slice(group * 8, (group + 1) * 8)
                for s in range(4):
                    value = turn[h, at_pair, pl.ds(4 * which + s, 8, stride=8), :]
                    if weight is not None:
                        value = value * weight[nodes, lanes]
                    out[4 * half + s, nodes, lanes] = value


def store_tiles(value_of, half, turn, out_ref, emit):
    rows = slice(4 * half, 4 * half + 4)
    for core in range(2):
        for at_pair, pair in enumerate(PAIRS[core]):
            for h in range(2):
                lanes = slice(h * LANES, (h + 1) * LANES)
                for which, group in enumerate(pair):
                    for s in range(4):
                        turn[h, 4 * core + at_pair, pl.ds(4 * which + s, 8, stride=8), :] = value_of(
                            4 * half + s, slice(group * 8, (group + 1) * 8), lanes
                        )
                tiles = [turn[h, 4 * core + at_pair, at * 8 : (at + 1) * 8] for at in range(8)]
                tiles = exchange(tiles)
                for which, group in enumerate(pair):
                    for at in range(8):
                        place = 8 * h + at
                        owner = owner_of(group - 8, place) if group >= 8 else group
                        out_ref[group // 8, owner, place, rows] = tiles[at][
                            4 * which : 4 * which + 4
                        ]
        emit(core, half)


def total(parts):
    half = parts[:, :LANES] + parts[:, LANES:]
    return jnp.broadcast_to(jnp.sum(half, axis=(0, 1), keepdims=True), (1, ELEMENTS))


def fold(value):
    return jnp.sum(value.reshape(GROUPS, 8, ELEMENTS), axis=0)


def solve(b_ref, out_ref, half, weigh_in, weigh_out, by_owner, scratch, emit):
    mass, diag, faces, k_ref, r, p, q, alphas, turn = scratch
    load_tiles(b_ref, half, turn, mass if weigh_in else None, p.at[0], by_owner)
    modes = (2 * half, 2 * half + 1)
    empty = jnp.zeros((8, ELEMENTS), F32)

    def add(whole, part):
        part = fold(part)
        return part if whole is None else whole + part

    def operate(sweep, n, alpha, beta):
        last = sweep == ITERS - 1
        norm = curve = bend = None
        for s in (4 * half + n % 2, 4 * half + 2 + n % 2):
            if sweep == 0:
                rest = now = p[0, s]
            else:
                before = p[sweep - 1, s]
                rest = (before if sweep == 1 else r[s]) - alpha * q[s]
                now = rest + beta * before
                p[sweep, s] = now
                if not last:
                    r[s] = rest
            norm = add(norm, rest * rest)
            high = now.astype(BF16).astype(F32)
            halves = jnp.concatenate([high, now - high], axis=0).astype(BF16)
            image = jnp.dot(k_ref[...], halves, preferred_element_type=F32)
            ahead = pltpu.roll(now[: PADDED - 8], ELEMENTS - RADIAL, 1)
            behind = pltpu.roll(now[8:], RADIAL, 1)
            image = (
                image[:PADDED]
                + image[PADDED:]
                + diag[n] * now
                - faces[0] * jnp.concatenate([empty, ahead], axis=0)
                - faces[1] * jnp.concatenate([behind, empty], axis=0)
            )
            outward = pltpu.roll(now[:16], ELEMENTS - 1, 1)
            inward = pltpu.roll(now[72:], 1, 1)
            image = jnp.concatenate(
                [
                    image[:16] - faces[3, :16] * inward,
                    image[16:72],
                    image[72:] - faces[2, 72:] * outward,
                ],
                axis=0,
            )
            curve = add(curve, now * image)
            if not last:
                q[s] = image
                bend = add(bend, image * image)
        curve = total(curve)
        alpha = total(norm) / curve
        alphas[sweep * 4 + n] = alpha
        if last:
            return alpha, None
        return alpha, jnp.maximum(alpha * (total(bend) / curve) - 1.0, 0.0)

    steps = [(None, None)] * 2
    for sweep in range(ITERS):
        steps = [operate(sweep, n, *steps[n % 2]) for n in modes]

    def value_of(s, rows, lanes):
        n = s // 4 * 2 + s % 2
        value = alphas[n, :, lanes] * p[0, s, rows, lanes]
        for sweep in range(1, ITERS):
            value = value + alphas[sweep * 4 + n, :, lanes] * p[sweep, s, rows, lanes]
        return value * mass[rows, lanes] if weigh_out else value

    store_tiles(value_of, half, turn, out_ref, emit)


FIELD = pltpu.VMEM((8, PADDED, ELEMENTS), F32)
SOLVE_SCRATCH = [
    pltpu.VMEM((PADDED, ELEMENTS), F32),
    pltpu.VMEM((4, PADDED, ELEMENTS), F32),
    pltpu.VMEM((4, PADDED, ELEMENTS), F32),
    pltpu.VMEM((2 * PADDED, 2 * PADDED), BF16),
    FIELD,
    pltpu.VMEM((ITERS, 8, PADDED, ELEMENTS), F32),
    FIELD,
    pltpu.VMEM((ITERS * 4, 1, ELEMENTS), F32),
    pltpu.VMEM((2, GROUPS, 64, LANES), F32),
]


def split(value):
    high = value.astype(BF16)
    return high, (value - high.astype(F32)).astype(BF16)


def apply(t_ref, which, field):
    high, low = split(field)
    width = field.shape[1]
    if width == LANES:
        both = jnp.concatenate([high, low], axis=1)
        out = jnp.dot(t_ref[which], both, preferred_element_type=F32)
        return out[:HALF, :LANES] + out[:HALF, LANES:] + out[HALF:, :LANES]
    out = jnp.dot(t_ref[which], high, preferred_element_type=F32)
    out = out[:HALF] + out[HALF:]
    return out + jnp.dot(t_ref[which, :HALF], low, preferred_element_type=F32)


def parts_of(u_ref):
    out = []
    for odd in range(2):
        tiles = u_ref[odd].reshape(32, 2, 8, LANES)
        one, two = mix(tiles[:, 0], tiles[:, 1])
        out.append((one.reshape(HALF, LANES), two.reshape(HALF, LANES)))
    return out


def parts_to(out_ref, parts):
    for odd in range(2):
        real, imag = parts[odd]
        one, two = mix(real.reshape(32, 8, LANES), imag.reshape(32, 8, LANES))
        out_ref[odd] = jnp.stack([one, two], axis=1).reshape(64, 8, LANES)


def column_tables(c_ref):
    row = lax.broadcasted_iota(jnp.int32, (HALF, LANES), 0)
    for odd in range(2):
        mode = 2 * ((row // 32 % 4 * 2 + row // 128) * 32 + row % 32) + odd
        c_ref[odd] = mode.astype(F32) / MODES
        c_ref[2 + odd] = jnp.where(mode == 0, 1.0 / PLANES, 2.0 / PLANES).astype(F32)
    c_ref[4] = jnp.where(row % 2 == 0, 1.0, -1.0).astype(F32)


def signs(c_ref, width):
    return jnp.concatenate([c_ref[4]] * (width // LANES), axis=1)


def without_first(value):
    head = lax.broadcasted_iota(jnp.int32, (8, value.shape[1]), 0) == 0
    return jnp.concatenate([jnp.where(head, 0.0, value[:8]), value[8:]], axis=0)


def to_planes(t_ref, c_ref, cos_fields, sin_fields, out_ref):
    sign = signs(c_ref, cos_fields[0].shape[1])
    cos_even, cos_odd = apply(t_ref, 0, cos_fields[0]), apply(t_ref, 1, cos_fields[1])
    sin_even, sin_odd = apply(t_ref, 2, sin_fields[0]), apply(t_ref, 3, sin_fields[1])
    quarter_cos = jnp.sum(sign * cos_fields[0], axis=0, keepdims=True)
    quarter_sin = jnp.sum(sign * sin_fields[1], axis=0, keepdims=True)
    cos, sin = cos_even + cos_odd, sin_even + sin_odd
    out_ref[0] = cos - sin
    out_ref[1] = cos + sin
    cos, sin = cos_even - cos_odd, sin_even - sin_odd
    out_ref[2] = cos + sin
    out_ref[3] = cos - sin
    out_ref[1, 0:1] = quarter_cos - quarter_sin
    out_ref[3, 0:1] = quarter_cos + quarter_sin


def from_planes(t_ref, c_ref, values):
    sign = signs(c_ref, values[0].shape[1])
    quarter, three = values[1][0:1], values[3][0:1]
    one = values[0]
    two, four = without_first(values[1]), without_first(values[3])
    plus, minus = one + two, one - two
    plus_far, minus_far = values[2] + four, values[2] - four
    a_even = apply(t_ref, 4, plus + plus_far) + sign * (quarter + three)
    a_odd = apply(t_ref, 5, plus - plus_far)
    b_even = -apply(t_ref, 6, minus - minus_far)
    b_odd = -apply(t_ref, 7, minus + minus_far) - sign * (quarter - three)
    return (a_even, b_even), (a_odd, b_odd)


def state_planes(parts, t_ref, c_ref, out_ref):
    cos_fields, sin_fields = [], []
    for odd in range(2):
        real, imag = parts[odd]
        fraction = c_ref[odd]
        cos_fields.append(jnp.concatenate([real, -fraction * imag], axis=1))
        sin_fields.append(jnp.concatenate([imag, fraction * real], axis=1))
    to_planes(t_ref, c_ref, cos_fields, sin_fields, out_ref)


def first_stage(u_ref, t_ref, c_ref, planes, out_ref):
    parts = parts_of(u_ref)
    state_planes(parts, t_ref, c_ref, planes)
    values = [planes[at, :, :LANES] * planes[at, :, LANES:] for at in range(4)]
    found = from_planes(t_ref, c_ref, values)
    out = []
    for odd in range(2):
        weight = c_ref[2 + odd]
        out.append(tuple(parts[odd][c] - weight * found[odd][c] for c in range(2)))
    parts_to(out_ref, out)


def adjoint_planes(s_ref, t_ref, c_ref, out_ref):
    parts = parts_of(s_ref)
    weights = [c_ref[2 + odd] for odd in range(2)]
    to_planes(
        t_ref,
        c_ref,
        [weights[odd] * parts[odd][0] for odd in range(2)],
        [weights[odd] * parts[odd][1] for odd in range(2)],
        out_ref,
    )


def finish(t_ref, c_ref, s_ref, planes, adjoint, out_ref):
    values = []
    for at in range(4):
        factor = adjoint[at]
        values.append(planes[at] * jnp.concatenate([factor, factor], axis=1))
    found = from_planes(t_ref, c_ref, values)
    parts = parts_of(s_ref)
    out = []
    for odd in range(2):
        fraction = c_ref[odd]
        a, b = found[odd]
        out.append(
            (
                parts[odd][0] - a[:, LANES:] - fraction * b[:, :LANES],
                parts[odd][1] - b[:, LANES:] + fraction * a[:, :LANES],
            )
        )
    parts_to(out_ref, out)


COUNT = N_MODE * N_MER
SPARE = GROUPS - 8


def send(source, target, mode, mer, sems, at):
    pltpu.make_async_remote_copy(
        src_ref=source,
        dst_ref=target,
        send_sem=sems[0].at[at],
        recv_sem=sems[1].at[at],
        device_id={"mode": mode, "mer": mer},
        device_id_type=pl.DeviceIdType.MESH,
    ).start()


def wait(blank, tiles, sem, rows=8):
    whole = blank.at[pl.ds(0, tiles), pl.ds(0, rows)]
    pltpu.make_async_copy(whole, whole, sem).wait()


def wait_either(double, blank, tiles_double, tiles_single, sem, rows=8):
    @pl.when(double)
    def _():
        wait(blank, tiles_double, sem, rows)

    @pl.when(jnp.logical_not(double))
    def _():
        wait(blank, tiles_single, sem, rows)


def place_at(mer, k):
    step = lax.rem(7 * k, N_MER)
    y = lax.rem(lax.rem(mer, 4) + lax.rem(step, 4), 4)
    z = lax.rem(mer // 4 + step // 4, 4)
    return z * 4 + y


def extra(x, mer):
    turn = lax.rem(lax.rem(mer, 4) + mer // 4, 4)
    return lax.rem(x + 4 - turn, 4)


def groups_on(mode, core):
    x = mode // 2
    return [2 * lax.rem(x + step, 4) + core for step in (1, 3, 2, 0)]


def each_group(mode, cores, act):
    for core in cores:
        one, two, three, own = groups_on(mode, core)
        act(one, core)
        act(two, core)
        act(three, core)

        @pl.when(lax.rem(mode, 2) != core)
        def _(own=own, core=core):
            act(own, core)


def each_place(mer, act):
    def body(k, _):
        act(place_at(mer, k))
        return 0

    lax.fori_loop(1, N_MER, body, 0)


def each_other(mode, mer, cores, act):
    groups = [(other, core) for core in cores for other in groups_on(mode, core)]

    def body(place):
        for other, core in groups:
            act(other, core, place)

    each_place(mer, body)
    each_group(mode, cores, lambda other, core: act(other, core, mer))


def order_of(mode):
    return lax.rem(mode, 2) * 4 + mode // 2


def program_kernel(
    state_ref,
    cotangent_hbm,
    mass_ref,
    inverse_ref,
    d_ref,
    t_hbm,
    out_hbm,
    cotangent_in,
    t_ref,
    copy_sems,
    rows,
    native_out,
    native_in,
    mode_out,
    mode_in,
    plane_out,
    plane_in,
    metric_out,
    metric_in,
    u_planes,
    planes,
    s_planes,
    c_ref,
    count,
    ready,
    blank,
    send_sems,
    recv_sems,
    *solve_scratch,
):
    mode = lax.axis_index("mode")
    mer = lax.axis_index("mer")
    odd, eighth = mer // 8, lax.rem(mer, 8)
    row = order_of(mode) * 8 + eighth
    mine_extra = extra(mode // 2, mer)
    double = (lax.rem(mode, 2) == 0) & (mine_extra < SPARE)
    slots = jnp.where(double, 2, 1)
    sems = (send_sems, recv_sems)
    mass, diag, faces, k_ref = solve_scratch[:4]
    turn = solve_scratch[8]
    sent = []

    cotangent_copy = pltpu.make_async_copy(cotangent_hbm, cotangent_in, copy_sems.at[0])
    table_copy = pltpu.make_async_copy(t_hbm, t_ref, copy_sems.at[1])
    cotangent_copy.start()
    table_copy.start()
    barrier = pltpu.get_barrier_semaphore()

    def greet(semaphore, other, place):
        pl.semaphore_signal(
            semaphore,
            inc=1,
            device_id={"mode": other, "mer": place},
            device_id_type=pl.DeviceIdType.MESH,
        )

    each_group(mode, (0, 1), lambda other, core: greet(barrier, other, mer))
    each_place(mer, lambda place: greet(barrier, mode, place))
    native_to_tiles(state_ref, native_out.at[0], rows, turn)
    pl.semaphore_wait(barrier, N_MODE - 1 + N_MER - 1)
    each_group(mode, (0, 1), lambda other, core: greet(ready, other, mer))

    def each_slot(act):
        def body(k, _):
            act(slots - 1 - k)
            return 0

        lax.fori_loop(0, slots, body, 0)

    def send_to_planes(source, target, at):
        def emit(core, half):
            rows = pl.ds(4 * half, 4)

            def act(other, core, place):
                def single():
                    send(
                        source.at[0, other, place, rows],
                        target.at[0, odd, row, rows],
                        other,
                        place,
                        sems,
                        at + half,
                    )

                if core == 1:
                    single()
                    return
                owns_two = extra(other // 2, place) < SPARE
                pl.when(jnp.logical_not(owns_two))(single)

                @pl.when(owns_two)
                def _():
                    send(
                        source.at[:, other, place, rows],
                        target.at[:, odd, row, rows],
                        other,
                        place,
                        sems,
                        at + half,
                    )

            each_other(mode, mer, (core,), act)
            if core == 1:
                target[:, odd, row, 4 * half : 4 * half + 4] = source[
                    :, mode, mer, 4 * half : 4 * half + 4
                ]

        for half in range(2):
            sent.append((at + half, 16 * GROUPS - 2, 16 * GROUPS - 1, 4))
        return emit

    def wait_planes(at):
        for half in range(2):
            wait_either(double, blank, 2 * (COUNT - 1), COUNT - 1, recv_sems.at[at + half], 4)

    def send_to_modes(source, target, at):
        target[0, mode, mer] = source[0, odd, row]

        @pl.when(double)
        def _():
            target[1, mode, mer] = source[1, odd, row]

        for half in range(2):
            rows = pl.ds(4 * half, 4)

            def act(other, core, place, rows=rows, half=half):
                index = order_of(other) * 8 + lax.rem(place, 8)
                piece = source.at[0, place // 8, index, rows]
                send(piece, target.at[0, mode, mer, rows], other, place, sems, at + half)

            def act_double(other, core, place, rows=rows, half=half):
                index = order_of(other) * 8 + lax.rem(place, 8)
                piece = source.at[:, place // 8, index, rows]
                send(piece, target.at[:, mode, mer, rows], other, place, sems, at + half)

            @pl.when(double)
            def _(act_double=act_double):
                each_other(mode, mer, (0, 1), act_double)

            @pl.when(jnp.logical_not(double))
            def _(act=act):
                each_other(mode, mer, (0, 1), act)

            sent.append((at + half, 2 * (COUNT - 1), COUNT - 1, 4))

    def wait_modes(at, half):
        wait_either(
            double, blank, 16 * GROUPS - 2, 16 * GROUPS - 1, recv_sems.at[at + half], 4
        )

    mine = pl.ds(pl.multiple_of(order_of(mode) * 8, 8), 8)
    plane_in[0, 0, :, mine] = native_out[0, 0, mode]
    plane_in[0, 1, :, mine] = native_out[0, 1, mine_extra]

    def send_extra_state(other, core):
        index = extra(other // 2, mer)

        @pl.when(index < SPARE)
        def _():
            send(native_out.at[0, 1, index], plane_in.at[0, 1, :, mine], other, mer, sems, 0)

    def send_state(other, core):
        send(native_out.at[0, 0, other], plane_in.at[0, 0, :, mine], other, mer, sems, 0)

    each_group(mode, (0,), send_extra_state)
    each_group(mode, (0, 1), send_state)
    sent.append((0, N_MER * (GROUPS - 2), N_MER * (GROUPS - 1), 8))

    cotangent_copy.wait()
    native_to_tiles(cotangent_in, native_out.at[1], rows, turn)
    mode_in[0, 0, :, mer] = native_out[1, 0, :, odd, eighth]
    mode_in[0, 1, 0:SPARE, mer] = native_out[1, 1, 0:SPARE, odd, eighth]
    metric_rows(mass_ref, inverse_ref, rows, metric_out)
    metric_in[mer] = metric_out[...]

    def send_cotangent(place):
        which, at = place // 8, lax.rem(place, 8)
        send(native_out.at[1, 0, :, which, at], mode_in.at[0, 0, :, mer], mode, place, sems, 2)
        send(
            native_out.at[1, 1, 0:SPARE, which, at],
            mode_in.at[0, 1, 0:SPARE, mer],
            mode,
            place,
            sems,
            2,
        )
        send(metric_out, metric_in.at[mer], mode, place, sems, 3)

    each_place(mer, send_cotangent)
    sent.append((2, (N_MER - 1) * GROUPS, (N_MER - 1) * GROUPS, 8))
    sent.append((3, (N_MER - 1) * 4, (N_MER - 1) * 4, 8))

    stiffness_tables(d_ref, k_ref)
    column_tables(c_ref)
    face_tables(faces, count)
    wait(blank, (N_MER - 1) * 4, recv_sems.at[3])
    metric_tables(metric_in, mode, mer, mass, diag, count, turn)
    table_copy.wait()

    wait_either(double, blank, 2 * (N_MODE - 1) * N_MER, (N_MODE - 1) * N_MER, recv_sems.at[0])

    def first(slot):
        first_stage(plane_in.at[0, slot], t_ref, c_ref, u_planes.at[slot], plane_out.at[0, slot])

    each_slot(first)
    pl.semaphore_wait(ready, N_MODE - 1)
    send_to_modes(plane_out.at[0], mode_in.at[1], 4)

    wait(blank, (N_MER - 1) * GROUPS, recv_sems.at[2])
    emit = send_to_planes(mode_out.at[0], plane_in.at[1], 6)
    for half in range(2):
        solve(mode_in.at[0], mode_out.at[0], half, False, True, False, solve_scratch, emit)

    emit = send_to_planes(mode_out.at[1], plane_in.at[2], 8)
    for half in range(2):
        wait_modes(4, half)
        solve(mode_in.at[1], mode_out.at[1], half, True, False, True, solve_scratch, emit)

    def multiplier(slot):
        adjoint_planes(plane_in.at[1, slot], t_ref, c_ref, s_planes.at[slot])

    wait_planes(6)
    each_slot(multiplier)

    def second(slot):
        state_planes(parts_of(plane_in.at[2, slot]), t_ref, c_ref, planes)
        finish(t_ref, c_ref, plane_in.at[1, slot], planes, s_planes.at[slot], plane_out.at[1, slot])

    wait_planes(8)
    each_slot(second)
    send_to_modes(plane_out.at[1], mode_in.at[2], 10)

    emit = send_to_planes(mode_out.at[2], plane_in.at[3], 12)
    for half in range(2):
        wait_modes(10, half)
        solve(mode_in.at[2], mode_out.at[2], half, False, True, True, solve_scratch, emit)

    def third(slot):
        s_in = plane_in.at[3, slot]
        adjoint_planes(s_in, t_ref, c_ref, s_planes.at[slot])
        finish(
            t_ref, c_ref, s_in, u_planes.at[slot], s_planes.at[slot], plane_out.at[2, slot]
        )
        native_in[slot, mode] = plane_out[2, slot, :, mine]

        def send_gradient(other, core):
            theirs = pl.ds(pl.multiple_of(order_of(other) * 8, 8), 8)
            send(plane_out.at[2, slot, :, theirs], native_in.at[slot, mode], other, mer, sems, 14)

        each_group(mode, (0, 1), send_gradient)

    wait_planes(12)
    each_slot(third)
    sent.append((14, 2 * (N_MODE - 1) * N_MER, (N_MODE - 1) * N_MER, 8))
    wait_either(double, blank, N_MER * (GROUPS - 2), N_MER * (GROUPS - 1), recv_sems.at[14])
    turned = lax.rem(lax.rem(mer, 4) + mer // 4, 4)
    copies = [pltpu.make_async_copy(native_in.at[0], out_hbm.at[0:N_MODE], copy_sems.at[2])]
    for index in range(SPARE):
        owner = 2 * lax.rem(index + turned, 4)
        copies.append(
            pltpu.make_async_copy(
                native_in.at[1, owner], out_hbm.at[N_MODE + index], copy_sems.at[3 + index]
            )
        )
    for copy in copies:
        copy.start()
    for at, tiles_double, tiles_single, rows_each in sent:
        wait_either(double, blank, tiles_double, tiles_single, send_sems.at[at], rows_each)
    for copy in copies:
        copy.wait()


def program(state, cotangent, mass, inverse, derivative, table):
    by_mode = (2, N_MODE, N_MER, 8, LANES)
    by_native = (2, N_MODE, 2, 8, 8, LANES)
    by_plane = (2, 2, COUNT // 2, 8, LANES)
    vmem = pl.BlockSpec(memory_space=pltpu.VMEM)
    hbm = pl.BlockSpec(memory_space=pl.ANY)

    def scratch(count, shape):
        return pltpu.VMEM((count,) + shape, F32)

    return pl.pallas_call(
        program_kernel,
        out_shape=jax.ShapeDtypeStruct((GROUPS, 2, 8, 8, LANES), F32),
        in_specs=[vmem, hbm, vmem, vmem, vmem, hbm],
        out_specs=hbm,
        scratch_shapes=[
            pltpu.VMEM((NODE, NODE, ELEM_DEV * LANES), F32),
            pltpu.VMEM((8, 2 * HALF, HALF), BF16),
            pltpu.SemaphoreType.DMA((6,)),
            pltpu.VMEM((PADDED * ELEM_DEV, LANES), F32),
            scratch(2, by_native),
            pltpu.VMEM(by_native, F32),
            scratch(3, by_mode),
            scratch(3, by_mode),
            scratch(3, by_plane),
            scratch(4, by_plane),
            pltpu.VMEM((2, 16, LANES), F32),
            scratch(N_MER, (2, 16, LANES)),
            scratch(2, (4, HALF, 2 * LANES)),
            scratch(4, (HALF, 2 * LANES)),
            scratch(2, (4, HALF, LANES)),
            scratch(5, (HALF, LANES)),
            pltpu.VMEM((PADDED, ELEMENTS), F32),
            pltpu.SemaphoreType.REGULAR,
            pltpu.VMEM((2 * COUNT, 8, LANES), F32),
            pltpu.SemaphoreType.DMA((15,)),
            pltpu.SemaphoreType.DMA((15,)),
            *SOLVE_SCRATCH,
        ],
        compiler_params=pltpu.CompilerParams(
            collective_id=0, has_side_effects=True, vmem_limit_bytes=60 << 20
        ),
        name="program",
    )(state, cotangent, mass, inverse, derivative, table)


def shards(cotangent, checkpoint, mass, inv_radius_sq, derivative):
    table = jnp.asarray(tables())
    return tiles_to_native(program(checkpoint, cotangent, mass, inv_radius_sq, derivative, table))


def solution(mesh):
    return jax.shard_map(
        shards,
        mesh=mesh,
        in_specs=(
            P(None, None, ("mer", "mode")),
            P(None, None, ("mer", "mode")),
            P(None, None, "mer"),
            P(None, None, "mer"),
            P(),
        ),
        out_specs=P(None, None, ("mer", "mode")),
        check_vma=False,
    )
```

```python
import functools
import math

import jax
import jax.numpy as jnp
import ml_dtypes
import numpy as np
from jax import lax
from jax.experimental import pallas as pl
from jax.experimental.pallas import tpu as pltpu
from jax.sharding import PartitionSpec as P

NODE = 9
NODES = NODE * NODE
RADIAL = 8
ITERS = 4
MODES = 512
HALF = 256
PLANES = 1024
ELEMENTS = 256
N_MODE = 8
N_MER = 16
ELEM_DEV = 16
GROUPS = 11
PADDED = GROUPS * 8
LANES = 128
AZIMUTH_WEIGHT = 4.0
HIGHEST = lax.Precision.HIGHEST
F32 = jnp.float32
BF16 = jnp.bfloat16


def tables():
    order = np.arange(HALF).reshape(4, 2, HALF // N_MODE).transpose(1, 0, 2).reshape(-1)
    out = []
    for wave in (np.cos, np.sin):
        for odd in range(2):
            index = np.outer(np.arange(HALF), 2 * order + odd) % PLANES
            values = wave(index.astype(np.float64) * (2.0 * math.pi / PLANES)).astype(np.float32)
            high = values.astype(ml_dtypes.bfloat16)
            low = (values - high.astype(np.float32)).astype(ml_dtypes.bfloat16)
            out.append((high, low))
    both = [np.concatenate(pair) for pair in out]
    turned = [np.concatenate([high.T, low.T]) for high, low in out]
    return np.stack(both + turned)


def mix(first, second):
    shape = first.shape
    axis = len(shape) - 2
    low = lax.broadcasted_iota(jnp.int32, shape, axis) % 4 < 2
    return (
        jnp.where(low, first, pltpu.roll(second, 2, axis)),
        jnp.where(low, pltpu.roll(first, 6, axis), second),
    )


def exchange(tiles):
    tiles = list(tiles)
    axis = tiles[0].ndim - 1
    block = lax.broadcasted_iota(jnp.int32, tiles[0].shape, axis) // 16
    for bit in (1, 2, 4):
        clear = (block & bit) == 0
        for at in range(8):
            if at & bit:
                continue
            one, two = tiles[at], tiles[at | bit]
            tiles[at] = jnp.where(clear, one, pltpu.roll(two, 16 * bit, axis))
            tiles[at | bit] = jnp.where(clear, pltpu.roll(one, LANES - 16 * bit, axis), two)
    return tiles


def native_to_tiles(x_ref, out_ref, rows, turn):
    rows[pl.ds(NODES * ELEM_DEV, PADDED * ELEM_DEV - NODES * ELEM_DEV), :] = jnp.zeros(
        ((PADDED - NODES) * ELEM_DEV, LANES), F32
    )
    for i in range(NODE):
        for e in range(ELEM_DEV):
            rows[pl.ds(i * NODE * ELEM_DEV + e, NODE, stride=ELEM_DEV), :] = x_ref[
                i, :, e * LANES : (e + 1) * LANES
            ]
    for group in range(GROUPS):
        turned = rows[group * LANES : (group + 1) * LANES, :].T
        turn[0, group] = turned[:64]
        turn[1, group] = turned[64:]
        for odd in range(2):
            real = turn[0, group, pl.ds(odd, 32, stride=2), :].reshape(4, 8, LANES)
            imag = turn[1, group, pl.ds(odd, 32, stride=2), :].reshape(4, 8, LANES)
            one, two = mix(real, imag)
            out_ref[group // 8, group % 8, odd] = jnp.stack([one, two], axis=1).reshape(8, 8, LANES)


def tiles_to_native_kernel(t_hbm, out_hbm, tiles_in, rows, turn, native, in_sems, out_sems):
    parts = ((0, 6, 0, 5), (6, GROUPS, 5, NODE))
    loads, stores = [], []
    for at, (start, stop, first, last) in enumerate(parts):
        groups, nodes = pl.ds(start, stop - start), pl.ds(first, last - first)
        loads.append(
            pltpu.make_async_copy(t_hbm.at[groups], tiles_in.at[groups], in_sems.at[at])
        )
        stores.append(pltpu.make_async_copy(native.at[nodes], out_hbm.at[nodes], out_sems.at[at]))
        loads[at].start()
    for at, (start, stop, first, last) in enumerate(parts):
        loads[at].wait()
        for group in range(start, stop):
            for odd in range(2):
                tiles = tiles_in[group, odd].reshape(4, 2, 8, LANES)
                real, imag = mix(tiles[:, 0], tiles[:, 1])
                turn[0, group, pl.ds(odd, 32, stride=2), :] = real.reshape(32, LANES)
                turn[1, group, pl.ds(odd, 32, stride=2), :] = imag.reshape(32, LANES)
            both = jnp.concatenate([turn[0, group], turn[1, group]], axis=0)
            rows[group * LANES : (group + 1) * LANES, :] = both.T
        for i in range(first, last):
            for e in range(ELEM_DEV):
                native[i, :, e * LANES : (e + 1) * LANES] = rows[
                    pl.ds(i * NODE * ELEM_DEV + e, NODE, stride=ELEM_DEV), :
                ]
        stores[at].start()
    for store in stores:
        store.wait()


def tiles_to_native(tiles):
    hbm = pl.BlockSpec(memory_space=pltpu.HBM)
    shape = (NODE, NODE, ELEM_DEV * LANES)
    return pl.pallas_call(
        tiles_to_native_kernel,
        out_shape=jax.ShapeDtypeStruct(shape, F32),
        in_specs=[hbm],
        out_specs=hbm,
        scratch_shapes=[
            pltpu.VMEM((GROUPS, 2, 8, 8, LANES), F32),
            pltpu.VMEM((PADDED * ELEM_DEV, LANES), F32),
            pltpu.VMEM((2, GROUPS, 64, LANES), F32),
            pltpu.VMEM(shape, F32),
            pltpu.SemaphoreType.DMA((2,)),
            pltpu.SemaphoreType.DMA((2,)),
        ],
        compiler_params=pltpu.CompilerParams(vmem_limit_bytes=62 << 20),
        name="tiles_to_native",
    )(tiles)


def stiffness_tables(d_ref, k_ref):
    def dot(a, b):
        return jnp.dot(a, b, precision=HIGHEST, preferred_element_type=F32)

    derivative = d_ref[...]
    stiffness = lax.dot_general(
        derivative, derivative, (((0,), (0,)), ((), ())), precision=HIGHEST, preferred_element_type=F32
    )

    def pick(shape, node_axis, outer):
        node = lax.broadcasted_iota(jnp.int32, shape, node_axis)
        other = lax.broadcasted_iota(jnp.int32, shape, 1 - node_axis)
        place = node // NODE if outer else node % NODE
        return jnp.where((place == other) & (node < NODES), 1.0, 0.0).astype(F32)

    outer, inner = pick((PADDED, NODE), 0, True), pick((PADDED, NODE), 0, False)
    outer_t, inner_t = pick((NODE, PADDED), 1, True), pick((NODE, PADDED), 1, False)
    whole = dot(dot(outer, stiffness), outer_t) * dot(inner, inner_t)
    whole = whole + dot(dot(inner, stiffness), inner_t) * dot(outer, outer_t)
    high = whole.astype(BF16).astype(F32)
    low = whole - high
    top = jnp.concatenate([high, high], axis=1)
    bottom = jnp.concatenate([low, jnp.zeros_like(low)], axis=1)
    k_ref[...] = jnp.concatenate([top, bottom], axis=0).astype(BF16)


def metric_rows(mass_ref, inverse_ref, rows, out_ref):
    lane = lax.broadcasted_iota(jnp.int32, (ELEM_DEV, LANES), 1) % ELEM_DEV
    element = lax.broadcasted_iota(jnp.int32, (ELEM_DEV, LANES), 0)
    repeat = jnp.where(lane == element, 1.0, 0.0).astype(F32)
    shape = (PADDED, LANES)
    node = lax.broadcasted_iota(jnp.int32, shape, 0)
    block = lax.broadcasted_iota(jnp.int32, shape, 1) // ELEM_DEV
    keep = (node % 8 == block) & (node < NODES)
    for kind, ref in ((0, mass_ref), (1, inverse_ref)):
        for i in range(NODE):
            rows[i * NODE : (i + 1) * NODE, :ELEM_DEV] = ref[i]
        values = jnp.dot(
            rows[:PADDED, :ELEM_DEV], repeat, precision=HIGHEST, preferred_element_type=F32
        )
        values = jnp.where(keep, values, 0.0).reshape(GROUPS, 8, LANES)
        out_ref[kind, :GROUPS] = jnp.sum(values, axis=1)
        out_ref[kind, GROUPS:] = jnp.zeros((16 - GROUPS, LANES), F32)


def face_tables(faces, count):
    shape = (PADDED, ELEMENTS)
    node = lax.broadcasted_iota(jnp.int32, shape, 0)
    element = lax.broadcasted_iota(jnp.int32, shape, 1)
    inside = node < NODES
    upper = (node % NODE == NODE - 1) & (element < ELEMENTS - RADIAL) & inside
    lower = (node % NODE == 0) & (element >= RADIAL) & inside
    outer = (node // NODE == NODE - 1) & (element % RADIAL != RADIAL - 1) & inside
    inner = (node // NODE == 0) & (element % RADIAL != 0)
    marks = [jnp.where(mark, 1.0, 0.0).astype(F32) for mark in (upper, lower, outer, inner)]
    for at in range(4):
        faces[at] = marks[at]
    count[...] = marks[0] + marks[1] + marks[2] + marks[3]


def metric_tables(m_ref, mode_group, place, mass, diag, count, turn):
    inverse = diag.at[0]
    for kind, out in ((0, mass), (1, inverse)):
        for h in range(2):
            rows = exchange([m_ref[8 * h + at, kind] for at in range(8)])
            for at in range(8):
                for group in range(GROUPS):
                    turn[h, group, at : at + 1] = rows[at][group : group + 1]
            for group in range(GROUPS):
                out[group * 8 : (group + 1) * 8, h * LANES : (h + 1) * LANES] = turn[h, group, 0:8]
    values = inverse[...]
    for n in range(4):
        offset = lax.rem(place, 8) // 2 * 8 + lax.rem(place, 2) * 2 + n // 2 * 4 + n % 2
        number = mode_group * 64 + 2 * offset + place // 8
        fraction = number.astype(F32) / MODES
        diag[n] = mass[...] * (1.0 + AZIMUTH_WEIGHT * fraction * fraction * values) + count[...]


def owner_of(extra_group, place):
    return 2 * ((extra_group + place % 4 + place // 4) % 4)


CHUNKS = ((0, 0, 3), (0, 3, 6), (0, 6, 8), (1, 0, 3))


def load_tiles(b_ref, turn, weight, out, by_owner):
    for slot, start, stop in CHUNKS:
        for h in range(2):
            tiles = []
            for place in range(8 * h, 8 * h + 8):
                if slot and by_owner:
                    tiles.append(
                        jnp.stack([b_ref[1, owner_of(at, place), place] for at in range(start, stop)])
                    )
                else:
                    tiles.append(b_ref[slot, start:stop, place])
            tiles = exchange(tiles)
            for at in range(8):
                turn[h, 8 * slot + start : 8 * slot + stop, at * 8 : (at + 1) * 8] = tiles[at]
    for s in range(8):
        for h in range(2):
            lanes = slice(h * LANES, (h + 1) * LANES)
            for group in range(GROUPS):
                rows = slice(group * 8, (group + 1) * 8)
                value = turn[h, group, pl.ds(s, 8, stride=8), :]
                if weight is not None:
                    value = value * weight[rows, lanes]
                out[s, rows, lanes] = value


OWNED = (
    ((1, 0), (1, 1), (1, 2), (0, 0), (0, 2), (0, 4), (0, 6)),
    ((0, 1), (0, 3), (0, 5), (0, 7)),
)


def store_tiles(value_of, turn, out_ref, emit):
    for core in range(2):
        for s in range(8):
            for slot, at_group in OWNED[core]:
                group = 8 * slot + at_group
                for h in range(2):
                    turn[h, group, pl.ds(s, 8, stride=8), :] = value_of(
                        s, slice(group * 8, (group + 1) * 8), slice(h * LANES, (h + 1) * LANES)
                    )
        for slot, at_group in OWNED[core]:
            for h in range(2):
                group = 8 * slot + at_group
                tiles = exchange([turn[h, group, at * 8 : (at + 1) * 8] for at in range(8)])
                for at in range(8):
                    place = 8 * h + at
                    owner = owner_of(at_group, place) if slot else at_group
                    out_ref[slot, owner, place] = tiles[at]
        emit(core)


def total(parts):
    half = parts[:, :LANES] + parts[:, LANES:]
    return jnp.broadcast_to(jnp.sum(half, axis=(0, 1), keepdims=True), (1, ELEMENTS))


def fold(value):
    return jnp.sum(value.reshape(GROUPS, 8, ELEMENTS), axis=0)


def solve(b_ref, out_ref, weigh_in, weigh_out, by_owner, scratch, emit):
    mass, diag, faces, k_ref, r, p, q, alphas, turn = scratch
    load_tiles(b_ref, turn, mass if weigh_in else None, r, by_owner)
    empty = jnp.zeros((8, ELEMENTS), F32)

    def add(whole, part):
        part = fold(part)
        return part if whole is None else whole + part

    def operate(sweep, n, alpha, beta):
        norm = curve = bend = None
        for s in (n // 2 * 4 + n % 2, n // 2 * 4 + 2 + n % 2):
            rest = r[s] - alpha * q[s]
            now = rest + beta * p[lax.rem(sweep + ITERS - 1, ITERS), s]
            r[s] = rest
            p[sweep, s] = now
            norm = add(norm, rest * rest)
            high = now.astype(BF16).astype(F32)
            halves = jnp.concatenate([high, now - high], axis=0).astype(BF16)
            image = jnp.dot(k_ref[...], halves, preferred_element_type=F32)
            ahead = pltpu.roll(now[: PADDED - 8], ELEMENTS - RADIAL, 1)
            behind = pltpu.roll(now[8:], RADIAL, 1)
            image = (
                image[:PADDED]
                + image[PADDED:]
                + diag[n] * now
                - faces[0] * jnp.concatenate([empty, ahead], axis=0)
                - faces[1] * jnp.concatenate([behind, empty], axis=0)
            )
            outward = pltpu.roll(now[:16], ELEMENTS - 1, 1)
            inward = pltpu.roll(now[72:], 1, 1)
            image = jnp.concatenate(
                [
                    image[:16] - faces[3, :16] * inward,
                    image[16:72],
                    image[72:] - faces[2, 72:] * outward,
                ],
                axis=0,
            )
            q[s] = image
            curve = add(curve, now * image)
            bend = add(bend, image * image)
        curve = total(curve)
        alpha = total(norm) / curve
        alphas[sweep * 4 + n] = alpha
        return alpha, jnp.maximum(alpha * (total(bend) / curve) - 1.0, 0.0)

    none = jnp.zeros((1, ELEMENTS), F32)
    lax.fori_loop(
        0,
        ITERS,
        lambda sweep, steps: tuple(operate(sweep, n, *steps[n]) for n in range(4)),
        ((none, none),) * 4,
    )

    def value_of(s, rows, lanes):
        n = s // 4 * 2 + s % 2
        value = alphas[n, :, lanes] * p[0, s, rows, lanes]
        for sweep in range(1, ITERS):
            value = value + alphas[sweep * 4 + n, :, lanes] * p[sweep, s, rows, lanes]
        return value * mass[rows, lanes] if weigh_out else value

    store_tiles(value_of, turn, out_ref, emit)


FIELD = pltpu.VMEM((8, PADDED, ELEMENTS), F32)
SOLVE_SCRATCH = [
    pltpu.VMEM((PADDED, ELEMENTS), F32),
    pltpu.VMEM((4, PADDED, ELEMENTS), F32),
    pltpu.VMEM((4, PADDED, ELEMENTS), F32),
    pltpu.VMEM((2 * PADDED, 2 * PADDED), BF16),
    FIELD,
    pltpu.VMEM((ITERS, 8, PADDED, ELEMENTS), F32),
    FIELD,
    pltpu.VMEM((ITERS * 4, 1, ELEMENTS), F32),
    pltpu.VMEM((2, GROUPS, 64, LANES), F32),
]


def split(value):
    high = value.astype(BF16)
    return high, (value - high.astype(F32)).astype(BF16)


def apply(t_ref, which, field):
    high, low = split(field)
    width = field.shape[1]
    if width == LANES:
        both = jnp.concatenate([high, low], axis=1)
        out = jnp.dot(t_ref[which], both, preferred_element_type=F32)
        return out[:HALF, :LANES] + out[:HALF, LANES:] + out[HALF:, :LANES]
    out = jnp.dot(t_ref[which], high, preferred_element_type=F32)
    out = out[:HALF] + out[HALF:]
    return out + jnp.dot(t_ref[which, :HALF], low, preferred_element_type=F32)


def parts_of(u_ref):
    out = []
    for odd in range(2):
        tiles = u_ref[odd].reshape(32, 2, 8, LANES)
        one, two = mix(tiles[:, 0], tiles[:, 1])
        out.append((one.reshape(HALF, LANES), two.reshape(HALF, LANES)))
    return out


def parts_to(out_ref, parts):
    for odd in range(2):
        real, imag = parts[odd]
        one, two = mix(real.reshape(32, 8, LANES), imag.reshape(32, 8, LANES))
        out_ref[odd] = jnp.stack([one, two], axis=1).reshape(64, 8, LANES)


def column_tables(c_ref):
    row = lax.broadcasted_iota(jnp.int32, (HALF, LANES), 0)
    for odd in range(2):
        mode = 2 * ((row // 32 % 4 * 2 + row // 128) * 32 + row % 32) + odd
        c_ref[odd] = mode.astype(F32) / MODES
        c_ref[2 + odd] = jnp.where(mode == 0, 1.0 / PLANES, 2.0 / PLANES).astype(F32)
    c_ref[4] = jnp.where(row % 2 == 0, 1.0, -1.0).astype(F32)


def signs(c_ref, width):
    return jnp.concatenate([c_ref[4]] * (width // LANES), axis=1)


def without_first(value):
    head = lax.broadcasted_iota(jnp.int32, (8, value.shape[1]), 0) == 0
    return jnp.concatenate([jnp.where(head, 0.0, value[:8]), value[8:]], axis=0)


def to_planes(t_ref, c_ref, cos_fields, sin_fields, out_ref):
    sign = signs(c_ref, cos_fields[0].shape[1])
    cos_even, cos_odd = apply(t_ref, 0, cos_fields[0]), apply(t_ref, 1, cos_fields[1])
    sin_even, sin_odd = apply(t_ref, 2, sin_fields[0]), apply(t_ref, 3, sin_fields[1])
    quarter_cos = jnp.sum(sign * cos_fields[0], axis=0, keepdims=True)
    quarter_sin = jnp.sum(sign * sin_fields[1], axis=0, keepdims=True)
    cos, sin = cos_even + cos_odd, sin_even + sin_odd
    out_ref[0] = cos - sin
    out_ref[1] = cos + sin
    cos, sin = cos_even - cos_odd, sin_even - sin_odd
    out_ref[2] = cos + sin
    out_ref[3] = cos - sin
    out_ref[1, 0:1] = quarter_cos - quarter_sin
    out_ref[3, 0:1] = quarter_cos + quarter_sin


def from_planes(t_ref, c_ref, values):
    sign = signs(c_ref, values[0].shape[1])
    quarter, three = values[1][0:1], values[3][0:1]
    one = values[0]
    two, four = without_first(values[1]), without_first(values[3])
    plus, minus = one + two, one - two
    plus_far, minus_far = values[2] + four, values[2] - four
    a_even = apply(t_ref, 4, plus + plus_far) + sign * (quarter + three)
    a_odd = apply(t_ref, 5, plus - plus_far)
    b_even = -apply(t_ref, 6, minus - minus_far)
    b_odd = -apply(t_ref, 7, minus + minus_far) - sign * (quarter - three)
    return (a_even, b_even), (a_odd, b_odd)


def state_planes(parts, t_ref, c_ref, out_ref):
    cos_fields, sin_fields = [], []
    for odd in range(2):
        real, imag = parts[odd]
        fraction = c_ref[odd]
        cos_fields.append(jnp.concatenate([real, -fraction * imag], axis=1))
        sin_fields.append(jnp.concatenate([imag, fraction * real], axis=1))
    to_planes(t_ref, c_ref, cos_fields, sin_fields, out_ref)


def first_stage(u_ref, t_ref, c_ref, planes, out_ref):
    parts = parts_of(u_ref)
    state_planes(parts, t_ref, c_ref, planes)
    values = [planes[at, :, :LANES] * planes[at, :, LANES:] for at in range(4)]
    found = from_planes(t_ref, c_ref, values)
    out = []
    for odd in range(2):
        weight = c_ref[2 + odd]
        out.append(tuple(parts[odd][c] - weight * found[odd][c] for c in range(2)))
    parts_to(out_ref, out)


def adjoint_planes(s_ref, t_ref, c_ref, out_ref):
    parts = parts_of(s_ref)
    weights = [c_ref[2 + odd] for odd in range(2)]
    to_planes(
        t_ref,
        c_ref,
        [weights[odd] * parts[odd][0] for odd in range(2)],
        [weights[odd] * parts[odd][1] for odd in range(2)],
        out_ref,
    )


def finish(t_ref, c_ref, s_ref, planes, adjoint, out_ref):
    values = []
    for at in range(4):
        factor = adjoint[at]
        values.append(planes[at] * jnp.concatenate([factor, factor], axis=1))
    found = from_planes(t_ref, c_ref, values)
    parts = parts_of(s_ref)
    out = []
    for odd in range(2):
        fraction = c_ref[odd]
        a, b = found[odd]
        out.append(
            (
                parts[odd][0] - a[:, LANES:] - fraction * b[:, :LANES],
                parts[odd][1] - b[:, LANES:] + fraction * a[:, :LANES],
            )
        )
    parts_to(out_ref, out)


COUNT = N_MODE * N_MER
SPARE = GROUPS - 8


def send(source, target, mode, mer, sems, at):
    pltpu.make_async_remote_copy(
        src_ref=source,
        dst_ref=target,
        send_sem=sems[0].at[at],
        recv_sem=sems[1].at[at],
        device_id={"mode": mode, "mer": mer},
        device_id_type=pl.DeviceIdType.MESH,
    ).start()


def wait(blank, tiles, sem, rows=8):
    whole = blank.at[pl.ds(0, tiles), pl.ds(0, rows)]
    pltpu.make_async_copy(whole, whole, sem).wait()


def wait_either(double, blank, tiles_double, tiles_single, sem, rows=8):
    @pl.when(double)
    def _():
        wait(blank, tiles_double, sem, rows)

    @pl.when(jnp.logical_not(double))
    def _():
        wait(blank, tiles_single, sem, rows)


def place_at(mer, k):
    step = lax.rem(7 * k, N_MER)
    y = lax.rem(lax.rem(mer, 4) + lax.rem(step, 4), 4)
    z = lax.rem(mer // 4 + step // 4, 4)
    return z * 4 + y


def extra(x, mer):
    turn = lax.rem(lax.rem(mer, 4) + mer // 4, 4)
    return lax.rem(x + 4 - turn, 4)


def groups_on(mode, core):
    x = mode // 2
    return [2 * lax.rem(x + step, 4) + core for step in (1, 3, 2, 0)]


def each_group(mode, cores, act):
    for core in cores:
        one, two, three, own = groups_on(mode, core)
        act(one, core)
        act(two, core)
        act(three, core)

        @pl.when(lax.rem(mode, 2) != core)
        def _(own=own, core=core):
            act(own, core)


def each_place(mer, act):
    def body(k, _):
        act(place_at(mer, k))
        return 0

    lax.fori_loop(1, N_MER, body, 0)


def each_other(mode, mer, cores, act):
    groups = [(other, core) for core in cores for other in groups_on(mode, core)]

    def body(place):
        for other, core in groups:
            act(other, core, place)

    each_place(mer, body)
    each_group(mode, cores, lambda other, core: act(other, core, mer))


def order_of(mode):
    return lax.rem(mode, 2) * 4 + mode // 2


def program_kernel(
    state_ref,
    cotangent_hbm,
    mass_ref,
    inverse_ref,
    d_ref,
    t_hbm,
    out_hbm,
    cotangent_in,
    t_ref,
    copy_sems,
    rows,
    native_out,
    native_in,
    mode_out,
    mode_in,
    plane_out,
    plane_in,
    metric_out,
    metric_in,
    u_planes,
    planes,
    s_planes,
    c_ref,
    count,
    ready,
    blank,
    send_sems,
    recv_sems,
    *solve_scratch,
):
    mode = lax.axis_index("mode")
    mer = lax.axis_index("mer")
    odd, eighth = mer // 8, lax.rem(mer, 8)
    row = order_of(mode) * 8 + eighth
    mine_extra = extra(mode // 2, mer)
    double = (lax.rem(mode, 2) == 0) & (mine_extra < SPARE)
    slots = jnp.where(double, 2, 1)
    sems = (send_sems, recv_sems)
    mass, diag, faces, k_ref = solve_scratch[:4]
    turn = solve_scratch[8]
    sent = []

    cotangent_copy = pltpu.make_async_copy(cotangent_hbm, cotangent_in, copy_sems.at[0])
    table_copy = pltpu.make_async_copy(t_hbm, t_ref, copy_sems.at[1])
    cotangent_copy.start()
    table_copy.start()
    barrier = pltpu.get_barrier_semaphore()

    def greet(semaphore, other, place):
        pl.semaphore_signal(
            semaphore,
            inc=1,
            device_id={"mode": other, "mer": place},
            device_id_type=pl.DeviceIdType.MESH,
        )

    each_group(mode, (0, 1), lambda other, core: greet(barrier, other, mer))
    each_place(mer, lambda place: greet(barrier, mode, place))
    native_to_tiles(state_ref, native_out.at[0], rows, turn)
    pl.semaphore_wait(barrier, N_MODE - 1 + N_MER - 1)
    each_group(mode, (0, 1), lambda other, core: greet(ready, other, mer))

    def each_slot(act):
        def body(k, _):
            act(slots - 1 - k)
            return 0

        lax.fori_loop(0, slots, body, 0)

    def send_to_planes(source, target, at):
        def act(other, core, place):
            def single():
                send(source.at[0, other, place], target.at[0, odd, row], other, place, sems, at)

            if core == 1:
                single()
                return
            owns_two = extra(other // 2, place) < SPARE
            pl.when(jnp.logical_not(owns_two))(single)

            @pl.when(owns_two)
            def _():
                send(source.at[:, other, place], target.at[:, odd, row], other, place, sems, at)

        def emit(core):
            each_other(mode, mer, (core,), act)
            if core == 1:
                target[:, odd, row] = source[:, mode, mer]

        sent.append((at, 16 * GROUPS - 2, 16 * GROUPS - 1, 8))
        return emit

    def wait_planes(at):
        wait_either(double, blank, 2 * (COUNT - 1), COUNT - 1, recv_sems.at[at])

    def send_to_modes(source, target, at):
        target[0, mode, mer] = source[0, odd, row]

        def act(other, core, place):
            index = order_of(other) * 8 + lax.rem(place, 8)
            piece = source.at[0, place // 8, index]
            send(piece, target.at[0, mode, mer], other, place, sems, at)

        def act_double(other, core, place):
            index = order_of(other) * 8 + lax.rem(place, 8)
            piece = source.at[:, place // 8, index]
            send(piece, target.at[:, mode, mer], other, place, sems, at)

        @pl.when(double)
        def _():
            target[1, mode, mer] = source[1, odd, row]
            each_other(mode, mer, (0, 1), act_double)

        @pl.when(jnp.logical_not(double))
        def _():
            each_other(mode, mer, (0, 1), act)

        sent.append((at, 2 * (COUNT - 1), COUNT - 1, 8))

    def wait_modes(at):
        wait_either(double, blank, 16 * GROUPS - 2, 16 * GROUPS - 1, recv_sems.at[at])

    mine = pl.ds(pl.multiple_of(order_of(mode) * 8, 8), 8)
    plane_in[0, 0, :, mine] = native_out[0, 0, mode]
    plane_in[0, 1, :, mine] = native_out[0, 1, mine_extra]

    def send_extra_state(other, core):
        index = extra(other // 2, mer)

        @pl.when(index < SPARE)
        def _():
            send(native_out.at[0, 1, index], plane_in.at[0, 1, :, mine], other, mer, sems, 0)

    def send_state(other, core):
        send(native_out.at[0, 0, other], plane_in.at[0, 0, :, mine], other, mer, sems, 0)

    each_group(mode, (0,), send_extra_state)
    each_group(mode, (0, 1), send_state)
    sent.append((0, N_MER * (GROUPS - 2), N_MER * (GROUPS - 1), 8))

    cotangent_copy.wait()
    native_to_tiles(cotangent_in, native_out.at[1], rows, turn)
    mode_in[0, 0, :, mer] = native_out[1, 0, :, odd, eighth]
    mode_in[0, 1, 0:SPARE, mer] = native_out[1, 1, 0:SPARE, odd, eighth]
    metric_rows(mass_ref, inverse_ref, rows, metric_out)
    metric_in[mer] = metric_out[...]

    def send_cotangent(place):
        which, at = place // 8, lax.rem(place, 8)
        send(native_out.at[1, 0, :, which, at], mode_in.at[0, 0, :, mer], mode, place, sems, 2)
        send(
            native_out.at[1, 1, 0:SPARE, which, at],
            mode_in.at[0, 1, 0:SPARE, mer],
            mode,
            place,
            sems,
            2,
        )
        send(metric_out, metric_in.at[mer], mode, place, sems, 3)

    each_place(mer, send_cotangent)
    sent.append((2, (N_MER - 1) * GROUPS, (N_MER - 1) * GROUPS, 8))
    sent.append((3, (N_MER - 1) * 4, (N_MER - 1) * 4, 8))

    p_ref, q_ref = solve_scratch[5:7]
    p_ref[ITERS - 1] = jnp.zeros((8, PADDED, ELEMENTS), F32)
    q_ref[...] = jnp.zeros((8, PADDED, ELEMENTS), F32)
    stiffness_tables(d_ref, k_ref)
    column_tables(c_ref)
    face_tables(faces, count)
    wait(blank, (N_MER - 1) * 4, recv_sems.at[3])
    metric_tables(metric_in, mode, mer, mass, diag, count, turn)
    table_copy.wait()

    wait_either(double, blank, 2 * (N_MODE - 1) * N_MER, (N_MODE - 1) * N_MER, recv_sems.at[0])

    def first(slot):
        first_stage(plane_in.at[0, slot], t_ref, c_ref, u_planes.at[slot], plane_out.at[0, slot])

    each_slot(first)
    pl.semaphore_wait(ready, N_MODE - 1)
    send_to_modes(plane_out.at[0], mode_in.at[1], 4)

    wait(blank, (N_MER - 1) * GROUPS, recv_sems.at[2])
    emit = send_to_planes(mode_out.at[0], plane_in.at[1], 5)
    solve(mode_in.at[0], mode_out.at[0], False, True, False, solve_scratch, emit)

    wait_modes(4)
    emit = send_to_planes(mode_out.at[1], plane_in.at[2], 6)
    solve(mode_in.at[1], mode_out.at[1], True, False, True, solve_scratch, emit)

    def multiplier(slot):
        adjoint_planes(plane_in.at[1, slot], t_ref, c_ref, s_planes.at[slot])

    wait_planes(5)
    each_slot(multiplier)

    def second(slot):
        state_planes(parts_of(plane_in.at[2, slot]), t_ref, c_ref, planes)
        finish(t_ref, c_ref, plane_in.at[1, slot], planes, s_planes.at[slot], plane_out.at[1, slot])

    wait_planes(6)
    each_slot(second)
    send_to_modes(plane_out.at[1], mode_in.at[2], 7)

    wait_modes(7)
    emit = send_to_planes(mode_out.at[2], plane_in.at[3], 8)
    solve(mode_in.at[2], mode_out.at[2], False, True, True, solve_scratch, emit)

    def third(slot):
        s_in = plane_in.at[3, slot]
        adjoint_planes(s_in, t_ref, c_ref, s_planes.at[slot])
        finish(
            t_ref, c_ref, s_in, u_planes.at[slot], s_planes.at[slot], plane_out.at[2, slot]
        )
        native_in[slot, mode] = plane_out[2, slot, :, mine]

        def send_gradient(other, core):
            theirs = pl.ds(pl.multiple_of(order_of(other) * 8, 8), 8)
            send(plane_out.at[2, slot, :, theirs], native_in.at[slot, mode], other, mer, sems, 9)

        each_group(mode, (0, 1), send_gradient)

    wait_planes(8)
    each_slot(third)
    sent.append((9, 2 * (N_MODE - 1) * N_MER, (N_MODE - 1) * N_MER, 8))
    wait_either(double, blank, N_MER * (GROUPS - 2), N_MER * (GROUPS - 1), recv_sems.at[9])
    turned = lax.rem(lax.rem(mer, 4) + mer // 4, 4)
    copies = [pltpu.make_async_copy(native_in.at[0], out_hbm.at[0:N_MODE], copy_sems.at[2])]
    for index in range(SPARE):
        owner = 2 * lax.rem(index + turned, 4)
        copies.append(
            pltpu.make_async_copy(
                native_in.at[1, owner], out_hbm.at[N_MODE + index], copy_sems.at[3 + index]
            )
        )
    for copy in copies:
        copy.start()
    for at, tiles_double, tiles_single, rows_each in sent:
        wait_either(double, blank, tiles_double, tiles_single, send_sems.at[at], rows_each)
    for copy in copies:
        copy.wait()


def program(state, cotangent, mass, inverse, derivative, table):
    by_mode = (2, N_MODE, N_MER, 8, LANES)
    by_native = (2, N_MODE, 2, 8, 8, LANES)
    by_plane = (2, 2, COUNT // 2, 8, LANES)
    vmem = pl.BlockSpec(memory_space=pltpu.VMEM)
    hbm = pl.BlockSpec(memory_space=pl.ANY)

    def scratch(count, shape):
        return pltpu.VMEM((count,) + shape, F32)

    return pl.pallas_call(
        program_kernel,
        out_shape=jax.ShapeDtypeStruct((GROUPS, 2, 8, 8, LANES), F32),
        in_specs=[vmem, hbm, vmem, vmem, vmem, hbm],
        out_specs=hbm,
        scratch_shapes=[
            pltpu.VMEM((NODE, NODE, ELEM_DEV * LANES), F32),
            pltpu.VMEM((8, 2 * HALF, HALF), BF16),
            pltpu.SemaphoreType.DMA((6,)),
            pltpu.VMEM((PADDED * ELEM_DEV, LANES), F32),
            scratch(2, by_native),
            pltpu.VMEM(by_native, F32),
            scratch(3, by_mode),
            scratch(3, by_mode),
            scratch(3, by_plane),
            scratch(4, by_plane),
            pltpu.VMEM((2, 16, LANES), F32),
            scratch(N_MER, (2, 16, LANES)),
            scratch(2, (4, HALF, 2 * LANES)),
            scratch(4, (HALF, 2 * LANES)),
            scratch(2, (4, HALF, LANES)),
            scratch(5, (HALF, LANES)),
            pltpu.VMEM((PADDED, ELEMENTS), F32),
            pltpu.SemaphoreType.REGULAR,
            pltpu.VMEM((2 * COUNT, 8, LANES), F32),
            pltpu.SemaphoreType.DMA((10,)),
            pltpu.SemaphoreType.DMA((10,)),
            *SOLVE_SCRATCH,
        ],
        compiler_params=pltpu.CompilerParams(
            collective_id=0, has_side_effects=True, vmem_limit_bytes=60 << 20
        ),
        name="program",
    )(state, cotangent, mass, inverse, derivative, table)


def shards(cotangent, checkpoint, mass, inv_radius_sq, derivative):
    table = jnp.asarray(tables())
    return tiles_to_native(program(checkpoint, cotangent, mass, inv_radius_sq, derivative, table))


def solution(mesh):
    return jax.shard_map(
        shards,
        mesh=mesh,
        in_specs=(
            P(None, None, ("mer", "mode")),
            P(None, None, ("mer", "mode")),
            P(None, None, "mer"),
            P(None, None, "mer"),
            P(),
        ),
        out_specs=P(None, None, ("mer", "mode")),
        check_vma=False,
    )
```

```python
import functools
import math

import jax
import jax.numpy as jnp
import ml_dtypes
import numpy as np
from jax import lax
from jax.experimental import pallas as pl
from jax.experimental.pallas import tpu as pltpu
from jax.sharding import PartitionSpec as P

NODE = 9
NODES = NODE * NODE
RADIAL = 8
ITERS = 4
MODES = 512
HALF = 256
PLANES = 1024
ELEMENTS = 256
N_MODE = 8
N_MER = 16
ELEM_DEV = 16
GROUPS = 11
PADDED = GROUPS * 8
LANES = 128
AZIMUTH_WEIGHT = 4.0
HIGHEST = lax.Precision.HIGHEST
F32 = jnp.float32
BF16 = jnp.bfloat16


def tables():
    order = np.arange(HALF).reshape(4, 2, HALF // N_MODE).transpose(1, 0, 2).reshape(-1)
    out = []
    for wave in (np.cos, np.sin):
        for odd in range(2):
            index = np.outer(np.arange(HALF), 2 * order + odd) % PLANES
            values = wave(index.astype(np.float64) * (2.0 * math.pi / PLANES)).astype(np.float32)
            high = values.astype(ml_dtypes.bfloat16)
            low = (values - high.astype(np.float32)).astype(ml_dtypes.bfloat16)
            out.append((high, low))
    both = [np.concatenate(pair) for pair in out]
    turned = [np.concatenate([high.T, low.T]) for high, low in out]
    return np.stack(both + turned)


def mix(first, second):
    shape = first.shape
    axis = len(shape) - 2
    low = lax.broadcasted_iota(jnp.int32, shape, axis) % 4 < 2
    return (
        jnp.where(low, first, pltpu.roll(second, 2, axis)),
        jnp.where(low, pltpu.roll(first, 6, axis), second),
    )


def exchange(tiles):
    tiles = list(tiles)
    axis = tiles[0].ndim - 1
    block = lax.broadcasted_iota(jnp.int32, tiles[0].shape, axis) // 16
    for bit in (1, 2, 4):
        clear = (block & bit) == 0
        for at in range(8):
            if at & bit:
                continue
            one, two = tiles[at], tiles[at | bit]
            tiles[at] = jnp.where(clear, one, pltpu.roll(two, 16 * bit, axis))
            tiles[at | bit] = jnp.where(clear, pltpu.roll(one, LANES - 16 * bit, axis), two)
    return tiles


def native_to_tiles(x_ref, out_ref, rows, turn):
    rows[pl.ds(NODES * ELEM_DEV, PADDED * ELEM_DEV - NODES * ELEM_DEV), :] = jnp.zeros(
        ((PADDED - NODES) * ELEM_DEV, LANES), F32
    )
    for i in range(NODE):
        for e in range(ELEM_DEV):
            rows[pl.ds(i * NODE * ELEM_DEV + e, NODE, stride=ELEM_DEV), :] = x_ref[
                i, :, e * LANES : (e + 1) * LANES
            ]
    for group in range(GROUPS):
        turned = rows[group * LANES : (group + 1) * LANES, :].T
        turn[0, group] = turned[:64]
        turn[1, group] = turned[64:]
        for odd in range(2):
            real = turn[0, group, pl.ds(odd, 32, stride=2), :].reshape(4, 8, LANES)
            imag = turn[1, group, pl.ds(odd, 32, stride=2), :].reshape(4, 8, LANES)
            one, two = mix(real, imag)
            out_ref[group // 8, group % 8, odd] = jnp.stack([one, two], axis=1).reshape(8, 8, LANES)


def tiles_to_native_kernel(t_hbm, out_hbm, tiles_in, rows, turn, native, in_sems, out_sems):
    parts = ((0, 6, 0, 5), (6, GROUPS, 5, NODE))
    loads, stores = [], []
    for at, (start, stop, first, last) in enumerate(parts):
        groups, nodes = pl.ds(start, stop - start), pl.ds(first, last - first)
        loads.append(
            pltpu.make_async_copy(t_hbm.at[groups], tiles_in.at[groups], in_sems.at[at])
        )
        stores.append(pltpu.make_async_copy(native.at[nodes], out_hbm.at[nodes], out_sems.at[at]))
        loads[at].start()
    for at, (start, stop, first, last) in enumerate(parts):
        loads[at].wait()
        for group in range(start, stop):
            for odd in range(2):
                tiles = tiles_in[group, odd].reshape(4, 2, 8, LANES)
                real, imag = mix(tiles[:, 0], tiles[:, 1])
                turn[0, group, pl.ds(odd, 32, stride=2), :] = real.reshape(32, LANES)
                turn[1, group, pl.ds(odd, 32, stride=2), :] = imag.reshape(32, LANES)
            both = jnp.concatenate([turn[0, group], turn[1, group]], axis=0)
            rows[group * LANES : (group + 1) * LANES, :] = both.T
        for i in range(first, last):
            for e in range(ELEM_DEV):
                native[i, :, e * LANES : (e + 1) * LANES] = rows[
                    pl.ds(i * NODE * ELEM_DEV + e, NODE, stride=ELEM_DEV), :
                ]
        stores[at].start()
    for store in stores:
        store.wait()


def tiles_to_native(tiles):
    hbm = pl.BlockSpec(memory_space=pltpu.HBM)
    shape = (NODE, NODE, ELEM_DEV * LANES)
    return pl.pallas_call(
        tiles_to_native_kernel,
        out_shape=jax.ShapeDtypeStruct(shape, F32),
        in_specs=[hbm],
        out_specs=hbm,
        scratch_shapes=[
            pltpu.VMEM((GROUPS, 2, 8, 8, LANES), F32),
            pltpu.VMEM((PADDED * ELEM_DEV, LANES), F32),
            pltpu.VMEM((2, GROUPS, 64, LANES), F32),
            pltpu.VMEM(shape, F32),
            pltpu.SemaphoreType.DMA((2,)),
            pltpu.SemaphoreType.DMA((2,)),
        ],
        compiler_params=pltpu.CompilerParams(vmem_limit_bytes=62 << 20),
        name="tiles_to_native",
    )(tiles)


def stiffness_tables(d_ref, k_ref):
    def dot(a, b):
        return jnp.dot(a, b, precision=HIGHEST, preferred_element_type=F32)

    derivative = d_ref[...]
    stiffness = lax.dot_general(
        derivative, derivative, (((0,), (0,)), ((), ())), precision=HIGHEST, preferred_element_type=F32
    )

    def pick(shape, node_axis, outer):
        node = lax.broadcasted_iota(jnp.int32, shape, node_axis)
        other = lax.broadcasted_iota(jnp.int32, shape, 1 - node_axis)
        place = node // NODE if outer else node % NODE
        return jnp.where((place == other) & (node < NODES), 1.0, 0.0).astype(F32)

    outer, inner = pick((PADDED, NODE), 0, True), pick((PADDED, NODE), 0, False)
    outer_t, inner_t = pick((NODE, PADDED), 1, True), pick((NODE, PADDED), 1, False)
    whole = dot(dot(outer, stiffness), outer_t) * dot(inner, inner_t)
    whole = whole + dot(dot(inner, stiffness), inner_t) * dot(outer, outer_t)
    high = whole.astype(BF16).astype(F32)
    low = whole - high
    shape = (PADDED, 2 * PADDED)
    node = lax.broadcasted_iota(jnp.int32, shape, 0)
    column = lax.broadcasted_iota(jnp.int32, shape, 1)
    either = (node // 8 == column // 16) & (node % 8 == column % 8)
    first = either & (column % 16 < 8)
    top = dot(high, jnp.where(either, 1.0, 0.0).astype(F32))
    bottom = dot(low, jnp.where(first, 1.0, 0.0).astype(F32))
    k_ref[...] = jnp.concatenate([top, bottom], axis=0).astype(BF16)


def metric_rows(mass_ref, inverse_ref, rows, out_ref):
    lane = lax.broadcasted_iota(jnp.int32, (ELEM_DEV, LANES), 1) % ELEM_DEV
    element = lax.broadcasted_iota(jnp.int32, (ELEM_DEV, LANES), 0)
    repeat = jnp.where(lane == element, 1.0, 0.0).astype(F32)
    shape = (PADDED, LANES)
    node = lax.broadcasted_iota(jnp.int32, shape, 0)
    block = lax.broadcasted_iota(jnp.int32, shape, 1) // ELEM_DEV
    keep = (node % 8 == block) & (node < NODES)
    for kind, ref in ((0, mass_ref), (1, inverse_ref)):
        for i in range(NODE):
            rows[i * NODE : (i + 1) * NODE, :ELEM_DEV] = ref[i]
        values = jnp.dot(
            rows[:PADDED, :ELEM_DEV], repeat, precision=HIGHEST, preferred_element_type=F32
        )
        values = jnp.where(keep, values, 0.0).reshape(GROUPS, 8, LANES)
        out_ref[kind, :GROUPS] = jnp.sum(values, axis=1)
        out_ref[kind, GROUPS:] = jnp.zeros((16 - GROUPS, LANES), F32)


def face_tables(faces, count):
    shape = (PADDED, ELEMENTS)
    node = lax.broadcasted_iota(jnp.int32, shape, 0)
    element = lax.broadcasted_iota(jnp.int32, shape, 1)
    inside = node < NODES
    upper = (node % NODE == NODE - 1) & (element < ELEMENTS - RADIAL) & inside
    lower = (node % NODE == 0) & (element >= RADIAL) & inside
    outer = (node // NODE == NODE - 1) & (element % RADIAL != RADIAL - 1) & inside
    inner = (node // NODE == 0) & (element % RADIAL != 0)
    marks = [jnp.where(mark, 1.0, 0.0).astype(F32) for mark in (upper, lower, outer, inner)]
    for at in range(4):
        faces[at] = marks[at]
    count[...] = marks[0] + marks[1] + marks[2] + marks[3]


def metric_tables(m_ref, mode_group, place, mass, diag, count, turn):
    inverse = diag.at[0]
    for kind, out in ((0, mass), (1, inverse)):
        for h in range(2):
            rows = exchange([m_ref[8 * h + at, kind] for at in range(8)])
            for at in range(8):
                for group in range(GROUPS):
                    turn[h, group, at : at + 1] = rows[at][group : group + 1]
            for group in range(GROUPS):
                out[group * 8 : (group + 1) * 8, h * LANES : (h + 1) * LANES] = turn[h, group, 0:8]
    values = inverse[...]
    for n in range(4):
        offset = lax.rem(place, 8) // 2 * 8 + lax.rem(place, 2) * 2 + n // 2 * 4 + n % 2
        number = mode_group * 64 + 2 * offset + place // 8
        fraction = number.astype(F32) / MODES
        diag[n] = mass[...] * (1.0 + AZIMUTH_WEIGHT * fraction * fraction * values) + count[...]


def owner_of(extra_group, place):
    return 2 * ((extra_group + place % 4 + place // 4) % 4)


CHUNKS = ((0, 0, 3), (0, 3, 6), (0, 6, 8), (1, 0, 3))


def load_tiles(b_ref, turn, weight, out, by_owner):
    for slot, start, stop in CHUNKS:
        for h in range(2):
            tiles = []
            for place in range(8 * h, 8 * h + 8):
                if slot and by_owner:
                    tiles.append(
                        jnp.stack([b_ref[1, owner_of(at, place), place] for at in range(start, stop)])
                    )
                else:
                    tiles.append(b_ref[slot, start:stop, place])
            tiles = exchange(tiles)
            for at in range(8):
                turn[h, 8 * slot + start : 8 * slot + stop, at * 8 : (at + 1) * 8] = tiles[at]
    for s in range(8):
        for h in range(2):
            lanes = slice(h * LANES, (h + 1) * LANES)
            for group in range(GROUPS):
                rows = slice(group * 8, (group + 1) * 8)
                value = turn[h, group, pl.ds(s, 8, stride=8), :]
                if weight is not None:
                    value = value * weight[rows, lanes]
                out[s, rows, lanes] = value


OWNED = (
    ((1, 0), (1, 1), (1, 2), (0, 0), (0, 2), (0, 4), (0, 6)),
    ((0, 1), (0, 3), (0, 5), (0, 7)),
)


def store_tiles(value_of, turn, out_ref, emit):
    for core in range(2):
        for s in range(8):
            for slot, at_group in OWNED[core]:
                group = 8 * slot + at_group
                for h in range(2):
                    turn[h, group, pl.ds(s, 8, stride=8), :] = value_of(
                        s, slice(group * 8, (group + 1) * 8), slice(h * LANES, (h + 1) * LANES)
                    )
        for slot, at_group in OWNED[core]:
            for h in range(2):
                group = 8 * slot + at_group
                tiles = exchange([turn[h, group, at * 8 : (at + 1) * 8] for at in range(8)])
                for at in range(8):
                    place = 8 * h + at
                    owner = owner_of(at_group, place) if slot else at_group
                    out_ref[slot, owner, place] = tiles[at]
        emit(core)


def total(parts):
    half = parts[:, :LANES] + parts[:, LANES:]
    return jnp.broadcast_to(jnp.sum(half, axis=(0, 1), keepdims=True), (1, ELEMENTS))


def solve(b_ref, out_ref, weigh_in, weigh_out, by_owner, scratch, emit):
    mass, diag, faces, k_ref, r, p, q, alphas, turn, units = scratch
    load_tiles(b_ref, turn, mass if weigh_in else None, r, by_owner)

    def operate(sweep, n, alpha, beta):
        norm = curve = bend = jnp.zeros((8, ELEMENTS), F32)
        before = lax.rem(sweep + ITERS - 1, ITERS)
        for s in (n // 2 * 4 + n % 2, n // 2 * 4 + 2 + n % 2):
            for tile in range(GROUPS):
                rows = slice(8 * tile, 8 * tile + 8)
                rest = r[s, rows] - alpha * q[s, rows]
                now = rest + beta * p[before, s, rows]
                r[s, rows] = rest
                p[sweep, s, rows] = now
                norm = norm + rest * rest
                high = now.astype(BF16).astype(F32)
                unit = jnp.concatenate([high, now - high], axis=0).astype(BF16)
                units[s, 16 * tile : 16 * tile + 16] = unit
            image = jnp.dot(k_ref[...], units[s], preferred_element_type=F32)

            def moved(tile, shift, s=s):
                return pltpu.roll(p[sweep, s, 8 * tile : 8 * tile + 8], shift, 1)

            for tile in range(GROUPS):
                rows = slice(8 * tile, 8 * tile + 8)
                now = p[sweep, s, rows]
                value = image[rows] + image[PADDED + 8 * tile : PADDED + 8 * tile + 8]
                value = value + diag[n, rows] * now
                if tile not in (0, 9):
                    value = value - faces[0, rows] * moved(tile - 1, ELEMENTS - RADIAL)
                if tile not in (8, 10):
                    value = value - faces[1, rows] * moved(tile + 1, RADIAL)
                if tile < 2:
                    value = value - faces[3, rows] * moved(tile + 9, 1)
                if tile > 8:
                    value = value - faces[2, rows] * moved(tile - 9, ELEMENTS - 1)
                q[s, rows] = value
                curve = curve + now * value
                bend = bend + value * value
        curve = total(curve)
        alpha = total(norm) / curve
        alphas[sweep * 4 + n] = alpha
        return alpha, jnp.maximum(alpha * (total(bend) / curve) - 1.0, 0.0)

    none = jnp.zeros((1, ELEMENTS), F32)
    lax.fori_loop(
        0,
        ITERS,
        lambda sweep, steps: tuple(operate(sweep, n, *steps[n]) for n in range(4)),
        ((none, none),) * 4,
    )

    def value_of(s, rows, lanes):
        n = s // 4 * 2 + s % 2
        value = alphas[n, :, lanes] * p[0, s, rows, lanes]
        for sweep in range(1, ITERS):
            value = value + alphas[sweep * 4 + n, :, lanes] * p[sweep, s, rows, lanes]
        return value * mass[rows, lanes] if weigh_out else value

    store_tiles(value_of, turn, out_ref, emit)


FIELD = pltpu.VMEM((8, PADDED, ELEMENTS), F32)
SOLVE_SCRATCH = [
    pltpu.VMEM((PADDED, ELEMENTS), F32),
    pltpu.VMEM((4, PADDED, ELEMENTS), F32),
    pltpu.VMEM((4, PADDED, ELEMENTS), F32),
    pltpu.VMEM((2 * PADDED, 2 * PADDED), BF16),
    FIELD,
    pltpu.VMEM((ITERS, 8, PADDED, ELEMENTS), F32),
    FIELD,
    pltpu.VMEM((ITERS * 4, 1, ELEMENTS), F32),
    pltpu.VMEM((2, GROUPS, 64, LANES), F32),
    pltpu.VMEM((8, 2 * PADDED, ELEMENTS), BF16),
]


def split(value):
    high = value.astype(BF16)
    return high, (value - high.astype(F32)).astype(BF16)


def apply(t_ref, which, field):
    high, low = split(field)
    width = field.shape[1]
    if width == LANES:
        both = jnp.concatenate([high, low], axis=1)
        out = jnp.dot(t_ref[which], both, preferred_element_type=F32)
        return out[:HALF, :LANES] + out[:HALF, LANES:] + out[HALF:, :LANES]
    out = jnp.dot(t_ref[which], high, preferred_element_type=F32)
    out = out[:HALF] + out[HALF:]
    return out + jnp.dot(t_ref[which, :HALF], low, preferred_element_type=F32)


def parts_of(u_ref):
    out = []
    for odd in range(2):
        tiles = u_ref[odd].reshape(32, 2, 8, LANES)
        one, two = mix(tiles[:, 0], tiles[:, 1])
        out.append((one.reshape(HALF, LANES), two.reshape(HALF, LANES)))
    return out


def parts_to(out_ref, parts):
    for odd in range(2):
        real, imag = parts[odd]
        one, two = mix(real.reshape(32, 8, LANES), imag.reshape(32, 8, LANES))
        out_ref[odd] = jnp.stack([one, two], axis=1).reshape(64, 8, LANES)


def column_tables(c_ref):
    row = lax.broadcasted_iota(jnp.int32, (HALF, LANES), 0)
    for odd in range(2):
        mode = 2 * ((row // 32 % 4 * 2 + row // 128) * 32 + row % 32) + odd
        c_ref[odd] = mode.astype(F32) / MODES
        c_ref[2 + odd] = jnp.where(mode == 0, 1.0 / PLANES, 2.0 / PLANES).astype(F32)
    c_ref[4] = jnp.where(row % 2 == 0, 1.0, -1.0).astype(F32)


def signs(c_ref, width):
    return jnp.concatenate([c_ref[4]] * (width // LANES), axis=1)


def without_first(value):
    head = lax.broadcasted_iota(jnp.int32, (8, value.shape[1]), 0) == 0
    return jnp.concatenate([jnp.where(head, 0.0, value[:8]), value[8:]], axis=0)


def to_planes(t_ref, c_ref, cos_fields, sin_fields, out_ref):
    sign = signs(c_ref, cos_fields[0].shape[1])
    cos_even, cos_odd = apply(t_ref, 0, cos_fields[0]), apply(t_ref, 1, cos_fields[1])
    sin_even, sin_odd = apply(t_ref, 2, sin_fields[0]), apply(t_ref, 3, sin_fields[1])
    quarter_cos = jnp.sum(sign * cos_fields[0], axis=0, keepdims=True)
    quarter_sin = jnp.sum(sign * sin_fields[1], axis=0, keepdims=True)
    cos, sin = cos_even + cos_odd, sin_even + sin_odd
    out_ref[0] = cos - sin
    out_ref[1] = cos + sin
    cos, sin = cos_even - cos_odd, sin_even - sin_odd
    out_ref[2] = cos + sin
    out_ref[3] = cos - sin
    out_ref[1, 0:1] = quarter_cos - quarter_sin
    out_ref[3, 0:1] = quarter_cos + quarter_sin


def from_planes(t_ref, c_ref, values):
    sign = signs(c_ref, values[0].shape[1])
    quarter, three = values[1][0:1], values[3][0:1]
    one = values[0]
    two, four = without_first(values[1]), without_first(values[3])
    plus, minus = one + two, one - two
    plus_far, minus_far = values[2] + four, values[2] - four
    a_even = apply(t_ref, 4, plus + plus_far) + sign * (quarter + three)
    a_odd = apply(t_ref, 5, plus - plus_far)
    b_even = -apply(t_ref, 6, minus - minus_far)
    b_odd = -apply(t_ref, 7, minus + minus_far) - sign * (quarter - three)
    return (a_even, b_even), (a_odd, b_odd)


def state_planes(parts, t_ref, c_ref, out_ref):
    cos_fields, sin_fields = [], []
    for odd in range(2):
        real, imag = parts[odd]
        fraction = c_ref[odd]
        cos_fields.append(jnp.concatenate([real, -fraction * imag], axis=1))
        sin_fields.append(jnp.concatenate([imag, fraction * real], axis=1))
    to_planes(t_ref, c_ref, cos_fields, sin_fields, out_ref)


def first_stage(u_ref, t_ref, c_ref, planes, out_ref):
    parts = parts_of(u_ref)
    state_planes(parts, t_ref, c_ref, planes)
    values = [planes[at, :, :LANES] * planes[at, :, LANES:] for at in range(4)]
    found = from_planes(t_ref, c_ref, values)
    out = []
    for odd in range(2):
        weight = c_ref[2 + odd]
        out.append(tuple(parts[odd][c] - weight * found[odd][c] for c in range(2)))
    parts_to(out_ref, out)


def adjoint_planes(s_ref, t_ref, c_ref, out_ref):
    parts = parts_of(s_ref)
    weights = [c_ref[2 + odd] for odd in range(2)]
    to_planes(
        t_ref,
        c_ref,
        [weights[odd] * parts[odd][0] for odd in range(2)],
        [weights[odd] * parts[odd][1] for odd in range(2)],
        out_ref,
    )


def finish(t_ref, c_ref, s_ref, planes, adjoint, out_ref):
    values = []
    for at in range(4):
        factor = adjoint[at]
        values.append(planes[at] * jnp.concatenate([factor, factor], axis=1))
    found = from_planes(t_ref, c_ref, values)
    parts = parts_of(s_ref)
    out = []
    for odd in range(2):
        fraction = c_ref[odd]
        a, b = found[odd]
        out.append(
            (
                parts[odd][0] - a[:, LANES:] - fraction * b[:, :LANES],
                parts[odd][1] - b[:, LANES:] + fraction * a[:, :LANES],
            )
        )
    parts_to(out_ref, out)


COUNT = N_MODE * N_MER
SPARE = GROUPS - 8


def send(source, target, mode, mer, sems, at):
    pltpu.make_async_remote_copy(
        src_ref=source,
        dst_ref=target,
        send_sem=sems[0].at[at],
        recv_sem=sems[1].at[at],
        device_id={"mode": mode, "mer": mer},
        device_id_type=pl.DeviceIdType.MESH,
    ).start()


def wait(blank, tiles, sem, rows=8):
    whole = blank.at[pl.ds(0, tiles), pl.ds(0, rows)]
    pltpu.make_async_copy(whole, whole, sem).wait()


def wait_either(double, blank, tiles_double, tiles_single, sem, rows=8):
    @pl.when(double)
    def _():
        wait(blank, tiles_double, sem, rows)

    @pl.when(jnp.logical_not(double))
    def _():
        wait(blank, tiles_single, sem, rows)


def place_at(mer, k):
    step = lax.rem(7 * k, N_MER)
    y = lax.rem(lax.rem(mer, 4) + lax.rem(step, 4), 4)
    z = lax.rem(mer // 4 + step // 4, 4)
    return z * 4 + y


def extra(x, mer):
    turn = lax.rem(lax.rem(mer, 4) + mer // 4, 4)
    return lax.rem(x + 4 - turn, 4)


def groups_on(mode, core):
    x = mode // 2
    return [2 * lax.rem(x + step, 4) + core for step in (1, 3, 2, 0)]


def each_group(mode, cores, act):
    for core in cores:
        one, two, three, own = groups_on(mode, core)
        act(one, core)
        act(two, core)
        act(three, core)

        @pl.when(lax.rem(mode, 2) != core)
        def _(own=own, core=core):
            act(own, core)


def each_place(mer, act):
    def body(k, _):
        act(place_at(mer, k))
        return 0

    lax.fori_loop(1, N_MER, body, 0)


def each_other(mode, mer, cores, act):
    groups = [(other, core) for core in cores for other in groups_on(mode, core)]

    def body(place):
        for other, core in groups:
            act(other, core, place)

    each_place(mer, body)
    each_group(mode, cores, lambda other, core: act(other, core, mer))


def order_of(mode):
    return lax.rem(mode, 2) * 4 + mode // 2


def program_kernel(
    state_ref,
    cotangent_hbm,
    mass_ref,
    inverse_ref,
    d_ref,
    t_hbm,
    out_hbm,
    cotangent_in,
    t_ref,
    copy_sems,
    rows,
    native_out,
    native_in,
    mode_out,
    mode_in,
    plane_out,
    plane_in,
    metric_out,
    metric_in,
    u_planes,
    planes,
    s_planes,
    c_ref,
    count,
    ready,
    blank,
    send_sems,
    recv_sems,
    *solve_scratch,
):
    mode = lax.axis_index("mode")
    mer = lax.axis_index("mer")
    odd, eighth = mer // 8, lax.rem(mer, 8)
    row = order_of(mode) * 8 + eighth
    mine_extra = extra(mode // 2, mer)
    double = (lax.rem(mode, 2) == 0) & (mine_extra < SPARE)
    slots = jnp.where(double, 2, 1)
    sems = (send_sems, recv_sems)
    mass, diag, faces, k_ref = solve_scratch[:4]
    turn = solve_scratch[8]
    sent = []

    cotangent_copy = pltpu.make_async_copy(cotangent_hbm, cotangent_in, copy_sems.at[0])
    table_copy = pltpu.make_async_copy(t_hbm, t_ref, copy_sems.at[1])
    cotangent_copy.start()
    table_copy.start()
    barrier = pltpu.get_barrier_semaphore()

    def greet(semaphore, other, place):
        pl.semaphore_signal(
            semaphore,
            inc=1,
            device_id={"mode": other, "mer": place},
            device_id_type=pl.DeviceIdType.MESH,
        )

    each_group(mode, (0, 1), lambda other, core: greet(barrier, other, mer))
    each_place(mer, lambda place: greet(barrier, mode, place))
    native_to_tiles(state_ref, native_out.at[0], rows, turn)
    pl.semaphore_wait(barrier, N_MODE - 1 + N_MER - 1)
    each_group(mode, (0, 1), lambda other, core: greet(ready, other, mer))

    def each_slot(act):
        def body(k, _):
            act(slots - 1 - k)
            return 0

        lax.fori_loop(0, slots, body, 0)

    def send_to_planes(source, target, at):
        def act(other, core, place):
            def single():
                send(source.at[0, other, place], target.at[0, odd, row], other, place, sems, at)

            if core == 1:
                single()
                return
            owns_two = extra(other // 2, place) < SPARE
            pl.when(jnp.logical_not(owns_two))(single)

            @pl.when(owns_two)
            def _():
                send(source.at[:, other, place], target.at[:, odd, row], other, place, sems, at)

        def emit(core):
            each_other(mode, mer, (core,), act)
            if core == 1:
                target[:, odd, row] = source[:, mode, mer]

        sent.append((at, 16 * GROUPS - 2, 16 * GROUPS - 1, 8))
        return emit

    def wait_planes(at):
        wait_either(double, blank, 2 * (COUNT - 1), COUNT - 1, recv_sems.at[at])

    def send_to_modes(source, target, at):
        target[0, mode, mer] = source[0, odd, row]

        def act(other, core, place):
            index = order_of(other) * 8 + lax.rem(place, 8)
            piece = source.at[0, place // 8, index]
            send(piece, target.at[0, mode, mer], other, place, sems, at)

        def act_double(other, core, place):
            index = order_of(other) * 8 + lax.rem(place, 8)
            piece = source.at[:, place // 8, index]
            send(piece, target.at[:, mode, mer], other, place, sems, at)

        @pl.when(double)
        def _():
            target[1, mode, mer] = source[1, odd, row]
            each_other(mode, mer, (0, 1), act_double)

        @pl.when(jnp.logical_not(double))
        def _():
            each_other(mode, mer, (0, 1), act)

        sent.append((at, 2 * (COUNT - 1), COUNT - 1, 8))

    def wait_modes(at):
        wait_either(double, blank, 16 * GROUPS - 2, 16 * GROUPS - 1, recv_sems.at[at])

    mine = pl.ds(pl.multiple_of(order_of(mode) * 8, 8), 8)
    plane_in[0, 0, :, mine] = native_out[0, 0, mode]
    plane_in[0, 1, :, mine] = native_out[0, 1, mine_extra]

    def send_extra_state(other, core):
        index = extra(other // 2, mer)

        @pl.when(index < SPARE)
        def _():
            send(native_out.at[0, 1, index], plane_in.at[0, 1, :, mine], other, mer, sems, 0)

    def send_state(other, core):
        send(native_out.at[0, 0, other], plane_in.at[0, 0, :, mine], other, mer, sems, 0)

    each_group(mode, (0,), send_extra_state)
    each_group(mode, (0, 1), send_state)
    sent.append((0, N_MER * (GROUPS - 2), N_MER * (GROUPS - 1), 8))

    cotangent_copy.wait()
    native_to_tiles(cotangent_in, native_out.at[1], rows, turn)
    mode_in[0, 0, :, mer] = native_out[1, 0, :, odd, eighth]
    mode_in[0, 1, 0:SPARE, mer] = native_out[1, 1, 0:SPARE, odd, eighth]
    metric_rows(mass_ref, inverse_ref, rows, metric_out)
    metric_in[mer] = metric_out[...]

    def send_cotangent(place):
        which, at = place // 8, lax.rem(place, 8)
        send(native_out.at[1, 0, :, which, at], mode_in.at[0, 0, :, mer], mode, place, sems, 2)
        send(
            native_out.at[1, 1, 0:SPARE, which, at],
            mode_in.at[0, 1, 0:SPARE, mer],
            mode,
            place,
            sems,
            2,
        )
        send(metric_out, metric_in.at[mer], mode, place, sems, 3)

    each_place(mer, send_cotangent)
    sent.append((2, (N_MER - 1) * GROUPS, (N_MER - 1) * GROUPS, 8))
    sent.append((3, (N_MER - 1) * 4, (N_MER - 1) * 4, 8))

    p_ref, q_ref = solve_scratch[5:7]
    p_ref[ITERS - 1] = jnp.zeros((8, PADDED, ELEMENTS), F32)
    q_ref[...] = jnp.zeros((8, PADDED, ELEMENTS), F32)
    stiffness_tables(d_ref, k_ref)
    column_tables(c_ref)
    face_tables(faces, count)
    wait(blank, (N_MER - 1) * 4, recv_sems.at[3])
    metric_tables(metric_in, mode, mer, mass, diag, count, turn)
    table_copy.wait()

    wait_either(double, blank, 2 * (N_MODE - 1) * N_MER, (N_MODE - 1) * N_MER, recv_sems.at[0])

    def first(slot):
        first_stage(plane_in.at[0, slot], t_ref, c_ref, u_planes.at[slot], plane_out.at[0, slot])

    each_slot(first)
    pl.semaphore_wait(ready, N_MODE - 1)
    send_to_modes(plane_out.at[0], mode_in.at[1], 4)

    wait(blank, (N_MER - 1) * GROUPS, recv_sems.at[2])
    emit = send_to_planes(mode_out.at[0], plane_in.at[1], 5)
    solve(mode_in.at[0], mode_out.at[0], False, True, False, solve_scratch, emit)

    wait_modes(4)
    emit = send_to_planes(mode_out.at[1], plane_in.at[2], 6)
    solve(mode_in.at[1], mode_out.at[1], True, False, True, solve_scratch, emit)

    def multiplier(slot):
        adjoint_planes(plane_in.at[1, slot], t_ref, c_ref, s_planes.at[slot])

    wait_planes(5)
    each_slot(multiplier)

    def second(slot):
        state_planes(parts_of(plane_in.at[2, slot]), t_ref, c_ref, planes)
        finish(t_ref, c_ref, plane_in.at[1, slot], planes, s_planes.at[slot], plane_out.at[1, slot])

    wait_planes(6)
    each_slot(second)
    send_to_modes(plane_out.at[1], mode_in.at[2], 7)

    wait_modes(7)
    emit = send_to_planes(mode_out.at[2], plane_in.at[3], 8)
    solve(mode_in.at[2], mode_out.at[2], False, True, True, solve_scratch, emit)

    def third(slot):
        s_in = plane_in.at[3, slot]
        adjoint_planes(s_in, t_ref, c_ref, s_planes.at[slot])
        finish(
            t_ref, c_ref, s_in, u_planes.at[slot], s_planes.at[slot], plane_out.at[2, slot]
        )
        native_in[slot, mode] = plane_out[2, slot, :, mine]

        def send_gradient(other, core):
            theirs = pl.ds(pl.multiple_of(order_of(other) * 8, 8), 8)
            send(plane_out.at[2, slot, :, theirs], native_in.at[slot, mode], other, mer, sems, 9)

        each_group(mode, (0, 1), send_gradient)

    wait_planes(8)
    each_slot(third)
    sent.append((9, 2 * (N_MODE - 1) * N_MER, (N_MODE - 1) * N_MER, 8))
    wait_either(double, blank, N_MER * (GROUPS - 2), N_MER * (GROUPS - 1), recv_sems.at[9])
    turned = lax.rem(lax.rem(mer, 4) + mer // 4, 4)
    copies = [pltpu.make_async_copy(native_in.at[0], out_hbm.at[0:N_MODE], copy_sems.at[2])]
    for index in range(SPARE):
        owner = 2 * lax.rem(index + turned, 4)
        copies.append(
            pltpu.make_async_copy(
                native_in.at[1, owner], out_hbm.at[N_MODE + index], copy_sems.at[3 + index]
            )
        )
    for copy in copies:
        copy.start()
    for at, tiles_double, tiles_single, rows_each in sent:
        wait_either(double, blank, tiles_double, tiles_single, send_sems.at[at], rows_each)
    for copy in copies:
        copy.wait()


def program(state, cotangent, mass, inverse, derivative, table):
    by_mode = (2, N_MODE, N_MER, 8, LANES)
    by_native = (2, N_MODE, 2, 8, 8, LANES)
    by_plane = (2, 2, COUNT // 2, 8, LANES)
    vmem = pl.BlockSpec(memory_space=pltpu.VMEM)
    hbm = pl.BlockSpec(memory_space=pl.ANY)

    def scratch(count, shape):
        return pltpu.VMEM((count,) + shape, F32)

    return pl.pallas_call(
        program_kernel,
        out_shape=jax.ShapeDtypeStruct((GROUPS, 2, 8, 8, LANES), F32),
        in_specs=[vmem, hbm, vmem, vmem, vmem, hbm],
        out_specs=hbm,
        scratch_shapes=[
            pltpu.VMEM((NODE, NODE, ELEM_DEV * LANES), F32),
            pltpu.VMEM((8, 2 * HALF, HALF), BF16),
            pltpu.SemaphoreType.DMA((6,)),
            pltpu.VMEM((PADDED * ELEM_DEV, LANES), F32),
            scratch(2, by_native),
            pltpu.VMEM(by_native, F32),
            scratch(3, by_mode),
            scratch(3, by_mode),
            scratch(3, by_plane),
            scratch(4, by_plane),
            pltpu.VMEM((2, 16, LANES), F32),
            scratch(N_MER, (2, 16, LANES)),
            scratch(2, (4, HALF, 2 * LANES)),
            scratch(4, (HALF, 2 * LANES)),
            scratch(2, (4, HALF, LANES)),
            scratch(5, (HALF, LANES)),
            pltpu.VMEM((PADDED, ELEMENTS), F32),
            pltpu.SemaphoreType.REGULAR,
            pltpu.VMEM((2 * COUNT, 8, LANES), F32),
            pltpu.SemaphoreType.DMA((10,)),
            pltpu.SemaphoreType.DMA((10,)),
            *SOLVE_SCRATCH,
        ],
        compiler_params=pltpu.CompilerParams(
            collective_id=0, has_side_effects=True, vmem_limit_bytes=60 << 20
        ),
        name="program",
    )(state, cotangent, mass, inverse, derivative, table)


def shards(cotangent, checkpoint, mass, inv_radius_sq, derivative):
    table = jnp.asarray(tables())
    return tiles_to_native(program(checkpoint, cotangent, mass, inv_radius_sq, derivative, table))


def solution(mesh):
    return jax.shard_map(
        shards,
        mesh=mesh,
        in_specs=(
            P(None, None, ("mer", "mode")),
            P(None, None, ("mer", "mode")),
            P(None, None, "mer"),
            P(None, None, "mer"),
            P(),
        ),
        out_specs=P(None, None, ("mer", "mode")),
        check_vma=False,
    )
```

```python
import functools
import math

import jax
import jax.numpy as jnp
import ml_dtypes
import numpy as np
from jax import lax
from jax.experimental import pallas as pl
from jax.experimental.pallas import tpu as pltpu
from jax.sharding import PartitionSpec as P

NODE = 9
NODES = NODE * NODE
RADIAL = 8
ITERS = 4
MODES = 512
HALF = 256
PLANES = 1024
ELEMENTS = 256
N_MODE = 8
N_MER = 16
ELEM_DEV = 16
GROUPS = 11
PADDED = GROUPS * 8
LANES = 128
AZIMUTH_WEIGHT = 4.0
HIGHEST = lax.Precision.HIGHEST
F32 = jnp.float32
BF16 = jnp.bfloat16


def tables():
    order = np.arange(HALF).reshape(4, 2, HALF // N_MODE).transpose(1, 0, 2).reshape(-1)
    out = []
    for wave in (np.cos, np.sin):
        for odd in range(2):
            index = np.outer(np.arange(HALF), 2 * order + odd) % PLANES
            values = wave(index.astype(np.float64) * (2.0 * math.pi / PLANES)).astype(np.float32)
            high = values.astype(ml_dtypes.bfloat16)
            low = (values - high.astype(np.float32)).astype(ml_dtypes.bfloat16)
            out.append((high, low))
    both = [np.concatenate(pair) for pair in out]
    turned = [np.concatenate([high.T, low.T]) for high, low in out]
    return np.stack(both + turned)


def mix(first, second):
    shape = first.shape
    axis = len(shape) - 2
    low = lax.broadcasted_iota(jnp.int32, shape, axis) % 4 < 2
    return (
        jnp.where(low, first, pltpu.roll(second, 2, axis)),
        jnp.where(low, pltpu.roll(first, 6, axis), second),
    )


def exchange(tiles):
    tiles = list(tiles)
    axis = tiles[0].ndim - 1
    block = lax.broadcasted_iota(jnp.int32, tiles[0].shape, axis) // 16
    for bit in (1, 2, 4):
        clear = (block & bit) == 0
        for at in range(8):
            if at & bit:
                continue
            one, two = tiles[at], tiles[at | bit]
            tiles[at] = jnp.where(clear, one, pltpu.roll(two, 16 * bit, axis))
            tiles[at | bit] = jnp.where(clear, pltpu.roll(one, LANES - 16 * bit, axis), two)
    return tiles


def native_to_tiles(x_ref, out_ref, rows, turn):
    rows[pl.ds(NODES * ELEM_DEV, PADDED * ELEM_DEV - NODES * ELEM_DEV), :] = jnp.zeros(
        ((PADDED - NODES) * ELEM_DEV, LANES), F32
    )
    for i in range(NODE):
        for e in range(ELEM_DEV):
            rows[pl.ds(i * NODE * ELEM_DEV + e, NODE, stride=ELEM_DEV), :] = x_ref[
                i, :, e * LANES : (e + 1) * LANES
            ]
    for group in range(GROUPS):
        turned = rows[group * LANES : (group + 1) * LANES, :].T
        turn[0, group] = turned[:64]
        turn[1, group] = turned[64:]
        for odd in range(2):
            real = turn[0, group, pl.ds(odd, 32, stride=2), :].reshape(4, 8, LANES)
            imag = turn[1, group, pl.ds(odd, 32, stride=2), :].reshape(4, 8, LANES)
            one, two = mix(real, imag)
            out_ref[group // 8, group % 8, odd] = jnp.stack([one, two], axis=1).reshape(8, 8, LANES)


def tiles_to_native_kernel(t_hbm, out_hbm, tiles_in, rows, turn, native, in_sems, out_sems):
    parts = ((0, 6, 0, 5), (6, GROUPS, 5, NODE))
    loads, stores = [], []
    for at, (start, stop, first, last) in enumerate(parts):
        groups, nodes = pl.ds(start, stop - start), pl.ds(first, last - first)
        loads.append(
            pltpu.make_async_copy(t_hbm.at[groups], tiles_in.at[groups], in_sems.at[at])
        )
        stores.append(pltpu.make_async_copy(native.at[nodes], out_hbm.at[nodes], out_sems.at[at]))
        loads[at].start()
    for at, (start, stop, first, last) in enumerate(parts):
        loads[at].wait()
        for group in range(start, stop):
            for odd in range(2):
                tiles = tiles_in[group, odd].reshape(4, 2, 8, LANES)
                real, imag = mix(tiles[:, 0], tiles[:, 1])
                turn[0, group, pl.ds(odd, 32, stride=2), :] = real.reshape(32, LANES)
                turn[1, group, pl.ds(odd, 32, stride=2), :] = imag.reshape(32, LANES)
            both = jnp.concatenate([turn[0, group], turn[1, group]], axis=0)
            rows[group * LANES : (group + 1) * LANES, :] = both.T
        for i in range(first, last):
            for e in range(ELEM_DEV):
                native[i, :, e * LANES : (e + 1) * LANES] = rows[
                    pl.ds(i * NODE * ELEM_DEV + e, NODE, stride=ELEM_DEV), :
                ]
        stores[at].start()
    for store in stores:
        store.wait()


def tiles_to_native(tiles):
    hbm = pl.BlockSpec(memory_space=pltpu.HBM)
    shape = (NODE, NODE, ELEM_DEV * LANES)
    return pl.pallas_call(
        tiles_to_native_kernel,
        out_shape=jax.ShapeDtypeStruct(shape, F32),
        in_specs=[hbm],
        out_specs=hbm,
        scratch_shapes=[
            pltpu.VMEM((GROUPS, 2, 8, 8, LANES), F32),
            pltpu.VMEM((PADDED * ELEM_DEV, LANES), F32),
            pltpu.VMEM((2, GROUPS, 64, LANES), F32),
            pltpu.VMEM(shape, F32),
            pltpu.SemaphoreType.DMA((2,)),
            pltpu.SemaphoreType.DMA((2,)),
        ],
        compiler_params=pltpu.CompilerParams(vmem_limit_bytes=62 << 20),
        name="tiles_to_native",
    )(tiles)


def stiffness_tables(d_ref, k_ref):
    def dot(a, b):
        return jnp.dot(a, b, precision=HIGHEST, preferred_element_type=F32)

    derivative = d_ref[...]
    stiffness = lax.dot_general(
        derivative, derivative, (((0,), (0,)), ((), ())), precision=HIGHEST, preferred_element_type=F32
    )

    def pick(shape, node_axis, outer):
        node = lax.broadcasted_iota(jnp.int32, shape, node_axis)
        other = lax.broadcasted_iota(jnp.int32, shape, 1 - node_axis)
        place = node // NODE if outer else node % NODE
        return jnp.where((place == other) & (node < NODES), 1.0, 0.0).astype(F32)

    outer, inner = pick((PADDED, NODE), 0, True), pick((PADDED, NODE), 0, False)
    outer_t, inner_t = pick((NODE, PADDED), 1, True), pick((NODE, PADDED), 1, False)
    whole = dot(dot(outer, stiffness), outer_t) * dot(inner, inner_t)
    whole = whole + dot(dot(inner, stiffness), inner_t) * dot(outer, outer_t)
    high = whole.astype(BF16).astype(F32)
    low = whole - high
    shape = (PADDED, 2 * PADDED)
    node = lax.broadcasted_iota(jnp.int32, shape, 0)
    column = lax.broadcasted_iota(jnp.int32, shape, 1)
    either = (node // 8 == column // 16) & (node % 8 == column % 8)
    first = either & (column % 16 < 8)
    top = dot(high, jnp.where(either, 1.0, 0.0).astype(F32))
    bottom = dot(low, jnp.where(first, 1.0, 0.0).astype(F32))
    k_ref[...] = jnp.concatenate([top, bottom], axis=0).astype(BF16)


def metric_rows(mass_ref, inverse_ref, rows, out_ref):
    lane = lax.broadcasted_iota(jnp.int32, (ELEM_DEV, LANES), 1) % ELEM_DEV
    element = lax.broadcasted_iota(jnp.int32, (ELEM_DEV, LANES), 0)
    repeat = jnp.where(lane == element, 1.0, 0.0).astype(F32)
    shape = (PADDED, LANES)
    node = lax.broadcasted_iota(jnp.int32, shape, 0)
    block = lax.broadcasted_iota(jnp.int32, shape, 1) // ELEM_DEV
    keep = (node % 8 == block) & (node < NODES)
    for kind, ref in ((0, mass_ref), (1, inverse_ref)):
        for i in range(NODE):
            rows[i * NODE : (i + 1) * NODE, :ELEM_DEV] = ref[i]
        values = jnp.dot(
            rows[:PADDED, :ELEM_DEV], repeat, precision=HIGHEST, preferred_element_type=F32
        )
        values = jnp.where(keep, values, 0.0).reshape(GROUPS, 8, LANES)
        out_ref[kind, :GROUPS] = jnp.sum(values, axis=1)
        out_ref[kind, GROUPS:] = jnp.zeros((16 - GROUPS, LANES), F32)


def face_tables():
    node = np.arange(PADDED)[:, None]
    element = np.arange(ELEMENTS)[None, :]
    inside = node < NODES
    marks = [
        (node % NODE == NODE - 1) & (element < ELEMENTS - RADIAL) & inside,
        (node % NODE == 0) & (element >= RADIAL) & inside,
        (node // NODE == NODE - 1) & (element % RADIAL != RADIAL - 1) & inside,
        (node // NODE == 0) & (element % RADIAL != 0) & inside,
    ]
    marks = np.stack(marks).astype(np.float32)
    return np.concatenate([marks, marks.sum(axis=0, keepdims=True)])


def metric_tables(m_ref, mode_group, place, mass, diag, faces, turn):
    inverse = diag.at[0]
    for kind, out in ((0, mass), (1, inverse)):
        for h in range(2):
            rows = exchange([m_ref[8 * h + at, kind] for at in range(8)])
            for at in range(8):
                for group in range(GROUPS):
                    turn[h, group, at : at + 1] = rows[at][group : group + 1]
            for group in range(GROUPS):
                out[group * 8 : (group + 1) * 8, h * LANES : (h + 1) * LANES] = turn[h, group, 0:8]
    values = inverse[...]
    for n in range(4):
        offset = lax.rem(place, 8) // 2 * 8 + lax.rem(place, 2) * 2 + n // 2 * 4 + n % 2
        number = mode_group * 64 + 2 * offset + place // 8
        fraction = number.astype(F32) / MODES
        diag[n] = mass[...] * (1.0 + AZIMUTH_WEIGHT * fraction * fraction * values) + faces[4]


def owner_of(extra_group, place):
    return 2 * ((extra_group + place % 4 + place // 4) % 4)


CHUNKS = ((0, 0, 3), (0, 3, 6), (0, 6, 8), (1, 0, 3))


def load_tiles(b_ref, turn, weight, out, by_owner):
    for slot, start, stop in CHUNKS:
        for h in range(2):
            tiles = []
            for place in range(8 * h, 8 * h + 8):
                if slot and by_owner:
                    tiles.append(
                        jnp.stack([b_ref[1, owner_of(at, place), place] for at in range(start, stop)])
                    )
                else:
                    tiles.append(b_ref[slot, start:stop, place])
            tiles = exchange(tiles)
            for at in range(8):
                turn[h, 8 * slot + start : 8 * slot + stop, at * 8 : (at + 1) * 8] = tiles[at]
    for s in range(8):
        for h in range(2):
            lanes = slice(h * LANES, (h + 1) * LANES)
            for group in range(GROUPS):
                rows = slice(group * 8, (group + 1) * 8)
                value = turn[h, group, pl.ds(s, 8, stride=8), :]
                if weight is not None:
                    value = value * weight[rows, lanes]
                out[s, rows, lanes] = value


OWNED = (
    ((1, 0), (1, 1), (1, 2), (0, 0), (0, 2), (0, 4), (0, 6)),
    ((0, 1), (0, 3), (0, 5), (0, 7)),
)


def store_tiles(value_of, turn, out_ref, emit):
    for core in range(2):
        for s in range(8):
            for slot, at_group in OWNED[core]:
                group = 8 * slot + at_group
                for h in range(2):
                    turn[h, group, pl.ds(s, 8, stride=8), :] = value_of(
                        s, slice(group * 8, (group + 1) * 8), slice(h * LANES, (h + 1) * LANES)
                    )
        for slot, at_group in OWNED[core]:
            for h in range(2):
                group = 8 * slot + at_group
                tiles = exchange([turn[h, group, at * 8 : (at + 1) * 8] for at in range(8)])
                for at in range(8):
                    place = 8 * h + at
                    owner = owner_of(at_group, place) if slot else at_group
                    out_ref[slot, owner, place] = tiles[at]
        emit(core)


def total(parts):
    half = parts[:, :LANES] + parts[:, LANES:]
    return jnp.broadcast_to(jnp.sum(half, axis=(0, 1), keepdims=True), (1, ELEMENTS))


def solve(b_ref, out_ref, weigh_in, weigh_out, by_owner, scratch, emit):
    mass, diag, faces, k_ref, r, p, q, alphas, turn, units = scratch
    load_tiles(b_ref, turn, mass if weigh_in else None, p.at[0], by_owner)

    def operate(sweep, n, alpha, beta):
        norm = curve = bend = jnp.zeros((8, ELEMENTS), F32)
        last = sweep == ITERS - 1
        for s in (n // 2 * 4 + n % 2, n // 2 * 4 + 2 + n % 2):
            for tile in range(GROUPS):
                rows = slice(8 * tile, 8 * tile + 8)
                if sweep == 0:
                    rest = now = p[0, s, rows]
                else:
                    before = p[sweep - 1, s, rows]
                    rest = (before if sweep == 1 else r[s, rows]) - alpha * q[s, rows]
                    now = rest + beta * before
                    p[sweep, s, rows] = now
                    if not last:
                        r[s, rows] = rest
                norm = norm + rest * rest
                high = now.astype(BF16).astype(F32)
                unit = jnp.concatenate([high, now - high], axis=0).astype(BF16)
                units[s, 16 * tile : 16 * tile + 16] = unit
            image = jnp.dot(k_ref[...], units[s], preferred_element_type=F32)

            def moved(tile, shift, s=s):
                return pltpu.roll(p[sweep, s, 8 * tile : 8 * tile + 8], shift, 1)

            for tile in range(GROUPS):
                rows = slice(8 * tile, 8 * tile + 8)
                now = p[sweep, s, rows]
                value = image[rows] + image[PADDED + 8 * tile : PADDED + 8 * tile + 8]
                value = value + diag[n, rows] * now
                if tile not in (0, 9):
                    value = value - faces[0, rows] * moved(tile - 1, ELEMENTS - RADIAL)
                if tile not in (8, 10):
                    value = value - faces[1, rows] * moved(tile + 1, RADIAL)
                if tile < 2:
                    value = value - faces[3, rows] * moved(tile + 9, 1)
                if tile > 8:
                    value = value - faces[2, rows] * moved(tile - 9, ELEMENTS - 1)
                curve = curve + now * value
                if not last:
                    q[s, rows] = value
                    bend = bend + value * value
        curve = total(curve)
        alpha = total(norm) / curve
        alphas[sweep * 4 + n] = alpha
        if last:
            return alpha, None
        return alpha, jnp.maximum(alpha * (total(bend) / curve) - 1.0, 0.0)

    steps = [(None, None)] * 4
    for sweep in range(ITERS):
        steps = [operate(sweep, n, *steps[n]) for n in range(4)]

    def value_of(s, rows, lanes):
        n = s // 4 * 2 + s % 2
        value = alphas[n, :, lanes] * p[0, s, rows, lanes]
        for sweep in range(1, ITERS):
            value = value + alphas[sweep * 4 + n, :, lanes] * p[sweep, s, rows, lanes]
        return value * mass[rows, lanes] if weigh_out else value

    store_tiles(value_of, turn, out_ref, emit)


FIELD = pltpu.VMEM((8, PADDED, ELEMENTS), F32)
SOLVE_SCRATCH = [
    pltpu.VMEM((PADDED, ELEMENTS), F32),
    pltpu.VMEM((4, PADDED, ELEMENTS), F32),
    pltpu.VMEM((5, PADDED, ELEMENTS), F32),
    pltpu.VMEM((2 * PADDED, 2 * PADDED), BF16),
    FIELD,
    pltpu.VMEM((ITERS, 8, PADDED, ELEMENTS), F32),
    FIELD,
    pltpu.VMEM((ITERS * 4, 1, ELEMENTS), F32),
    pltpu.VMEM((2, GROUPS, 64, LANES), F32),
    pltpu.VMEM((8, 2 * PADDED, ELEMENTS), BF16),
]


def split(value):
    high = value.astype(BF16)
    return high, (value - high.astype(F32)).astype(BF16)


def apply(t_ref, which, field):
    high, low = split(field)
    width = field.shape[1]
    if width == LANES:
        both = jnp.concatenate([high, low], axis=1)
        out = jnp.dot(t_ref[which], both, preferred_element_type=F32)
        return out[:HALF, :LANES] + out[:HALF, LANES:] + out[HALF:, :LANES]
    out = jnp.dot(t_ref[which], high, preferred_element_type=F32)
    out = out[:HALF] + out[HALF:]
    return out + jnp.dot(t_ref[which, :HALF], low, preferred_element_type=F32)


def parts_of(u_ref):
    out = []
    for odd in range(2):
        tiles = u_ref[odd].reshape(32, 2, 8, LANES)
        one, two = mix(tiles[:, 0], tiles[:, 1])
        out.append((one.reshape(HALF, LANES), two.reshape(HALF, LANES)))
    return out


def parts_to(out_ref, parts):
    for odd in range(2):
        real, imag = parts[odd]
        one, two = mix(real.reshape(32, 8, LANES), imag.reshape(32, 8, LANES))
        out_ref[odd] = jnp.stack([one, two], axis=1).reshape(64, 8, LANES)


def column_tables():
    row = np.arange(HALF)
    modes = [2 * ((row // 32 % 4 * 2 + row // 128) * 32 + row % 32) + odd for odd in range(2)]
    columns = [mode / MODES for mode in modes]
    columns += [np.where(mode == 0, 1.0 / PLANES, 2.0 / PLANES) for mode in modes]
    columns.append(np.where(row % 2 == 0, 1.0, -1.0))
    return np.repeat(np.stack(columns).astype(np.float32)[:, :, None], LANES, axis=2)


def signs(c_ref, width):
    return jnp.concatenate([c_ref[4]] * (width // LANES), axis=1)


def without_first(value):
    head = lax.broadcasted_iota(jnp.int32, (8, value.shape[1]), 0) == 0
    return jnp.concatenate([jnp.where(head, 0.0, value[:8]), value[8:]], axis=0)


def to_planes(t_ref, c_ref, cos_fields, sin_fields, out_ref):
    sign = signs(c_ref, cos_fields[0].shape[1])
    cos_even, cos_odd = apply(t_ref, 0, cos_fields[0]), apply(t_ref, 1, cos_fields[1])
    sin_even, sin_odd = apply(t_ref, 2, sin_fields[0]), apply(t_ref, 3, sin_fields[1])
    quarter_cos = jnp.sum(sign * cos_fields[0], axis=0, keepdims=True)
    quarter_sin = jnp.sum(sign * sin_fields[1], axis=0, keepdims=True)
    cos, sin = cos_even + cos_odd, sin_even + sin_odd
    out_ref[0] = cos - sin
    out_ref[1] = cos + sin
    cos, sin = cos_even - cos_odd, sin_even - sin_odd
    out_ref[2] = cos + sin
    out_ref[3] = cos - sin
    out_ref[1, 0:1] = quarter_cos - quarter_sin
    out_ref[3, 0:1] = quarter_cos + quarter_sin


def from_planes(t_ref, c_ref, values):
    sign = signs(c_ref, values[0].shape[1])
    quarter, three = values[1][0:1], values[3][0:1]
    one = values[0]
    two, four = without_first(values[1]), without_first(values[3])
    plus, minus = one + two, one - two
    plus_far, minus_far = values[2] + four, values[2] - four
    a_even = apply(t_ref, 4, plus + plus_far) + sign * (quarter + three)
    a_odd = apply(t_ref, 5, plus - plus_far)
    b_even = -apply(t_ref, 6, minus - minus_far)
    b_odd = -apply(t_ref, 7, minus + minus_far) - sign * (quarter - three)
    return (a_even, b_even), (a_odd, b_odd)


def state_planes(parts, t_ref, c_ref, out_ref):
    cos_fields, sin_fields = [], []
    for odd in range(2):
        real, imag = parts[odd]
        fraction = c_ref[odd]
        cos_fields.append(jnp.concatenate([real, -fraction * imag], axis=1))
        sin_fields.append(jnp.concatenate([imag, fraction * real], axis=1))
    to_planes(t_ref, c_ref, cos_fields, sin_fields, out_ref)


def first_stage(u_ref, t_ref, c_ref, planes, out_ref):
    parts = parts_of(u_ref)
    state_planes(parts, t_ref, c_ref, planes)
    values = [planes[at, :, :LANES] * planes[at, :, LANES:] for at in range(4)]
    found = from_planes(t_ref, c_ref, values)
    out = []
    for odd in range(2):
        weight = c_ref[2 + odd]
        out.append(tuple(parts[odd][c] - weight * found[odd][c] for c in range(2)))
    parts_to(out_ref, out)


def adjoint_planes(s_ref, t_ref, c_ref, out_ref):
    parts = parts_of(s_ref)
    weights = [c_ref[2 + odd] for odd in range(2)]
    to_planes(
        t_ref,
        c_ref,
        [weights[odd] * parts[odd][0] for odd in range(2)],
        [weights[odd] * parts[odd][1] for odd in range(2)],
        out_ref,
    )


def finish(t_ref, c_ref, s_ref, planes, adjoint, out_ref):
    values = []
    for at in range(4):
        factor = adjoint[at]
        values.append(planes[at] * jnp.concatenate([factor, factor], axis=1))
    found = from_planes(t_ref, c_ref, values)
    parts = parts_of(s_ref)
    out = []
    for odd in range(2):
        fraction = c_ref[odd]
        a, b = found[odd]
        out.append(
            (
                parts[odd][0] - a[:, LANES:] - fraction * b[:, :LANES],
                parts[odd][1] - b[:, LANES:] + fraction * a[:, :LANES],
            )
        )
    parts_to(out_ref, out)


COUNT = N_MODE * N_MER
SPARE = GROUPS - 8


def send(source, target, mode, mer, sems, at):
    pltpu.make_async_remote_copy(
        src_ref=source,
        dst_ref=target,
        send_sem=sems[0].at[at],
        recv_sem=sems[1].at[at],
        device_id={"mode": mode, "mer": mer},
        device_id_type=pl.DeviceIdType.MESH,
    ).start()


def wait(blank, tiles, sem, rows=8):
    whole = blank.at[pl.ds(0, tiles), pl.ds(0, rows)]
    pltpu.make_async_copy(whole, whole, sem).wait()


def wait_either(double, blank, tiles_double, tiles_single, sem, rows=8):
    @pl.when(double)
    def _():
        wait(blank, tiles_double, sem, rows)

    @pl.when(jnp.logical_not(double))
    def _():
        wait(blank, tiles_single, sem, rows)


def place_at(mer, k):
    step = lax.rem(7 * k, N_MER)
    y = lax.rem(lax.rem(mer, 4) + lax.rem(step, 4), 4)
    z = lax.rem(mer // 4 + step // 4, 4)
    return z * 4 + y


def extra(x, mer):
    turn = lax.rem(lax.rem(mer, 4) + mer // 4, 4)
    return lax.rem(x + 4 - turn, 4)


def groups_on(mode, core):
    x = mode // 2
    return [2 * lax.rem(x + step, 4) + core for step in (1, 3, 2, 0)]


def each_group(mode, cores, act):
    for core in cores:
        one, two, three, own = groups_on(mode, core)
        act(one, core)
        act(two, core)
        act(three, core)

        @pl.when(lax.rem(mode, 2) != core)
        def _(own=own, core=core):
            act(own, core)


def each_place(mer, act):
    def body(k, _):
        act(place_at(mer, k))
        return 0

    lax.fori_loop(1, N_MER, body, 0)


def each_other(mode, mer, cores, act):
    groups = [(other, core) for core in cores for other in groups_on(mode, core)]

    def body(place):
        for other, core in groups:
            act(other, core, place)

    each_place(mer, body)
    each_group(mode, cores, lambda other, core: act(other, core, mer))


def order_of(mode):
    return lax.rem(mode, 2) * 4 + mode // 2


def program_kernel(
    state_ref,
    cotangent_hbm,
    mass_ref,
    inverse_ref,
    d_ref,
    t_hbm,
    c_hbm,
    f_hbm,
    out_hbm,
    cotangent_in,
    t_ref,
    copy_sems,
    rows,
    native_out,
    native_in,
    mode_out,
    mode_in,
    plane_out,
    plane_in,
    metric_out,
    metric_in,
    u_planes,
    planes,
    s_planes,
    c_ref,
    ready,
    blank,
    send_sems,
    recv_sems,
    *solve_scratch,
):
    mode = lax.axis_index("mode")
    mer = lax.axis_index("mer")
    odd, eighth = mer // 8, lax.rem(mer, 8)
    row = order_of(mode) * 8 + eighth
    mine_extra = extra(mode // 2, mer)
    double = (lax.rem(mode, 2) == 0) & (mine_extra < SPARE)
    slots = jnp.where(double, 2, 1)
    sems = (send_sems, recv_sems)
    mass, diag, faces, k_ref = solve_scratch[:4]
    turn = solve_scratch[8]
    sent = []

    cotangent_copy = pltpu.make_async_copy(cotangent_hbm, cotangent_in, copy_sems.at[0])
    table_copy = pltpu.make_async_copy(t_hbm, t_ref, copy_sems.at[1])
    cotangent_copy.start()
    table_copy.start()
    constant_copies = [
        pltpu.make_async_copy(c_hbm, c_ref, copy_sems.at[6]),
        pltpu.make_async_copy(f_hbm, faces, copy_sems.at[7]),
    ]
    for copy in constant_copies:
        copy.start()
    barrier = pltpu.get_barrier_semaphore()

    def greet(semaphore, other, place):
        pl.semaphore_signal(
            semaphore,
            inc=1,
            device_id={"mode": other, "mer": place},
            device_id_type=pl.DeviceIdType.MESH,
        )

    each_group(mode, (0, 1), lambda other, core: greet(barrier, other, mer))
    each_place(mer, lambda place: greet(barrier, mode, place))
    native_to_tiles(state_ref, native_out.at[0], rows, turn)
    pl.semaphore_wait(barrier, N_MODE - 1 + N_MER - 1)
    each_group(mode, (0, 1), lambda other, core: greet(ready, other, mer))

    def each_slot(act):
        def body(k, _):
            act(slots - 1 - k)
            return 0

        lax.fori_loop(0, slots, body, 0)

    def send_to_planes(source, target, at):
        def act(other, core, place):
            def single():
                send(source.at[0, other, place], target.at[0, odd, row], other, place, sems, at)

            if core == 1:
                single()
                return
            owns_two = extra(other // 2, place) < SPARE
            pl.when(jnp.logical_not(owns_two))(single)

            @pl.when(owns_two)
            def _():
                send(source.at[:, other, place], target.at[:, odd, row], other, place, sems, at)

        def emit(core):
            each_other(mode, mer, (core,), act)
            if core == 1:
                target[:, odd, row] = source[:, mode, mer]

        sent.append((at, 16 * GROUPS - 2, 16 * GROUPS - 1, 8))
        return emit

    def wait_planes(at):
        wait_either(double, blank, 2 * (COUNT - 1), COUNT - 1, recv_sems.at[at])

    def send_to_modes(source, target, at):
        target[0, mode, mer] = source[0, odd, row]

        def act(other, core, place):
            index = order_of(other) * 8 + lax.rem(place, 8)
            piece = source.at[0, place // 8, index]
            send(piece, target.at[0, mode, mer], other, place, sems, at)

        def act_double(other, core, place):
            index = order_of(other) * 8 + lax.rem(place, 8)
            piece = source.at[:, place // 8, index]
            send(piece, target.at[:, mode, mer], other, place, sems, at)

        @pl.when(double)
        def _():
            target[1, mode, mer] = source[1, odd, row]
            each_other(mode, mer, (0, 1), act_double)

        @pl.when(jnp.logical_not(double))
        def _():
            each_other(mode, mer, (0, 1), act)

        sent.append((at, 2 * (COUNT - 1), COUNT - 1, 8))

    def wait_modes(at):
        wait_either(double, blank, 16 * GROUPS - 2, 16 * GROUPS - 1, recv_sems.at[at])

    mine = pl.ds(pl.multiple_of(order_of(mode) * 8, 8), 8)
    plane_in[0, 0, :, mine] = native_out[0, 0, mode]
    plane_in[0, 1, :, mine] = native_out[0, 1, mine_extra]

    def send_extra_state(other, core):
        index = extra(other // 2, mer)

        @pl.when(index < SPARE)
        def _():
            send(native_out.at[0, 1, index], plane_in.at[0, 1, :, mine], other, mer, sems, 0)

    def send_state(other, core):
        send(native_out.at[0, 0, other], plane_in.at[0, 0, :, mine], other, mer, sems, 0)

    each_group(mode, (0,), send_extra_state)
    each_group(mode, (0, 1), send_state)
    sent.append((0, N_MER * (GROUPS - 2), N_MER * (GROUPS - 1), 8))

    metric_rows(mass_ref, inverse_ref, rows, metric_out)
    metric_in[mer] = metric_out[...]

    def send_metric(place):
        send(metric_out, metric_in.at[mer], mode, place, sems, 3)

    each_place(mer, send_metric)
    cotangent_copy.wait()
    native_to_tiles(cotangent_in, native_out.at[1], rows, turn)
    mode_in[0, 0, :, mer] = native_out[1, 0, :, odd, eighth]
    mode_in[0, 1, 0:SPARE, mer] = native_out[1, 1, 0:SPARE, odd, eighth]

    def send_cotangent(place):
        which, at = place // 8, lax.rem(place, 8)
        send(native_out.at[1, 0, :, which, at], mode_in.at[0, 0, :, mer], mode, place, sems, 2)
        send(
            native_out.at[1, 1, 0:SPARE, which, at],
            mode_in.at[0, 1, 0:SPARE, mer],
            mode,
            place,
            sems,
            2,
        )

    each_place(mer, send_cotangent)
    sent.append((2, (N_MER - 1) * GROUPS, (N_MER - 1) * GROUPS, 8))
    sent.append((3, (N_MER - 1) * 4, (N_MER - 1) * 4, 8))

    stiffness_tables(d_ref, k_ref)
    for copy in constant_copies:
        copy.wait()
    wait(blank, (N_MER - 1) * 4, recv_sems.at[3])
    metric_tables(metric_in, mode, mer, mass, diag, faces, turn)
    table_copy.wait()

    wait_either(double, blank, 2 * (N_MODE - 1) * N_MER, (N_MODE - 1) * N_MER, recv_sems.at[0])

    def first(slot):
        first_stage(plane_in.at[0, slot], t_ref, c_ref, u_planes.at[slot], plane_out.at[0, slot])

    each_slot(first)
    pl.semaphore_wait(ready, N_MODE - 1)
    send_to_modes(plane_out.at[0], mode_in.at[1], 4)

    wait(blank, (N_MER - 1) * GROUPS, recv_sems.at[2])
    emit = send_to_planes(mode_out.at[0], plane_in.at[1], 5)
    solve(mode_in.at[0], mode_out.at[0], False, True, False, solve_scratch, emit)

    wait_modes(4)
    emit = send_to_planes(mode_out.at[1], plane_in.at[2], 6)
    solve(mode_in.at[1], mode_out.at[1], True, False, True, solve_scratch, emit)

    def multiplier(slot):
        adjoint_planes(plane_in.at[1, slot], t_ref, c_ref, s_planes.at[slot])

    wait_planes(5)
    each_slot(multiplier)

    def second(slot):
        state_planes(parts_of(plane_in.at[2, slot]), t_ref, c_ref, planes)
        finish(t_ref, c_ref, plane_in.at[1, slot], planes, s_planes.at[slot], plane_out.at[1, slot])

    wait_planes(6)
    each_slot(second)
    send_to_modes(plane_out.at[1], mode_in.at[2], 7)

    wait_modes(7)
    emit = send_to_planes(mode_out.at[2], plane_in.at[3], 8)
    solve(mode_in.at[2], mode_out.at[2], False, True, True, solve_scratch, emit)

    def third(slot):
        s_in = plane_in.at[3, slot]
        adjoint_planes(s_in, t_ref, c_ref, s_planes.at[slot])
        finish(
            t_ref, c_ref, s_in, u_planes.at[slot], s_planes.at[slot], plane_out.at[2, slot]
        )
        native_in[slot, mode] = plane_out[2, slot, :, mine]

        def send_gradient(other, core):
            theirs = pl.ds(pl.multiple_of(order_of(other) * 8, 8), 8)
            send(plane_out.at[2, slot, :, theirs], native_in.at[slot, mode], other, mer, sems, 9)

        each_group(mode, (0, 1), send_gradient)

    wait_planes(8)
    each_slot(third)
    sent.append((9, 2 * (N_MODE - 1) * N_MER, (N_MODE - 1) * N_MER, 8))
    wait_either(double, blank, N_MER * (GROUPS - 2), N_MER * (GROUPS - 1), recv_sems.at[9])
    turned = lax.rem(lax.rem(mer, 4) + mer // 4, 4)
    copies = [pltpu.make_async_copy(native_in.at[0], out_hbm.at[0:N_MODE], copy_sems.at[2])]
    for index in range(SPARE):
        owner = 2 * lax.rem(index + turned, 4)
        copies.append(
            pltpu.make_async_copy(
                native_in.at[1, owner], out_hbm.at[N_MODE + index], copy_sems.at[3 + index]
            )
        )
    for copy in copies:
        copy.start()
    for at, tiles_double, tiles_single, rows_each in sent:
        wait_either(double, blank, tiles_double, tiles_single, send_sems.at[at], rows_each)
    for copy in copies:
        copy.wait()


def program(state, cotangent, mass, inverse, derivative, *constants):
    by_mode = (2, N_MODE, N_MER, 8, LANES)
    by_native = (2, N_MODE, 2, 8, 8, LANES)
    by_plane = (2, 2, COUNT // 2, 8, LANES)
    vmem = pl.BlockSpec(memory_space=pltpu.VMEM)
    hbm = pl.BlockSpec(memory_space=pl.ANY)

    def scratch(count, shape):
        return pltpu.VMEM((count,) + shape, F32)

    return pl.pallas_call(
        program_kernel,
        out_shape=jax.ShapeDtypeStruct((GROUPS, 2, 8, 8, LANES), F32),
        in_specs=[vmem, hbm, vmem, vmem, vmem, hbm, hbm, hbm],
        out_specs=hbm,
        scratch_shapes=[
            pltpu.VMEM((NODE, NODE, ELEM_DEV * LANES), F32),
            pltpu.VMEM((8, 2 * HALF, HALF), BF16),
            pltpu.SemaphoreType.DMA((8,)),
            pltpu.VMEM((PADDED * ELEM_DEV, LANES), F32),
            scratch(2, by_native),
            pltpu.VMEM(by_native, F32),
            scratch(3, by_mode),
            scratch(3, by_mode),
            scratch(3, by_plane),
            scratch(4, by_plane),
            pltpu.VMEM((2, 16, LANES), F32),
            scratch(N_MER, (2, 16, LANES)),
            scratch(2, (4, HALF, 2 * LANES)),
            scratch(4, (HALF, 2 * LANES)),
            scratch(2, (4, HALF, LANES)),
            scratch(5, (HALF, LANES)),
            pltpu.SemaphoreType.REGULAR,
            pltpu.VMEM((2 * COUNT, 8, LANES), F32),
            pltpu.SemaphoreType.DMA((10,)),
            pltpu.SemaphoreType.DMA((10,)),
            *SOLVE_SCRATCH,
        ],
        compiler_params=pltpu.CompilerParams(
            collective_id=0, has_side_effects=True, vmem_limit_bytes=60 << 20
        ),
        name="program",
    )(state, cotangent, mass, inverse, derivative, *constants)


def shards(cotangent, checkpoint, mass, inv_radius_sq, derivative):
    constants = [jnp.asarray(values()) for values in (tables, column_tables, face_tables)]
    return tiles_to_native(
        program(checkpoint, cotangent, mass, inv_radius_sq, derivative, *constants)
    )


def solution(mesh):
    return jax.shard_map(
        shards,
        mesh=mesh,
        in_specs=(
            P(None, None, ("mer", "mode")),
            P(None, None, ("mer", "mode")),
            P(None, None, "mer"),
            P(None, None, "mer"),
            P(),
        ),
        out_specs=P(None, None, ("mer", "mode")),
        check_vma=False,
    )
```

```python
import functools
import math

import jax
import jax.numpy as jnp
import ml_dtypes
import numpy as np
from jax import lax
from jax.experimental import pallas as pl
from jax.experimental.pallas import tpu as pltpu
from jax.sharding import PartitionSpec as P

NODE = 9
NODES = NODE * NODE
RADIAL = 8
ITERS = 4
MODES = 512
HALF = 256
PLANES = 1024
ELEMENTS = 256
N_MODE = 8
N_MER = 16
ELEM_DEV = 16
GROUPS = 11
PADDED = GROUPS * 8
LANES = 128
AZIMUTH_WEIGHT = 4.0
HIGHEST = lax.Precision.HIGHEST
F32 = jnp.float32
BF16 = jnp.bfloat16


def tables():
    order = np.arange(HALF).reshape(4, 2, HALF // N_MODE).transpose(1, 0, 2).reshape(-1)
    out = []
    for wave in (np.cos, np.sin):
        for odd in range(2):
            index = np.outer(np.arange(HALF), 2 * order + odd) % PLANES
            values = wave(index.astype(np.float64) * (2.0 * math.pi / PLANES)).astype(np.float32)
            high = values.astype(ml_dtypes.bfloat16)
            low = (values - high.astype(np.float32)).astype(ml_dtypes.bfloat16)
            out.append((high, low))
    both = [np.concatenate(pair) for pair in out]
    turned = [np.concatenate([high.T, low.T]) for high, low in out]
    return np.stack(both + turned)


def mix(first, second):
    shape = first.shape
    axis = len(shape) - 2
    low = lax.broadcasted_iota(jnp.int32, shape, axis) % 4 < 2
    return (
        jnp.where(low, first, pltpu.roll(second, 2, axis)),
        jnp.where(low, pltpu.roll(first, 6, axis), second),
    )


def exchange(tiles):
    tiles = list(tiles)
    axis = tiles[0].ndim - 1
    block = lax.broadcasted_iota(jnp.int32, tiles[0].shape, axis) // 16
    for bit in (1, 2, 4):
        clear = (block & bit) == 0
        for at in range(8):
            if at & bit:
                continue
            one, two = tiles[at], tiles[at | bit]
            tiles[at] = jnp.where(clear, one, pltpu.roll(two, 16 * bit, axis))
            tiles[at | bit] = jnp.where(clear, pltpu.roll(one, LANES - 16 * bit, axis), two)
    return tiles


def native_to_tiles(x_ref, out_ref, rows, turn):
    rows[pl.ds(NODES * ELEM_DEV, PADDED * ELEM_DEV - NODES * ELEM_DEV), :] = jnp.zeros(
        ((PADDED - NODES) * ELEM_DEV, LANES), F32
    )
    for i in range(NODE):
        for e in range(ELEM_DEV):
            rows[pl.ds(i * NODE * ELEM_DEV + e, NODE, stride=ELEM_DEV), :] = x_ref[
                i, :, e * LANES : (e + 1) * LANES
            ]
    for group in range(GROUPS):
        turned = rows[group * LANES : (group + 1) * LANES, :].T
        turn[0, group] = turned[:64]
        turn[1, group] = turned[64:]
        for odd in range(2):
            real = turn[0, group, pl.ds(odd, 32, stride=2), :].reshape(4, 8, LANES)
            imag = turn[1, group, pl.ds(odd, 32, stride=2), :].reshape(4, 8, LANES)
            one, two = mix(real, imag)
            out_ref[group // 8, group % 8, odd] = jnp.stack([one, two], axis=1).reshape(8, 8, LANES)


def tiles_to_native_kernel(t_hbm, out_hbm, tiles_in, rows, turn, native, in_sems, out_sems):
    parts = ((0, 6, 0, 5), (6, GROUPS, 5, NODE))
    loads, stores = [], []
    for at, (start, stop, first, last) in enumerate(parts):
        groups, nodes = pl.ds(start, stop - start), pl.ds(first, last - first)
        loads.append(
            pltpu.make_async_copy(t_hbm.at[groups], tiles_in.at[groups], in_sems.at[at])
        )
        stores.append(pltpu.make_async_copy(native.at[nodes], out_hbm.at[nodes], out_sems.at[at]))
        loads[at].start()
    for at, (start, stop, first, last) in enumerate(parts):
        loads[at].wait()
        for group in range(start, stop):
            for odd in range(2):
                tiles = tiles_in[group, odd].reshape(4, 2, 8, LANES)
                real, imag = mix(tiles[:, 0], tiles[:, 1])
                turn[0, group, pl.ds(odd, 32, stride=2), :] = real.reshape(32, LANES)
                turn[1, group, pl.ds(odd, 32, stride=2), :] = imag.reshape(32, LANES)
            both = jnp.concatenate([turn[0, group], turn[1, group]], axis=0)
            rows[group * LANES : (group + 1) * LANES, :] = both.T
        for i in range(first, last):
            for e in range(ELEM_DEV):
                native[i, :, e * LANES : (e + 1) * LANES] = rows[
                    pl.ds(i * NODE * ELEM_DEV + e, NODE, stride=ELEM_DEV), :
                ]
        stores[at].start()
    for store in stores:
        store.wait()


def tiles_to_native(tiles):
    hbm = pl.BlockSpec(memory_space=pltpu.HBM)
    shape = (NODE, NODE, ELEM_DEV * LANES)
    return pl.pallas_call(
        tiles_to_native_kernel,
        out_shape=jax.ShapeDtypeStruct(shape, F32),
        in_specs=[hbm],
        out_specs=hbm,
        scratch_shapes=[
            pltpu.VMEM((GROUPS, 2, 8, 8, LANES), F32),
            pltpu.VMEM((PADDED * ELEM_DEV, LANES), F32),
            pltpu.VMEM((2, GROUPS, 64, LANES), F32),
            pltpu.VMEM(shape, F32),
            pltpu.SemaphoreType.DMA((2,)),
            pltpu.SemaphoreType.DMA((2,)),
        ],
        compiler_params=pltpu.CompilerParams(vmem_limit_bytes=62 << 20),
        name="tiles_to_native",
    )(tiles)


def stiffness_tables(d_ref, k_ref):
    def dot(a, b):
        return jnp.dot(a, b, precision=HIGHEST, preferred_element_type=F32)

    derivative = d_ref[...]
    stiffness = lax.dot_general(
        derivative, derivative, (((0,), (0,)), ((), ())), precision=HIGHEST, preferred_element_type=F32
    )

    def pick(shape, node_axis, outer):
        node = lax.broadcasted_iota(jnp.int32, shape, node_axis)
        other = lax.broadcasted_iota(jnp.int32, shape, 1 - node_axis)
        place = node // NODE if outer else node % NODE
        return jnp.where((place == other) & (node < NODES), 1.0, 0.0).astype(F32)

    outer, inner = pick((PADDED, NODE), 0, True), pick((PADDED, NODE), 0, False)
    outer_t, inner_t = pick((NODE, PADDED), 1, True), pick((NODE, PADDED), 1, False)
    whole = dot(dot(outer, stiffness), outer_t) * dot(inner, inner_t)
    whole = whole + dot(dot(inner, stiffness), inner_t) * dot(outer, outer_t)
    high = whole.astype(BF16).astype(F32)
    low = whole - high
    top = jnp.concatenate([high, high], axis=1)
    bottom = jnp.concatenate([low, jnp.zeros_like(low)], axis=1)
    k_ref[...] = jnp.concatenate([top, bottom], axis=0).astype(BF16)


def metric_rows(mass_ref, inverse_ref, rows, out_ref):
    lane = lax.broadcasted_iota(jnp.int32, (ELEM_DEV, LANES), 1) % ELEM_DEV
    element = lax.broadcasted_iota(jnp.int32, (ELEM_DEV, LANES), 0)
    repeat = jnp.where(lane == element, 1.0, 0.0).astype(F32)
    shape = (PADDED, LANES)
    node = lax.broadcasted_iota(jnp.int32, shape, 0)
    block = lax.broadcasted_iota(jnp.int32, shape, 1) // ELEM_DEV
    keep = (node % 8 == block) & (node < NODES)
    for kind, ref in ((0, mass_ref), (1, inverse_ref)):
        for i in range(NODE):
            rows[i * NODE : (i + 1) * NODE, :ELEM_DEV] = ref[i]
        values = jnp.dot(
            rows[:PADDED, :ELEM_DEV], repeat, precision=HIGHEST, preferred_element_type=F32
        )
        values = jnp.where(keep, values, 0.0).reshape(GROUPS, 8, LANES)
        out_ref[kind, :GROUPS] = jnp.sum(values, axis=1)
        out_ref[kind, GROUPS:] = jnp.zeros((16 - GROUPS, LANES), F32)


def metric_tables(m_ref, mode_group, place, mass, diag, faces, turn):
    inverse = diag.at[0]
    for kind, out in ((0, mass), (1, inverse)):
        for h in range(2):
            rows = exchange([m_ref[8 * h + at, kind] for at in range(8)])
            for at in range(8):
                for group in range(GROUPS):
                    turn[h, group, at : at + 1] = rows[at][group : group + 1]
            for group in range(GROUPS):
                out[group * 8 : (group + 1) * 8, h * LANES : (h + 1) * LANES] = turn[h, group, 0:8]
    shape = (PADDED, ELEMENTS)
    node = lax.broadcasted_iota(jnp.int32, shape, 0)
    element = lax.broadcasted_iota(jnp.int32, shape, 1)
    inside = node < NODES
    upper = (node % NODE == NODE - 1) & (element < ELEMENTS - RADIAL) & inside
    lower = (node % NODE == 0) & (element >= RADIAL) & inside
    outer = (node // NODE == NODE - 1) & (element % RADIAL != RADIAL - 1) & inside
    inner = (node // NODE == 0) & (element % RADIAL != 0)
    marks = [jnp.where(mark, 1.0, 0.0).astype(F32) for mark in (upper, lower, outer, inner)]
    for at in range(4):
        faces[at] = marks[at]
    count = marks[0] + marks[1] + marks[2] + marks[3]
    values = inverse[...]
    for n in range(4):
        offset = lax.rem(place, 8) // 2 * 8 + lax.rem(place, 2) * 2 + n // 2 * 4 + n % 2
        number = mode_group * 64 + 2 * offset + place // 8
        fraction = number.astype(F32) / MODES
        diag[n] = mass[...] * (1.0 + AZIMUTH_WEIGHT * fraction * fraction * values) + count


def owner_of(extra_group, place):
    return 2 * ((extra_group + place % 4 + place // 4) % 4)


PAIRS = (((0, 2), (4, 6), (8, 9), (10,)), ((1, 3), (5, 7)))


def load_tiles(b_ref, half, turn, weight, out, by_owner):
    rows = slice(4 * half, 4 * half + 4)

    def piece(group, place):
        if group < 8:
            return b_ref[0, group, place, rows]
        return b_ref[1, owner_of(group - 8, place) if by_owner else group - 8, place, rows]

    for at_pair, pair in enumerate(PAIRS[0] + PAIRS[1]):
        for h in range(2):
            tiles = []
            for place in range(8 * h, 8 * h + 8):
                tiles.append(
                    jnp.concatenate([piece(pair[0], place), piece(pair[-1], place)], axis=0)
                )
            tiles = exchange(tiles)
            for at in range(8):
                turn[h, at_pair, at * 8 : (at + 1) * 8] = tiles[at]
            lanes = slice(h * LANES, (h + 1) * LANES)
            for which, group in enumerate(pair):
                nodes = slice(group * 8, (group + 1) * 8)
                for s in range(4):
                    value = turn[h, at_pair, pl.ds(4 * which + s, 8, stride=8), :]
                    if weight is not None:
                        value = value * weight[nodes, lanes]
                    out[4 * half + s, nodes, lanes] = value


def store_tiles(value_of, half, turn, out_ref, emit):
    rows = slice(4 * half, 4 * half + 4)
    for core in range(2):
        for at_pair, pair in enumerate(PAIRS[core]):
            for h in range(2):
                lanes = slice(h * LANES, (h + 1) * LANES)
                for which, group in enumerate(pair):
                    for s in range(4):
                        turn[h, 4 * core + at_pair, pl.ds(4 * which + s, 8, stride=8), :] = value_of(
                            4 * half + s, slice(group * 8, (group + 1) * 8), lanes
                        )
                tiles = [turn[h, 4 * core + at_pair, at * 8 : (at + 1) * 8] for at in range(8)]
                tiles = exchange(tiles)
                for which, group in enumerate(pair):
                    for at in range(8):
                        place = 8 * h + at
                        owner = owner_of(group - 8, place) if group >= 8 else group
                        out_ref[group // 8, owner, place, rows] = tiles[at][
                            4 * which : 4 * which + 4
                        ]
        emit(core, half)


def total(parts):
    half = parts[:, :LANES] + parts[:, LANES:]
    return jnp.broadcast_to(jnp.sum(half, axis=(0, 1), keepdims=True), (1, ELEMENTS))


def fold(value):
    return jnp.sum(value.reshape(GROUPS, 8, ELEMENTS), axis=0)


def solve(b_ref, out_ref, half, weigh_in, weigh_out, by_owner, scratch, emit):
    mass, diag, faces, k_ref, r, p, q, alphas, turn = scratch
    load_tiles(b_ref, half, turn, mass if weigh_in else None, r, by_owner)
    modes = (2 * half, 2 * half + 1)

    def rows_of(n):
        return (4 * half + n % 2, 4 * half + 2 + n % 2)

    def square(n):
        one, two = rows_of(n)
        return total(fold(r[one] * r[one]) + fold(r[two] * r[two]))

    norms = tuple(square(n) for n in modes)
    for n in modes:
        for s in rows_of(n):
            p[ITERS - 1, s] = jnp.zeros((PADDED, ELEMENTS), F32)
    empty = jnp.zeros((8, ELEMENTS), F32)

    def operate(sweep, before, n, beta, norm):
        curve = None
        for s in rows_of(n):
            now = r[s] + beta * p[before, s]
            p[sweep, s] = now
            high = now.astype(BF16).astype(F32)
            halves = jnp.concatenate([high, now - high], axis=0).astype(BF16)
            image = jnp.dot(k_ref[...], halves, preferred_element_type=F32)
            ahead = pltpu.roll(now[: PADDED - 8], ELEMENTS - RADIAL, 1)
            behind = pltpu.roll(now[8:], RADIAL, 1)
            image = (
                image[:PADDED]
                + image[PADDED:]
                + diag[n] * now
                - faces[0] * jnp.concatenate([empty, ahead], axis=0)
                - faces[1] * jnp.concatenate([behind, empty], axis=0)
            )
            outward = pltpu.roll(now[:16], ELEMENTS - 1, 1)
            inward = pltpu.roll(now[72:], 1, 1)
            image = jnp.concatenate(
                [
                    image[:16] - faces[3, :16] * inward,
                    image[16:72],
                    image[72:] - faces[2, 72:] * outward,
                ],
                axis=0,
            )
            q[s] = image
            part = fold(now * image)
            curve = part if curve is None else curve + part
        alpha = norm / total(curve)
        alphas[sweep * 4 + n] = alpha
        return alpha

    def reduce(n, alpha):
        part = None
        for s in rows_of(n):
            value = r[s] - alpha * q[s]
            r[s] = value
            add = fold(value * value)
            part = add if part is None else part + add
        return total(part)

    def sweep_body(sweep, carry):
        norms, betas = carry
        before = lax.rem(sweep + ITERS - 1, ITERS)
        step = [operate(sweep, before, n, betas[n % 2], norms[n % 2]) for n in modes]
        after = tuple(reduce(n, step[n % 2]) for n in modes)
        return after, tuple(after[n] / norms[n] for n in range(2))

    none = (jnp.zeros((1, ELEMENTS), F32),) * 2
    norms, betas = lax.fori_loop(0, ITERS - 1, sweep_body, (norms, none))
    for n in modes:
        operate(ITERS - 1, ITERS - 2, n, betas[n % 2], norms[n % 2])

    def value_of(s, rows, lanes):
        n = s // 4 * 2 + s % 2
        value = alphas[n, :, lanes] * p[0, s, rows, lanes]
        for sweep in range(1, ITERS):
            value = value + alphas[sweep * 4 + n, :, lanes] * p[sweep, s, rows, lanes]
        return value * mass[rows, lanes] if weigh_out else value

    store_tiles(value_of, half, turn, out_ref, emit)


FIELD = pltpu.VMEM((8, PADDED, ELEMENTS), F32)
SOLVE_SCRATCH = [
    pltpu.VMEM((PADDED, ELEMENTS), F32),
    pltpu.VMEM((4, PADDED, ELEMENTS), F32),
    pltpu.VMEM((4, PADDED, ELEMENTS), F32),
    pltpu.VMEM((2 * PADDED, 2 * PADDED), BF16),
    FIELD,
    pltpu.VMEM((ITERS, 8, PADDED, ELEMENTS), F32),
    FIELD,
    pltpu.VMEM((ITERS * 4, 1, ELEMENTS), F32),
    pltpu.VMEM((2, GROUPS, 64, LANES), F32),
]


def split(value):
    high = value.astype(BF16)
    return high, (value - high.astype(F32)).astype(BF16)


def apply(t_ref, which, field):
    high, low = split(field)
    width = field.shape[1]
    if width == LANES:
        both = jnp.concatenate([high, low], axis=1)
        out = jnp.dot(t_ref[which], both, preferred_element_type=F32)
        return out[:HALF, :LANES] + out[:HALF, LANES:] + out[HALF:, :LANES]
    out = jnp.dot(t_ref[which], high, preferred_element_type=F32)
    out = out[:HALF] + out[HALF:]
    return out + jnp.dot(t_ref[which, :HALF], low, preferred_element_type=F32)


def parts_of(u_ref):
    out = []
    for odd in range(2):
        tiles = u_ref[odd].reshape(32, 2, 8, LANES)
        one, two = mix(tiles[:, 0], tiles[:, 1])
        out.append((one.reshape(HALF, LANES), two.reshape(HALF, LANES)))
    return out


def parts_to(out_ref, parts):
    for odd in range(2):
        real, imag = parts[odd]
        one, two = mix(real.reshape(32, 8, LANES), imag.reshape(32, 8, LANES))
        out_ref[odd] = jnp.stack([one, two], axis=1).reshape(64, 8, LANES)


def mode_rows(odd):
    row = lax.broadcasted_iota(jnp.int32, (HALF, LANES), 0)
    mode = 2 * ((row // 32 % 4 * 2 + row // 128) * 32 + row % 32) + odd
    fraction = mode.astype(F32) / MODES
    weight = jnp.where(mode == 0, 1.0 / PLANES, 2.0 / PLANES).astype(F32)
    sign = jnp.where(row % 2 == 0, 1.0, -1.0).astype(F32)
    return fraction, weight, sign


def first_row(shape):
    return lax.broadcasted_iota(jnp.int32, shape, 0) == 0


def to_planes(t_ref, cos_fields, sin_fields, out_ref):
    sign = mode_rows(0)[2][:, :1]
    cos_even, cos_odd = apply(t_ref, 0, cos_fields[0]), apply(t_ref, 1, cos_fields[1])
    sin_even, sin_odd = apply(t_ref, 2, sin_fields[0]), apply(t_ref, 3, sin_fields[1])
    quarter_cos = jnp.sum(sign * cos_fields[0], axis=0, keepdims=True)
    quarter_sin = jnp.sum(sign * sin_fields[1], axis=0, keepdims=True)
    cos, sin = cos_even + cos_odd, sin_even + sin_odd
    out_ref[0] = cos - sin
    out_ref[1] = cos + sin
    cos, sin = cos_even - cos_odd, sin_even - sin_odd
    out_ref[2] = cos + sin
    out_ref[3] = cos - sin
    out_ref[1, 0:1] = quarter_cos - quarter_sin
    out_ref[3, 0:1] = quarter_cos + quarter_sin


def from_planes(t_ref, values):
    shape = values[0].shape
    sign = mode_rows(0)[2][:, :1]
    first = first_row(shape)
    quarter, three = values[1][0:1], values[3][0:1]
    one = values[0]
    two = jnp.where(first, 0.0, values[1])
    four = jnp.where(first, 0.0, values[3])
    plus, minus = one + two, one - two
    plus_far, minus_far = values[2] + four, values[2] - four
    a_even = apply(t_ref, 4, plus + plus_far) + sign * (quarter + three)
    a_odd = apply(t_ref, 5, plus - plus_far)
    b_even = -apply(t_ref, 6, minus - minus_far)
    b_odd = -apply(t_ref, 7, minus + minus_far) - sign * (quarter - three)
    return (a_even, b_even), (a_odd, b_odd)


def state_planes(parts, t_ref, out_ref):
    cos_fields, sin_fields = [], []
    for odd in range(2):
        real, imag = parts[odd]
        fraction = mode_rows(odd)[0]
        cos_fields.append(jnp.concatenate([real, -fraction * imag], axis=1))
        sin_fields.append(jnp.concatenate([imag, fraction * real], axis=1))
    to_planes(t_ref, cos_fields, sin_fields, out_ref)


def first_stage(u_ref, t_ref, planes, out_ref):
    parts = parts_of(u_ref)
    state_planes(parts, t_ref, planes)
    values = [planes[at, :, :LANES] * planes[at, :, LANES:] for at in range(4)]
    found = from_planes(t_ref, values)
    out = []
    for odd in range(2):
        weight = mode_rows(odd)[1]
        out.append(tuple(parts[odd][c] - weight * found[odd][c] for c in range(2)))
    parts_to(out_ref, out)


def adjoint_planes(s_ref, t_ref, out_ref):
    parts = parts_of(s_ref)
    weights = [mode_rows(odd)[1] for odd in range(2)]
    to_planes(
        t_ref,
        [weights[odd] * parts[odd][0] for odd in range(2)],
        [weights[odd] * parts[odd][1] for odd in range(2)],
        out_ref,
    )


def finish(t_ref, s_ref, planes, adjoint, out_ref):
    values = []
    for at in range(4):
        factor = adjoint[at]
        values.append(planes[at] * jnp.concatenate([factor, factor], axis=1))
    found = from_planes(t_ref, values)
    parts = parts_of(s_ref)
    out = []
    for odd in range(2):
        fraction = mode_rows(odd)[0]
        a, b = found[odd]
        out.append(
            (
                parts[odd][0] - a[:, LANES:] - fraction * b[:, :LANES],
                parts[odd][1] - b[:, LANES:] + fraction * a[:, :LANES],
            )
        )
    parts_to(out_ref, out)


COUNT = N_MODE * N_MER
SPARE = GROUPS - 8


def send(source, target, mode, mer, sems, at):
    pltpu.make_async_remote_copy(
        src_ref=source,
        dst_ref=target,
        send_sem=sems[0].at[at],
        recv_sem=sems[1].at[at],
        device_id={"mode": mode, "mer": mer},
        device_id_type=pl.DeviceIdType.MESH,
    ).start()


def wait(blank, tiles, sem, rows=8):
    whole = blank.at[pl.ds(0, tiles), pl.ds(0, rows)]
    pltpu.make_async_copy(whole, whole, sem).wait()


def wait_either(double, blank, tiles_double, tiles_single, sem, rows=8):
    @pl.when(double)
    def _():
        wait(blank, tiles_double, sem, rows)

    @pl.when(jnp.logical_not(double))
    def _():
        wait(blank, tiles_single, sem, rows)


def place_at(mer, k):
    step = lax.rem(7 * k, N_MER)
    y = lax.rem(lax.rem(mer, 4) + lax.rem(step, 4), 4)
    z = lax.rem(mer // 4 + step // 4, 4)
    return z * 4 + y


def extra(x, mer):
    turn = lax.rem(lax.rem(mer, 4) + mer // 4, 4)
    return lax.rem(x + 4 - turn, 4)


def groups_on(mode, core):
    x = mode // 2
    return [2 * lax.rem(x + step, 4) + core for step in (1, 3, 2, 0)]


def each_group(mode, cores, act):
    for core in cores:
        one, two, three, own = groups_on(mode, core)
        act(one, core)
        act(two, core)
        act(three, core)

        @pl.when(lax.rem(mode, 2) != core)
        def _(own=own, core=core):
            act(own, core)


def each_place(mer, act):
    def body(k, _):
        act(place_at(mer, k))
        return 0

    lax.fori_loop(1, N_MER, body, 0)


def each_other(mode, mer, cores, act):
    groups = [(other, core) for core in cores for other in groups_on(mode, core)]

    def body(place):
        for other, core in groups:
            act(other, core, place)

    each_place(mer, body)
    each_group(mode, cores, lambda other, core: act(other, core, mer))


def order_of(mode):
    return lax.rem(mode, 2) * 4 + mode // 2


def program_kernel(
    state_ref,
    cotangent_hbm,
    mass_ref,
    inverse_ref,
    d_ref,
    t_hbm,
    out_hbm,
    cotangent_in,
    t_ref,
    copy_sems,
    rows,
    native_out,
    native_in,
    mode_out,
    mode_in,
    plane_out,
    plane_in,
    metric_out,
    metric_in,
    u_planes,
    planes,
    s_planes,
    ready,
    blank,
    send_sems,
    recv_sems,
    *solve_scratch,
):
    mode = lax.axis_index("mode")
    mer = lax.axis_index("mer")
    odd, eighth = mer // 8, lax.rem(mer, 8)
    row = order_of(mode) * 8 + eighth
    mine_extra = extra(mode // 2, mer)
    double = (lax.rem(mode, 2) == 0) & (mine_extra < SPARE)
    slots = jnp.where(double, 2, 1)
    sems = (send_sems, recv_sems)
    mass, diag, faces, k_ref = solve_scratch[:4]
    turn = solve_scratch[8]
    sent = []

    cotangent_copy = pltpu.make_async_copy(cotangent_hbm, cotangent_in, copy_sems.at[0])
    table_copy = pltpu.make_async_copy(t_hbm, t_ref, copy_sems.at[1])
    cotangent_copy.start()
    table_copy.start()
    barrier = pltpu.get_barrier_semaphore()

    def greet(semaphore, other, place):
        pl.semaphore_signal(
            semaphore,
            inc=1,
            device_id={"mode": other, "mer": place},
            device_id_type=pl.DeviceIdType.MESH,
        )

    each_group(mode, (0, 1), lambda other, core: greet(barrier, other, mer))
    each_place(mer, lambda place: greet(barrier, mode, place))
    native_to_tiles(state_ref, native_out.at[0], rows, turn)
    pl.semaphore_wait(barrier, N_MODE - 1 + N_MER - 1)
    each_group(mode, (0, 1), lambda other, core: greet(ready, other, mer))

    def each_slot(act):
        def body(k, _):
            act(slots - 1 - k)
            return 0

        lax.fori_loop(0, slots, body, 0)

    def send_to_planes(source, target, at, whole=False):
        def emit(core, half):
            if whole and half == 0:
                return
            rows = pl.ds(0, 8) if whole else pl.ds(4 * half, 4)

            def act(other, core, place):
                def single():
                    send(
                        source.at[0, other, place, rows],
                        target.at[0, odd, row, rows],
                        other,
                        place,
                        sems,
                        at + half,
                    )

                if core == 1:
                    single()
                    return
                owns_two = extra(other // 2, place) < SPARE
                pl.when(jnp.logical_not(owns_two))(single)

                @pl.when(owns_two)
                def _():
                    send(
                        source.at[:, other, place, rows],
                        target.at[:, odd, row, rows],
                        other,
                        place,
                        sems,
                        at + half,
                    )

            each_other(mode, mer, (core,), act)
            if core == 1:
                own = slice(0, 8) if whole else slice(4 * half, 4 * half + 4)
                target[:, odd, row, own] = source[:, mode, mer, own]

        for half in range(1 if whole else 0, 2):
            sent.append((at + half, 16 * GROUPS - 2, 16 * GROUPS - 1, 8 if whole else 4))
        return emit

    def wait_planes(at, whole=False):
        for half in range(1 if whole else 0, 2):
            sem = recv_sems.at[at + half]
            wait_either(double, blank, 2 * (COUNT - 1), COUNT - 1, sem, 8 if whole else 4)

    def send_to_modes(source, target, at, whole=False):
        target[0, mode, mer] = source[0, odd, row]

        @pl.when(double)
        def _():
            target[1, mode, mer] = source[1, odd, row]

        for half in range(1 if whole else 0, 2):
            rows = pl.ds(0, 8) if whole else pl.ds(4 * half, 4)

            def act(other, core, place, rows=rows, half=half):
                index = order_of(other) * 8 + lax.rem(place, 8)
                piece = source.at[0, place // 8, index, rows]
                send(piece, target.at[0, mode, mer, rows], other, place, sems, at + half)

            def act_double(other, core, place, rows=rows, half=half):
                index = order_of(other) * 8 + lax.rem(place, 8)
                piece = source.at[:, place // 8, index, rows]
                send(piece, target.at[:, mode, mer, rows], other, place, sems, at + half)

            @pl.when(double)
            def _(act_double=act_double):
                each_other(mode, mer, (0, 1), act_double)

            @pl.when(jnp.logical_not(double))
            def _(act=act):
                each_other(mode, mer, (0, 1), act)

            sent.append((at + half, 2 * (COUNT - 1), COUNT - 1, 8 if whole else 4))

    def wait_modes(at, half, rows=4):
        wait_either(
            double, blank, 16 * GROUPS - 2, 16 * GROUPS - 1, recv_sems.at[at + half], rows
        )

    mine = pl.ds(pl.multiple_of(order_of(mode) * 8, 8), 8)
    plane_in[0, 0, :, mine] = native_out[0, 0, mode]
    plane_in[0, 1, :, mine] = native_out[0, 1, mine_extra]

    def send_extra_state(other, core):
        index = extra(other // 2, mer)

        @pl.when(index < SPARE)
        def _():
            send(native_out.at[0, 1, index], plane_in.at[0, 1, :, mine], other, mer, sems, 0)

    def send_state(other, core):
        send(native_out.at[0, 0, other], plane_in.at[0, 0, :, mine], other, mer, sems, 0)

    each_group(mode, (0,), send_extra_state)
    each_group(mode, (0, 1), send_state)
    sent.append((0, N_MER * (GROUPS - 2), N_MER * (GROUPS - 1), 8))

    cotangent_copy.wait()
    native_to_tiles(cotangent_in, native_out.at[1], rows, turn)
    mode_in[0, 0, :, mer] = native_out[1, 0, :, odd, eighth]
    mode_in[0, 1, 0:SPARE, mer] = native_out[1, 1, 0:SPARE, odd, eighth]
    metric_rows(mass_ref, inverse_ref, rows, metric_out)
    metric_in[mer] = metric_out[...]

    def send_cotangent(place):
        which, at = place // 8, lax.rem(place, 8)
        send(native_out.at[1, 0, :, which, at], mode_in.at[0, 0, :, mer], mode, place, sems, 2)
        send(
            native_out.at[1, 1, 0:SPARE, which, at],
            mode_in.at[0, 1, 0:SPARE, mer],
            mode,
            place,
            sems,
            2,
        )
        send(metric_out, metric_in.at[mer], mode, place, sems, 3)

    each_place(mer, send_cotangent)
    sent.append((2, (N_MER - 1) * GROUPS, (N_MER - 1) * GROUPS, 8))
    sent.append((3, (N_MER - 1) * 4, (N_MER - 1) * 4, 8))

    stiffness_tables(d_ref, k_ref)
    table_copy.wait()

    wait_either(double, blank, 2 * (N_MODE - 1) * N_MER, (N_MODE - 1) * N_MER, recv_sems.at[0])

    def first(slot):
        first_stage(plane_in.at[0, slot], t_ref, u_planes.at[slot], plane_out.at[0, slot])

    each_slot(first)
    pl.semaphore_wait(ready, N_MODE - 1)
    send_to_modes(plane_out.at[0], mode_in.at[1], 4, whole=True)

    wait(blank, (N_MER - 1) * 4, recv_sems.at[3])
    metric_tables(metric_in, mode, mer, mass, diag, faces, turn)
    wait(blank, (N_MER - 1) * GROUPS, recv_sems.at[2])
    emit = send_to_planes(mode_out.at[0], plane_in.at[1], 6, whole=True)
    for half in range(2):
        solve(mode_in.at[0], mode_out.at[0], half, False, True, False, solve_scratch, emit)

    emit = send_to_planes(mode_out.at[1], plane_in.at[2], 8)
    wait_modes(4, 1, 8)
    for half in range(2):
        solve(mode_in.at[1], mode_out.at[1], half, True, False, True, solve_scratch, emit)

    def multiplier(slot):
        adjoint_planes(plane_in.at[1, slot], t_ref, s_planes.at[slot])

    wait_planes(6, whole=True)
    each_slot(multiplier)

    def second(slot):
        state_planes(parts_of(plane_in.at[2, slot]), t_ref, planes)
        finish(t_ref, plane_in.at[1, slot], planes, s_planes.at[slot], plane_out.at[1, slot])

    wait_planes(8)
    each_slot(second)
    send_to_modes(plane_out.at[1], mode_in.at[2], 10)

    emit = send_to_planes(mode_out.at[2], plane_in.at[3], 12)
    for half in range(2):
        wait_modes(10, half)
        solve(mode_in.at[2], mode_out.at[2], half, False, True, True, solve_scratch, emit)

    def third(slot):
        adjoint_planes(plane_in.at[3, slot], t_ref, s_planes.at[slot])
        finish(
            t_ref, plane_in.at[3, slot], u_planes.at[slot], s_planes.at[slot], plane_out.at[2, slot]
        )
        native_in[slot, mode] = plane_out[2, slot, :, mine]

        def send_gradient(other, core):
            theirs = pl.ds(pl.multiple_of(order_of(other) * 8, 8), 8)
            send(plane_out.at[2, slot, :, theirs], native_in.at[slot, mode], other, mer, sems, 14)

        each_group(mode, (0, 1), send_gradient)

    wait_planes(12)
    each_slot(third)
    sent.append((14, 2 * (N_MODE - 1) * N_MER, (N_MODE - 1) * N_MER, 8))
    wait_either(double, blank, N_MER * (GROUPS - 2), N_MER * (GROUPS - 1), recv_sems.at[14])
    turned = lax.rem(lax.rem(mer, 4) + mer // 4, 4)
    copies = [pltpu.make_async_copy(native_in.at[0], out_hbm.at[0:N_MODE], copy_sems.at[2])]
    for index in range(SPARE):
        owner = 2 * lax.rem(index + turned, 4)
        copies.append(
            pltpu.make_async_copy(
                native_in.at[1, owner], out_hbm.at[N_MODE + index], copy_sems.at[3 + index]
            )
        )
    for copy in copies:
        copy.start()
    for at, tiles_double, tiles_single, rows_each in sent:
        wait_either(double, blank, tiles_double, tiles_single, send_sems.at[at], rows_each)
    for copy in copies:
        copy.wait()


def program(state, cotangent, mass, inverse, derivative, table):
    by_mode = (2, N_MODE, N_MER, 8, LANES)
    by_native = (2, N_MODE, 2, 8, 8, LANES)
    by_plane = (2, 2, COUNT // 2, 8, LANES)
    vmem = pl.BlockSpec(memory_space=pltpu.VMEM)
    hbm = pl.BlockSpec(memory_space=pl.ANY)

    def scratch(count, shape):
        return pltpu.VMEM((count,) + shape, F32)

    return pl.pallas_call(
        program_kernel,
        out_shape=jax.ShapeDtypeStruct((GROUPS, 2, 8, 8, LANES), F32),
        in_specs=[vmem, hbm, vmem, vmem, vmem, hbm],
        out_specs=hbm,
        scratch_shapes=[
            pltpu.VMEM((NODE, NODE, ELEM_DEV * LANES), F32),
            pltpu.VMEM((8, 2 * HALF, HALF), BF16),
            pltpu.SemaphoreType.DMA((6,)),
            pltpu.VMEM((PADDED * ELEM_DEV, LANES), F32),
            scratch(2, by_native),
            pltpu.VMEM(by_native, F32),
            scratch(3, by_mode),
            scratch(3, by_mode),
            scratch(3, by_plane),
            scratch(4, by_plane),
            pltpu.VMEM((2, 16, LANES), F32),
            scratch(N_MER, (2, 16, LANES)),
            scratch(2, (4, HALF, 2 * LANES)),
            scratch(4, (HALF, 2 * LANES)),
            scratch(2, (4, HALF, LANES)),
            pltpu.SemaphoreType.REGULAR,
            pltpu.VMEM((2 * COUNT, 8, LANES), F32),
            pltpu.SemaphoreType.DMA((15,)),
            pltpu.SemaphoreType.DMA((15,)),
            *SOLVE_SCRATCH,
        ],
        compiler_params=pltpu.CompilerParams(
            collective_id=0, has_side_effects=True, vmem_limit_bytes=60 << 20
        ),
        name="program",
    )(state, cotangent, mass, inverse, derivative, table)


def shards(cotangent, checkpoint, mass, inv_radius_sq, derivative):
    table = jnp.asarray(tables())
    return tiles_to_native(program(checkpoint, cotangent, mass, inv_radius_sq, derivative, table))


def solution(mesh):
    return jax.shard_map(
        shards,
        mesh=mesh,
        in_specs=(
            P(None, None, ("mer", "mode")),
            P(None, None, ("mer", "mode")),
            P(None, None, "mer"),
            P(None, None, "mer"),
            P(),
        ),
        out_specs=P(None, None, ("mer", "mode")),
        check_vma=False,
    )
```

```python
import functools
import math

import jax
import jax.numpy as jnp
import ml_dtypes
import numpy as np
from jax import lax
from jax.experimental import pallas as pl
from jax.experimental.pallas import tpu as pltpu
from jax.sharding import PartitionSpec as P

NODE = 9
NODES = NODE * NODE
RADIAL = 8
ITERS = 4
MODES = 512
HALF = 256
PLANES = 1024
ELEMENTS = 256
N_MODE = 8
N_MER = 16
ELEM_DEV = 16
GROUPS = 11
PADDED = GROUPS * 8
LANES = 128
AZIMUTH_WEIGHT = 4.0
HIGHEST = lax.Precision.HIGHEST
F32 = jnp.float32
BF16 = jnp.bfloat16


def tables():
    order = np.arange(HALF).reshape(4, 2, HALF // N_MODE).transpose(1, 0, 2).reshape(-1)
    out = []
    for wave in (np.cos, np.sin):
        for odd in range(2):
            index = np.outer(np.arange(HALF), 2 * order + odd) % PLANES
            values = wave(index.astype(np.float64) * (2.0 * math.pi / PLANES)).astype(np.float32)
            high = values.astype(ml_dtypes.bfloat16)
            low = (values - high.astype(np.float32)).astype(ml_dtypes.bfloat16)
            out.append((high, low))
    both = [np.concatenate(pair) for pair in out]
    turned = [np.concatenate([high.T, low.T]) for high, low in out]
    return np.stack(both + turned)


def mix(first, second):
    shape = first.shape
    axis = len(shape) - 2
    low = lax.broadcasted_iota(jnp.int32, shape, axis) % 4 < 2
    return (
        jnp.where(low, first, pltpu.roll(second, 2, axis)),
        jnp.where(low, pltpu.roll(first, 6, axis), second),
    )


def exchange(tiles):
    tiles = list(tiles)
    axis = tiles[0].ndim - 1
    block = lax.broadcasted_iota(jnp.int32, tiles[0].shape, axis) // 16
    for bit in (1, 2, 4):
        clear = (block & bit) == 0
        for at in range(8):
            if at & bit:
                continue
            one, two = tiles[at], tiles[at | bit]
            tiles[at] = jnp.where(clear, one, pltpu.roll(two, 16 * bit, axis))
            tiles[at | bit] = jnp.where(clear, pltpu.roll(one, LANES - 16 * bit, axis), two)
    return tiles


def native_to_tiles(x_ref, out_ref, rows, turn):
    rows[pl.ds(NODES * ELEM_DEV, PADDED * ELEM_DEV - NODES * ELEM_DEV), :] = jnp.zeros(
        ((PADDED - NODES) * ELEM_DEV, LANES), F32
    )
    for i in range(NODE):
        for e in range(ELEM_DEV):
            rows[pl.ds(i * NODE * ELEM_DEV + e, NODE, stride=ELEM_DEV), :] = x_ref[
                i, :, e * LANES : (e + 1) * LANES
            ]
    for group in range(GROUPS):
        turned = rows[group * LANES : (group + 1) * LANES, :].T
        turn[0, group] = turned[:64]
        turn[1, group] = turned[64:]
        for odd in range(2):
            real = turn[0, group, pl.ds(odd, 32, stride=2), :].reshape(4, 8, LANES)
            imag = turn[1, group, pl.ds(odd, 32, stride=2), :].reshape(4, 8, LANES)
            one, two = mix(real, imag)
            out_ref[group // 8, group % 8, odd] = jnp.stack([one, two], axis=1).reshape(8, 8, LANES)


def tiles_to_native_kernel(t_hbm, out_hbm, tiles_in, rows, turn, native, in_sems, out_sems):
    parts = ((0, 6, 0, 5), (6, GROUPS, 5, NODE))
    loads, stores = [], []
    for at, (start, stop, first, last) in enumerate(parts):
        groups, nodes = pl.ds(start, stop - start), pl.ds(first, last - first)
        loads.append(
            pltpu.make_async_copy(t_hbm.at[groups], tiles_in.at[groups], in_sems.at[at])
        )
        stores.append(pltpu.make_async_copy(native.at[nodes], out_hbm.at[nodes], out_sems.at[at]))
        loads[at].start()
    for at, (start, stop, first, last) in enumerate(parts):
        loads[at].wait()
        for group in range(start, stop):
            for odd in range(2):
                tiles = tiles_in[group, odd].reshape(4, 2, 8, LANES)
                real, imag = mix(tiles[:, 0], tiles[:, 1])
                turn[0, group, pl.ds(odd, 32, stride=2), :] = real.reshape(32, LANES)
                turn[1, group, pl.ds(odd, 32, stride=2), :] = imag.reshape(32, LANES)
            both = jnp.concatenate([turn[0, group], turn[1, group]], axis=0)
            rows[group * LANES : (group + 1) * LANES, :] = both.T
        for i in range(first, last):
            for e in range(ELEM_DEV):
                native[i, :, e * LANES : (e + 1) * LANES] = rows[
                    pl.ds(i * NODE * ELEM_DEV + e, NODE, stride=ELEM_DEV), :
                ]
        stores[at].start()
    for store in stores:
        store.wait()


def tiles_to_native(tiles):
    hbm = pl.BlockSpec(memory_space=pltpu.HBM)
    shape = (NODE, NODE, ELEM_DEV * LANES)
    return pl.pallas_call(
        tiles_to_native_kernel,
        out_shape=jax.ShapeDtypeStruct(shape, F32),
        in_specs=[hbm],
        out_specs=hbm,
        scratch_shapes=[
            pltpu.VMEM((GROUPS, 2, 8, 8, LANES), F32),
            pltpu.VMEM((PADDED * ELEM_DEV, LANES), F32),
            pltpu.VMEM((2, GROUPS, 64, LANES), F32),
            pltpu.VMEM(shape, F32),
            pltpu.SemaphoreType.DMA((2,)),
            pltpu.SemaphoreType.DMA((2,)),
        ],
        compiler_params=pltpu.CompilerParams(vmem_limit_bytes=62 << 20),
        name="tiles_to_native",
    )(tiles)


def stiffness_tables(d_ref, k_ref):
    def dot(a, b):
        return jnp.dot(a, b, precision=HIGHEST, preferred_element_type=F32)

    derivative = d_ref[...]
    stiffness = lax.dot_general(
        derivative, derivative, (((0,), (0,)), ((), ())), precision=HIGHEST, preferred_element_type=F32
    )

    def pick(shape, node_axis, outer):
        node = lax.broadcasted_iota(jnp.int32, shape, node_axis)
        other = lax.broadcasted_iota(jnp.int32, shape, 1 - node_axis)
        place = node // NODE if outer else node % NODE
        return jnp.where((place == other) & (node < NODES), 1.0, 0.0).astype(F32)

    outer, inner = pick((PADDED, NODE), 0, True), pick((PADDED, NODE), 0, False)
    outer_t, inner_t = pick((NODE, PADDED), 1, True), pick((NODE, PADDED), 1, False)
    whole = dot(dot(outer, stiffness), outer_t) * dot(inner, inner_t)
    whole = whole + dot(dot(inner, stiffness), inner_t) * dot(outer, outer_t)
    high = whole.astype(BF16).astype(F32)
    low = whole - high
    top = jnp.concatenate([high, high], axis=1)
    bottom = jnp.concatenate([low, jnp.zeros_like(low)], axis=1)
    k_ref[...] = jnp.concatenate([top, bottom], axis=0).astype(BF16)


def metric_rows(mass_ref, inverse_ref, rows, out_ref):
    lane = lax.broadcasted_iota(jnp.int32, (ELEM_DEV, LANES), 1) % ELEM_DEV
    element = lax.broadcasted_iota(jnp.int32, (ELEM_DEV, LANES), 0)
    repeat = jnp.where(lane == element, 1.0, 0.0).astype(F32)
    shape = (PADDED, LANES)
    node = lax.broadcasted_iota(jnp.int32, shape, 0)
    block = lax.broadcasted_iota(jnp.int32, shape, 1) // ELEM_DEV
    keep = (node % 8 == block) & (node < NODES)
    for kind, ref in ((0, mass_ref), (1, inverse_ref)):
        for i in range(NODE):
            rows[i * NODE : (i + 1) * NODE, :ELEM_DEV] = ref[i]
        values = jnp.dot(
            rows[:PADDED, :ELEM_DEV], repeat, precision=HIGHEST, preferred_element_type=F32
        )
        values = jnp.where(keep, values, 0.0).reshape(GROUPS, 8, LANES)
        out_ref[kind, :GROUPS] = jnp.sum(values, axis=1)
        out_ref[kind, GROUPS:] = jnp.zeros((16 - GROUPS, LANES), F32)


def face_tables():
    node = np.arange(PADDED)[:, None]
    element = np.arange(ELEMENTS)[None, :]
    inside = node < NODES
    marks = [
        (node % NODE == NODE - 1) & (element < ELEMENTS - RADIAL) & inside,
        (node % NODE == 0) & (element >= RADIAL) & inside,
        (node // NODE == NODE - 1) & (element % RADIAL != RADIAL - 1) & inside,
        (node // NODE == 0) & (element % RADIAL != 0) & inside,
    ]
    marks = np.stack(marks).astype(np.float32)
    return np.concatenate([marks, marks.sum(axis=0, keepdims=True)])


def metric_tables(m_ref, mode_group, place, mass, diag, faces, turn):
    inverse = diag.at[0]
    for kind, out in ((0, mass), (1, inverse)):
        for h in range(2):
            rows = exchange([m_ref[8 * h + at, kind] for at in range(8)])
            for at in range(8):
                for group in range(GROUPS):
                    turn[h, group, at : at + 1] = rows[at][group : group + 1]
            for group in range(GROUPS):
                out[group * 8 : (group + 1) * 8, h * LANES : (h + 1) * LANES] = turn[h, group, 0:8]
    values = inverse[...]
    for n in range(4):
        offset = lax.rem(place, 8) // 2 * 8 + lax.rem(place, 2) * 2 + n // 2 * 4 + n % 2
        number = mode_group * 64 + 2 * offset + place // 8
        fraction = number.astype(F32) / MODES
        diag[n] = mass[...] * (1.0 + AZIMUTH_WEIGHT * fraction * fraction * values) + faces[4]


def owner_of(extra_group, place):
    return 2 * ((extra_group + place % 4 + place // 4) % 4)


PAIRS = (((0, 2), (4, 6), (8, 9), (10,)), ((1, 3), (5, 7)))


def load_tiles(b_ref, half, turn, weight, out, by_owner):
    rows = slice(4 * half, 4 * half + 4)

    def piece(group, place):
        if group < 8:
            return b_ref[0, group, place, rows]
        return b_ref[1, owner_of(group - 8, place) if by_owner else group - 8, place, rows]

    for at_pair, pair in enumerate(PAIRS[0] + PAIRS[1]):
        for h in range(2):
            tiles = []
            for place in range(8 * h, 8 * h + 8):
                tiles.append(
                    jnp.concatenate([piece(pair[0], place), piece(pair[-1], place)], axis=0)
                )
            tiles = exchange(tiles)
            for at in range(8):
                turn[h, at_pair, at * 8 : (at + 1) * 8] = tiles[at]
            lanes = slice(h * LANES, (h + 1) * LANES)
            for which, group in enumerate(pair):
                nodes = slice(group * 8, (group + 1) * 8)
                for s in range(4):
                    value = turn[h, at_pair, pl.ds(4 * which + s, 8, stride=8), :]
                    if weight is not None:
                        value = value * weight[nodes, lanes]
                    out[4 * half + s, nodes, lanes] = value


def store_tiles(value_of, half, turn, out_ref, emit):
    rows = slice(4 * half, 4 * half + 4)
    for core in range(2):
        for at_pair, pair in enumerate(PAIRS[core]):
            for h in range(2):
                lanes = slice(h * LANES, (h + 1) * LANES)
                for which, group in enumerate(pair):
                    for s in range(4):
                        turn[h, 4 * core + at_pair, pl.ds(4 * which + s, 8, stride=8), :] = value_of(
                            4 * half + s, slice(group * 8, (group + 1) * 8), lanes
                        )
                tiles = [turn[h, 4 * core + at_pair, at * 8 : (at + 1) * 8] for at in range(8)]
                tiles = exchange(tiles)
                for which, group in enumerate(pair):
                    for at in range(8):
                        place = 8 * h + at
                        owner = owner_of(group - 8, place) if group >= 8 else group
                        out_ref[group // 8, owner, place, rows] = tiles[at][
                            4 * which : 4 * which + 4
                        ]
        emit(core, half)


def total(parts):
    half = parts[:, :LANES] + parts[:, LANES:]
    return jnp.broadcast_to(jnp.sum(half, axis=(0, 1), keepdims=True), (1, ELEMENTS))


def fold(value):
    return jnp.sum(value.reshape(GROUPS, 8, ELEMENTS), axis=0)


def solve(b_ref, out_ref, half, weigh_in, weigh_out, by_owner, scratch, emit):
    mass, diag, faces, k_ref, r, p, q, alphas, turn = scratch
    load_tiles(b_ref, half, turn, mass if weigh_in else None, r, by_owner)
    modes = (2 * half, 2 * half + 1)

    def rows_of(n):
        return (4 * half + n % 2, 4 * half + 2 + n % 2)

    def square(n):
        one, two = rows_of(n)
        return total(fold(r[one] * r[one]) + fold(r[two] * r[two]))

    norms = tuple(square(n) for n in modes)
    for n in modes:
        for s in rows_of(n):
            p[ITERS - 1, s] = jnp.zeros((PADDED, ELEMENTS), F32)
    empty = jnp.zeros((8, ELEMENTS), F32)

    def operate(sweep, before, n, beta, norm):
        curve = None
        for s in rows_of(n):
            now = r[s] + beta * p[before, s]
            p[sweep, s] = now
            high = now.astype(BF16).astype(F32)
            halves = jnp.concatenate([high, now - high], axis=0).astype(BF16)
            image = jnp.dot(k_ref[...], halves, preferred_element_type=F32)
            ahead = pltpu.roll(now[: PADDED - 8], ELEMENTS - RADIAL, 1)
            behind = pltpu.roll(now[8:], RADIAL, 1)
            image = (
                image[:PADDED]
                + image[PADDED:]
                + diag[n] * now
                - faces[0] * jnp.concatenate([empty, ahead], axis=0)
                - faces[1] * jnp.concatenate([behind, empty], axis=0)
            )
            outward = pltpu.roll(now[:16], ELEMENTS - 1, 1)
            inward = pltpu.roll(now[72:], 1, 1)
            image = jnp.concatenate(
                [
                    image[:16] - faces[3, :16] * inward,
                    image[16:72],
                    image[72:] - faces[2, 72:] * outward,
                ],
                axis=0,
            )
            q[s] = image
            part = fold(now * image)
            curve = part if curve is None else curve + part
        alpha = norm / total(curve)
        alphas[sweep * 4 + n] = alpha
        return alpha

    def reduce(n, alpha):
        part = None
        for s in rows_of(n):
            value = r[s] - alpha * q[s]
            r[s] = value
            add = fold(value * value)
            part = add if part is None else part + add
        return total(part)

    def sweep_body(sweep, carry):
        norms, betas = carry
        before = lax.rem(sweep + ITERS - 1, ITERS)
        step = [operate(sweep, before, n, betas[n % 2], norms[n % 2]) for n in modes]
        after = tuple(reduce(n, step[n % 2]) for n in modes)
        return after, tuple(after[n] / norms[n] for n in range(2))

    none = (jnp.zeros((1, ELEMENTS), F32),) * 2
    norms, betas = lax.fori_loop(0, ITERS - 1, sweep_body, (norms, none))
    for n in modes:
        operate(ITERS - 1, ITERS - 2, n, betas[n % 2], norms[n % 2])

    def value_of(s, rows, lanes):
        n = s // 4 * 2 + s % 2
        value = alphas[n, :, lanes] * p[0, s, rows, lanes]
        for sweep in range(1, ITERS):
            value = value + alphas[sweep * 4 + n, :, lanes] * p[sweep, s, rows, lanes]
        return value * mass[rows, lanes] if weigh_out else value

    store_tiles(value_of, half, turn, out_ref, emit)


FIELD = pltpu.VMEM((8, PADDED, ELEMENTS), F32)
SOLVE_SCRATCH = [
    pltpu.VMEM((PADDED, ELEMENTS), F32),
    pltpu.VMEM((4, PADDED, ELEMENTS), F32),
    pltpu.VMEM((5, PADDED, ELEMENTS), F32),
    pltpu.VMEM((2 * PADDED, 2 * PADDED), BF16),
    FIELD,
    pltpu.VMEM((ITERS, 8, PADDED, ELEMENTS), F32),
    FIELD,
    pltpu.VMEM((ITERS * 4, 1, ELEMENTS), F32),
    pltpu.VMEM((2, GROUPS, 64, LANES), F32),
]


def split(value):
    high = value.astype(BF16)
    return high, (value - high.astype(F32)).astype(BF16)


def apply(t_ref, which, field):
    high, low = split(field)
    width = field.shape[1]
    if width == LANES:
        both = jnp.concatenate([high, low], axis=1)
        out = jnp.dot(t_ref[which], both, preferred_element_type=F32)
        return out[:HALF, :LANES] + out[:HALF, LANES:] + out[HALF:, :LANES]
    out = jnp.dot(t_ref[which], high, preferred_element_type=F32)
    out = out[:HALF] + out[HALF:]
    return out + jnp.dot(t_ref[which, :HALF], low, preferred_element_type=F32)


def parts_of(u_ref):
    out = []
    for odd in range(2):
        tiles = u_ref[odd].reshape(32, 2, 8, LANES)
        one, two = mix(tiles[:, 0], tiles[:, 1])
        out.append((one.reshape(HALF, LANES), two.reshape(HALF, LANES)))
    return out


def parts_to(out_ref, parts):
    for odd in range(2):
        real, imag = parts[odd]
        one, two = mix(real.reshape(32, 8, LANES), imag.reshape(32, 8, LANES))
        out_ref[odd] = jnp.stack([one, two], axis=1).reshape(64, 8, LANES)


def column_tables():
    row = np.arange(HALF)
    modes = [2 * ((row // 32 % 4 * 2 + row // 128) * 32 + row % 32) + odd for odd in range(2)]
    columns = [mode / MODES for mode in modes]
    columns += [np.where(mode == 0, 1.0 / PLANES, 2.0 / PLANES) for mode in modes]
    columns.append(np.where(row % 2 == 0, 1.0, -1.0))
    return np.repeat(np.stack(columns).astype(np.float32)[:, :, None], LANES, axis=2)


def signs(c_ref, width):
    return jnp.concatenate([c_ref[4]] * (width // LANES), axis=1)


def without_first(value):
    head = lax.broadcasted_iota(jnp.int32, (8, value.shape[1]), 0) == 0
    return jnp.concatenate([jnp.where(head, 0.0, value[:8]), value[8:]], axis=0)


def to_planes(t_ref, c_ref, cos_fields, sin_fields, out_ref):
    sign = signs(c_ref, cos_fields[0].shape[1])
    cos_even, cos_odd = apply(t_ref, 0, cos_fields[0]), apply(t_ref, 1, cos_fields[1])
    sin_even, sin_odd = apply(t_ref, 2, sin_fields[0]), apply(t_ref, 3, sin_fields[1])
    quarter_cos = jnp.sum(sign * cos_fields[0], axis=0, keepdims=True)
    quarter_sin = jnp.sum(sign * sin_fields[1], axis=0, keepdims=True)
    cos, sin = cos_even + cos_odd, sin_even + sin_odd
    out_ref[0] = cos - sin
    out_ref[1] = cos + sin
    cos, sin = cos_even - cos_odd, sin_even - sin_odd
    out_ref[2] = cos + sin
    out_ref[3] = cos - sin
    out_ref[1, 0:1] = quarter_cos - quarter_sin
    out_ref[3, 0:1] = quarter_cos + quarter_sin


def from_planes(t_ref, c_ref, values):
    sign = signs(c_ref, values[0].shape[1])
    quarter, three = values[1][0:1], values[3][0:1]
    one = values[0]
    two, four = without_first(values[1]), without_first(values[3])
    plus, minus = one + two, one - two
    plus_far, minus_far = values[2] + four, values[2] - four
    a_even = apply(t_ref, 4, plus + plus_far) + sign * (quarter + three)
    a_odd = apply(t_ref, 5, plus - plus_far)
    b_even = -apply(t_ref, 6, minus - minus_far)
    b_odd = -apply(t_ref, 7, minus + minus_far) - sign * (quarter - three)
    return (a_even, b_even), (a_odd, b_odd)


def state_planes(parts, t_ref, c_ref, out_ref):
    cos_fields, sin_fields = [], []
    for odd in range(2):
        real, imag = parts[odd]
        fraction = c_ref[odd]
        cos_fields.append(jnp.concatenate([real, -fraction * imag], axis=1))
        sin_fields.append(jnp.concatenate([imag, fraction * real], axis=1))
    to_planes(t_ref, c_ref, cos_fields, sin_fields, out_ref)


def first_stage(u_ref, t_ref, c_ref, planes, out_ref):
    parts = parts_of(u_ref)
    state_planes(parts, t_ref, c_ref, planes)
    values = [planes[at, :, :LANES] * planes[at, :, LANES:] for at in range(4)]
    found = from_planes(t_ref, c_ref, values)
    out = []
    for odd in range(2):
        weight = c_ref[2 + odd]
        out.append(tuple(parts[odd][c] - weight * found[odd][c] for c in range(2)))
    parts_to(out_ref, out)


def adjoint_planes(s_ref, t_ref, c_ref, out_ref):
    parts = parts_of(s_ref)
    weights = [c_ref[2 + odd] for odd in range(2)]
    to_planes(
        t_ref,
        c_ref,
        [weights[odd] * parts[odd][0] for odd in range(2)],
        [weights[odd] * parts[odd][1] for odd in range(2)],
        out_ref,
    )


def finish(t_ref, c_ref, s_ref, planes, adjoint, out_ref):
    values = []
    for at in range(4):
        factor = adjoint[at]
        values.append(planes[at] * jnp.concatenate([factor, factor], axis=1))
    found = from_planes(t_ref, c_ref, values)
    parts = parts_of(s_ref)
    out = []
    for odd in range(2):
        fraction = c_ref[odd]
        a, b = found[odd]
        out.append(
            (
                parts[odd][0] - a[:, LANES:] - fraction * b[:, :LANES],
                parts[odd][1] - b[:, LANES:] + fraction * a[:, :LANES],
            )
        )
    parts_to(out_ref, out)


COUNT = N_MODE * N_MER
SPARE = GROUPS - 8


def send(source, target, mode, mer, sems, at):
    pltpu.make_async_remote_copy(
        src_ref=source,
        dst_ref=target,
        send_sem=sems[0].at[at],
        recv_sem=sems[1].at[at],
        device_id={"mode": mode, "mer": mer},
        device_id_type=pl.DeviceIdType.MESH,
    ).start()


def wait(blank, tiles, sem, rows=8):
    whole = blank.at[pl.ds(0, tiles), pl.ds(0, rows)]
    pltpu.make_async_copy(whole, whole, sem).wait()


def wait_either(double, blank, tiles_double, tiles_single, sem, rows=8):
    @pl.when(double)
    def _():
        wait(blank, tiles_double, sem, rows)

    @pl.when(jnp.logical_not(double))
    def _():
        wait(blank, tiles_single, sem, rows)


def place_at(mer, k):
    step = lax.rem(7 * k, N_MER)
    y = lax.rem(lax.rem(mer, 4) + lax.rem(step, 4), 4)
    z = lax.rem(mer // 4 + step // 4, 4)
    return z * 4 + y


def extra(x, mer):
    turn = lax.rem(lax.rem(mer, 4) + mer // 4, 4)
    return lax.rem(x + 4 - turn, 4)


def groups_on(mode, core):
    x = mode // 2
    return [2 * lax.rem(x + step, 4) + core for step in (1, 3, 2, 0)]


def each_group(mode, cores, act):
    for core in cores:
        one, two, three, own = groups_on(mode, core)
        act(one, core)
        act(two, core)
        act(three, core)

        @pl.when(lax.rem(mode, 2) != core)
        def _(own=own, core=core):
            act(own, core)


def each_place(mer, act):
    def body(k, _):
        act(place_at(mer, k))
        return 0

    lax.fori_loop(1, N_MER, body, 0)


def each_other(mode, mer, cores, act):
    groups = [(other, core) for core in cores for other in groups_on(mode, core)]

    def body(place):
        for other, core in groups:
            act(other, core, place)

    each_place(mer, body)
    each_group(mode, cores, lambda other, core: act(other, core, mer))


def order_of(mode):
    return lax.rem(mode, 2) * 4 + mode // 2


def program_kernel(
    state_ref,
    cotangent_hbm,
    mass_ref,
    inverse_ref,
    d_ref,
    t_hbm,
    c_hbm,
    f_hbm,
    out_hbm,
    cotangent_in,
    t_ref,
    copy_sems,
    rows,
    native_out,
    native_in,
    mode_out,
    mode_in,
    plane_out,
    plane_in,
    metric_out,
    metric_in,
    u_planes,
    planes,
    s_planes,
    c_ref,
    ready,
    blank,
    send_sems,
    recv_sems,
    *solve_scratch,
):
    mode = lax.axis_index("mode")
    mer = lax.axis_index("mer")
    odd, eighth = mer // 8, lax.rem(mer, 8)
    row = order_of(mode) * 8 + eighth
    mine_extra = extra(mode // 2, mer)
    double = (lax.rem(mode, 2) == 0) & (mine_extra < SPARE)
    slots = jnp.where(double, 2, 1)
    sems = (send_sems, recv_sems)
    mass, diag, faces, k_ref = solve_scratch[:4]
    turn = solve_scratch[8]
    sent = []

    cotangent_copy = pltpu.make_async_copy(cotangent_hbm, cotangent_in, copy_sems.at[0])
    table_copy = pltpu.make_async_copy(t_hbm, t_ref, copy_sems.at[1])
    cotangent_copy.start()
    table_copy.start()
    constant_copies = [
        pltpu.make_async_copy(c_hbm, c_ref, copy_sems.at[6]),
        pltpu.make_async_copy(f_hbm, faces, copy_sems.at[7]),
    ]
    for copy in constant_copies:
        copy.start()
    barrier = pltpu.get_barrier_semaphore()

    def greet(semaphore, other, place):
        pl.semaphore_signal(
            semaphore,
            inc=1,
            device_id={"mode": other, "mer": place},
            device_id_type=pl.DeviceIdType.MESH,
        )

    each_group(mode, (0, 1), lambda other, core: greet(barrier, other, mer))
    each_place(mer, lambda place: greet(barrier, mode, place))
    native_to_tiles(state_ref, native_out.at[0], rows, turn)
    pl.semaphore_wait(barrier, N_MODE - 1 + N_MER - 1)
    each_group(mode, (0, 1), lambda other, core: greet(ready, other, mer))

    def each_slot(act):
        def body(k, _):
            act(slots - 1 - k)
            return 0

        lax.fori_loop(0, slots, body, 0)

    def send_to_planes(source, target, at, whole=False):
        def emit(core, half):
            if whole and half == 0:
                return
            rows = pl.ds(0, 8) if whole else pl.ds(4 * half, 4)

            def act(other, core, place):
                def single():
                    send(
                        source.at[0, other, place, rows],
                        target.at[0, odd, row, rows],
                        other,
                        place,
                        sems,
                        at + half,
                    )

                if core == 1:
                    single()
                    return
                owns_two = extra(other // 2, place) < SPARE
                pl.when(jnp.logical_not(owns_two))(single)

                @pl.when(owns_two)
                def _():
                    send(
                        source.at[:, other, place, rows],
                        target.at[:, odd, row, rows],
                        other,
                        place,
                        sems,
                        at + half,
                    )

            each_other(mode, mer, (core,), act)
            if core == 1:
                own = slice(0, 8) if whole else slice(4 * half, 4 * half + 4)
                target[:, odd, row, own] = source[:, mode, mer, own]

        for half in range(1 if whole else 0, 2):
            sent.append((at + half, 16 * GROUPS - 2, 16 * GROUPS - 1, 8 if whole else 4))
        return emit

    def wait_planes(at, whole=False):
        for half in range(1 if whole else 0, 2):
            sem = recv_sems.at[at + half]
            wait_either(double, blank, 2 * (COUNT - 1), COUNT - 1, sem, 8 if whole else 4)

    def send_to_modes(source, target, at, whole=False):
        target[0, mode, mer] = source[0, odd, row]

        @pl.when(double)
        def _():
            target[1, mode, mer] = source[1, odd, row]

        for half in range(1 if whole else 0, 2):
            rows = pl.ds(0, 8) if whole else pl.ds(4 * half, 4)

            def act(other, core, place, rows=rows, half=half):
                index = order_of(other) * 8 + lax.rem(place, 8)
                piece = source.at[0, place // 8, index, rows]
                send(piece, target.at[0, mode, mer, rows], other, place, sems, at + half)

            def act_double(other, core, place, rows=rows, half=half):
                index = order_of(other) * 8 + lax.rem(place, 8)
                piece = source.at[:, place // 8, index, rows]
                send(piece, target.at[:, mode, mer, rows], other, place, sems, at + half)

            @pl.when(double)
            def _(act_double=act_double):
                each_other(mode, mer, (0, 1), act_double)

            @pl.when(jnp.logical_not(double))
            def _(act=act):
                each_other(mode, mer, (0, 1), act)

            sent.append((at + half, 2 * (COUNT - 1), COUNT - 1, 8 if whole else 4))

    def wait_modes(at, half, rows=4):
        wait_either(
            double, blank, 16 * GROUPS - 2, 16 * GROUPS - 1, recv_sems.at[at + half], rows
        )

    mine = pl.ds(pl.multiple_of(order_of(mode) * 8, 8), 8)
    plane_in[0, 0, :, mine] = native_out[0, 0, mode]
    plane_in[0, 1, :, mine] = native_out[0, 1, mine_extra]

    def send_extra_state(other, core):
        index = extra(other // 2, mer)

        @pl.when(index < SPARE)
        def _():
            send(native_out.at[0, 1, index], plane_in.at[0, 1, :, mine], other, mer, sems, 0)

    def send_state(other, core):
        send(native_out.at[0, 0, other], plane_in.at[0, 0, :, mine], other, mer, sems, 0)

    each_group(mode, (0,), send_extra_state)
    each_group(mode, (0, 1), send_state)
    sent.append((0, N_MER * (GROUPS - 2), N_MER * (GROUPS - 1), 8))

    cotangent_copy.wait()
    native_to_tiles(cotangent_in, native_out.at[1], rows, turn)
    mode_in[0, 0, :, mer] = native_out[1, 0, :, odd, eighth]
    mode_in[0, 1, 0:SPARE, mer] = native_out[1, 1, 0:SPARE, odd, eighth]
    metric_rows(mass_ref, inverse_ref, rows, metric_out)
    metric_in[mer] = metric_out[...]

    def send_cotangent(place):
        which, at = place // 8, lax.rem(place, 8)
        send(native_out.at[1, 0, :, which, at], mode_in.at[0, 0, :, mer], mode, place, sems, 2)
        send(
            native_out.at[1, 1, 0:SPARE, which, at],
            mode_in.at[0, 1, 0:SPARE, mer],
            mode,
            place,
            sems,
            2,
        )
        send(metric_out, metric_in.at[mer], mode, place, sems, 3)

    each_place(mer, send_cotangent)
    sent.append((2, (N_MER - 1) * GROUPS, (N_MER - 1) * GROUPS, 8))
    sent.append((3, (N_MER - 1) * 4, (N_MER - 1) * 4, 8))

    stiffness_tables(d_ref, k_ref)
    table_copy.wait()
    for copy in constant_copies:
        copy.wait()

    wait_either(double, blank, 2 * (N_MODE - 1) * N_MER, (N_MODE - 1) * N_MER, recv_sems.at[0])

    def first(slot):
        first_stage(plane_in.at[0, slot], t_ref, c_ref, u_planes.at[slot], plane_out.at[0, slot])

    each_slot(first)
    pl.semaphore_wait(ready, N_MODE - 1)
    send_to_modes(plane_out.at[0], mode_in.at[1], 4, whole=True)

    wait(blank, (N_MER - 1) * 4, recv_sems.at[3])
    metric_tables(metric_in, mode, mer, mass, diag, faces, turn)
    wait(blank, (N_MER - 1) * GROUPS, recv_sems.at[2])
    emit = send_to_planes(mode_out.at[0], plane_in.at[1], 6, whole=True)
    for half in range(2):
        solve(mode_in.at[0], mode_out.at[0], half, False, True, False, solve_scratch, emit)

    emit = send_to_planes(mode_out.at[1], plane_in.at[2], 8)
    wait_modes(4, 1, 8)
    for half in range(2):
        solve(mode_in.at[1], mode_out.at[1], half, True, False, True, solve_scratch, emit)

    def multiplier(slot):
        adjoint_planes(plane_in.at[1, slot], t_ref, c_ref, s_planes.at[slot])

    wait_planes(6, whole=True)
    each_slot(multiplier)

    def second(slot):
        state_planes(parts_of(plane_in.at[2, slot]), t_ref, c_ref, planes)
        finish(t_ref, c_ref, plane_in.at[1, slot], planes, s_planes.at[slot], plane_out.at[1, slot])

    wait_planes(8)
    each_slot(second)
    send_to_modes(plane_out.at[1], mode_in.at[2], 10)

    emit = send_to_planes(mode_out.at[2], plane_in.at[3], 12)
    for half in range(2):
        wait_modes(10, half)
        solve(mode_in.at[2], mode_out.at[2], half, False, True, True, solve_scratch, emit)

    def third(slot):
        adjoint_planes(plane_in.at[3, slot], t_ref, c_ref, s_planes.at[slot])
        finish(
            t_ref, c_ref, plane_in.at[3, slot], u_planes.at[slot], s_planes.at[slot], plane_out.at[2, slot]
        )
        native_in[slot, mode] = plane_out[2, slot, :, mine]

        def send_gradient(other, core):
            theirs = pl.ds(pl.multiple_of(order_of(other) * 8, 8), 8)
            send(plane_out.at[2, slot, :, theirs], native_in.at[slot, mode], other, mer, sems, 14)

        each_group(mode, (0, 1), send_gradient)

    wait_planes(12)
    each_slot(third)
    sent.append((14, 2 * (N_MODE - 1) * N_MER, (N_MODE - 1) * N_MER, 8))
    wait_either(double, blank, N_MER * (GROUPS - 2), N_MER * (GROUPS - 1), recv_sems.at[14])
    turned = lax.rem(lax.rem(mer, 4) + mer // 4, 4)
    copies = [pltpu.make_async_copy(native_in.at[0], out_hbm.at[0:N_MODE], copy_sems.at[2])]
    for index in range(SPARE):
        owner = 2 * lax.rem(index + turned, 4)
        copies.append(
            pltpu.make_async_copy(
                native_in.at[1, owner], out_hbm.at[N_MODE + index], copy_sems.at[3 + index]
            )
        )
    for copy in copies:
        copy.start()
    for at, tiles_double, tiles_single, rows_each in sent:
        wait_either(double, blank, tiles_double, tiles_single, send_sems.at[at], rows_each)
    for copy in copies:
        copy.wait()


def program(state, cotangent, mass, inverse, derivative, *constants):
    by_mode = (2, N_MODE, N_MER, 8, LANES)
    by_native = (2, N_MODE, 2, 8, 8, LANES)
    by_plane = (2, 2, COUNT // 2, 8, LANES)
    vmem = pl.BlockSpec(memory_space=pltpu.VMEM)
    hbm = pl.BlockSpec(memory_space=pl.ANY)

    def scratch(count, shape):
        return pltpu.VMEM((count,) + shape, F32)

    return pl.pallas_call(
        program_kernel,
        out_shape=jax.ShapeDtypeStruct((GROUPS, 2, 8, 8, LANES), F32),
        in_specs=[vmem, hbm, vmem, vmem, vmem, hbm, hbm, hbm],
        out_specs=hbm,
        scratch_shapes=[
            pltpu.VMEM((NODE, NODE, ELEM_DEV * LANES), F32),
            pltpu.VMEM((8, 2 * HALF, HALF), BF16),
            pltpu.SemaphoreType.DMA((8,)),
            pltpu.VMEM((PADDED * ELEM_DEV, LANES), F32),
            scratch(2, by_native),
            pltpu.VMEM(by_native, F32),
            scratch(3, by_mode),
            scratch(3, by_mode),
            scratch(3, by_plane),
            scratch(4, by_plane),
            pltpu.VMEM((2, 16, LANES), F32),
            scratch(N_MER, (2, 16, LANES)),
            scratch(2, (4, HALF, 2 * LANES)),
            scratch(4, (HALF, 2 * LANES)),
            scratch(2, (4, HALF, LANES)),
            scratch(5, (HALF, LANES)),
            pltpu.SemaphoreType.REGULAR,
            pltpu.VMEM((2 * COUNT, 8, LANES), F32),
            pltpu.SemaphoreType.DMA((15,)),
            pltpu.SemaphoreType.DMA((15,)),
            *SOLVE_SCRATCH,
        ],
        compiler_params=pltpu.CompilerParams(
            collective_id=0, has_side_effects=True, vmem_limit_bytes=60 << 20
        ),
        name="program",
    )(state, cotangent, mass, inverse, derivative, *constants)


def shards(cotangent, checkpoint, mass, inv_radius_sq, derivative):
    constants = [jnp.asarray(values()) for values in (tables, column_tables, face_tables)]
    return tiles_to_native(
        program(checkpoint, cotangent, mass, inv_radius_sq, derivative, *constants)
    )


def solution(mesh):
    return jax.shard_map(
        shards,
        mesh=mesh,
        in_specs=(
            P(None, None, ("mer", "mode")),
            P(None, None, ("mer", "mode")),
            P(None, None, "mer"),
            P(None, None, "mer"),
            P(),
        ),
        out_specs=P(None, None, ("mer", "mode")),
        check_vma=False,
    )
```
